32 devices in a mesh: gx: 8 (over z, x), gy: 4 (over y, core).
Axes of the slice: x: 2, y: 2, z: 4, core: 2. Of those that a mesh axis runs over, the one named last changes fastest.
Arguments:
- depth: float32 [1024, 2048], P('gx', 'gy'), may hold values from 0.3 to 1.2
- momentum_x: float32 [1024, 2048], P('gx', 'gy'), may hold values from -3 to 3
- momentum_y: float32 [1024, 2048], P('gx', 'gy'), may hold values from -3 to 3
- bed: float32 [1024, 2048], P('gx', 'gy'), may hold values from -1 to 1
- wet: int32 [1024, 2048], P('gx', 'gy'), may hold values 0 or 1
Outputs:
- new_depth: float32 [1024, 2048], P('gx', 'gy')
- velocity_x: float32 [1024, 2048], P('gx', 'gy')
- velocity_y: float32 [1024, 2048], P('gx', 'gy')
The draws below stay inside these ranges and needn't reach their ends.
All inputs are finite; a program needn't handle non-finite values. No bound on the sum of `wet` on one device may be relied on, other than what follows from the above.
Results may differ from the reference program's by a relative error of at most 0.0013.
Values sent between devices are 32-bit elements; how exact they have to be, the bound alone decides.
No kernel may reach another device: no remote copies, remote signals or barrier semaphores. Data moves between devices by JAX's collectives and lax.ppermute only.
A program may use at most 64 MiB of HBM per device.

```python
import jax
import jax.numpy as jnp
from jax import lax

CY = 512
NX = 1024
NY = 2048
N_GY = 4


def set_ends(values, rng, smallest, top_value):
    dims = values.shape
    place = [jax.random.randint(jax.random.fold_in(rng, axis), (), 0, dims[axis]) for axis in range(len(dims))]
    values = values.at[tuple(place)].set(smallest)
    longest = dims.index(max(dims))
    place[longest] = (place[longest] + 1) % dims[longest]
    return values.at[tuple(place)].set(top_value)


def shard_levels(key, extent, pieces, smallest, largest):
    level, own = 1.0, jax.random.fold_in(key, 6)
    for dim, parts in pieces:
        heights = jnp.exp(jax.random.uniform(jax.random.fold_in(own, dim), (parts,), jnp.float32, smallest / len(pieces), largest / len(pieces)))
        level = level * jnp.repeat(heights, extent[dim] // parts).reshape([-1 if axis == dim else 1 for axis in range(len(extent))])
    return level


def noise(key, dims, scale, bound, pieces=(), kind=jnp.bfloat16):
    drawn = scale * jax.random.normal(key, dims, jnp.float32)
    if pieces:
        drawn = drawn * shard_levels(key, dims, pieces, -0.22, 0.18)
    return jnp.clip(drawn, -bound, bound).astype(kind)


def setup_inputs(seed: int = 0) -> dict:
    arg_keys = jax.random.split(jax.random.key(seed), 6)
    return {
        "depth": jnp.clip(0.3 + 0.90000004 * jax.random.uniform(arg_keys[0], (NX, NY), jnp.float32) ** shard_levels(arg_keys[0], (NX, NY), ((0, 8), (1, 4)), -0.2, 0.2), 0.3, 1.2),
        "momentum_x": noise(arg_keys[1], (NX, NY), 0.5, 3.0, ((0, 8), (1, 4)), jnp.float32),
        "momentum_y": noise(arg_keys[2], (NX, NY), 0.5, 3.0, ((0, 8), (1, 4)), jnp.float32),
        "bed": jnp.clip(jax.random.uniform(arg_keys[3], (NX, NY), jnp.float32, -1.0, 1.0) * shard_levels(arg_keys[3], (NX, NY), ((0, 8), (1, 4)), -0.4, 0.0), -1.0, 1.0),
        "wet": set_ends((jax.random.randint(arg_keys[4], (NX, NY), 0, 8) < 7).astype(jnp.int32), jax.random.fold_in(arg_keys[4], 1), 0, 1),
    }


gravity = 9.81
ratio_x = 0.05
ratio_y = 0.05

def minmod(left, right):
    return 0.5 * (jnp.sign(left) + jnp.sign(right)) * jnp.minimum(jnp.abs(left), jnp.abs(right))

def window(values, start, stop, line_axis):
    return lax.slice_in_dim(values, start, stop, axis=line_axis)

def physical(height, normal, across):
    speed_n = normal / height
    fluxes = (normal, normal * speed_n + 0.5 * gravity * height * height, across * speed_n)
    return (fluxes, jnp.abs(speed_n) + jnp.sqrt(gravity * height))

def face_terms(depth, normal, across, wet_cells, line_axis):
    length = depth.shape[line_axis]
    states = (depth, normal, across)
    slopes = [minmod(window(field, 1, length - 1, line_axis) - window(field, 0, length - 2, line_axis), window(field, 2, length, line_axis) - window(field, 1, length - 1, line_axis)) for field in states]
    lefts = [window(field, 1, length - 2, line_axis) + 0.5 * window(slope, 0, length - 3, line_axis) for field, slope in zip(states, slopes)]
    rights = [window(field, 2, length - 1, line_axis) - 0.5 * window(slope, 1, length - 2, line_axis) for field, slope in zip(states, slopes)]
    opened = window(wet_cells, 1, length - 2, line_axis) * window(wet_cells, 2, length - 1, line_axis)
    safe_left = jnp.where(opened > 0.5, lefts[0], 1.0)
    safe_right = jnp.where(opened > 0.5, rights[0], 1.0)
    flux_left, speed_left = physical(safe_left, lefts[1], lefts[2])
    flux_right, speed_right = physical(safe_right, rights[1], rights[2])
    fastest = jnp.maximum(speed_left, speed_right)
    result = []
    for flux_a, flux_b, state_a, state_b in zip(flux_left, flux_right, lefts, rights):
        face = opened * (0.5 * (flux_a + flux_b) - 0.5 * fastest * (state_b - state_a))
        count = face.shape[line_axis]
        result.append(window(face, 1, count, line_axis) - window(face, 0, count - 1, line_axis))
    return result

def predict(padded):
    along_x = padded[:, :, 2:-2]
    along_y = padded[:, 2:-2, :]
    center = padded[:, 2:-2, 2:-2]
    depth, flow_x, flow_y, wet_cells = (center[0], center[1], center[2], center[4])
    mass_x, normal_x, shear_x = face_terms(along_x[0], along_x[1], along_x[2], along_x[4], 0)
    mass_y, normal_y, shear_y = face_terms(along_y[0], along_y[2], along_y[1], along_y[4], 1)
    bed_x = 0.5 * (along_x[3, 3:-1] - along_x[3, 1:-3])
    bed_y = 0.5 * (along_y[3, :, 3:-1] - along_y[3, :, 1:-3])
    new_depth = depth - wet_cells * (ratio_x * mass_x + ratio_y * mass_y)
    push_x = wet_cells * (flow_x - ratio_x * normal_x - ratio_y * shear_y - ratio_x * gravity * depth * bed_x)
    push_y = wet_cells * (flow_y - ratio_x * shear_x - ratio_y * normal_y - ratio_y * gravity * depth * bed_y)
    return (new_depth, push_x, push_y)

def thomas(coefficient, right):

    def forward(carry, row):
        prev_upper, prev_right = carry
        coef_row, right_row = row
        denom = 1.0 + 2.0 * coef_row + coef_row * prev_upper
        upper_new = -coef_row / denom
        right_new = (right_row + coef_row * prev_right) / denom
        return ((upper_new, right_new), (upper_new, right_new))
    zeros = jnp.zeros(right.shape[1:], jnp.float32)
    carry_end, (uppers, rights) = lax.scan(forward, (zeros, zeros), (coefficient, right))

    def backward(after_value, row):
        upper_row, right_row = row
        value = right_row - upper_row * after_value
        return (value, value)
    last_value, solved = lax.scan(backward, zeros, (uppers, rights), reverse=True)
    return solved

def reference(depth, momentum_x, momentum_y, bed, wet):
    stacked = jnp.stack([depth, momentum_x, momentum_y, bed, wet.astype(jnp.float32)])
    padded = jnp.pad(stacked, ((0, 0), (2, 2), (2, 2)))

    def one_block(index):
        block = lax.dynamic_slice_in_dim(padded, index * CY, CY + 4, axis=2)
        return jnp.stack(predict(block))
    blocks = lax.map(one_block, jnp.arange(N_GY, dtype=jnp.int32))
    fields = jnp.transpose(blocks, (1, 2, 0, 3)).reshape(3, NX, NY)
    scale_x = (NX / 4.0) ** 2 / 3.0
    scale_y = (NY / 4.0) ** 2 / 3.0
    coef_x = scale_x * depth * depth
    coef_y = scale_y * depth * depth
    flux_u = thomas(coef_x, fields[1])
    flux_v = thomas(coef_y.T, fields[2].T).T
    return (fields[0], flux_u / depth, flux_v / depth)
```

```python
import jax
import jax.numpy as jnp
from jax import lax
from jax.sharding import PartitionSpec as P

gravity = 9.81
ratio_x = 0.05
ratio_y = 0.05


def with_halo(block, sides, width):
    for axis, dim in sides:
        count = lax.axis_size(axis)
        forward = [(i, i + 1) for i in range(count - 1)]
        backward = [(target, source) for source, target in forward]
        low = lax.ppermute(
            lax.slice_in_dim(block, block.shape[dim] - width, None, axis=dim), axis, forward
        )
        high = lax.ppermute(lax.slice_in_dim(block, 0, width, axis=dim), axis, backward)
        block = jnp.concatenate([low, block, high], axis=dim)
    return block


def minmod(left, right):
    return 0.5 * (jnp.sign(left) + jnp.sign(right)) * jnp.minimum(jnp.abs(left), jnp.abs(right))


def window(values, start, stop, line_axis):
    return lax.slice_in_dim(values, start, stop, axis=line_axis)


def physical(height, normal, across):
    speed_n = normal / height
    fluxes = (normal, normal * speed_n + 0.5 * gravity * height * height, across * speed_n)
    return (fluxes, jnp.abs(speed_n) + jnp.sqrt(gravity * height))


def face_terms(depth, normal, across, wet_cells, line_axis):
    length = depth.shape[line_axis]
    states = (depth, normal, across)
    slopes = [
        minmod(
            window(field, 1, length - 1, line_axis) - window(field, 0, length - 2, line_axis),
            window(field, 2, length, line_axis) - window(field, 1, length - 1, line_axis),
        )
        for field in states
    ]
    lefts = [
        window(field, 1, length - 2, line_axis) + 0.5 * window(slope, 0, length - 3, line_axis)
        for field, slope in zip(states, slopes)
    ]
    rights = [
        window(field, 2, length - 1, line_axis) - 0.5 * window(slope, 1, length - 2, line_axis)
        for field, slope in zip(states, slopes)
    ]
    opened = window(wet_cells, 1, length - 2, line_axis) * window(
        wet_cells, 2, length - 1, line_axis
    )
    safe_left = jnp.where(opened > 0.5, lefts[0], 1.0)
    safe_right = jnp.where(opened > 0.5, rights[0], 1.0)
    flux_left, speed_left = physical(safe_left, lefts[1], lefts[2])
    flux_right, speed_right = physical(safe_right, rights[1], rights[2])
    fastest = jnp.maximum(speed_left, speed_right)
    result = []
    for flux_a, flux_b, state_a, state_b in zip(flux_left, flux_right, lefts, rights):
        face = opened * (0.5 * (flux_a + flux_b) - 0.5 * fastest * (state_b - state_a))
        count = face.shape[line_axis]
        result.append(window(face, 1, count, line_axis) - window(face, 0, count - 1, line_axis))
    return result


def predict(padded):
    along_x = padded[:, :, 2:-2]
    along_y = padded[:, 2:-2, :]
    center = padded[:, 2:-2, 2:-2]
    depth, flow_x, flow_y, wet_cells = (center[0], center[1], center[2], center[4])
    mass_x, normal_x, shear_x = face_terms(along_x[0], along_x[1], along_x[2], along_x[4], 0)
    mass_y, normal_y, shear_y = face_terms(along_y[0], along_y[2], along_y[1], along_y[4], 1)
    bed_x = 0.5 * (along_x[3, 3:-1] - along_x[3, 1:-3])
    bed_y = 0.5 * (along_y[3, :, 3:-1] - along_y[3, :, 1:-3])
    new_depth = depth - wet_cells * (ratio_x * mass_x + ratio_y * mass_y)
    push_x = wet_cells * (
        flow_x - ratio_x * normal_x - ratio_y * shear_y - ratio_x * gravity * depth * bed_x
    )
    push_y = wet_cells * (
        flow_y - ratio_x * shear_x - ratio_y * normal_y - ratio_y * gravity * depth * bed_y
    )
    return (new_depth, push_x, push_y)


def earlier(values, stride, line_axis, fill):
    which = line_axis % values.ndim
    widths = [(0, 0)] * values.ndim
    widths[which] = (stride, 0)
    padded = jnp.pad(values, widths, constant_values=fill)
    return lax.slice_in_dim(padded, 0, values.shape[which], axis=which)


def later(values, stride, line_axis, fill):
    which = line_axis % values.ndim
    widths = [(0, 0)] * values.ndim
    widths[which] = (0, stride)
    padded = jnp.pad(values, widths, constant_values=fill)
    return lax.slice_in_dim(padded, stride, stride + values.shape[which], axis=which)


def eliminate(rows, below, above):
    lower, diagonal, upper, right = rows
    left_factor = lower / below[1]
    right_factor = upper / above[1]
    return (
        -left_factor * below[0],
        diagonal - left_factor * below[2] - right_factor * above[0],
        -right_factor * above[2],
        right - left_factor * below[3] - right_factor * above[3],
    )


def reduce_lines(lower, diagonal, upper, right, line_axis):
    count = diagonal.shape[line_axis % diagonal.ndim]
    rows = (lower, diagonal, upper, right)
    stride = 1
    while stride < count:
        below = tuple(
            (
                earlier(member, stride, line_axis, fill)
                for member, fill in zip(rows, (0.0, 1.0, 0.0, 0.0))
            )
        )
        above = tuple(
            (
                later(member, stride, line_axis, fill)
                for member, fill in zip(rows, (0.0, 1.0, 0.0, 0.0))
            )
        )
        rows = lax.optimization_barrier(eliminate(rows, below, above))
        stride *= 2
    return rows[3] / rows[1]


def separator_rows(last_six, next_three):
    solved_y, solved_g, solved_e, sep_coef, sep_diag, sep_right = last_six
    first_y, first_g, first_e = next_three
    return (
        -sep_coef * solved_g,
        sep_diag - sep_coef * solved_e - sep_coef * first_g,
        -sep_coef * first_e,
        sep_right + sep_coef * solved_y + sep_coef * first_y,
    )


def local_spikes(coefficient, right, line_axis):
    which = line_axis % 2
    count = coefficient.shape[which]
    inner = lax.slice_in_dim(coefficient, 0, count - 1, axis=which)
    position = lax.broadcasted_iota(jnp.int32, inner.shape, which)
    zeros = jnp.zeros_like(inner)
    sources = jnp.stack(
        [
            lax.slice_in_dim(right, 0, count - 1, axis=which),
            jnp.where(position == 0, inner, zeros),
            jnp.where(position == count - 2, inner, zeros),
        ]
    )
    solved = reduce_lines(-inner, 1.0 + 2.0 * inner, -inner, sources, line_axis)
    first = lax.index_in_dim(solved, 0, which + 1, keepdims=False)
    final = lax.index_in_dim(solved, count - 2, which + 1, keepdims=False)
    sep_coef = lax.index_in_dim(coefficient, count - 1, which, keepdims=False)
    sep_right = lax.index_in_dim(right, count - 1, which, keepdims=False)
    last_six = jnp.concatenate([final, jnp.stack([sep_coef, 1.0 + 2.0 * sep_coef, sep_right])])
    return (solved, first, last_six)


def assemble(solved, own, previous, line_axis):
    which = line_axis % 2
    own_wide = jnp.expand_dims(own, which)
    prev_wide = jnp.expand_dims(previous, which)
    inner = solved[0] + solved[1] * prev_wide + solved[2] * own_wide
    return jnp.concatenate([inner, own_wide], axis=which)


def pick_rows(whole, index):
    first_all = whole[:3]
    rows = separator_rows(whole[3:], later(first_all, 1, -2, 0.0))
    solved = reduce_lines(rows[0], rows[1], rows[2], rows[3], -2)
    own = lax.dynamic_index_in_dim(solved, index, 0, keepdims=False)
    previous = lax.dynamic_index_in_dim(earlier(solved, 1, -2, 0.0), index, 0, keepdims=False)
    return (own, previous)


def gather_line(packed, axis):
    copies = jnp.broadcast_to(packed[None], (lax.axis_size(axis), *packed.shape))
    whole = lax.all_to_all(copies, axis, split_axis=0, concat_axis=0)
    return jnp.swapaxes(whole, 0, 1)


def interface_x(first, last_six):
    packed = jnp.concatenate([first, last_six])
    whole = gather_line(packed, "gx")
    return pick_rows(whole, lax.axis_index("gx"))


def interface_y(first, last_six):
    packed = jnp.concatenate([first, last_six])
    whole = gather_line(packed, "gy")
    return pick_rows(whole, lax.axis_index("gy"))


def on_device(depth, momentum_x, momentum_y, bed, wet):
    stacked = jnp.stack([depth, momentum_x, momentum_y, bed, wet.astype(jnp.float32)])
    padded = with_halo(stacked, (("gx", 1), ("gy", 2)), 2)
    new_depth, push_x, push_y = predict(padded)
    cells_x = depth.shape[0] * lax.axis_size("gx")
    cells_y = depth.shape[1] * lax.axis_size("gy")
    scale_x = (cells_x / 4.0) ** 2 / 3.0
    scale_y = (cells_y / 4.0) ** 2 / 3.0
    coef_x = scale_x * depth * depth
    coef_y = scale_y * depth * depth
    solved_x, first_x, last_x = local_spikes(coef_x, push_x, -2)
    own_x, prev_x = interface_x(first_x, last_x)
    flux_u = assemble(solved_x, own_x, prev_x, -2)
    solved_y, first_y, last_y = local_spikes(coef_y, push_y, -1)
    own_y, prev_y = interface_y(first_y, last_y)
    flux_v = assemble(solved_y, own_y, prev_y, -1)
    return (new_depth, flux_u / depth, flux_v / depth)


def solution(mesh):
    placed = (P("gx", "gy"), P("gx", "gy"), P("gx", "gy"), P("gx", "gy"), P("gx", "gy"))
    return jax.shard_map(
        on_device,
        mesh=mesh,
        in_specs=placed,
        out_specs=(P("gx", "gy"), P("gx", "gy"), P("gx", "gy")),
        check_vma=False,
    )
```

```python
import jax
import jax.numpy as jnp
from jax import lax
from jax.sharding import PartitionSpec as P

gravity = 9.81
ratio_x = 0.05
ratio_y = 0.05


def with_halo(block, sides, width):
    for axis, dim in sides:
        count = lax.axis_size(axis)
        forward = [(i, i + 1) for i in range(count - 1)]
        backward = [(target, source) for source, target in forward]
        low = lax.ppermute(
            lax.slice_in_dim(block, block.shape[dim] - width, None, axis=dim), axis, forward
        )
        high = lax.ppermute(lax.slice_in_dim(block, 0, width, axis=dim), axis, backward)
        block = jnp.concatenate([low, block, high], axis=dim)
    return block


def minmod(left, right):
    return 0.5 * (jnp.sign(left) + jnp.sign(right)) * jnp.minimum(jnp.abs(left), jnp.abs(right))


def window(values, start, stop, line_axis):
    return lax.slice_in_dim(values, start, stop, axis=line_axis)


def physical(height, normal, across):
    speed_n = normal / height
    fluxes = (normal, normal * speed_n + 0.5 * gravity * height * height, across * speed_n)
    return (fluxes, jnp.abs(speed_n) + jnp.sqrt(gravity * height))


def face_terms(depth, normal, across, wet_cells, line_axis):
    length = depth.shape[line_axis]
    states = (depth, normal, across)
    slopes = [
        minmod(
            window(field, 1, length - 1, line_axis) - window(field, 0, length - 2, line_axis),
            window(field, 2, length, line_axis) - window(field, 1, length - 1, line_axis),
        )
        for field in states
    ]
    lefts = [
        window(field, 1, length - 2, line_axis) + 0.5 * window(slope, 0, length - 3, line_axis)
        for field, slope in zip(states, slopes)
    ]
    rights = [
        window(field, 2, length - 1, line_axis) - 0.5 * window(slope, 1, length - 2, line_axis)
        for field, slope in zip(states, slopes)
    ]
    opened = window(wet_cells, 1, length - 2, line_axis) * window(
        wet_cells, 2, length - 1, line_axis
    )
    safe_left = jnp.where(opened > 0.5, lefts[0], 1.0)
    safe_right = jnp.where(opened > 0.5, rights[0], 1.0)
    flux_left, speed_left = physical(safe_left, lefts[1], lefts[2])
    flux_right, speed_right = physical(safe_right, rights[1], rights[2])
    fastest = jnp.maximum(speed_left, speed_right)
    result = []
    for flux_a, flux_b, state_a, state_b in zip(flux_left, flux_right, lefts, rights):
        face = opened * (0.5 * (flux_a + flux_b) - 0.5 * fastest * (state_b - state_a))
        count = face.shape[line_axis]
        result.append(window(face, 1, count, line_axis) - window(face, 0, count - 1, line_axis))
    return result


def predict(padded):
    along_x = padded[:, :, 2:-2]
    along_y = padded[:, 2:-2, :]
    center = padded[:, 2:-2, 2:-2]
    depth, flow_x, flow_y, wet_cells = (center[0], center[1], center[2], center[4])
    mass_x, normal_x, shear_x = face_terms(along_x[0], along_x[1], along_x[2], along_x[4], 0)
    mass_y, normal_y, shear_y = face_terms(along_y[0], along_y[2], along_y[1], along_y[4], 1)
    bed_x = 0.5 * (along_x[3, 3:-1] - along_x[3, 1:-3])
    bed_y = 0.5 * (along_y[3, :, 3:-1] - along_y[3, :, 1:-3])
    new_depth = depth - wet_cells * (ratio_x * mass_x + ratio_y * mass_y)
    push_x = wet_cells * (
        flow_x - ratio_x * normal_x - ratio_y * shear_y - ratio_x * gravity * depth * bed_x
    )
    push_y = wet_cells * (
        flow_y - ratio_x * shear_x - ratio_y * normal_y - ratio_y * gravity * depth * bed_y
    )
    return (new_depth, push_x, push_y)


def earlier(values, stride, line_axis, fill):
    which = line_axis % values.ndim
    widths = [(0, 0)] * values.ndim
    widths[which] = (stride, 0)
    padded = jnp.pad(values, widths, constant_values=fill)
    return lax.slice_in_dim(padded, 0, values.shape[which], axis=which)


def later(values, stride, line_axis, fill):
    which = line_axis % values.ndim
    widths = [(0, 0)] * values.ndim
    widths[which] = (0, stride)
    padded = jnp.pad(values, widths, constant_values=fill)
    return lax.slice_in_dim(padded, stride, stride + values.shape[which], axis=which)


def eliminate(rows, below, above):
    lower, diagonal, upper, right = rows
    left_factor = lower / below[1]
    right_factor = upper / above[1]
    return (
        -left_factor * below[0],
        diagonal - left_factor * below[2] - right_factor * above[0],
        -right_factor * above[2],
        right - left_factor * below[3] - right_factor * above[3],
    )


def reduce_lines(lower, diagonal, upper, right, line_axis):
    count = diagonal.shape[line_axis % diagonal.ndim]
    rows = (lower, diagonal, upper, right)
    stride = 1
    while stride < count:
        below = tuple(
            (
                earlier(member, stride, line_axis, fill)
                for member, fill in zip(rows, (0.0, 1.0, 0.0, 0.0))
            )
        )
        above = tuple(
            (
                later(member, stride, line_axis, fill)
                for member, fill in zip(rows, (0.0, 1.0, 0.0, 0.0))
            )
        )
        rows = lax.optimization_barrier(eliminate(rows, below, above))
        stride *= 2
    return rows[3] / rows[1]


def separator_rows(last_six, next_three):
    solved_y, solved_g, solved_e, sep_coef, sep_diag, sep_right = last_six
    first_y, first_g, first_e = next_three
    return (
        -sep_coef * solved_g,
        sep_diag - sep_coef * solved_e - sep_coef * first_g,
        -sep_coef * first_e,
        sep_right + sep_coef * solved_y + sep_coef * first_y,
    )


def local_spikes(coefficient, right, line_axis):
    which = line_axis % 2
    count = coefficient.shape[which]
    inner = lax.slice_in_dim(coefficient, 0, count - 1, axis=which)
    position = lax.broadcasted_iota(jnp.int32, inner.shape, which)
    zeros = jnp.zeros_like(inner)
    sources = jnp.stack(
        [
            lax.slice_in_dim(right, 0, count - 1, axis=which),
            jnp.where(position == 0, inner, zeros),
            jnp.where(position == count - 2, inner, zeros),
        ]
    )
    solved = reduce_lines(-inner, 1.0 + 2.0 * inner, -inner, sources, line_axis)
    first = lax.index_in_dim(solved, 0, which + 1, keepdims=False)
    final = lax.index_in_dim(solved, count - 2, which + 1, keepdims=False)
    sep_coef = lax.index_in_dim(coefficient, count - 1, which, keepdims=False)
    sep_right = lax.index_in_dim(right, count - 1, which, keepdims=False)
    last_six = jnp.concatenate([final, jnp.stack([sep_coef, 1.0 + 2.0 * sep_coef, sep_right])])
    return (solved, first, last_six)


def assemble(solved, own, previous, line_axis):
    which = line_axis % 2
    own_wide = jnp.expand_dims(own, which)
    prev_wide = jnp.expand_dims(previous, which)
    inner = solved[0] + solved[1] * prev_wide + solved[2] * own_wide
    return jnp.concatenate([inner, own_wide], axis=which)


def pick_rows(whole, index):
    first_all = whole[:3]
    rows = separator_rows(whole[3:], later(first_all, 1, -2, 0.0))
    solved = reduce_lines(rows[0], rows[1], rows[2], rows[3], -2)
    own = lax.dynamic_index_in_dim(solved, index, 0, keepdims=False)
    previous = lax.dynamic_index_in_dim(earlier(solved, 1, -2, 0.0), index, 0, keepdims=False)
    return (own, previous)


def gather_sum(packed, axis):
    index = lax.axis_index(axis)
    place = lax.broadcasted_iota(jnp.int32, (1, lax.axis_size(axis), 1), 1)
    return lax.psum(jnp.where(place == index, packed[:, None, :], 0.0), axis)


def gather_direct(packed, axis):
    count = lax.axis_size(axis)
    index = lax.axis_index(axis)
    place = lax.broadcasted_iota(jnp.int32, (1, count, 1), 1)
    whole = jnp.where(place == index, packed[:, None, :], 0.0)
    for shift in range(1, count):
        pairs = [(i, (i + shift) % count) for i in range(count)]
        came = lax.ppermute(packed, axis, pairs)
        source = (index - shift) % count
        whole = jnp.where(place == source, came[:, None, :], whole)
    return whole


def interface_x(first, last_six):
    packed = jnp.concatenate([first, last_six])
    whole = gather_sum(packed, "gx")
    return pick_rows(whole, lax.axis_index("gx"))


def interface_y(first, last_six):
    packed = jnp.concatenate([first, last_six])
    whole = gather_direct(packed, "gy")
    return pick_rows(whole, lax.axis_index("gy"))


def on_device(depth, momentum_x, momentum_y, bed, wet):
    stacked = jnp.stack([depth, momentum_x, momentum_y, bed, wet.astype(jnp.float32)])
    padded = with_halo(stacked, (("gx", 1), ("gy", 2)), 2)
    new_depth, push_x, push_y = predict(padded)
    cells_x = depth.shape[0] * lax.axis_size("gx")
    cells_y = depth.shape[1] * lax.axis_size("gy")
    scale_x = (cells_x / 4.0) ** 2 / 3.0
    scale_y = (cells_y / 4.0) ** 2 / 3.0
    coef_x = scale_x * depth * depth
    coef_y = scale_y * depth * depth
    solved_x, first_x, last_x = local_spikes(coef_x, push_x, -2)
    own_x, prev_x = interface_x(first_x, last_x)
    flux_u = assemble(solved_x, own_x, prev_x, -2)
    solved_y, first_y, last_y = local_spikes(coef_y, push_y, -1)
    own_y, prev_y = interface_y(first_y, last_y)
    flux_v = assemble(solved_y, own_y, prev_y, -1)
    return (new_depth, flux_u / depth, flux_v / depth)


def solution(mesh):
    placed = (P("gx", "gy"), P("gx", "gy"), P("gx", "gy"), P("gx", "gy"), P("gx", "gy"))
    return jax.shard_map(
        on_device,
        mesh=mesh,
        in_specs=placed,
        out_specs=(P("gx", "gy"), P("gx", "gy"), P("gx", "gy")),
        check_vma=False,
    )
```

```python
import functools

import jax
import jax.numpy as jnp
from jax import lax
from jax.experimental import pallas as pl
from jax.experimental.pallas import tpu as pltpu
from jax.sharding import PartitionSpec as P

gravity = 9.81
ratio = 0.05
LANES = 128
SUB = 8
VMEM = pl.BlockSpec(memory_space=pltpu.VMEM)
ANY = pl.BlockSpec(memory_space=pl.ANY)
PARAMS = pltpu.CompilerParams(vmem_limit_bytes=24 * 1024 * 1024)


def lane_index(shape):
    return lax.broadcasted_iota(jnp.int32, shape, len(shape) - 1)


def row_index(shape):
    return lax.broadcasted_iota(jnp.int32, shape, len(shape) - 2)


def pack_kernel(h, p, q, b, m, xa, xb, ya, yb, top, bottom, left, right, itop, ibottom, ileft, iright, sems):
    rows, cols = h.shape
    copies = []
    for f, src in enumerate((h, p, q, b, m)):
        floats = f < 4
        spots = (
            (src.at[pl.ds(0, SUB), :], top.at[f] if floats else itop),
            (src.at[pl.ds(rows - SUB, SUB), :], bottom.at[f] if floats else ibottom),
            (src.at[:, pl.ds(0, LANES)], left.at[f] if floats else ileft),
            (src.at[:, pl.ds(cols - LANES, LANES)], right.at[f] if floats else iright),
        )
        for g, (piece, target) in enumerate(spots):
            copy = pltpu.make_async_copy(piece, target, sems.at[4 * f + g])
            copy.start()
            copies.append(copy)
    for copy in copies:
        copy.wait()
    first_x = jnp.concatenate(
        [top[0, 0:2, :], top[1, 0:2, :], top[2, 0:2, :], top[3, 0:1, :], itop[0:1, :].astype(jnp.float32)]
    )
    last_x = jnp.concatenate(
        [
            bottom[0, SUB - 2 : SUB, :],
            bottom[1, SUB - 2 : SUB, :],
            bottom[2, SUB - 2 : SUB, :],
            bottom[3, SUB - 1 : SUB, :],
            ibottom[SUB - 1 : SUB, :].astype(jnp.float32),
        ]
    )
    even_x = lax.axis_index("gx") % 2 == 0
    xa[...] = jnp.where(even_x, last_x, first_x)
    xb[...] = jnp.where(even_x, first_x, last_x)
    lane = lane_index((rows, LANES))

    def columns(block, imask, shifts):
        fields = [block[0], block[1], block[2], block[3], imask[...].astype(jnp.float32)]
        moved = [pltpu.roll(v, s, 1) if s else v for v, s in zip(fields, shifts)]
        out = moved[0]
        for start, v in zip((2, 4, 6, 7), moved[1:]):
            out = jnp.where(lane >= start, v, out)
        return out.T[0:SUB, :]

    first_y = columns(left, ileft, (0, 2, 4, 6, 7))
    last_y = columns(right, iright, (2, 4, 6, 7, 8))
    even_y = lax.axis_index("gy") % 2 == 0
    ya[...] = jnp.where(even_y, last_y, first_y)
    yb[...] = jnp.where(even_y, first_y, last_y)


def pack(h, p, q, b, m):
    rows, cols = h.shape
    f32, i32 = jnp.float32, jnp.int32
    slab_x = jax.ShapeDtypeStruct((SUB, cols), f32)
    slab_y = jax.ShapeDtypeStruct((SUB, rows), f32)
    return pl.pallas_call(
        pack_kernel,
        out_shape=(slab_x, slab_x, slab_y, slab_y),
        in_specs=[ANY] * 5,
        out_specs=(VMEM,) * 4,
        scratch_shapes=[
            pltpu.VMEM((4, SUB, cols), f32),
            pltpu.VMEM((4, SUB, cols), f32),
            pltpu.VMEM((4, rows, LANES), f32),
            pltpu.VMEM((4, rows, LANES), f32),
            pltpu.VMEM((SUB, cols), i32),
            pltpu.VMEM((SUB, cols), i32),
            pltpu.VMEM((rows, LANES), i32),
            pltpu.VMEM((rows, LANES), i32),
            pltpu.SemaphoreType.DMA((20,)),
        ],
        compiler_params=PARAMS,
        name="pack",
    )(h, p, q, b, m)


def low_high(axis, a, b):
    index, count = lax.axis_index(axis), lax.axis_size(axis)
    even = index % 2 == 0
    low = jnp.where(index > 0, jnp.where(even, b, a), 0.0)
    high = jnp.where(index < count - 1, jnp.where(even, a, b), 0.0)
    return low, high


def half_slope(a, c):
    return 0.5 * (jnp.maximum(jnp.minimum(a, c), 0.0) + jnp.minimum(jnp.maximum(a, c), 0.0))


def face_flux(left, right, opened):
    is_open = opened > 0.5
    hl = jnp.where(is_open, left[0], 1.0)
    hr = jnp.where(is_open, right[0], 1.0)
    joint = 1.0 / (hl * hr)
    ul = left[1] * (hr * joint)
    ur = right[1] * (hl * joint)
    gl = gravity * hl
    gr = gravity * hr
    fastest = jnp.maximum(jnp.abs(ul) + gl * lax.rsqrt(gl), jnp.abs(ur) + gr * lax.rsqrt(gr))
    scale = (0.5 * ratio) * opened
    mass = (left[1] + right[1]) - fastest * (right[0] - left[0])
    push = 0.5 * (gl * hl + gr * hr) + left[1] * ul + right[1] * ur - fastest * (right[1] - left[1])
    shear = left[2] * ul + right[2] * ur - fastest * (right[2] - left[2])
    return scale * mass, scale * push, scale * shear


def merge(one, two):
    t1, gl1, gr1, sl1, sr1 = one
    t2, gl2, gr2, sl2, sr2 = two
    shunt = gr1 + gl2
    inverse = 1.0 / (t1 + t2 + shunt)
    w1, w2 = t1 * inverse, t2 * inverse
    source = sr1 - sl2
    merged = (w1 * t2, gl1 + w1 * shunt, gr2 + w2 * shunt, sl1 - w1 * source, sr2 + w2 * source)
    return merged, (w1, w2, source * inverse)


def march_segments(steps, d_at, r_at):
    zero = jnp.zeros_like(d_at(0))
    alpha, gamma, beta, delta, c, e = zero, zero, zero, zero, zero, zero
    for k in range(steps):
        d = d_at(k)
        alpha = alpha + gamma
        gamma = gamma + d * (1.0 + alpha)
        beta = beta + delta
        delta = delta + d * ((k + 1.0) + beta)
        c = c + e
        e = e + (d * c - r_at(k))
    t = 1.0 / (steps + beta)
    sl = t * c
    return t, t * alpha, t * delta, sl, (1.0 + delta) * sl - e


def tree(segments):
    count = segments[0].shape[0]
    levels = []
    stride = 1
    while stride < count:
        after = tuple(pltpu.roll(v, count - stride, 0) for v in segments)
        segments, weights = merge(segments, after)
        levels.append(weights)
        stride *= 2
    return segments, levels


def tile_writes(tiled, whole, sems):
    rows, cols = whole.shape
    return [
        pltpu.make_async_copy(
            tiled.at[pl.ds(tile * rows, rows), :], whole.at[:, pl.ds(tile * LANES, LANES)], sems.at[tile]
        )
        for tile in range(cols // LANES)
    ]


def flux_kernel(
    h_ref, p_ref, q_ref, b_ref, m_ref, xa, xb, ya, yb,
    nd_ref, invh_ref, rx_ref, dyt_ref, ryt_ref, segx_ref, levx_ref, segy_ref, levy_ref, endx_ref, endy_ref,
    hs, ps, qs, bs, ms, nds, edge, edge_t, dperm, rperm, sems, out_sems,
    *, inv_cx, inv_cy,
):
    rows, cols = h_ref.shape
    steps = rows // SUB
    tiles = cols // LANES
    copies = []
    for f, (src, target) in enumerate(zip((h_ref, p_ref, q_ref, b_ref, m_ref), (hs, ps, qs, bs, ms))):
        for tile in range(tiles):
            copies.append(
                pltpu.make_async_copy(
                    src.at[:, pl.ds(tile * LANES, LANES)],
                    target.at[pl.ds(tile * rows, rows), :],
                    sems.at[f * tiles + tile],
                )
            )
            copies[-1].start()
    wide = cols + LANES
    low_x, high_x = low_high("gx", xa[...], xb[...])
    low_y, high_y = low_high("gy", ya[...], yb[...])
    edge[...] = jnp.zeros_like(edge)
    edge[126:128, :] = low_y[0:2]
    edge[0:2, :] = high_y[0:2]
    edge[122:124, :] = low_y[2:4]
    edge[124:126, :] = high_y[2:4]
    edge[118:120, :] = low_y[4:6]
    edge[120:122, :] = high_y[4:6]
    edge[115:116, :] = low_y[6:7]
    edge[116:117, :] = high_y[6:7]
    edge[111:112, :] = low_y[7:8]
    edge[112:113, :] = high_y[7:8]
    edge_t[...] = edge[...].T
    for copy in copies:
        copy.wait()

    def at(ref, k):
        return jnp.concatenate(
            [ref[pl.ds(tile * rows + k, SUB, stride=steps), :] for tile in range(tiles)], axis=1
        )

    sub = row_index((SUB, cols))

    def before(value, row):
        return jnp.where(sub == 0, row, pltpu.roll(value, 1, 0))

    def after(value, row):
        return jnp.where(sub == SUB - 1, row, pltpu.roll(value, SUB - 1, 0))

    field = []
    for ref, first in ((hs, 0), (ps, 2), (qs, 4)):
        w = {k: at(ref, k) for k in range(steps)}
        w[-1] = before(w[steps - 1], low_x[first + 1 : first + 2])
        w[-2] = before(w[steps - 2], low_x[first : first + 1])
        w[steps] = after(w[0], high_x[first : first + 1])
        w[steps + 1] = after(w[1], high_x[first + 1 : first + 2])
        field.append(w)
    bed = {k: at(bs, k) for k in range(steps)}
    bed[-1] = before(bed[steps - 1], low_x[6:7])
    bed[steps] = after(bed[0], high_x[6:7])
    wet = {k: at(ms, k).astype(jnp.float32) for k in range(steps)}
    wet[-1] = before(wet[steps - 1], low_x[7:8])
    wet[steps] = after(wet[0], high_x[7:8])

    def back(v):
        return pltpu.roll(v, 1, 1)

    def ahead(v):
        return pltpu.roll(v, wide - 1, 1)

    def x_states(k):
        pair = [half_slope(w[k] - w[k - 1], w[k + 1] - w[k]) for w in field]
        return [w[k] + s for w, s in zip(field, pair)], [w[k] - s for w, s in zip(field, pair)]

    def x_face(left, right, k):
        return face_flux(left, right, wet[k] * wet[k + 1])

    left_state, _ = x_states(-1)
    face_before = None
    for k in range(-1, steps):
        left_next, right_state = x_states(k + 1)
        face = x_face(left_state, right_state, k)
        left_state = left_next
        if k >= 0:
            dfx = [a - c for a, c in zip(face, face_before)]
            h, p, q, m = field[0][k], field[1][k], field[2][k], wet[k]
            side = edge_t[pl.ds(k, SUB, stride=steps), :]
            sides = [pltpu.roll(side, s, 1) if s else side for s in (0, 4, 8, 12, 16)]
            hw, pw, qw, bw, mw = (
                jnp.concatenate([v, t], axis=1) for v, t in zip((h, p, q, bed[k], m), sides)
            )
            lefts, rights = [], []
            for w in (hw, qw, pw):
                slope = w - back(w)
                half = half_slope(slope, ahead(slope))
                lefts.append(w + half)
                rights.append(ahead(w - half))
            faces = face_flux(lefts, rights, mw * ahead(mw))
            dgy = [(f - back(f))[:, :cols] for f in faces]
            bed_y = (ahead(bw) - back(bw))[:, :cols]
            bed_x = bed[k + 1] - bed[k - 1]
            pull = (0.5 * ratio * gravity) * h
            depth = h - m * (dfx[0] + dgy[0])
            for tile in range(tiles):
                nds[pl.ds(tile * rows + k, SUB, stride=steps), :] = depth[:, tile * LANES : (tile + 1) * LANES]
            px = m * (p - dfx[1] - dgy[2] - pull * bed_x)
            py = m * (q - dfx[2] - dgy[1] - pull * bed_y)
            inverse = 1.0 / h
            square = inverse * inverse
            here = slice(k * SUB, (k + 1) * SUB)
            invh_ref[here, :] = inverse
            rx_ref[here, :] = px * (inv_cx * square)
            dy = inv_cy * square
            dperm[here, :] = dy
            rperm[here, :] = py * dy
        face_before = face
    writes = tile_writes(nds, nd_ref, out_sems)
    for write in writes:
        write.start()

    def dx_at(k):
        inverse = invh_ref[k * SUB : (k + 1) * SUB, :]
        return inv_cx * (inverse * inverse)

    def rx_at(k):
        return rx_ref[k * SUB : (k + 1) * SUB, :]

    seg_x = march_segments(steps, dx_at, rx_at)
    ends, levels = tree(seg_x)
    for i, v in enumerate(seg_x[:2] + (seg_x[3],)):
        segx_ref[i] = v
    for i, weights in enumerate(levels):
        for j, v in enumerate(weights):
            levx_ref[3 * i + j] = v
    for i, v in enumerate(ends):
        endx_ref[i : i + 1, :] = v[0:1, :]
    endx_ref[5:8, :] = jnp.zeros((3, cols), jnp.float32)

    for tile in range(tiles):
        span = slice(tile * LANES, (tile + 1) * LANES)
        dyt_ref[span, :] = dperm[:, span].T
        ryt_ref[span, :] = rperm[:, span].T

    def gathered(ref, k):
        return jnp.concatenate(
            [ref[pl.ds(tile * LANES + k, SUB, stride=LANES // SUB), :] for tile in range(cols // LANES)]
        )

    seg_y = march_segments(LANES // SUB, lambda k: gathered(dyt_ref, k), lambda k: gathered(ryt_ref, k))
    ends, levels = tree(seg_y)
    for i, v in enumerate(seg_y[:2] + (seg_y[3],)):
        segy_ref[i] = v
    for i, weights in enumerate(levels):
        for j, v in enumerate(weights):
            levy_ref[3 * i + j] = v
    for i, v in enumerate(ends):
        endy_ref[i : i + 1, :] = v[0:1, :]
    endy_ref[5:8, :] = jnp.zeros((3, rows), jnp.float32)
    for write in writes:
        write.wait()


def log2(count):
    return (count - 1).bit_length()


def fluxes(h, p, q, b, m, slabs, inv_cx, inv_cy):
    rows, cols = h.shape
    segs = cols // LANES * SUB
    shapes = [
        (rows, cols),
        (rows, cols),
        (rows, cols),
        (cols, rows),
        (cols, rows),
        (3, SUB, cols),
        (3 * log2(SUB), SUB, cols),
        (3, segs, rows),
        (3 * log2(segs), segs, rows),
        (SUB, cols),
        (SUB, rows),
    ]
    return pl.pallas_call(
        functools.partial(flux_kernel, inv_cx=inv_cx, inv_cy=inv_cy),
        out_shape=tuple(jax.ShapeDtypeStruct(s, jnp.float32) for s in shapes),
        in_specs=[ANY] * 5 + [VMEM] * 4,
        out_specs=(ANY,) + (VMEM,) * (len(shapes) - 1),
        scratch_shapes=[
            *[pltpu.VMEM((cols // LANES * rows, LANES), v.dtype) for v in (h, p, q, b, m, h)],
            pltpu.VMEM((LANES, rows), jnp.float32),
            pltpu.VMEM((rows, LANES), jnp.float32),
            pltpu.VMEM((rows, cols), jnp.float32),
            pltpu.VMEM((rows, cols), jnp.float32),
            pltpu.SemaphoreType.DMA((5 * (cols // LANES),)),
            pltpu.SemaphoreType.DMA((cols // LANES,)),
        ],
        compiler_params=PARAMS,
        name="fluxes",
    )(h, p, q, b, m, *slabs)


def ordered(axis, stage, mine, theirs):
    is_low = (lax.axis_index(axis) >> stage) % 2 == 0
    rows = range(5)
    one = tuple(jnp.where(is_low, mine[i : i + 1, :], theirs[i : i + 1, :]) for i in rows)
    two = tuple(jnp.where(is_low, theirs[i : i + 1, :], mine[i : i + 1, :]) for i in rows)
    return is_low, merge(one, two)


def merge_kernel(*refs, axes, stage):
    count = len(axes)
    for axis, mine, theirs, out in zip(axes, refs[:count], refs[count : 2 * count], refs[2 * count :]):
        _, (merged, _) = ordered(axis, stage, mine, theirs)
        for i, v in enumerate(merged):
            out[i : i + 1, :] = v
        out[5:8, :] = jnp.zeros((3, out.shape[1]), jnp.float32)


def merge_call(axes, stage, mine, theirs):
    count = len(axes)
    return pl.pallas_call(
        functools.partial(merge_kernel, axes=axes, stage=stage),
        out_shape=tuple(jax.ShapeDtypeStruct(v.shape, v.dtype) for v in mine),
        in_specs=[VMEM] * (2 * count),
        out_specs=(VMEM,) * count,
        compiler_params=PARAMS,
        name="merge",
    )(*mine, *theirs)


def line_ends(axis, pairs):
    steps = []
    merged = None
    for stage, (mine, theirs) in enumerate(pairs):
        is_low, (merged, weights) = ordered(axis, stage, mine, theirs)
        steps.append((is_low, weights))
    t, _, gr, _, sr = merged
    left = jnp.zeros_like(t)
    right = sr / (t + gr + 1.0)
    for is_low, (w1, w2, source) in reversed(steps):
        middle = w1 * left + w2 * right + source
        left = jnp.where(is_low, left, middle)
        right = jnp.where(is_low, middle, right)
    return left, right


def segment_ends(left, right, lev_ref):
    shape = lev_ref.shape[1:]
    count = shape[0]
    at = row_index(shape)
    left = jnp.broadcast_to(left, shape)
    right = jnp.broadcast_to(right, shape)
    for level in reversed(range(log2(count))):
        stride = 1 << level
        middle = lev_ref[3 * level] * left + lev_ref[3 * level + 1] * right + lev_ref[3 * level + 2]
        upper = (at >> level) % 2 == 1
        left, right = (
            jnp.where(upper, pltpu.roll(middle, stride, 0), left),
            jnp.where(upper, pltpu.roll(right, stride, 0), middle),
        )
    return left, right


def solve_kernel(*refs, stages_x, stages_y, inv_cx):
    (invh_ref, rx_ref, dyt_ref, ryt_ref, segx_ref, levx_ref, segy_ref, levy_ref), refs = refs[:8], refs[8:]
    pairs_x, refs = refs[: 2 * stages_x], refs[2 * stages_x :]
    pairs_y, refs = refs[: 2 * stages_y], refs[2 * stages_y :]
    vx_ref, vy_ref, v_t, vxs, vys, sems_x, sems_y = refs
    rows, cols = vx_ref.shape
    steps = rows // SUB
    tiles = cols // LANES
    left, right = line_ends("gx", list(zip(pairs_x[0::2], pairs_x[1::2])))
    left, right = segment_ends(left, right, levx_ref)
    value = left
    change = segx_ref[0] * (right - left) - segx_ref[1] * left - segx_ref[2]
    for k in range(steps):
        here = slice(k * SUB, (k + 1) * SUB)
        inverse = invh_ref[here, :]
        value = value + change
        change = change + ((inv_cx * (inverse * inverse)) * value - rx_ref[here, :])
        speed = value * inverse
        for tile in range(tiles):
            vxs[pl.ds(tile * rows + k, SUB, stride=steps), :] = speed[:, tile * LANES : (tile + 1) * LANES]
    writes = tile_writes(vxs, vx_ref, sems_x)
    for write in writes:
        write.start()

    left, right = line_ends("gy", list(zip(pairs_y[0::2], pairs_y[1::2])))
    left, right = segment_ends(left, right, levy_ref)
    value = left
    change = segy_ref[0] * (right - left) - segy_ref[1] * left - segy_ref[2]
    jump = LANES // SUB
    for k in range(jump):
        spots = [pl.ds(tile * LANES + k, SUB, stride=jump) for tile in range(cols // LANES)]
        d = jnp.concatenate([dyt_ref[s, :] for s in spots])
        r = jnp.concatenate([ryt_ref[s, :] for s in spots])
        value = value + change
        change = change + (d * value - r)
        for tile, s in enumerate(spots):
            v_t[s, :] = value[tile * SUB : (tile + 1) * SUB, :]
    for tile, write in enumerate(tile_writes(vys, vy_ref, sems_y)):
        span = slice(tile * LANES, (tile + 1) * LANES)
        block = v_t[span, :].T * invh_ref[:, span]
        for k in range(steps):
            vys[pl.ds(tile * rows + k, SUB, stride=steps), :] = block[k * SUB : (k + 1) * SUB, :]
        write.start()
        writes.append(write)
    for write in writes:
        write.wait()


def solve(pieces, pairs_x, pairs_y, shape, inv_cx):
    rows, cols = shape
    flat_x = [v for pair in pairs_x for v in pair]
    flat_y = [v for pair in pairs_y for v in pair]
    out = jax.ShapeDtypeStruct(shape, jnp.float32)
    return pl.pallas_call(
        functools.partial(solve_kernel, stages_x=len(pairs_x), stages_y=len(pairs_y), inv_cx=inv_cx),
        out_shape=(out, out),
        in_specs=[VMEM] * (len(pieces) + len(flat_x) + len(flat_y)),
        out_specs=(ANY, ANY),
        scratch_shapes=[
            pltpu.VMEM((cols, rows), jnp.float32),
            pltpu.VMEM((cols // LANES * rows, LANES), jnp.float32),
            pltpu.VMEM((cols // LANES * rows, LANES), jnp.float32),
            pltpu.SemaphoreType.DMA((cols // LANES,)),
            pltpu.SemaphoreType.DMA((cols // LANES,)),
        ],
        compiler_params=PARAMS,
        name="solve",
    )(*pieces, *flat_x, *flat_y)


def swap(value, axis, offset):
    count = lax.axis_size(axis)
    other = [((i - offset) ^ 1) + offset for i in range(count)]
    return lax.ppermute(value, axis, [(i, o if 0 <= o < count else i) for i, o in enumerate(other)])


def cross(value, axis, stage):
    return lax.ppermute(value, axis, [(i, i ^ (1 << stage)) for i in range(lax.axis_size(axis))])


def on_device(h, p, q, b, m):
    rows, cols = h.shape
    count_x, count_y = lax.axis_size("gx"), lax.axis_size("gy")
    inv_cx = 3.0 / (rows * count_x / 4.0) ** 2
    inv_cy = 3.0 / (cols * count_y / 4.0) ** 2
    xa, xb, ya, yb = pack(h, p, q, b, m)
    slabs = (swap(xa, "gx", 0), swap(xb, "gx", 1), swap(ya, "gy", 0), swap(yb, "gy", 1))
    new_depth, *pieces, end_x, end_y = fluxes(h, p, q, b, m, slabs, inv_cx, inv_cy)
    stages = {"gx": log2(count_x), "gy": log2(count_y)}
    mine = {"gx": end_x, "gy": end_y}
    pairs = {"gx": [], "gy": []}
    for stage in range(max(stages.values())):
        axes = [a for a in ("gx", "gy") if stage < stages[a]]
        theirs = {a: cross(mine[a], a, stage) for a in axes}
        for a in axes:
            pairs[a].append((mine[a], theirs[a]))
        more = [a for a in axes if stage + 1 < stages[a]]
        if more:
            merged = merge_call(more, stage, [mine[a] for a in more], [theirs[a] for a in more])
            mine.update(zip(more, merged))
    vx, vy = solve(pieces, pairs["gx"], pairs["gy"], (rows, cols), inv_cx)
    return new_depth, vx, vy


def solution(mesh):
    spec = P("gx", "gy")
    return jax.shard_map(
        on_device,
        mesh=mesh,
        in_specs=(spec,) * 5,
        out_specs=(spec,) * 3,
        check_vma=False,
    )
```

```python
import functools

import jax
import jax.numpy as jnp
from jax import lax
from jax.experimental import pallas as pl
from jax.experimental.pallas import tpu as pltpu
from jax.sharding import PartitionSpec as P

gravity = 9.81
ratio = 0.05
LANES = 128
SUB = 8
VMEM = pl.BlockSpec(memory_space=pltpu.VMEM)
ANY = pl.BlockSpec(memory_space=pl.ANY)
HBM = pl.BlockSpec(memory_space=pltpu.HBM)
PARAMS = pltpu.CompilerParams(vmem_limit_bytes=24 * 1024 * 1024)


def lane_index(shape):
    return lax.broadcasted_iota(jnp.int32, shape, len(shape) - 1)


def row_index(shape):
    return lax.broadcasted_iota(jnp.int32, shape, len(shape) - 2)


def pack_kernel(h, p, q, b, m, xa, ya, top, bottom, left, right, itop, ibottom, ileft, iright, sems):
    rows, cols = h.shape
    copies = []
    for f, src in enumerate((h, p, q, b, m)):
        floats = f < 4
        spots = (
            (src.at[pl.ds(0, SUB), :], top.at[f] if floats else itop),
            (src.at[pl.ds(rows - SUB, SUB), :], bottom.at[f] if floats else ibottom),
            (src.at[:, pl.ds(0, LANES)], left.at[f] if floats else ileft),
            (src.at[:, pl.ds(cols - LANES, LANES)], right.at[f] if floats else iright),
        )
        for g, (piece, target) in enumerate(spots):
            copy = pltpu.make_async_copy(piece, target, sems.at[4 * f + g])
            copy.start()
            copies.append(copy)
    for copy in copies:
        copy.wait()
    first_x = jnp.concatenate(
        [top[0, 0:2, :], top[1, 0:2, :], top[2, 0:2, :], top[3, 0:1, :], itop[0:1, :].astype(jnp.float32)]
    )
    last_x = jnp.concatenate(
        [
            bottom[0, SUB - 2 : SUB, :],
            bottom[1, SUB - 2 : SUB, :],
            bottom[2, SUB - 2 : SUB, :],
            bottom[3, SUB - 1 : SUB, :],
            ibottom[SUB - 1 : SUB, :].astype(jnp.float32),
        ]
    )
    even_x = lax.axis_index("gx") % 2 == 0
    xa[0] = jnp.where(even_x, last_x, first_x)
    xa[1] = jnp.where(even_x, first_x, last_x)
    lane = lane_index((rows, LANES))

    def columns(block, imask, shifts):
        fields = [block[0], block[1], block[2], block[3], imask[...].astype(jnp.float32)]
        moved = [pltpu.roll(v, s, 1) if s else v for v, s in zip(fields, shifts)]
        out = moved[0]
        for start, v in zip((2, 4, 6, 7), moved[1:]):
            out = jnp.where(lane >= start, v, out)
        return out.T[0:SUB, :]

    first_y = columns(left, ileft, (0, 2, 4, 6, 7))
    last_y = columns(right, iright, (2, 4, 6, 7, 8))
    even_y = lax.axis_index("gy") % 2 == 0
    ya[0] = jnp.where(even_y, last_y, first_y)
    ya[1] = jnp.where(even_y, first_y, last_y)


def pack(h, p, q, b, m):
    rows, cols = h.shape
    f32, i32 = jnp.float32, jnp.int32
    slab_x = jax.ShapeDtypeStruct((2, SUB, cols), f32)
    slab_y = jax.ShapeDtypeStruct((2, SUB, rows), f32)
    return pl.pallas_call(
        pack_kernel,
        out_shape=(slab_x, slab_y),
        in_specs=[HBM] * 5,
        out_specs=(VMEM,) * 2,
        scratch_shapes=[
            pltpu.VMEM((4, SUB, cols), f32),
            pltpu.VMEM((4, SUB, cols), f32),
            pltpu.VMEM((4, rows, LANES), f32),
            pltpu.VMEM((4, rows, LANES), f32),
            pltpu.VMEM((SUB, cols), i32),
            pltpu.VMEM((SUB, cols), i32),
            pltpu.VMEM((rows, LANES), i32),
            pltpu.VMEM((rows, LANES), i32),
            pltpu.SemaphoreType.DMA((20,)),
        ],
        compiler_params=PARAMS,
        name="pack",
    )(h, p, q, b, m)


def low_high(axis, a, b):
    index, count = lax.axis_index(axis), lax.axis_size(axis)
    even = index % 2 == 0
    low = jnp.where(index > 0, jnp.where(even, b, a), 0.0)
    high = jnp.where(index < count - 1, jnp.where(even, a, b), 0.0)
    return low, high


def half_slope(a, c):
    return 0.5 * (jnp.maximum(jnp.minimum(a, c), 0.0) + jnp.minimum(jnp.maximum(a, c), 0.0))


def face_flux(left, right, opened):
    is_open = opened > 0.5
    hl = jnp.where(is_open, left[0], 1.0)
    hr = jnp.where(is_open, right[0], 1.0)
    joint = 1.0 / (hl * hr)
    ul = left[1] * (hr * joint)
    ur = right[1] * (hl * joint)
    gl = gravity * hl
    gr = gravity * hr
    fastest = jnp.maximum(jnp.abs(ul) + gl * lax.rsqrt(gl), jnp.abs(ur) + gr * lax.rsqrt(gr))
    scale = (0.5 * ratio) * opened
    mass = (left[1] + right[1]) - fastest * (right[0] - left[0])
    push = 0.5 * (gl * hl + gr * hr) + left[1] * ul + right[1] * ur - fastest * (right[1] - left[1])
    shear = left[2] * ul + right[2] * ur - fastest * (right[2] - left[2])
    return scale * mass, scale * push, scale * shear


def merge(one, two):
    t1, gl1, gr1, sl1, sr1 = one
    t2, gl2, gr2, sl2, sr2 = two
    shunt = gr1 + gl2
    inverse = 1.0 / (t1 + t2 + shunt)
    w1, w2 = t1 * inverse, t2 * inverse
    source = sr1 - sl2
    merged = (w1 * t2, gl1 + w1 * shunt, gr2 + w2 * shunt, sl1 - w1 * source, sr2 + w2 * source)
    return merged, (w1, w2, source * inverse)


def march_segments(steps, d_at, r_at):
    zero = jnp.zeros_like(d_at(0))
    alpha, gamma, beta, delta, c, e = zero, zero, zero, zero, zero, zero
    for k in range(steps):
        d = d_at(k)
        alpha = alpha + gamma
        gamma = gamma + d * (1.0 + alpha)
        beta = beta + delta
        delta = delta + d * ((k + 1.0) + beta)
        c = c + e
        e = e + (d * c - r_at(k))
    t = 1.0 / (steps + beta)
    sl = t * c
    return t, t * alpha, t * delta, sl, (1.0 + delta) * sl - e


def tree(segments):
    count = segments[0].shape[0]
    levels = []
    stride = 1
    while stride < count:
        after = tuple(pltpu.roll(v, count - stride, 0) for v in segments)
        segments, weights = merge(segments, after)
        levels.append(weights)
        stride *= 2
    return segments, levels


def tile_writes(tiled, whole, sems):
    rows, cols = whole.shape
    return [
        pltpu.make_async_copy(
            tiled.at[pl.ds(tile * rows, rows), :], whole.at[:, pl.ds(tile * LANES, LANES)], sems.at[tile]
        )
        for tile in range(cols // LANES)
    ]


def flux_kernel(
    h_ref, p_ref, q_ref, b_ref, m_ref, xa, xb, ya, yb,
    nd_ref, invh_ref, rx_ref, dyt_ref, ryt_ref, segx_ref, levx_ref, segy_ref, levy_ref, endx_ref, endy_ref,
    hs, ps, qs, bs, ms, nds, edge, edge_t, dperm, rperm, sems, out_sems,
    *, inv_cx, inv_cy,
):
    rows, cols = h_ref.shape
    steps = rows // SUB
    tiles = cols // LANES
    copies = []
    for f, (src, target) in enumerate(zip((h_ref, p_ref, q_ref, b_ref, m_ref), (hs, ps, qs, bs, ms))):
        for tile in range(tiles):
            copies.append(
                pltpu.make_async_copy(
                    src.at[:, pl.ds(tile * LANES, LANES)],
                    target.at[pl.ds(tile * rows, rows), :],
                    sems.at[f * tiles + tile],
                )
            )
            copies[-1].start()
    wide = cols + LANES
    low_x, high_x = low_high("gx", xa[...], xb[...])
    low_y, high_y = low_high("gy", ya[...], yb[...])
    edge[...] = jnp.zeros_like(edge)
    edge[126:128, :] = low_y[0:2]
    edge[0:2, :] = high_y[0:2]
    edge[122:124, :] = low_y[2:4]
    edge[124:126, :] = high_y[2:4]
    edge[118:120, :] = low_y[4:6]
    edge[120:122, :] = high_y[4:6]
    edge[115:116, :] = low_y[6:7]
    edge[116:117, :] = high_y[6:7]
    edge[111:112, :] = low_y[7:8]
    edge[112:113, :] = high_y[7:8]
    edge_t[...] = edge[...].T
    for copy in copies:
        copy.wait()

    def at(ref, k):
        return jnp.concatenate(
            [ref[pl.ds(tile * rows + k, SUB, stride=steps), :] for tile in range(tiles)], axis=1
        )

    sub = row_index((SUB, cols))

    def before(value, row):
        return jnp.where(sub == 0, row, pltpu.roll(value, 1, 0))

    def after(value, row):
        return jnp.where(sub == SUB - 1, row, pltpu.roll(value, SUB - 1, 0))

    field = []
    for ref, first in ((hs, 0), (ps, 2), (qs, 4)):
        w = {k: at(ref, k) for k in range(steps)}
        w[-1] = before(w[steps - 1], low_x[first + 1 : first + 2])
        w[-2] = before(w[steps - 2], low_x[first : first + 1])
        w[steps] = after(w[0], high_x[first : first + 1])
        w[steps + 1] = after(w[1], high_x[first + 1 : first + 2])
        field.append(w)
    bed = {k: at(bs, k) for k in range(steps)}
    bed[-1] = before(bed[steps - 1], low_x[6:7])
    bed[steps] = after(bed[0], high_x[6:7])
    wet = {k: at(ms, k).astype(jnp.float32) for k in range(steps)}
    wet[-1] = before(wet[steps - 1], low_x[7:8])
    wet[steps] = after(wet[0], high_x[7:8])

    def back(v):
        return pltpu.roll(v, 1, 1)

    def ahead(v):
        return pltpu.roll(v, wide - 1, 1)

    def x_states(k):
        pair = [half_slope(w[k] - w[k - 1], w[k + 1] - w[k]) for w in field]
        return [w[k] + s for w, s in zip(field, pair)], [w[k] - s for w, s in zip(field, pair)]

    def x_face(left, right, k):
        return face_flux(left, right, wet[k] * wet[k + 1])

    left_state, _ = x_states(-1)
    face_before = None
    for k in range(-1, steps):
        left_next, right_state = x_states(k + 1)
        face = x_face(left_state, right_state, k)
        left_state = left_next
        if k >= 0:
            dfx = [a - c for a, c in zip(face, face_before)]
            h, p, q, m = field[0][k], field[1][k], field[2][k], wet[k]
            side = edge_t[pl.ds(k, SUB, stride=steps), :]
            sides = [pltpu.roll(side, s, 1) if s else side for s in (0, 4, 8, 12, 16)]
            hw, pw, qw, bw, mw = (
                jnp.concatenate([v, t], axis=1) for v, t in zip((h, p, q, bed[k], m), sides)
            )
            lefts, rights = [], []
            for w in (hw, qw, pw):
                slope = w - back(w)
                half = half_slope(slope, ahead(slope))
                lefts.append(w + half)
                rights.append(ahead(w - half))
            faces = face_flux(lefts, rights, mw * ahead(mw))
            dgy = [(f - back(f))[:, :cols] for f in faces]
            bed_y = (ahead(bw) - back(bw))[:, :cols]
            bed_x = bed[k + 1] - bed[k - 1]
            pull = (0.5 * ratio * gravity) * h
            depth = h - m * (dfx[0] + dgy[0])
            for tile in range(tiles):
                nds[pl.ds(tile * rows + k, SUB, stride=steps), :] = depth[:, tile * LANES : (tile + 1) * LANES]
            px = m * (p - dfx[1] - dgy[2] - pull * bed_x)
            py = m * (q - dfx[2] - dgy[1] - pull * bed_y)
            inverse = 1.0 / h
            square = inverse * inverse
            here = slice(k * SUB, (k + 1) * SUB)
            invh_ref[here, :] = inverse
            rx_ref[here, :] = px * (inv_cx * square)
            dy = inv_cy * square
            dperm[here, :] = dy
            rperm[here, :] = py * dy
        face_before = face
    writes = tile_writes(nds, nd_ref, out_sems)
    for write in writes:
        write.start()

    def dx_at(k):
        inverse = invh_ref[k * SUB : (k + 1) * SUB, :]
        return inv_cx * (inverse * inverse)

    def rx_at(k):
        return rx_ref[k * SUB : (k + 1) * SUB, :]

    seg_x = march_segments(steps, dx_at, rx_at)
    ends, levels = tree(seg_x)
    for i, v in enumerate(seg_x[:2] + (seg_x[3],)):
        segx_ref[i] = v
    for i, weights in enumerate(levels):
        for j, v in enumerate(weights):
            levx_ref[3 * i + j] = v
    for i, v in enumerate(ends):
        endx_ref[i : i + 1, :] = v[0:1, :]
    endx_ref[5:8, :] = jnp.zeros((3, cols), jnp.float32)

    for tile in range(tiles):
        span = slice(tile * LANES, (tile + 1) * LANES)
        dyt_ref[span, :] = dperm[:, span].T
        ryt_ref[span, :] = rperm[:, span].T

    def gathered(ref, k):
        return jnp.concatenate(
            [ref[pl.ds(tile * LANES + k, SUB, stride=LANES // SUB), :] for tile in range(cols // LANES)]
        )

    seg_y = march_segments(LANES // SUB, lambda k: gathered(dyt_ref, k), lambda k: gathered(ryt_ref, k))
    ends, levels = tree(seg_y)
    for i, v in enumerate(seg_y[:2] + (seg_y[3],)):
        segy_ref[i] = v
    for i, weights in enumerate(levels):
        for j, v in enumerate(weights):
            levy_ref[3 * i + j] = v
    for i, v in enumerate(ends):
        endy_ref[i : i + 1, :] = v[0:1, :]
    endy_ref[5:8, :] = jnp.zeros((3, rows), jnp.float32)
    for write in writes:
        write.wait()


def log2(count):
    return (count - 1).bit_length()


def fluxes(h, p, q, b, m, slabs, inv_cx, inv_cy):
    rows, cols = h.shape
    segs = cols // LANES * SUB
    shapes = [
        (rows, cols),
        (rows, cols),
        (rows, cols),
        (cols, rows),
        (cols, rows),
        (3, SUB, cols),
        (3 * log2(SUB), SUB, cols),
        (3, segs, rows),
        (3 * log2(segs), segs, rows),
        (SUB, cols),
        (SUB, rows),
    ]
    return pl.pallas_call(
        functools.partial(flux_kernel, inv_cx=inv_cx, inv_cy=inv_cy),
        out_shape=tuple(jax.ShapeDtypeStruct(s, jnp.float32) for s in shapes),
        in_specs=[HBM] * 5 + [VMEM] * 4,
        out_specs=(ANY,) + (VMEM,) * (len(shapes) - 1),
        scratch_shapes=[
            *[pltpu.VMEM((cols // LANES * rows, LANES), v.dtype) for v in (h, p, q, b, m, h)],
            pltpu.VMEM((LANES, rows), jnp.float32),
            pltpu.VMEM((rows, LANES), jnp.float32),
            pltpu.VMEM((rows, cols), jnp.float32),
            pltpu.VMEM((rows, cols), jnp.float32),
            pltpu.SemaphoreType.DMA((5 * (cols // LANES),)),
            pltpu.SemaphoreType.DMA((cols // LANES,)),
        ],
        compiler_params=PARAMS,
        name="fluxes",
    )(h, p, q, b, m, *slabs)


def ordered(axis, stage, mine, theirs):
    is_low = (lax.axis_index(axis) >> stage) % 2 == 0
    rows = range(5)
    one = tuple(jnp.where(is_low, mine[i : i + 1, :], theirs[i : i + 1, :]) for i in rows)
    two = tuple(jnp.where(is_low, theirs[i : i + 1, :], mine[i : i + 1, :]) for i in rows)
    return is_low, merge(one, two)


def merge_kernel(*refs, axes, stage):
    count = len(axes)
    for axis, mine, theirs, out in zip(axes, refs[:count], refs[count : 2 * count], refs[2 * count :]):
        _, (merged, _) = ordered(axis, stage, mine, theirs)
        for i, v in enumerate(merged):
            out[i : i + 1, :] = v
        out[5:8, :] = jnp.zeros((3, out.shape[1]), jnp.float32)


def merge_call(axes, stage, mine, theirs):
    count = len(axes)
    return pl.pallas_call(
        functools.partial(merge_kernel, axes=axes, stage=stage),
        out_shape=tuple(jax.ShapeDtypeStruct(v.shape, v.dtype) for v in mine),
        in_specs=[VMEM] * (2 * count),
        out_specs=(VMEM,) * count,
        compiler_params=PARAMS,
        name="merge",
    )(*mine, *theirs)


def group_ends(group, left, right, place):
    if len(group) == 1:
        return left, right
    levels = [group]
    weights = []
    while len(levels[-1]) > 1:
        both = [merge(a, b) for a, b in zip(levels[-1][0::2], levels[-1][1::2])]
        levels.append([v for v, _ in both])
        weights.append([w for _, w in both])
    t, _, gr, _, sr = levels[-1][0]
    right = sr / (t + gr + 1.0)
    for depth in reversed(range(len(weights))):
        chosen = weights[depth][0]
        for n, other in enumerate(weights[depth][1:], 1):
            here = (place >> (depth + 1)) == n
            chosen = tuple(jnp.where(here, b, a) for a, b in zip(chosen, other))
        middle = chosen[0] * left + chosen[1] * right + chosen[2]
        lower = (place >> depth) % 2 == 0
        left, right = jnp.where(lower, left, middle), jnp.where(lower, middle, right)
    return left, right


def line_ends_x(mine, theirs, rest):
    is_low, (merged, (w1, w2, source)) = ordered("gx", 0, mine, theirs)
    group = [tuple(rest[n, i : i + 1, :] for i in range(5)) for n in range(rest.shape[0])]
    left, right = group_ends(group, jnp.zeros_like(w1), None, lax.axis_index("gx") // 2)
    middle = w1 * left + w2 * right + source
    return jnp.where(is_low, left, middle), jnp.where(is_low, middle, right)


def line_ends(axis, pairs):
    steps = []
    merged = None
    for stage, (mine, theirs) in enumerate(pairs):
        is_low, (merged, weights) = ordered(axis, stage, mine, theirs)
        steps.append((is_low, weights))
    t, _, gr, _, sr = merged
    left = jnp.zeros_like(t)
    right = sr / (t + gr + 1.0)
    for is_low, (w1, w2, source) in reversed(steps):
        middle = w1 * left + w2 * right + source
        left = jnp.where(is_low, left, middle)
        right = jnp.where(is_low, middle, right)
    return left, right


def segment_ends(left, right, lev_ref):
    shape = lev_ref.shape[1:]
    count = shape[0]
    at = row_index(shape)
    left = jnp.broadcast_to(left, shape)
    right = jnp.broadcast_to(right, shape)
    for level in reversed(range(log2(count))):
        stride = 1 << level
        middle = lev_ref[3 * level] * left + lev_ref[3 * level + 1] * right + lev_ref[3 * level + 2]
        upper = (at >> level) % 2 == 1
        left, right = (
            jnp.where(upper, pltpu.roll(middle, stride, 0), left),
            jnp.where(upper, pltpu.roll(right, stride, 0), middle),
        )
    return left, right


def solve_kernel(*refs, stages_y, inv_cx):
    (invh_ref, rx_ref, dyt_ref, ryt_ref, segx_ref, levx_ref, segy_ref, levy_ref), refs = refs[:8], refs[8:]
    pairs_x, refs = refs[:3], refs[3:]
    pairs_y, refs = refs[: 2 * stages_y], refs[2 * stages_y :]
    vx_ref, vy_ref, v_t, vxs, vys, sems_x, sems_y = refs
    rows, cols = vx_ref.shape
    steps = rows // SUB
    tiles = cols // LANES
    left, right = line_ends_x(*pairs_x)
    left, right = segment_ends(left, right, levx_ref)
    value = left
    change = segx_ref[0] * (right - left) - segx_ref[1] * left - segx_ref[2]
    for k in range(steps):
        here = slice(k * SUB, (k + 1) * SUB)
        inverse = invh_ref[here, :]
        value = value + change
        change = change + ((inv_cx * (inverse * inverse)) * value - rx_ref[here, :])
        speed = value * inverse
        for tile in range(tiles):
            vxs[pl.ds(tile * rows + k, SUB, stride=steps), :] = speed[:, tile * LANES : (tile + 1) * LANES]
    writes = tile_writes(vxs, vx_ref, sems_x)
    for write in writes:
        write.start()

    left, right = line_ends("gy", list(zip(pairs_y[0::2], pairs_y[1::2])))
    left, right = segment_ends(left, right, levy_ref)
    value = left
    change = segy_ref[0] * (right - left) - segy_ref[1] * left - segy_ref[2]
    jump = LANES // SUB
    for k in range(jump):
        spots = [pl.ds(tile * LANES + k, SUB, stride=jump) for tile in range(cols // LANES)]
        d = jnp.concatenate([dyt_ref[s, :] for s in spots])
        r = jnp.concatenate([ryt_ref[s, :] for s in spots])
        value = value + change
        change = change + (d * value - r)
        for tile, s in enumerate(spots):
            v_t[s, :] = value[tile * SUB : (tile + 1) * SUB, :]
    for tile, write in enumerate(tile_writes(vys, vy_ref, sems_y)):
        span = slice(tile * LANES, (tile + 1) * LANES)
        block = v_t[span, :].T * invh_ref[:, span]
        for k in range(steps):
            vys[pl.ds(tile * rows + k, SUB, stride=steps), :] = block[k * SUB : (k + 1) * SUB, :]
        write.start()
        writes.append(write)
    for write in writes:
        write.wait()


def solve(pieces, pairs_x, pairs_y, shape, inv_cx):
    rows, cols = shape
    flat_x = list(pairs_x)
    flat_y = [v for pair in pairs_y for v in pair]
    out = jax.ShapeDtypeStruct(shape, jnp.float32)
    return pl.pallas_call(
        functools.partial(solve_kernel, stages_y=len(pairs_y), inv_cx=inv_cx),
        out_shape=(out, out),
        in_specs=[VMEM] * (len(pieces) + len(flat_x) + len(flat_y)),
        out_specs=(ANY, ANY),
        scratch_shapes=[
            pltpu.VMEM((cols, rows), jnp.float32),
            pltpu.VMEM((cols // LANES * rows, LANES), jnp.float32),
            pltpu.VMEM((cols // LANES * rows, LANES), jnp.float32),
            pltpu.SemaphoreType.DMA((cols // LANES,)),
            pltpu.SemaphoreType.DMA((cols // LANES,)),
        ],
        compiler_params=PARAMS,
        name="solve",
    )(*pieces, *flat_x, *flat_y)


def hand_on(value, axis):
    count = lax.axis_size(axis)
    far = [i + 2 if i % 2 == 0 else i - 2 for i in range(count)]
    return lax.ppermute(value, axis, [(i, t if 0 <= t < count else i ^ 1) for i, t in enumerate(far)])


def spread(value, axis):
    count = lax.axis_size(axis)
    groups = [list(range(parity, count, 2)) for parity in (0, 1)]
    copies = jnp.broadcast_to(value[None], (count // 2, *value.shape))
    return lax.all_to_all(copies, axis, 0, 0, axis_index_groups=groups)


def cross(value, axis, stage):
    return lax.ppermute(value, axis, [(i, i ^ (1 << stage)) for i in range(lax.axis_size(axis))])


def on_device(h, p, q, b, m):
    rows, cols = h.shape
    count_x, count_y = lax.axis_size("gx"), lax.axis_size("gy")
    inv_cx = 3.0 / (rows * count_x / 4.0) ** 2
    inv_cy = 3.0 / (cols * count_y / 4.0) ** 2
    xa, ya = pack(h, p, q, b, m)
    near_x, near_y = cross(xa, "gx", 0), cross(ya, "gy", 0)
    slabs = (near_x[0], hand_on(near_x[1], "gx"), near_y[0], hand_on(near_y[1], "gy"))
    new_depth, *pieces, end_x, end_y = fluxes(h, p, q, b, m, slabs, inv_cx, inv_cy)
    their_x, their_y = cross(end_x, "gx", 0), cross(end_y, "gy", 0)
    pairs_y = [(end_y, their_y)]
    pair_x, pair_y = merge_call(("gx", "gy"), 0, [end_x, end_y], [their_x, their_y])
    rest = spread(pair_x, "gx")
    for stage in range(1, log2(count_y)):
        if stage > 1:
            (pair_y,) = merge_call(("gy",), stage - 1, [pairs_y[-1][0]], [pairs_y[-1][1]])
        pairs_y.append((pair_y, cross(pair_y, "gy", stage)))
    vx, vy = solve(pieces, (end_x, their_x, rest), pairs_y, (rows, cols), inv_cx)
    return new_depth, vx, vy


def solution(mesh):
    spec = P("gx", "gy")
    return jax.shard_map(
        on_device,
        mesh=mesh,
        in_specs=(spec,) * 5,
        out_specs=(spec,) * 3,
        check_vma=False,
    )
```

```python
import functools

import jax
import jax.numpy as jnp
from jax import lax
from jax.experimental import pallas as pl
from jax.experimental.pallas import tpu as pltpu
from jax.sharding import PartitionSpec as P

gravity = 9.81
ratio = 0.05
LANES = 128
SUB = 8
STEPS = LANES // SUB
F32 = jnp.float32
VMEM = pl.BlockSpec(memory_space=pltpu.VMEM)
HBM = pl.BlockSpec(memory_space=pltpu.HBM)
ANY = pl.BlockSpec(memory_space=pl.ANY)
PARAMS = pltpu.CompilerParams(vmem_limit_bytes=16 * 1024 * 1024)
WHOLE = pltpu.CompilerParams(vmem_limit_bytes=62 * 1024 * 1024)


def lane_index(shape):
    return lax.broadcasted_iota(jnp.int32, shape, len(shape) - 1)


def row_index(shape):
    return lax.broadcasted_iota(jnp.int32, shape, len(shape) - 2)


def at(tile, step):
    first = tile * LANES + step * SUB
    return slice(first, first + SUB)


def tile_span(tile):
    return slice(tile * LANES, (tile + 1) * LANES)


def spread_rows(tile, step):
    return pl.ds(tile * LANES + step, SUB, stride=STEPS)


def shape(*dims):
    return jax.ShapeDtypeStruct(dims, F32)


def pack_kernel(h, p, q, b, m, xa, ya, top, bottom, left, right, itop, ibottom, ileft, iright, sems):
    rows, cols = h.shape
    copies = []
    for f, src in enumerate((h, p, q, b, m)):
        floats = f < 4
        spots = (
            (src.at[pl.ds(0, SUB), :], top.at[f] if floats else itop),
            (src.at[pl.ds(rows - SUB, SUB), :], bottom.at[f] if floats else ibottom),
            (src.at[:, pl.ds(0, LANES)], left.at[f] if floats else ileft),
            (src.at[:, pl.ds(cols - LANES, LANES)], right.at[f] if floats else iright),
        )
        for g, (piece, target) in enumerate(spots):
            copy = pltpu.make_async_copy(piece, target, sems.at[4 * f + g])
            copy.start()
            copies.append(copy)
    for copy in copies:
        copy.wait()
    first_x = jnp.concatenate(
        [top[0, 0:2, :], top[1, 0:2, :], top[2, 0:2, :], top[3, 0:1, :], itop[0:1, :].astype(F32)]
    )
    last_x = jnp.concatenate(
        [
            bottom[0, SUB - 2 : SUB, :],
            bottom[1, SUB - 2 : SUB, :],
            bottom[2, SUB - 2 : SUB, :],
            bottom[3, SUB - 1 : SUB, :],
            ibottom[SUB - 1 : SUB, :].astype(F32),
        ]
    )
    even_x = lax.axis_index("gx") % 2 == 0
    xa[0] = jnp.where(even_x, last_x, first_x)
    xa[1] = jnp.where(even_x, first_x, last_x)
    lane = lane_index((rows, LANES))

    def columns(block, imask, shifts):
        def stacked(ref):
            return jnp.concatenate([ref[spread_rows(0, k), :] for k in range(STEPS)])

        fields = [stacked(block.at[f]) for f in range(4)] + [stacked(imask).astype(F32)]
        moved = [pltpu.roll(v, s, 1) if s else v for v, s in zip(fields, shifts)]
        out = moved[0]
        for start, v in zip((2, 4, 6, 7), moved[1:]):
            out = jnp.where(lane >= start, v, out)
        return out.T[0:SUB, :]

    first_y = columns(left, ileft, (0, 2, 4, 6, 7))
    last_y = columns(right, iright, (2, 4, 6, 7, 8))
    even_y = lax.axis_index("gy") % 2 == 0
    ya[0] = jnp.where(even_y, last_y, first_y)
    ya[1] = jnp.where(even_y, first_y, last_y)


def pack(h, p, q, b, m):
    rows, cols = h.shape
    i32 = jnp.int32
    return pl.pallas_call(
        pack_kernel,
        out_shape=(shape(2, SUB, cols), shape(2, SUB, rows)),
        in_specs=[HBM] * 5,
        out_specs=(VMEM,) * 2,
        scratch_shapes=[
            pltpu.VMEM((4, SUB, cols), F32),
            pltpu.VMEM((4, SUB, cols), F32),
            pltpu.VMEM((4, rows, LANES), F32),
            pltpu.VMEM((4, rows, LANES), F32),
            pltpu.VMEM((SUB, cols), i32),
            pltpu.VMEM((SUB, cols), i32),
            pltpu.VMEM((rows, LANES), i32),
            pltpu.VMEM((rows, LANES), i32),
            pltpu.SemaphoreType.DMA((20,)),
        ],
        compiler_params=WHOLE,
        name="pack",
    )(h, p, q, b, m)


def merge_coefficients(one, two):
    t1, gl1, gr1 = one
    t2, gl2, gr2 = two
    shunt = gr1 + gl2
    inverse = 1.0 / (t1 + t2 + shunt)
    w1, w2 = t1 * inverse, t2 * inverse
    return (w1 * t2, gl1 + w1 * shunt, gr2 + w2 * shunt), (w1, w2, inverse)


def merge_sources(one, two, weights):
    w1, w2, inverse = weights
    source = one[1] - two[0]
    return (one[0] - w1 * source, two[1] + w2 * source), source * inverse


def merge(one, two):
    coefficients, weights = merge_coefficients(one[:3], two[:3])
    sources, middle = merge_sources(one[3:], two[3:], weights)
    return coefficients + sources, weights[:2] + (middle,)


def log2(count):
    return (count - 1).bit_length()


def full(ref, step):
    return jnp.concatenate([ref[at(tile, step), :] for tile in range(ref.shape[0] // LANES)])


def march_depth(inv_ref, scale, out_t, out_w, levels):
    count = inv_ref.shape[0] // STEPS
    zero = jnp.zeros((count, LANES), F32)
    alpha, gamma, beta, delta = zero, zero, zero, zero
    for k in range(STEPS):
        inverse = full(inv_ref, k)
        d = scale * (inverse * inverse)
        alpha = alpha + gamma
        gamma = gamma + d * (1.0 + alpha)
        beta = beta + delta
        delta = delta + d * ((k + 1.0) + beta)
    t = 1.0 / (STEPS + beta)
    out_t[0] = t
    out_t[1] = t * alpha
    out_t[2] = 1.0 + delta
    coefficients = (t, t * alpha, t * delta)
    for level in range(levels):
        after = tuple(pltpu.roll(v, count - (1 << level), 0) for v in coefficients)
        coefficients, weights = merge_coefficients(coefficients, after)
        for j, v in enumerate(weights):
            out_w[3 * level + j] = v
    return coefficients


def prepare_kernel(
    h, p, q, b, m,
    hx, px, qx, bx, mx, ix, hy, py, qy, by, my, iy, tx, wx, ty, wy, endx, endy,
    hs, ps, qs, bs, ms, turned, sems,
    *, inv_cx, inv_cy,
):
    rows, cols = h.shape
    tiles = cols // LANES
    copies = []
    for f, (src, target) in enumerate(zip((h, p, q, b, m), (hs, ps, qs, bs, ms))):
        for tile in range(tiles):
            copies.append(
                pltpu.make_async_copy(
                    src.at[:, pl.ds(tile * LANES, LANES)],
                    target.at[pl.ds(tile * rows, rows), :],
                    sems.at[f * tiles + tile],
                )
            )
            copies[-1].start()
    for f, (src, xs, ys) in enumerate(
        ((hs, hx, hy), (ps, px, py), (qs, qx, qy), (bs, bx, by), (ms, mx, my))
    ):
        for tile in range(tiles):
            copies[f * tiles + tile].wait()
            for k in range(STEPS):
                xs[at(tile, k), :] = src[spread_rows(tile, k), :].astype(F32)
            turned[f % 2, tile_span(tile), :] = xs[tile_span(tile), :].T
            for k in range(STEPS):
                ys[at(tile, k), :] = turned[f % 2, spread_rows(tile, k), :]
        if f == 0:
            ix[...] = 1.0 / hx[...]
            iy[...] = 1.0 / hy[...]
            ends_x = march_depth(ix, inv_cx, tx, wx, log2(SUB))
            ends_y = march_depth(iy, inv_cy, ty, wy, log2(SUB * tiles))
            for i in range(3):
                for tile in range(tiles):
                    endx[i : i + 1, tile_span(tile)] = ends_x[i][tile * SUB : tile * SUB + 1, :]
                endy[i : i + 1, :] = ends_y[i][0:1, :]
            endx[3:8, :] = jnp.zeros((5, cols), F32)
            endy[3:8, :] = jnp.zeros((5, rows), F32)


def prepare(h, p, q, b, m, inv_cx, inv_cy):
    rows, cols = h.shape
    tiles = cols // LANES
    count = tiles * SUB
    stack = (tiles * LANES, LANES)
    shapes = [shape(*stack)] * 12 + [
        shape(3, count, LANES),
        shape(3 * log2(SUB), count, LANES),
        shape(3, count, LANES),
        shape(3 * log2(count), count, LANES),
        shape(SUB, cols),
        shape(SUB, rows),
    ]
    return pl.pallas_call(
        functools.partial(prepare_kernel, inv_cx=inv_cx, inv_cy=inv_cy),
        out_shape=tuple(shapes),
        in_specs=[HBM] * 5,
        out_specs=(VMEM,) * len(shapes),
        scratch_shapes=[
            *[pltpu.VMEM(stack, v.dtype) for v in (h, p, q, b, m)],
            pltpu.VMEM((2, *stack), F32),
            pltpu.SemaphoreType.DMA((5 * tiles,)),
        ],
        compiler_params=PARAMS,
        cost_estimate=pl.CostEstimate(flops=2_000_000, bytes_accessed=8_000_000, transcendentals=0),
        name="prepare",
    )(h, p, q, b, m)


def low_high(axis, near, far):
    index, count = lax.axis_index(axis), lax.axis_size(axis)
    even = index % 2 == 0
    low = jnp.where(index > 0, jnp.where(even, far, near), 0.0)
    high = jnp.where(index < count - 1, jnp.where(even, near, far), 0.0)
    return low, high


def half_slope(a, c):
    return 0.5 * (jnp.maximum(jnp.minimum(a, c), 0.0) + jnp.minimum(jnp.maximum(a, c), 0.0))


def face_flux(left, right, opened):
    is_open = opened > 0.5
    hl = jnp.where(is_open, left[0], 1.0)
    hr = jnp.where(is_open, right[0], 1.0)
    joint = 1.0 / (hl * hr)
    ul = left[1] * (hr * joint)
    ur = right[1] * (hl * joint)
    gl = gravity * hl
    gr = gravity * hr
    fastest = jnp.maximum(jnp.abs(ul) + gl * lax.rsqrt(gl), jnp.abs(ur) + gr * lax.rsqrt(gr))
    scale = (0.5 * ratio) * opened
    mass = (left[1] + right[1]) - fastest * (right[0] - left[0])
    push = 0.5 * (gl * hl + gr * hr) + left[1] * ul + right[1] * ur - fastest * (right[1] - left[1])
    shear = left[2] * ul + right[2] * ur - fastest * (right[2] - left[2])
    return scale * mass, scale * push, scale * shear


def extended(ref, tile, lows, highs):
    sub = row_index((SUB, LANES))
    out = {}
    for n, row in enumerate(lows, 1):
        value = ref[at(tile, STEPS - n), :]
        out[-n] = jnp.where(sub == 0, row, pltpu.roll(value, 1, 0))
    for n, row in enumerate(highs):
        value = ref[at(tile, n), :]
        out[STEPS + n] = jnp.where(sub == SUB - 1, row, pltpu.roll(value, SUB - 1, 0))
    return lambda k: out[k] if k in out else ref[at(tile, k), :]


def tile_fluxes(fields, bed, wet, store):
    def states(k):
        both = []
        for w in fields:
            here = w(k)
            both.append((here, half_slope(here - w(k - 1), w(k + 1) - here)))
        return [w + s for w, s in both], [w - s for w, s in both]

    left, _ = states(-1)
    before = None
    for k in range(-1, STEPS):
        left_next, right = states(k + 1)
        face = face_flux(left, right, wet(k) * wet(k + 1))
        left = left_next
        if k >= 0:
            store(k, [a - c for a, c in zip(face, before)], bed(k + 1) - bed(k - 1))
        before = face


def march_source(inv_ref, scale, r_ref, t_ref, w_ref, s_ref, levels):
    count = inv_ref.shape[0] // STEPS
    c = jnp.zeros((count, LANES), F32)
    e = c
    for k in range(STEPS):
        inverse = full(inv_ref, k)
        c = c + e
        e = e + (scale * (inverse * inverse) * c - full(r_ref, k))
    sl = t_ref[0] * c
    s_ref[0] = sl
    sources = (sl, t_ref[2] * sl - e)
    for level in range(levels):
        after = tuple(pltpu.roll(v, count - (1 << level), 0) for v in sources)
        sources, middle = merge_sources(sources, after, tuple(w_ref[3 * level + j] for j in range(3)))
        s_ref[1 + level] = middle
    return sources


def flux_kernel(
    near_x, far_x, near_y, far_y,
    hx, px, qx, bx, mx, ix, hy, py, qy, by, my, iy, tx, wx, ty, wy, coefx, coefy,
    depth, rx, ry, sx, sy, endx, endy,
    xpart, ypart, turned,
    *, inv_cx, inv_cy,
):
    tiles = hx.shape[0] // LANES
    low_x, high_x = low_high("gx", near_x[0], far_x[...])
    low_y, high_y = low_high("gy", near_y[0], far_y[...])

    for tile in range(tiles):
        span = tile_span(tile)

        def along_x(ref, row, layers):
            lows = [low_x[row + layers - 1 - n : row + layers - n, span] for n in range(layers)]
            highs = [high_x[row + n : row + n + 1, span] for n in range(layers)]
            return extended(ref, tile, lows, highs)

        def store_x(k, difference, bed):
            here = at(tile, k)
            for i in range(3):
                xpart[i, here, :] = difference[i]
            xpart[3, here, :] = bed

        tile_fluxes(
            [along_x(hx, 0, 2), along_x(px, 2, 2), along_x(qx, 4, 2)],
            along_x(bx, 6, 1), along_x(mx, 7, 1), store_x,
        )

        def along_y(ref, row, layers):
            lows, highs = [], []
            for n in range(layers):
                last = at(tile - 1, STEPS - 1 - n).stop - 1
                first = at(tile + 1, n).start
                lows.append(low_y[row + layers - 1 - n : row + layers - n, :] if tile == 0 else ref[last : last + 1, :])
                highs.append(high_y[row + n : row + n + 1, :] if tile == tiles - 1 else ref[first : first + 1, :])
            return extended(ref, tile, lows, highs)

        def store_y(k, difference, bed):
            here, natural = at(tile, k), spread_rows(tile, k)
            ypart[0, natural, :] = difference[0]
            ypart[1, here, :] = difference[1]
            ypart[2, natural, :] = difference[2]
            ypart[3, here, :] = bed

        tile_fluxes(
            [along_y(hy, 0, 2), along_y(qy, 4, 2), along_y(py, 2, 2)],
            along_y(by, 6, 1), along_y(my, 7, 1), store_y,
        )
        turned[span, :] = xpart[2, span, :].T
        from_y_mass = ypart[0, span, :].T
        from_y_shear = ypart[2, span, :].T
        h, m, inverse = hx[span, :], mx[span, :], ix[span, :]
        depth[span, :] = h - m * (xpart[0, span, :] + from_y_mass)
        push = px[span, :] - xpart[1, span, :] - from_y_shear - (0.5 * ratio * gravity) * h * xpart[3, span, :]
        rx[span, :] = (inv_cx * (inverse * inverse)) * m * push
        for k in range(STEPS):
            here = at(tile, k)
            inverse = iy[here, :]
            push = qy[here, :] - turned[spread_rows(tile, k), :] - ypart[1, here, :]
            push = push - (0.5 * ratio * gravity) * hy[here, :] * ypart[3, here, :]
            ry[here, :] = (inv_cy * (inverse * inverse)) * my[here, :] * push

    ends_x = march_source(ix, inv_cx, rx, tx, wx, sx, log2(SUB))
    ends_y = march_source(iy, inv_cy, ry, ty, wy, sy, log2(SUB * tiles))
    endx[...] = coefx[...]
    endy[...] = coefy[...]
    for i in range(2):
        for tile in range(tiles):
            endx[3 + i : 4 + i, tile_span(tile)] = ends_x[i][tile * SUB : tile * SUB + 1, :]
        endy[3 + i : 4 + i, :] = ends_y[i][0:1, :]


def fluxes(slabs, prepared, inv_cx, inv_cy):
    stack = prepared[0].shape
    count = stack[0] // STEPS
    shapes = (
        shape(*stack),
        shape(*stack),
        shape(*stack),
        shape(1 + log2(SUB), count, LANES),
        shape(1 + log2(count), count, LANES),
        shape(*prepared[-2].shape),
        shape(*prepared[-1].shape),
    )
    return pl.pallas_call(
        functools.partial(flux_kernel, inv_cx=inv_cx, inv_cy=inv_cy),
        out_shape=shapes,
        in_specs=[VMEM] * (len(slabs) + len(prepared)),
        out_specs=(VMEM,) * len(shapes),
        scratch_shapes=[
            pltpu.VMEM((4, *stack), F32),
            pltpu.VMEM((4, *stack), F32),
            pltpu.VMEM(stack, F32),
        ],
        compiler_params=PARAMS,
        name="fluxes",
    )(*slabs, *prepared)


def tile_write(tiled, whole, tile, sems):
    rows = whole.shape[0]
    return pltpu.make_async_copy(
        tiled.at[pl.ds(tile * rows, rows), :], whole.at[:, pl.ds(tile * LANES, LANES)], sems.at[tile]
    )


def write_scratch(cols):
    return [pltpu.VMEM((cols, LANES), F32), pltpu.SemaphoreType.DMA((cols // LANES,))]


def depth_kernel(depth, out, natural, sems):
    writes = []
    for tile in range(depth.shape[0] // LANES):
        for k in range(STEPS):
            natural[spread_rows(tile, k), :] = depth[at(tile, k), :]
        writes.append(tile_write(natural, out, tile, sems))
        writes[-1].start()
    for write in writes:
        write.wait()


def write_depth(depth, block):
    return pl.pallas_call(
        depth_kernel,
        out_shape=shape(*block),
        in_specs=[VMEM],
        out_specs=ANY,
        scratch_shapes=write_scratch(block[1]),
        compiler_params=PARAMS,
        cost_estimate=pl.CostEstimate(flops=100_000, bytes_accessed=2_000_000, transcendentals=0),
        name="write_depth",
    )(depth)


def ordered(axis, stage, mine, theirs):
    is_low = (lax.axis_index(axis) >> stage) % 2 == 0
    rows = range(5)
    one = tuple(jnp.where(is_low, mine[i : i + 1, :], theirs[i : i + 1, :]) for i in rows)
    two = tuple(jnp.where(is_low, theirs[i : i + 1, :], mine[i : i + 1, :]) for i in rows)
    return is_low, merge(one, two)


def merge_kernel(*refs, axes, stage):
    count = len(axes)
    for axis, mine, theirs, out in zip(axes, refs[:count], refs[count : 2 * count], refs[-count:]):
        _, (merged, _) = ordered(axis, stage, mine, theirs)
        for i, v in enumerate(merged):
            out[i : i + 1, :] = v
        out[5:8, :] = jnp.zeros((3, out.shape[1]), F32)


def merge_call(axes, stage, mine, theirs, also=()):
    count = len(axes)
    return pl.pallas_call(
        functools.partial(merge_kernel, axes=axes, stage=stage),
        out_shape=tuple(shape(*v.shape) for v in mine),
        in_specs=[VMEM] * (2 * count + len(also)),
        out_specs=(VMEM,) * count,
        compiler_params=PARAMS,
        name="merge",
    )(*mine, *theirs, *also)


def line_ends(axis, pairs):
    steps = []
    merged = None
    for stage, (mine, theirs) in enumerate(pairs):
        is_low, (merged, weights) = ordered(axis, stage, mine, theirs)
        steps.append((is_low, weights))
    t, _, gr, _, sr = merged
    left = jnp.zeros_like(t)
    right = sr / (t + gr + 1.0)
    for is_low, (w1, w2, source) in reversed(steps):
        middle = w1 * left + w2 * right + source
        left = jnp.where(is_low, left, middle)
        right = jnp.where(is_low, middle, right)
    return left, right


def segment_ends(left, right, w_ref, s_ref, levels):
    index = row_index(left.shape)
    for level in reversed(range(levels)):
        stride = 1 << level
        middle = w_ref[3 * level] * left + w_ref[3 * level + 1] * right + s_ref[1 + level]
        upper = (index >> level) % 2 == 1
        left, right = (
            jnp.where(upper, pltpu.roll(middle, stride, 0), left),
            jnp.where(upper, pltpu.roll(right, stride, 0), middle),
        )
    return left, right


def march_values(left, right, t_ref, s_ref, inv_ref, scale, r_ref, store):
    value = left
    change = t_ref[0] * (right - left) - t_ref[1] * left - s_ref[0]
    for k in range(STEPS):
        inverse = full(inv_ref, k)
        value = value + change
        change = change + (scale * (inverse * inverse) * value - full(r_ref, k))
        store(k, value * inverse)


def solve_x_kernel(inv_ref, r_ref, t_ref, w_ref, s_ref, *refs, scale):
    pairs, (out, natural, sems) = refs[:-3], refs[-3:]
    tiles = out.shape[1] // LANES
    ends = []
    for row in line_ends("gx", list(zip(pairs[0::2], pairs[1::2]))):
        ends.append(
            jnp.concatenate([jnp.broadcast_to(row[:, tile_span(t)], (SUB, LANES)) for t in range(tiles)])
        )
    left, right = segment_ends(*ends, w_ref, s_ref, log2(SUB))

    def store(k, speed):
        for tile in range(tiles):
            natural[spread_rows(tile, k), :] = speed[tile * SUB : (tile + 1) * SUB, :]

    march_values(left, right, t_ref, s_ref, inv_ref, scale, r_ref, store)
    writes = [tile_write(natural, out, tile, sems) for tile in range(tiles)]
    for write in writes:
        write.start()
    for write in writes:
        write.wait()


def solve_y_kernel(inv_ref, r_ref, t_ref, w_ref, s_ref, *refs, scale):
    pairs, (out, natural, sems, turned) = refs[:-4], refs[-4:]
    tiles = out.shape[1] // LANES
    ends = line_ends("gy", list(zip(pairs[0::2], pairs[1::2])))
    ends = [jnp.broadcast_to(row, (tiles * SUB, LANES)) for row in ends]
    left, right = segment_ends(*ends, w_ref, s_ref, log2(tiles * SUB))

    def store(k, speed):
        for tile in range(tiles):
            turned[spread_rows(tile, k), :] = speed[tile * SUB : (tile + 1) * SUB, :]

    march_values(left, right, t_ref, s_ref, inv_ref, scale, r_ref, store)
    writes = []
    for tile in range(tiles):
        block = turned[tile_span(tile), :].T
        for k in range(STEPS):
            natural[spread_rows(tile, k), :] = block[k * SUB : (k + 1) * SUB, :]
        writes.append(tile_write(natural, out, tile, sems))
        writes[-1].start()
    for write in writes:
        write.wait()


def solve(kernel, name, pieces, pairs, block, scale, extra=()):
    flat = [v for pair in pairs for v in pair]
    return pl.pallas_call(
        functools.partial(kernel, scale=scale),
        out_shape=shape(*block),
        in_specs=[VMEM] * (len(pieces) + len(flat)),
        out_specs=ANY,
        scratch_shapes=write_scratch(block[1]) + list(extra),
        compiler_params=PARAMS,
        cost_estimate=pl.CostEstimate(flops=1_000_000, bytes_accessed=4_000_000, transcendentals=0),
        name=name,
    )(*pieces, *flat)


def hand_on(value, axis):
    count = lax.axis_size(axis)
    far = [i + 2 if i % 2 == 0 else i - 2 for i in range(count)]
    return lax.ppermute(value, axis, [(i, t if 0 <= t < count else i ^ 1) for i, t in enumerate(far)])


def cross(value, axis, stage):
    return lax.ppermute(value, axis, [(i, i ^ (1 << stage)) for i in range(lax.axis_size(axis))])


def on_device(h, p, q, b, m):
    block = h.shape
    rows, cols = block
    count_x, count_y = lax.axis_size("gx"), lax.axis_size("gy")
    inv_cx = 3.0 / (rows * count_x / 4.0) ** 2
    inv_cy = 3.0 / (cols * count_y / 4.0) ** 2
    xa, ya = pack(h, p, q, b, m)
    near_x, near_y = cross(xa, "gx", 0), cross(ya, "gy", 0)
    slabs = (near_x, hand_on(near_x[1], "gx"), near_y, hand_on(near_y[1], "gy"))
    prepared = prepare(h, p, q, b, m, inv_cx, inv_cy)
    depth, rx, ry, sx, sy, end_x, end_y = fluxes(slabs, prepared, inv_cx, inv_cy)
    ix, iy = prepared[5], prepared[11]
    tx, wx, ty, wy = prepared[12:16]
    new_depth = write_depth(depth, block)
    stages = {"gx": log2(count_x), "gy": log2(count_y)}
    mine = {"gx": end_x, "gy": end_y}
    pairs = {"gx": [], "gy": []}
    for stage in range(max(stages.values())):
        axes = [a for a in ("gx", "gy") if stage < stages[a]]
        theirs = {a: cross(mine[a], a, stage) for a in axes}
        for a in axes:
            pairs[a].append((mine[a], theirs[a]))
        more = [a for a in axes if stage + 1 < stages[a]]
        if more:
            also = [theirs[a] for a in axes if a not in more]
            merged = merge_call(more, stage, [mine[a] for a in more], [theirs[a] for a in more], also)
            mine.update(zip(more, merged))
    turned = [pltpu.VMEM((cols, LANES), F32)]
    vy = solve(solve_y_kernel, "solve_y", (iy, ry, ty, wy, sy), pairs["gy"], block, inv_cy, turned)
    vx = solve(solve_x_kernel, "solve_x", (ix, rx, tx, wx, sx), pairs["gx"], block, inv_cx)
    return new_depth, vx, vy


def solution(mesh):
    spec = P("gx", "gy")
    return jax.shard_map(
        on_device,
        mesh=mesh,
        in_specs=(spec,) * 5,
        out_specs=(spec,) * 3,
        check_vma=False,
    )
```

```python
import functools

import jax
import jax.numpy as jnp
from jax import lax
from jax.experimental import pallas as pl
from jax.experimental.pallas import tpu as pltpu
from jax.sharding import PartitionSpec as P

gravity = 9.81
ratio = 0.05
LANES = 128
SUB = 8
STEPS = LANES // SUB
F32 = jnp.float32
VMEM = pl.BlockSpec(memory_space=pltpu.VMEM)
HBM = pl.BlockSpec(memory_space=pltpu.HBM)
ANY = pl.BlockSpec(memory_space=pl.ANY)
PARAMS = pltpu.CompilerParams(vmem_limit_bytes=16 * 1024 * 1024)
WHOLE = pltpu.CompilerParams(vmem_limit_bytes=62 * 1024 * 1024)


def lane_index(shape):
    return lax.broadcasted_iota(jnp.int32, shape, len(shape) - 1)


def row_index(shape):
    return lax.broadcasted_iota(jnp.int32, shape, len(shape) - 2)


def at(tile, step):
    first = tile * LANES + step * SUB
    return slice(first, first + SUB)


def tile_span(tile):
    return slice(tile * LANES, (tile + 1) * LANES)


def spread_rows(tile, step):
    return pl.ds(tile * LANES + step, SUB, stride=STEPS)


def shape(*dims):
    return jax.ShapeDtypeStruct(dims, F32)


def pack_kernel(h, p, q, b, m, xa, ya, top, bottom, left, right, itop, ibottom, ileft, iright, sems):
    rows, cols = h.shape
    sources = (h, p, q, b, m)

    def load(places, piece, first):
        copies = []
        for f, (src, target) in enumerate(zip(sources, places)):
            copies.append(pltpu.make_async_copy(src.at[piece], target, sems.at[first + f]))
            copies[-1].start()
        return copies

    def places(floats, whole):
        return [floats.at[f] for f in range(4)] + [whole]

    edges_x = load(places(top, itop), (pl.ds(0, SUB), slice(None)), 0)
    edges_x += load(places(bottom, ibottom), (pl.ds(rows - SUB, SUB), slice(None)), 5)
    edges_y = load(places(left, ileft), (slice(None), pl.ds(0, LANES)), 10)
    edges_y += load(places(right, iright), (slice(None), pl.ds(cols - LANES, LANES)), 15)
    for copy in edges_x:
        copy.wait()
    first_x = jnp.concatenate(
        [top[0, 0:2, :], top[1, 0:2, :], top[2, 0:2, :], top[3, 0:1, :], itop[0:1, :].astype(F32)]
    )
    last_x = jnp.concatenate(
        [
            bottom[0, SUB - 2 : SUB, :],
            bottom[1, SUB - 2 : SUB, :],
            bottom[2, SUB - 2 : SUB, :],
            bottom[3, SUB - 1 : SUB, :],
            ibottom[SUB - 1 : SUB, :].astype(F32),
        ]
    )
    even_x = lax.axis_index("gx") % 2 == 0
    xa[0] = jnp.where(even_x, last_x, first_x)
    xa[1] = jnp.where(even_x, first_x, last_x)
    for copy in edges_y:
        copy.wait()
    lane = lane_index((rows, LANES))
    out = jnp.zeros((rows, LANES), F32)
    for block, mask, start, shifts in (
        (left, ileft, 0, (0, 2, 4, 6, 7)),
        (right, iright, SUB, (10, 12, 14, 15, 16)),
    ):
        fields = [block.at[f] for f in range(4)] + [mask]
        for ref, to, shift in zip(fields, (0, 2, 4, 6, 7), shifts):
            value = jnp.concatenate([ref[spread_rows(0, k), :] for k in range(STEPS)]).astype(F32)
            out = jnp.where(lane >= start + to, pltpu.roll(value, shift, 1) if shift else value, out)
    turned = out.T
    first_y, last_y = turned[0:SUB, :], turned[SUB : 2 * SUB, :]
    even_y = lax.axis_index("gy") % 2 == 0
    ya[0] = jnp.where(even_y, last_y, first_y)
    ya[1] = jnp.where(even_y, first_y, last_y)


def pack(h, p, q, b, m):
    rows, cols = h.shape
    i32 = jnp.int32
    return pl.pallas_call(
        pack_kernel,
        out_shape=(shape(2, SUB, cols), shape(2, SUB, rows)),
        in_specs=[HBM] * 5,
        out_specs=(VMEM,) * 2,
        scratch_shapes=[
            pltpu.VMEM((4, SUB, cols), F32),
            pltpu.VMEM((4, SUB, cols), F32),
            pltpu.VMEM((4, rows, LANES), F32),
            pltpu.VMEM((4, rows, LANES), F32),
            pltpu.VMEM((SUB, cols), i32),
            pltpu.VMEM((SUB, cols), i32),
            pltpu.VMEM((rows, LANES), i32),
            pltpu.VMEM((rows, LANES), i32),
            pltpu.SemaphoreType.DMA((20,)),
        ],
        compiler_params=WHOLE,
        name="pack",
    )(h, p, q, b, m)


def merge_coefficients(one, two):
    t1, gl1, gr1 = one
    t2, gl2, gr2 = two
    shunt = gr1 + gl2
    inverse = 1.0 / (t1 + t2 + shunt)
    w1, w2 = t1 * inverse, t2 * inverse
    return (w1 * t2, gl1 + w1 * shunt, gr2 + w2 * shunt), (w1, w2, inverse)


def merge_sources(one, two, weights):
    w1, w2, inverse = weights
    source = one[1] - two[0]
    return (one[0] - w1 * source, two[1] + w2 * source), source * inverse


def merge(one, two):
    coefficients, weights = merge_coefficients(one[:3], two[:3])
    sources, middle = merge_sources(one[3:], two[3:], weights)
    return coefficients + sources, weights[:2] + (middle,)


def log2(count):
    return (count - 1).bit_length()


def full(ref, step):
    return jnp.concatenate([ref[at(tile, step), :] for tile in range(ref.shape[0] // LANES)])


def march_depth(inv_ref, scale, out_t, out_w, levels):
    count = inv_ref.shape[0] // STEPS
    zero = jnp.zeros((count, LANES), F32)
    alpha, gamma, beta, delta = zero, zero, zero, zero
    for k in range(STEPS):
        inverse = full(inv_ref, k)
        d = scale * (inverse * inverse)
        alpha = alpha + gamma
        gamma = gamma + d * (1.0 + alpha)
        beta = beta + delta
        delta = delta + d * ((k + 1.0) + beta)
    t = 1.0 / (STEPS + beta)
    out_t[0] = t
    out_t[1] = t * alpha
    out_t[2] = 1.0 + delta
    coefficients = (t, t * alpha, t * delta)
    for level in range(levels):
        after = tuple(pltpu.roll(v, count - (1 << level), 0) for v in coefficients)
        coefficients, weights = merge_coefficients(coefficients, after)
        for j, v in enumerate(weights):
            out_w[3 * level + j] = v
    return coefficients


def prepare_kernel(
    h, p, q, b, m,
    hx, px, qx, bx, mx, ix, hy, py, qy, by, my, iy, tx, wx, ty, wy, endx, endy,
    hs, ps, qs, bs, ms, turned, sems,
    *, inv_cx, inv_cy,
):
    rows, cols = h.shape
    tiles = cols // LANES
    copies = []
    for f, (src, target) in enumerate(zip((h, p, q, b, m), (hs, ps, qs, bs, ms))):
        for tile in range(tiles):
            copies.append(
                pltpu.make_async_copy(
                    src.at[:, pl.ds(tile * LANES, LANES)],
                    target.at[pl.ds(tile * rows, rows), :],
                    sems.at[f * tiles + tile],
                )
            )
            copies[-1].start()
    for f, (src, xs, ys) in enumerate(
        ((hs, hx, hy), (ps, px, py), (qs, qx, qy), (bs, bx, by), (ms, mx, my))
    ):
        for tile in range(tiles):
            copies[f * tiles + tile].wait()
            for k in range(STEPS):
                xs[at(tile, k), :] = src[spread_rows(tile, k), :].astype(F32)
            turned[f % 2, tile_span(tile), :] = xs[tile_span(tile), :].T
            for k in range(STEPS):
                ys[at(tile, k), :] = turned[f % 2, spread_rows(tile, k), :]
        if f == 0:
            ix[...] = 1.0 / hx[...]
            iy[...] = 1.0 / hy[...]
            ends_x = march_depth(ix, inv_cx, tx, wx, log2(SUB))
            ends_y = march_depth(iy, inv_cy, ty, wy, log2(SUB * tiles))
            for i in range(3):
                for tile in range(tiles):
                    endx[i : i + 1, tile_span(tile)] = ends_x[i][tile * SUB : tile * SUB + 1, :]
                endy[i : i + 1, :] = ends_y[i][0:1, :]
            endx[3:8, :] = jnp.zeros((5, cols), F32)
            endy[3:8, :] = jnp.zeros((5, rows), F32)


def prepare(h, p, q, b, m, inv_cx, inv_cy):
    rows, cols = h.shape
    tiles = cols // LANES
    count = tiles * SUB
    stack = (tiles * LANES, LANES)
    shapes = [shape(*stack)] * 12 + [
        shape(3, count, LANES),
        shape(3 * log2(SUB), count, LANES),
        shape(3, count, LANES),
        shape(3 * log2(count), count, LANES),
        shape(SUB, cols),
        shape(SUB, rows),
    ]
    return pl.pallas_call(
        functools.partial(prepare_kernel, inv_cx=inv_cx, inv_cy=inv_cy),
        out_shape=tuple(shapes),
        in_specs=[HBM] * 5,
        out_specs=(VMEM,) * len(shapes),
        scratch_shapes=[
            *[pltpu.VMEM(stack, v.dtype) for v in (h, p, q, b, m)],
            pltpu.VMEM((2, *stack), F32),
            pltpu.SemaphoreType.DMA((5 * tiles,)),
        ],
        compiler_params=PARAMS,
        cost_estimate=pl.CostEstimate(flops=2_000_000, bytes_accessed=8_000_000, transcendentals=0),
        name="prepare",
    )(h, p, q, b, m)


def low_high(axis, near, far):
    index, count = lax.axis_index(axis), lax.axis_size(axis)
    even = index % 2 == 0
    low = jnp.where(index > 0, jnp.where(even, far, near), 0.0)
    high = jnp.where(index < count - 1, jnp.where(even, near, far), 0.0)
    return low, high


def half_slope(a, c):
    return 0.5 * (jnp.maximum(jnp.minimum(a, c), 0.0) + jnp.minimum(jnp.maximum(a, c), 0.0))


def face_flux(left, right, opened):
    is_open = opened > 0.5
    hl = jnp.where(is_open, left[0], 1.0)
    hr = jnp.where(is_open, right[0], 1.0)
    joint = 1.0 / (hl * hr)
    ul = left[1] * (hr * joint)
    ur = right[1] * (hl * joint)
    gl = gravity * hl
    gr = gravity * hr
    fastest = jnp.maximum(jnp.abs(ul) + gl * lax.rsqrt(gl), jnp.abs(ur) + gr * lax.rsqrt(gr))
    scale = (0.5 * ratio) * opened
    mass = (left[1] + right[1]) - fastest * (right[0] - left[0])
    push = 0.5 * (gl * hl + gr * hr) + left[1] * ul + right[1] * ur - fastest * (right[1] - left[1])
    shear = left[2] * ul + right[2] * ur - fastest * (right[2] - left[2])
    return scale * mass, scale * push, scale * shear


def extended(ref, tile, lows, highs):
    sub = row_index((SUB, LANES))
    out = {}
    for n, row in enumerate(lows, 1):
        value = ref[at(tile, STEPS - n), :]
        out[-n] = jnp.where(sub == 0, row, pltpu.roll(value, 1, 0))
    for n, row in enumerate(highs):
        value = ref[at(tile, n), :]
        out[STEPS + n] = jnp.where(sub == SUB - 1, row, pltpu.roll(value, SUB - 1, 0))
    return lambda k: out[k] if k in out else ref[at(tile, k), :]


def tile_fluxes(fields, bed, wet, store):
    def states(k):
        both = []
        for w in fields:
            here = w(k)
            both.append((here, half_slope(here - w(k - 1), w(k + 1) - here)))
        return [w + s for w, s in both], [w - s for w, s in both]

    left, _ = states(-1)
    before = None
    for k in range(-1, STEPS):
        left_next, right = states(k + 1)
        face = face_flux(left, right, wet(k) * wet(k + 1))
        left = left_next
        if k >= 0:
            store(k, [a - c for a, c in zip(face, before)], bed(k + 1) - bed(k - 1))
        before = face


def march_source(inv_ref, scale, r_ref, t_ref, w_ref, s_ref, levels):
    count = inv_ref.shape[0] // STEPS
    c = jnp.zeros((count, LANES), F32)
    e = c
    for k in range(STEPS):
        inverse = full(inv_ref, k)
        c = c + e
        e = e + (scale * (inverse * inverse) * c - full(r_ref, k))
    sl = t_ref[0] * c
    s_ref[0] = sl
    sources = (sl, t_ref[2] * sl - e)
    for level in range(levels):
        after = tuple(pltpu.roll(v, count - (1 << level), 0) for v in sources)
        sources, middle = merge_sources(sources, after, tuple(w_ref[3 * level + j] for j in range(3)))
        s_ref[1 + level] = middle
    return sources


def flux_kernel(
    near_x, far_x, near_y, far_y,
    hx, px, qx, bx, mx, ix, hy, py, qy, by, my, iy, tx, wx, ty, wy, coefx, coefy,
    depth, rx, ry, sx, sy, endx, endy, tally,
    xpart, ypart, turned,
    *, inv_cx, inv_cy,
):
    tiles = hx.shape[0] // LANES
    low_x, high_x = low_high("gx", near_x[0], far_x[0:SUB, :])
    low_y, high_y = low_high("gy", near_y[0], far_y[0:SUB, :])

    for tile in range(tiles):
        span = tile_span(tile)

        def along_x(ref, row, layers):
            lows = [low_x[row + layers - 1 - n : row + layers - n, span] for n in range(layers)]
            highs = [high_x[row + n : row + n + 1, span] for n in range(layers)]
            return extended(ref, tile, lows, highs)

        def store_x(k, difference, bed):
            here = at(tile, k)
            for i in range(3):
                xpart[i, here, :] = difference[i]
            xpart[3, here, :] = bed

        tile_fluxes(
            [along_x(hx, 0, 2), along_x(px, 2, 2), along_x(qx, 4, 2)],
            along_x(bx, 6, 1), along_x(mx, 7, 1), store_x,
        )

        def along_y(ref, row, layers):
            lows, highs = [], []
            for n in range(layers):
                last = at(tile - 1, STEPS - 1 - n).stop - 1
                first = at(tile + 1, n).start
                lows.append(low_y[row + layers - 1 - n : row + layers - n, :] if tile == 0 else ref[last : last + 1, :])
                highs.append(high_y[row + n : row + n + 1, :] if tile == tiles - 1 else ref[first : first + 1, :])
            return extended(ref, tile, lows, highs)

        def store_y(k, difference, bed):
            here, natural = at(tile, k), spread_rows(tile, k)
            ypart[0, natural, :] = difference[0]
            ypart[1, here, :] = difference[1]
            ypart[2, natural, :] = difference[2]
            ypart[3, here, :] = bed

        tile_fluxes(
            [along_y(hy, 0, 2), along_y(qy, 4, 2), along_y(py, 2, 2)],
            along_y(by, 6, 1), along_y(my, 7, 1), store_y,
        )
        turned[span, :] = xpart[2, span, :].T
        from_y_mass = ypart[0, span, :].T
        from_y_shear = ypart[2, span, :].T
        h, m, inverse = hx[span, :], mx[span, :], ix[span, :]
        depth[span, :] = h - m * (xpart[0, span, :] + from_y_mass)
        push = px[span, :] - xpart[1, span, :] - from_y_shear - (0.5 * ratio * gravity) * h * xpart[3, span, :]
        rx[span, :] = (inv_cx * (inverse * inverse)) * m * push
        for k in range(STEPS):
            here = at(tile, k)
            inverse = iy[here, :]
            push = qy[here, :] - turned[spread_rows(tile, k), :] - ypart[1, here, :]
            push = push - (0.5 * ratio * gravity) * hy[here, :] * ypart[3, here, :]
            ry[here, :] = (inv_cy * (inverse * inverse)) * my[here, :] * push

    ends_x = march_source(ix, inv_cx, rx, tx, wx, sx, log2(SUB))
    ends_y = march_source(iy, inv_cy, ry, ty, wy, sy, log2(SUB * tiles))
    endx[...] = coefx[...]
    endy[...] = coefy[...]
    for i in range(2):
        for tile in range(tiles):
            endx[3 + i : 4 + i, tile_span(tile)] = ends_x[i][tile * SUB : tile * SUB + 1, :]
        endy[3 + i : 4 + i, :] = ends_y[i][0:1, :]
    tally[...] = jnp.zeros_like(tally)
    tally[0:SUB, :] = endy[...]


def fluxes(slabs, prepared, inv_cx, inv_cy):
    stack = prepared[0].shape
    count = stack[0] // STEPS
    shapes = (
        shape(*stack),
        shape(*stack),
        shape(*stack),
        shape(1 + log2(SUB), count, LANES),
        shape(1 + log2(count), count, LANES),
        shape(*prepared[-2].shape),
        shape(*prepared[-1].shape),
        shape(3 * SUB, prepared[-1].shape[1]),
    )
    return pl.pallas_call(
        functools.partial(flux_kernel, inv_cx=inv_cx, inv_cy=inv_cy),
        out_shape=shapes,
        in_specs=[VMEM] * (len(slabs) + len(prepared)),
        out_specs=(VMEM,) * len(shapes),
        scratch_shapes=[
            pltpu.VMEM((4, *stack), F32),
            pltpu.VMEM((4, *stack), F32),
            pltpu.VMEM(stack, F32),
        ],
        compiler_params=PARAMS,
        name="fluxes",
    )(*slabs, *prepared)


def tile_write(tiled, whole, tile, sems):
    rows = whole.shape[0]
    return pltpu.make_async_copy(
        tiled.at[pl.ds(tile * rows, rows), :], whole.at[:, pl.ds(tile * LANES, LANES)], sems.at[tile]
    )


def write_scratch(cols):
    return [pltpu.VMEM((cols, LANES), F32), pltpu.SemaphoreType.DMA((cols // LANES,))]


def depth_kernel(depth, out, natural, sems):
    writes = []
    for tile in range(depth.shape[0] // LANES):
        for k in range(STEPS):
            natural[spread_rows(tile, k), :] = depth[at(tile, k), :]
        writes.append(tile_write(natural, out, tile, sems))
        writes[-1].start()
    for write in writes:
        write.wait()


def write_depth(depth, block):
    return pl.pallas_call(
        depth_kernel,
        out_shape=shape(*block),
        in_specs=[VMEM],
        out_specs=ANY,
        scratch_shapes=write_scratch(block[1]),
        compiler_params=PARAMS,
        cost_estimate=pl.CostEstimate(flops=100_000, bytes_accessed=2_000_000, transcendentals=0),
        name="write_depth",
    )(depth)


def rows_of(ref):
    return tuple(ref[i : i + 1, :] for i in range(5))


def ordered(axis, stage, mine, theirs):
    is_low = (lax.axis_index(axis) >> stage) % 2 == 0
    one = tuple(jnp.where(is_low, a, b) for a, b in zip(mine, theirs))
    two = tuple(jnp.where(is_low, b, a) for a, b in zip(mine, theirs))
    return is_low, merge(one, two)


def merge_kernel(mine, theirs, *refs, axis, stage):
    out = refs[-1]
    _, (merged, _) = ordered(axis, stage, rows_of(mine), rows_of(theirs))
    for i, v in enumerate(merged):
        out[i : i + 1, :] = v
    out[5:8, :] = jnp.zeros((3, out.shape[1]), F32)


def merge_call(axis, stage, mine, theirs, beside):
    return pl.pallas_call(
        functools.partial(merge_kernel, axis=axis, stage=stage),
        out_shape=shape(*mine.shape),
        in_specs=[VMEM] * (2 + len(beside)),
        out_specs=VMEM,
        compiler_params=PARAMS,
        name="merge",
    )(mine, theirs, *beside)


def line_ends(axis, refs):
    steps = []
    parts = [rows_of(ref) for ref in refs]
    stage = 0
    while len(parts) > 4:
        is_low, (_, weights) = ordered(axis, stage, *parts[:2])
        steps.append((is_low, weights))
        parts = parts[2:]
        stage += 1
    is_low, (own, weights) = ordered(axis, stage, *parts[:2])
    steps.append((is_low, weights))
    _, (other, _) = ordered(axis, stage, *parts[2:])
    is_low, (whole, weights) = ordered(axis, stage + 1, own, other)
    steps.append((is_low, weights))
    t, _, gr, _, sr = whole
    left = jnp.zeros_like(t)
    right = sr / (t + gr + 1.0)
    for is_low, (w1, w2, source) in reversed(steps):
        middle = w1 * left + w2 * right + source
        left = jnp.where(is_low, left, middle)
        right = jnp.where(is_low, middle, right)
    return left, right


def segment_ends(left, right, w_ref, s_ref, levels):
    index = row_index(left.shape)
    for level in reversed(range(levels)):
        stride = 1 << level
        middle = w_ref[3 * level] * left + w_ref[3 * level + 1] * right + s_ref[1 + level]
        upper = (index >> level) % 2 == 1
        left, right = (
            jnp.where(upper, pltpu.roll(middle, stride, 0), left),
            jnp.where(upper, pltpu.roll(right, stride, 0), middle),
        )
    return left, right


def march_values(left, right, t_ref, s_ref, inv_ref, scale, r_ref, store):
    value = left
    change = t_ref[0] * (right - left) - t_ref[1] * left - s_ref[0]
    for k in range(STEPS):
        inverse = full(inv_ref, k)
        value = value + change
        change = change + (scale * (inverse * inverse) * value - full(r_ref, k))
        store(k, value * inverse)


def solve_x_kernel(inv_ref, r_ref, t_ref, w_ref, s_ref, *refs, scale):
    parts, (out, natural, sems) = refs[:-3], refs[-3:]
    tiles = out.shape[1] // LANES
    ends = []
    for row in line_ends("gx", parts):
        ends.append(
            jnp.concatenate([jnp.broadcast_to(row[:, tile_span(t)], (SUB, LANES)) for t in range(tiles)])
        )
    left, right = segment_ends(*ends, w_ref, s_ref, log2(SUB))

    def store(k, speed):
        for tile in range(tiles):
            natural[spread_rows(tile, k), :] = speed[tile * SUB : (tile + 1) * SUB, :]

    march_values(left, right, t_ref, s_ref, inv_ref, scale, r_ref, store)
    writes = [tile_write(natural, out, tile, sems) for tile in range(tiles)]
    for write in writes:
        write.start()
    for write in writes:
        write.wait()


def solve_y_kernel(inv_ref, r_ref, t_ref, w_ref, s_ref, *refs, scale):
    parts, (out, natural, sems, turned) = refs[:-4], refs[-4:]
    tiles = out.shape[1] // LANES
    ends = line_ends("gy", parts)
    ends = [jnp.broadcast_to(row, (tiles * SUB, LANES)) for row in ends]
    left, right = segment_ends(*ends, w_ref, s_ref, log2(tiles * SUB))

    def store(k, speed):
        for tile in range(tiles):
            turned[spread_rows(tile, k), :] = speed[tile * SUB : (tile + 1) * SUB, :]

    march_values(left, right, t_ref, s_ref, inv_ref, scale, r_ref, store)
    writes = []
    for tile in range(tiles):
        block = turned[tile_span(tile), :].T
        for k in range(STEPS):
            natural[spread_rows(tile, k), :] = block[k * SUB : (k + 1) * SUB, :]
        writes.append(tile_write(natural, out, tile, sems))
        writes[-1].start()
    for write in writes:
        write.wait()


def solve(kernel, name, pieces, parts, block, scale, extra=()):
    return pl.pallas_call(
        functools.partial(kernel, scale=scale),
        out_shape=shape(*block),
        in_specs=[VMEM] * (len(pieces) + len(parts)),
        out_specs=ANY,
        scratch_shapes=write_scratch(block[1]) + list(extra),
        compiler_params=PARAMS,
        cost_estimate=pl.CostEstimate(flops=1_000_000, bytes_accessed=4_000_000, transcendentals=0),
        name=name,
    )(*pieces, *parts)


def hand_on(value, axis):
    count = lax.axis_size(axis)
    far = [i + 2 if i % 2 == 0 else i - 2 for i in range(count)]
    return lax.ppermute(value, axis, [(i, t if 0 <= t < count else i ^ 1) for i, t in enumerate(far)])


def cross(value, axis, mask):
    return lax.ppermute(value, axis, [(i, i ^ mask) for i in range(lax.axis_size(axis))])


def parts_of_line(axis, mine, relay, beside=(), tall=None):
    parts = []
    last = log2(lax.axis_size(axis)) - 2
    for stage in range(last):
        theirs = cross(mine, axis, 1 << stage)
        parts += [mine, theirs]
        mine = merge_call(axis, stage, mine, theirs, beside)
    if relay:
        first = cross(mine, axis, 1 << last)
        second = cross(mine if tall is None else tall, axis, 2 << last)
        both = cross(second[0:SUB], axis, 1 << last)
    else:
        both = cross(mine, axis, 3 << last)
        second = cross(mine, axis, 2 << last)
        first = cross(mine, axis, 1 << last)
    return parts + [mine, first, second, both]


def on_device(h, p, q, b, m):
    block = h.shape
    rows, cols = block
    inv_cx = 3.0 / (rows * lax.axis_size("gx") / 4.0) ** 2
    inv_cy = 3.0 / (cols * lax.axis_size("gy") / 4.0) ** 2
    xa, ya = pack(h, p, q, b, m)
    near_x, near_y = cross(xa, "gx", 1), cross(ya, "gy", 1)
    far_y = hand_on(jnp.pad(near_y[1], ((0, 5 * SUB), (0, 0))), "gy")
    far_x = hand_on(near_x[1], "gx")
    prepared = prepare(h, p, q, b, m, inv_cx, inv_cy)
    depth, rx, ry, sx, sy, end_x, end_y, tall_y = fluxes((near_x, far_x, near_y, far_y), prepared, inv_cx, inv_cy)
    ix, iy = prepared[5], prepared[11]
    tx, wx, ty, wy = prepared[12:16]
    new_depth = write_depth(depth, block)
    parts_y = parts_of_line("gy", end_y, True, tall=tall_y if lax.axis_size("gy") == 4 else None)
    parts_x = parts_of_line("gx", end_x, False, parts_y[1:2])
    turned = [pltpu.VMEM((cols, LANES), F32)]
    vy = solve(solve_y_kernel, "solve_y", (iy, ry, ty, wy, sy), parts_y, block, inv_cy, turned)
    vx = solve(solve_x_kernel, "solve_x", (ix, rx, tx, wx, sx), parts_x, block, inv_cx)
    return new_depth, vx, vy


def solution(mesh):
    spec = P("gx", "gy")
    return jax.shard_map(
        on_device,
        mesh=mesh,
        in_specs=(spec,) * 5,
        out_specs=(spec,) * 3,
        check_vma=False,
    )
```

```python
import functools

import jax
import jax.numpy as jnp
from jax import lax
from jax.experimental import pallas as pl
from jax.experimental.pallas import tpu as pltpu
from jax.sharding import PartitionSpec as P

gravity = 9.81
ratio = 0.05
LANES = 128
SUB = 8
STEPS = LANES // SUB
F32 = jnp.float32
VMEM = pl.BlockSpec(memory_space=pltpu.VMEM)
HBM = pl.BlockSpec(memory_space=pltpu.HBM)
ANY = pl.BlockSpec(memory_space=pl.ANY)
PARAMS = pltpu.CompilerParams(vmem_limit_bytes=16 * 1024 * 1024)


def lane_index(shape):
    return lax.broadcasted_iota(jnp.int32, shape, len(shape) - 1)


def row_index(shape):
    return lax.broadcasted_iota(jnp.int32, shape, len(shape) - 2)


def at(tile, step):
    first = tile * LANES + step * SUB
    return slice(first, first + SUB)


def tile_span(tile):
    return slice(tile * LANES, (tile + 1) * LANES)


def spread_rows(tile, step):
    return pl.ds(tile * LANES + step, SUB, stride=STEPS)


def shape(*dims):
    return jax.ShapeDtypeStruct(dims, F32)


def pack_kernel(h, p, q, b, m, xa, ya, hs, ps, qs, bs, ms, top, bottom, itop, ibottom, sems_x, sems):
    rows, cols = h.shape
    tiles = cols // LANES
    sources = (h, p, q, b, m)
    stacks = (hs, ps, qs, bs, ms)
    edges = []
    for f, src in enumerate(sources):
        for side, (target, whole, row) in enumerate(((top, itop, 0), (bottom, ibottom, rows - SUB))):
            copy = pltpu.make_async_copy(
                src.at[pl.ds(row, SUB), :], target.at[f] if f < 4 else whole, sems_x.at[2 * f + side]
            )
            copy.start()
            edges.append(copy)
    loads = {}
    for tile in [0, tiles - 1] + list(range(1, tiles - 1)):
        for f, (src, target) in enumerate(zip(sources, stacks)):
            copy = pltpu.make_async_copy(
                src.at[:, pl.ds(tile * LANES, LANES)],
                target.at[pl.ds(tile * rows, rows), :],
                sems.at[f * tiles + tile],
            )
            copy.start()
            loads[tile, f] = copy
    for copy in edges:
        copy.wait()
    first_x = jnp.concatenate(
        [top[0, 0:2, :], top[1, 0:2, :], top[2, 0:2, :], top[3, 0:1, :], itop[0:1, :].astype(F32)]
    )
    last_x = jnp.concatenate(
        [
            bottom[0, SUB - 2 : SUB, :],
            bottom[1, SUB - 2 : SUB, :],
            bottom[2, SUB - 2 : SUB, :],
            bottom[3, SUB - 1 : SUB, :],
            ibottom[SUB - 1 : SUB, :].astype(F32),
        ]
    )
    even_x = lax.axis_index("gx") % 2 == 0
    xa[0] = jnp.where(even_x, last_x, first_x)
    xa[1] = jnp.where(even_x, first_x, last_x)
    lane = lane_index((rows, LANES))
    out = jnp.zeros((rows, LANES), F32)
    for tile, start, shifts in ((0, 0, (0, 2, 4, 6, 7)), (tiles - 1, SUB, (10, 12, 14, 15, 16))):
        for f, (ref, to, shift) in enumerate(zip(stacks, (0, 2, 4, 6, 7), shifts)):
            loads[tile, f].wait()
            value = jnp.concatenate([ref[spread_rows(tile, k), :] for k in range(STEPS)]).astype(F32)
            out = jnp.where(lane >= start + to, pltpu.roll(value, shift, 1) if shift else value, out)
    turned = out.T
    first_y, last_y = turned[0:SUB, :], turned[SUB : 2 * SUB, :]
    even_y = lax.axis_index("gy") % 2 == 0
    ya[0] = jnp.where(even_y, last_y, first_y)
    ya[1] = jnp.where(even_y, first_y, last_y)
    for tile in range(1, tiles - 1):
        for f in range(len(sources)):
            loads[tile, f].wait()


def pack(*fields):
    rows, cols = fields[0].shape
    tiles = cols // LANES
    stacks = [jax.ShapeDtypeStruct((tiles * rows, LANES), v.dtype) for v in fields]
    return pl.pallas_call(
        pack_kernel,
        out_shape=(shape(2, SUB, cols), shape(2, SUB, rows), *stacks),
        in_specs=[HBM] * 5,
        out_specs=(VMEM,) * 7,
        scratch_shapes=[
            pltpu.VMEM((4, SUB, cols), F32),
            pltpu.VMEM((4, SUB, cols), F32),
            pltpu.VMEM((SUB, cols), jnp.int32),
            pltpu.VMEM((SUB, cols), jnp.int32),
            pltpu.SemaphoreType.DMA((10,)),
            pltpu.SemaphoreType.DMA((5 * tiles,)),
        ],
        compiler_params=PARAMS,
        name="pack",
    )(*[pltpu.with_memory_space_constraint(v, pltpu.HBM) for v in fields])


def tie_kernel(both, _, out):
    out[...] = both[1]


def second_of(both, after):
    return pl.pallas_call(
        tie_kernel,
        out_shape=shape(*both.shape[1:]),
        in_specs=[VMEM, VMEM],
        out_specs=VMEM,
        compiler_params=PARAMS,
        name="second_of",
    )(both, after)


def merge_coefficients(one, two):
    t1, gl1, gr1 = one
    t2, gl2, gr2 = two
    shunt = gr1 + gl2
    inverse = 1.0 / (t1 + t2 + shunt)
    w1, w2 = t1 * inverse, t2 * inverse
    return (w1 * t2, gl1 + w1 * shunt, gr2 + w2 * shunt), (w1, w2, inverse)


def merge_sources(one, two, weights):
    w1, w2, inverse = weights
    source = one[1] - two[0]
    return (one[0] - w1 * source, two[1] + w2 * source), source * inverse


def merge(one, two):
    coefficients, weights = merge_coefficients(one[:3], two[:3])
    sources, middle = merge_sources(one[3:], two[3:], weights)
    return coefficients + sources, weights[:2] + (middle,)


def log2(count):
    return (count - 1).bit_length()


def full(ref, step):
    return jnp.concatenate([ref[at(tile, step), :] for tile in range(ref.shape[0] // LANES)])


def march_depth(inv_ref, scale, out_t, out_w, levels):
    count = inv_ref.shape[0] // STEPS
    zero = jnp.zeros((count, LANES), F32)
    alpha, gamma, beta, delta = zero, zero, zero, zero
    for k in range(STEPS):
        inverse = full(inv_ref, k)
        d = scale * (inverse * inverse)
        alpha = alpha + gamma
        gamma = gamma + d * (1.0 + alpha)
        beta = beta + delta
        delta = delta + d * ((k + 1.0) + beta)
    t = 1.0 / (STEPS + beta)
    out_t[0] = t
    out_t[1] = t * alpha
    out_t[2] = 1.0 + delta
    coefficients = (t, t * alpha, t * delta)
    for level in range(levels):
        after = tuple(pltpu.roll(v, count - (1 << level), 0) for v in coefficients)
        coefficients, weights = merge_coefficients(coefficients, after)
        for j, v in enumerate(weights):
            out_w[3 * level + j] = v
    return coefficients


def lay_out(src, xs, ys, turned):
    for tile in range(src.shape[0] // LANES):
        for k in range(STEPS):
            xs[at(tile, k), :] = src[spread_rows(tile, k), :].astype(F32)
        turned[tile_span(tile), :] = xs[tile_span(tile), :].T
        for k in range(STEPS):
            ys[at(tile, k), :] = turned[spread_rows(tile, k), :]


def prepare_depth_kernel(hs, hx, hy, ix, iy, tx, wx, ty, wy, endx, endy, turned, *, inv_cx, inv_cy):
    tiles = hs.shape[0] // LANES
    lay_out(hs, hx, hy, turned)
    ix[...] = 1.0 / hx[...]
    iy[...] = 1.0 / hy[...]
    ends_x = march_depth(ix, inv_cx, tx, wx, log2(SUB))
    ends_y = march_depth(iy, inv_cy, ty, wy, log2(SUB * tiles))
    for i in range(3):
        for tile in range(tiles):
            endx[i : i + 1, tile_span(tile)] = ends_x[i][tile * SUB : tile * SUB + 1, :]
        endy[i : i + 1, :] = ends_y[i][0:1, :]
    endx[3:8, :] = jnp.zeros((5, endx.shape[1]), F32)
    endy[3:8, :] = jnp.zeros((5, endy.shape[1]), F32)


def prepare_depth(hs, inv_cx, inv_cy):
    stack = hs.shape
    count = stack[0] // STEPS
    shapes = [shape(*stack)] * 4 + [
        shape(3, count, LANES),
        shape(3 * log2(SUB), count, LANES),
        shape(3, count, LANES),
        shape(3 * log2(count), count, LANES),
        shape(SUB, stack[0]),
        shape(SUB, LANES),
    ]
    return pl.pallas_call(
        functools.partial(prepare_depth_kernel, inv_cx=inv_cx, inv_cy=inv_cy),
        out_shape=tuple(shapes),
        in_specs=[VMEM],
        out_specs=(VMEM,) * len(shapes),
        scratch_shapes=[pltpu.VMEM(stack, F32)],
        compiler_params=PARAMS,
        cost_estimate=pl.CostEstimate(flops=2_000_000, bytes_accessed=4_000_000, transcendentals=0),
        name="prepare_depth",
    )(hs)


def prepare_rest_kernel(*refs):
    sources, outs, turned = refs[:4], refs[4:12], refs[12]
    for f, src in enumerate(sources):
        lay_out(src, outs[2 * f], outs[2 * f + 1], turned.at[f % 2])


def prepare_rest(*sources):
    stack = sources[0].shape
    return pl.pallas_call(
        prepare_rest_kernel,
        out_shape=(shape(*stack),) * 8,
        in_specs=[VMEM] * 4,
        out_specs=(VMEM,) * 8,
        scratch_shapes=[pltpu.VMEM((2, *stack), F32)],
        compiler_params=PARAMS,
        cost_estimate=pl.CostEstimate(flops=2_000_000, bytes_accessed=6_000_000, transcendentals=0),
        name="prepare_rest",
    )(*sources)


def low_high(axis, near, far):
    index, count = lax.axis_index(axis), lax.axis_size(axis)
    even = index % 2 == 0
    low = jnp.where(index > 0, jnp.where(even, far, near), 0.0)
    high = jnp.where(index < count - 1, jnp.where(even, near, far), 0.0)
    return low, high


def half_slope(a, c):
    return 0.5 * (jnp.maximum(jnp.minimum(a, c), 0.0) + jnp.minimum(jnp.maximum(a, c), 0.0))


def face_flux(left, right, opened):
    is_open = opened > 0.5
    hl = jnp.where(is_open, left[0], 1.0)
    hr = jnp.where(is_open, right[0], 1.0)
    joint = 1.0 / (hl * hr)
    ul = left[1] * (hr * joint)
    ur = right[1] * (hl * joint)
    gl = gravity * hl
    gr = gravity * hr
    fastest = jnp.maximum(jnp.abs(ul) + gl * lax.rsqrt(gl), jnp.abs(ur) + gr * lax.rsqrt(gr))
    scale = (0.5 * ratio) * opened
    mass = (left[1] + right[1]) - fastest * (right[0] - left[0])
    push = 0.5 * (gl * hl + gr * hr) + left[1] * ul + right[1] * ur - fastest * (right[1] - left[1])
    shear = left[2] * ul + right[2] * ur - fastest * (right[2] - left[2])
    return scale * mass, scale * push, scale * shear


def extended(ref, tile, lows, highs):
    sub = row_index((SUB, LANES))
    out = {}
    for n, row in enumerate(lows, 1):
        value = ref[at(tile, STEPS - n), :]
        out[-n] = jnp.where(sub == 0, row, pltpu.roll(value, 1, 0))
    for n, row in enumerate(highs):
        value = ref[at(tile, n), :]
        out[STEPS + n] = jnp.where(sub == SUB - 1, row, pltpu.roll(value, SUB - 1, 0))
    return lambda k: out[k] if k in out else ref[at(tile, k), :]


def tile_fluxes(fields, bed, wet, store):
    def states(k):
        both = []
        for w in fields:
            here = w(k)
            both.append((here, half_slope(here - w(k - 1), w(k + 1) - here)))
        return [w + s for w, s in both], [w - s for w, s in both]

    left, _ = states(-1)
    before = None
    for k in range(-1, STEPS):
        left_next, right = states(k + 1)
        face = face_flux(left, right, wet(k) * wet(k + 1))
        left = left_next
        if k >= 0:
            store(k, [a - c for a, c in zip(face, before)], bed(k + 1) - bed(k - 1))
        before = face


def march_source(inv_ref, scale, r_ref, t_ref, w_ref, s_ref, levels):
    count = inv_ref.shape[0] // STEPS
    c = jnp.zeros((count, LANES), F32)
    e = c
    for k in range(STEPS):
        inverse = full(inv_ref, k)
        c = c + e
        e = e + (scale * (inverse * inverse) * c - full(r_ref, k))
    sl = t_ref[0] * c
    s_ref[0] = sl
    sources = (sl, t_ref[2] * sl - e)
    for level in range(levels):
        after = tuple(pltpu.roll(v, count - (1 << level), 0) for v in sources)
        sources, middle = merge_sources(sources, after, tuple(w_ref[3 * level + j] for j in range(3)))
        s_ref[1 + level] = middle
    return sources


def flux_y_kernel(near, far, hy, py, qy, by, my, mass, shear, normal, across, along):
    tiles = hy.shape[0] // LANES
    low, high = low_high("gy", near[0], far[0:SUB, :])
    for tile in range(tiles):

        def extend(ref, row, layers):
            lows, highs = [], []
            for n in range(layers):
                last = at(tile - 1, STEPS - 1 - n).stop - 1
                first = at(tile + 1, n).start
                lows.append(low[row + layers - 1 - n : row + layers - n, :] if tile == 0 else ref[last : last + 1, :])
                highs.append(high[row + n : row + n + 1, :] if tile == tiles - 1 else ref[first : first + 1, :])
            return extended(ref, tile, lows, highs)

        def store(k, difference, bed):
            here, natural = at(tile, k), spread_rows(tile, k)
            across[natural, :] = difference[0]
            along[natural, :] = difference[2]
            pull = (0.5 * ratio * gravity) * hy[here, :]
            normal[here, :] = qy[here, :] - difference[1] - pull * bed

        tile_fluxes([extend(hy, 0, 2), extend(qy, 4, 2), extend(py, 2, 2)], extend(by, 6, 1), extend(my, 7, 1), store)
        span = tile_span(tile)
        mass[span, :] = across[span, :].T
        shear[span, :] = along[span, :].T


def fluxes_y(*arrays):
    stack = arrays[2].shape
    return pl.pallas_call(
        flux_y_kernel,
        out_shape=(shape(*stack),) * 3,
        in_specs=[VMEM] * len(arrays),
        out_specs=(VMEM,) * 3,
        scratch_shapes=[pltpu.VMEM(stack, F32)] * 2,
        compiler_params=PARAMS,
        cost_estimate=pl.CostEstimate(flops=4_000_000, bytes_accessed=4_000_000, transcendentals=0),
        name="fluxes_y",
    )(*arrays)


def flux_x_kernel(
    near, far, hx, px, qx, bx, mx, ix, iy, my, mass_y, shear_y, normal_y, tx, wx, ty, wy, coefx, coefy,
    depth, rx, ry, sx, sy, endx, endy, tally,
    across, turned,
    *, inv_cx, inv_cy,
):
    tiles = hx.shape[0] // LANES
    low, high = low_high("gx", near[0], far[...])
    for tile in range(tiles):
        span = tile_span(tile)

        def extend(ref, row, layers):
            lows = [low[row + layers - 1 - n : row + layers - n, span] for n in range(layers)]
            highs = [high[row + n : row + n + 1, span] for n in range(layers)]
            return extended(ref, tile, lows, highs)

        def store(k, difference, bed):
            here = at(tile, k)
            h, m, inverse = hx[here, :], mx[here, :], ix[here, :]
            depth[here, :] = h - m * (difference[0] + mass_y[here, :])
            push = px[here, :] - difference[1] - shear_y[here, :] - (0.5 * ratio * gravity) * h * bed
            rx[here, :] = (inv_cx * (inverse * inverse)) * m * push
            across[here, :] = difference[2]

        tile_fluxes([extend(hx, 0, 2), extend(px, 2, 2), extend(qx, 4, 2)], extend(bx, 6, 1), extend(mx, 7, 1), store)
        turned[span, :] = across[span, :].T
        for k in range(STEPS):
            here = at(tile, k)
            inverse = iy[here, :]
            push = normal_y[here, :] - turned[spread_rows(tile, k), :]
            ry[here, :] = (inv_cy * (inverse * inverse)) * my[here, :] * push

    ends_x = march_source(ix, inv_cx, rx, tx, wx, sx, log2(SUB))
    ends_y = march_source(iy, inv_cy, ry, ty, wy, sy, log2(SUB * tiles))
    endx[...] = coefx[...]
    endy[...] = coefy[...]
    for i in range(2):
        for tile in range(tiles):
            endx[3 + i : 4 + i, tile_span(tile)] = ends_x[i][tile * SUB : tile * SUB + 1, :]
        endy[3 + i : 4 + i, :] = ends_y[i][0:1, :]
    tally[...] = jnp.zeros_like(tally)
    tally[0:SUB, :] = endy[...]


def fluxes_x(*arrays, inv_cx, inv_cy):
    stack = arrays[2].shape
    count = stack[0] // STEPS
    shapes = (
        shape(*stack),
        shape(*stack),
        shape(*stack),
        shape(1 + log2(SUB), count, LANES),
        shape(1 + log2(count), count, LANES),
        shape(*arrays[-2].shape),
        shape(*arrays[-1].shape),
        shape(3 * SUB, arrays[-1].shape[1]),
    )
    return pl.pallas_call(
        functools.partial(flux_x_kernel, inv_cx=inv_cx, inv_cy=inv_cy),
        out_shape=shapes,
        in_specs=[VMEM] * len(arrays),
        out_specs=(VMEM,) * len(shapes),
        scratch_shapes=[pltpu.VMEM(stack, F32)] * 2,
        compiler_params=PARAMS,
        name="fluxes_x",
    )(*arrays)


def tile_write(tiled, whole, tile, sems):
    rows = whole.shape[0]
    return pltpu.make_async_copy(
        tiled.at[pl.ds(tile * rows, rows), :], whole.at[:, pl.ds(tile * LANES, LANES)], sems.at[tile]
    )


def write_scratch(cols):
    return [pltpu.VMEM((cols, LANES), F32), pltpu.SemaphoreType.DMA((cols // LANES,))]


def depth_kernel(depth, out, natural, sems):
    writes = []
    for tile in range(depth.shape[0] // LANES):
        for k in range(STEPS):
            natural[spread_rows(tile, k), :] = depth[at(tile, k), :]
        writes.append(tile_write(natural, out, tile, sems))
        writes[-1].start()
    for write in writes:
        write.wait()


def write_depth(depth, block):
    return pl.pallas_call(
        depth_kernel,
        out_shape=shape(*block),
        in_specs=[VMEM],
        out_specs=ANY,
        scratch_shapes=write_scratch(block[1]),
        compiler_params=PARAMS,
        cost_estimate=pl.CostEstimate(flops=100_000, bytes_accessed=2_000_000, transcendentals=0),
        name="write_depth",
    )(depth)


def rows_of(ref):
    return tuple(ref[i : i + 1, :] for i in range(5))


def ordered(axis, stage, mine, theirs):
    is_low = (lax.axis_index(axis) >> stage) % 2 == 0
    one = tuple(jnp.where(is_low, a, b) for a, b in zip(mine, theirs))
    two = tuple(jnp.where(is_low, b, a) for a, b in zip(mine, theirs))
    return is_low, merge(one, two)


def merge_kernel(mine, theirs, *refs, axis, stage):
    out = refs[-1]
    _, (merged, _) = ordered(axis, stage, rows_of(mine), rows_of(theirs))
    for i, v in enumerate(merged):
        out[i : i + 1, :] = v
    out[5:8, :] = jnp.zeros((3, out.shape[1]), F32)


def merge_call(axis, stage, mine, theirs, beside):
    return pl.pallas_call(
        functools.partial(merge_kernel, axis=axis, stage=stage),
        out_shape=shape(*mine.shape),
        in_specs=[VMEM] * (2 + len(beside)),
        out_specs=VMEM,
        compiler_params=PARAMS,
        name="merge",
    )(mine, theirs, *beside)


def line_ends(axis, refs):
    steps = []
    parts = [rows_of(ref) for ref in refs]
    stage = 0
    while len(parts) > 4:
        is_low, (_, weights) = ordered(axis, stage, *parts[:2])
        steps.append((is_low, weights))
        parts = parts[2:]
        stage += 1
    is_low, (own, weights) = ordered(axis, stage, *parts[:2])
    steps.append((is_low, weights))
    _, (other, _) = ordered(axis, stage, *parts[2:])
    is_low, (whole, weights) = ordered(axis, stage + 1, own, other)
    steps.append((is_low, weights))
    t, _, gr, _, sr = whole
    left = jnp.zeros_like(t)
    right = sr / (t + gr + 1.0)
    for is_low, (w1, w2, source) in reversed(steps):
        middle = w1 * left + w2 * right + source
        left = jnp.where(is_low, left, middle)
        right = jnp.where(is_low, middle, right)
    return left, right


def segment_ends(left, right, w_ref, s_ref, levels):
    index = row_index(left.shape)
    for level in reversed(range(levels)):
        stride = 1 << level
        middle = w_ref[3 * level] * left + w_ref[3 * level + 1] * right + s_ref[1 + level]
        upper = (index >> level) % 2 == 1
        left, right = (
            jnp.where(upper, pltpu.roll(middle, stride, 0), left),
            jnp.where(upper, pltpu.roll(right, stride, 0), middle),
        )
    return left, right


def march_values(left, right, t_ref, s_ref, inv_ref, scale, r_ref, store):
    value = left
    change = t_ref[0] * (right - left) - t_ref[1] * left - s_ref[0]
    for k in range(STEPS):
        inverse = full(inv_ref, k)
        value = value + change
        change = change + (scale * (inverse * inverse) * value - full(r_ref, k))
        store(k, value * inverse)


def solve_x_kernel(inv_ref, r_ref, t_ref, w_ref, s_ref, *refs, scale):
    parts, (out, natural, sems) = refs[:-3], refs[-3:]
    tiles = out.shape[1] // LANES
    ends = []
    for row in line_ends("gx", parts):
        ends.append(
            jnp.concatenate([jnp.broadcast_to(row[:, tile_span(t)], (SUB, LANES)) for t in range(tiles)])
        )
    left, right = segment_ends(*ends, w_ref, s_ref, log2(SUB))

    def store(k, speed):
        for tile in range(tiles):
            natural[spread_rows(tile, k), :] = speed[tile * SUB : (tile + 1) * SUB, :]

    march_values(left, right, t_ref, s_ref, inv_ref, scale, r_ref, store)
    writes = [tile_write(natural, out, tile, sems) for tile in range(tiles)]
    for write in writes:
        write.start()
    for write in writes:
        write.wait()


def solve_y_kernel(inv_ref, r_ref, t_ref, w_ref, s_ref, *refs, scale):
    parts, (out, natural, sems, turned) = refs[:-4], refs[-4:]
    tiles = out.shape[1] // LANES
    ends = line_ends("gy", parts)
    ends = [jnp.broadcast_to(row, (tiles * SUB, LANES)) for row in ends]
    left, right = segment_ends(*ends, w_ref, s_ref, log2(tiles * SUB))

    def store(k, speed):
        for tile in range(tiles):
            turned[spread_rows(tile, k), :] = speed[tile * SUB : (tile + 1) * SUB, :]

    march_values(left, right, t_ref, s_ref, inv_ref, scale, r_ref, store)
    writes = []
    for tile in range(tiles):
        block = turned[tile_span(tile), :].T
        for k in range(STEPS):
            natural[spread_rows(tile, k), :] = block[k * SUB : (k + 1) * SUB, :]
        writes.append(tile_write(natural, out, tile, sems))
        writes[-1].start()
    for write in writes:
        write.wait()


def solve(kernel, name, pieces, parts, block, scale, extra=()):
    return pl.pallas_call(
        functools.partial(kernel, scale=scale),
        out_shape=shape(*block),
        in_specs=[VMEM] * (len(pieces) + len(parts)),
        out_specs=ANY,
        scratch_shapes=write_scratch(block[1]) + list(extra),
        compiler_params=PARAMS,
        cost_estimate=pl.CostEstimate(flops=1_000_000, bytes_accessed=4_000_000, transcendentals=0),
        name=name,
    )(*pieces, *parts)


def hand_on(value, axis):
    count = lax.axis_size(axis)
    far = [i + 2 if i % 2 == 0 else i - 2 for i in range(count)]
    return lax.ppermute(value, axis, [(i, t if 0 <= t < count else i ^ 1) for i, t in enumerate(far)])


def cross(value, axis, mask):
    return lax.ppermute(value, axis, [(i, i ^ mask) for i in range(lax.axis_size(axis))])


def parts_of_line(axis, mine, relay, beside=(), tall=None):
    parts = []
    last = log2(lax.axis_size(axis)) - 2
    for stage in range(last):
        theirs = cross(mine, axis, 1 << stage)
        parts += [mine, theirs]
        mine = merge_call(axis, stage, mine, theirs, beside)
    if relay:
        first = cross(mine, axis, 1 << last)
        second = cross(mine if tall is None else tall, axis, 2 << last)
        both = cross(second[0:SUB], axis, 1 << last)
    else:
        first, second, both = (cross(mine, axis, n << last) for n in (1, 2, 3))
    return parts + [mine, first, second, both]


def on_device(h, p, q, b, m):
    block = h.shape
    rows, cols = block
    inv_cx = 3.0 / (rows * lax.axis_size("gx") / 4.0) ** 2
    inv_cy = 3.0 / (cols * lax.axis_size("gy") / 4.0) ** 2
    xa, ya, hs, ps, qs, bs, ms = pack(h, p, q, b, m)
    near_x, near_y = cross(xa, "gx", 1), cross(ya, "gy", 1)
    far_y = hand_on(jnp.pad(near_y[1], ((0, 5 * SUB), (0, 0))), "gy")
    hx, hy, ix, iy, tx, wx, ty, wy, coef_x, coef_y = prepare_depth(hs, inv_cx, inv_cy)
    far_x = hand_on(second_of(near_x, coef_x), "gx")
    px, py, qx, qy, bx, by, mx, my = prepare_rest(ps, qs, bs, ms)
    mass_y, shear_y, normal_y = fluxes_y(near_y, far_y, hy, py, qy, by, my)
    depth, rx, ry, sx, sy, end_x, end_y, tall_y = fluxes_x(
        near_x, far_x, hx, px, qx, bx, mx, ix, iy, my, mass_y, shear_y, normal_y,
        tx, wx, ty, wy, coef_x, coef_y, inv_cx=inv_cx, inv_cy=inv_cy,
    )
    new_depth = write_depth(depth, block)
    parts_y = parts_of_line("gy", end_y, True, tall=tall_y if lax.axis_size("gy") == 4 else None)
    parts_x = parts_of_line("gx", end_x, False, parts_y[1:2])
    turned = [pltpu.VMEM((cols, LANES), F32)]
    vy = solve(solve_y_kernel, "solve_y", (iy, ry, ty, wy, sy), parts_y, block, inv_cy, turned)
    vx = solve(solve_x_kernel, "solve_x", (ix, rx, tx, wx, sx), parts_x, block, inv_cx)
    return new_depth, vx, vy


def solution(mesh):
    spec = P("gx", "gy")
    return jax.shard_map(
        on_device,
        mesh=mesh,
        in_specs=(spec,) * 5,
        out_specs=(spec,) * 3,
        check_vma=False,
    )
```

```python
import functools

import jax
import jax.numpy as jnp
from jax import lax
from jax.experimental import pallas as pl
from jax.experimental.pallas import tpu as pltpu
from jax.sharding import PartitionSpec as P

gravity = 9.81
ratio = 0.05
LANES = 128
SUB = 8
STEPS = LANES // SUB
F32 = jnp.float32
VMEM = pl.BlockSpec(memory_space=pltpu.VMEM)
HBM = pl.BlockSpec(memory_space=pltpu.HBM)
ANY = pl.BlockSpec(memory_space=pl.ANY)
PARAMS = pltpu.CompilerParams(vmem_limit_bytes=16 * 1024 * 1024)


def lane_index(shape):
    return lax.broadcasted_iota(jnp.int32, shape, len(shape) - 1)


def row_index(shape):
    return lax.broadcasted_iota(jnp.int32, shape, len(shape) - 2)


def at(tile, step):
    first = tile * LANES + step * SUB
    return slice(first, first + SUB)


def tile_span(tile):
    return slice(tile * LANES, (tile + 1) * LANES)


def spread_rows(tile, step):
    return pl.ds(tile * LANES + step, SUB, stride=STEPS)


def shape(*dims):
    return jax.ShapeDtypeStruct(dims, F32)


def pack_kernel(h, p, q, b, m, xa, ya, hs, ps, qs, bs, ms, top, bottom, itop, ibottom, sems_x, sems):
    rows, cols = h.shape
    tiles = cols // LANES
    sources = (h, p, q, b, m)
    stacks = (hs, ps, qs, bs, ms)
    edges = []
    for f, src in enumerate(sources):
        for side, (target, whole, row) in enumerate(((top, itop, 0), (bottom, ibottom, rows - SUB))):
            copy = pltpu.make_async_copy(
                src.at[pl.ds(row, SUB), :], target.at[f] if f < 4 else whole, sems_x.at[2 * f + side]
            )
            copy.start()
            edges.append(copy)
    loads = {}
    for tile in [0, tiles - 1] + list(range(1, tiles - 1)):
        for f, (src, target) in enumerate(zip(sources, stacks)):
            copy = pltpu.make_async_copy(
                src.at[:, pl.ds(tile * LANES, LANES)],
                target.at[pl.ds(tile * rows, rows), :],
                sems.at[f * tiles + tile],
            )
            copy.start()
            loads[tile, f] = copy
    for copy in edges:
        copy.wait()
    first_x = jnp.concatenate(
        [top[0, 0:2, :], top[1, 0:2, :], top[2, 0:2, :], top[3, 0:1, :], itop[0:1, :].astype(F32)]
    )
    last_x = jnp.concatenate(
        [
            bottom[0, SUB - 2 : SUB, :],
            bottom[1, SUB - 2 : SUB, :],
            bottom[2, SUB - 2 : SUB, :],
            bottom[3, SUB - 1 : SUB, :],
            ibottom[SUB - 1 : SUB, :].astype(F32),
        ]
    )
    even_x = lax.axis_index("gx") % 2 == 0
    xa[0] = jnp.where(even_x, last_x, first_x)
    xa[1] = jnp.where(even_x, first_x, last_x)
    lane = lane_index((rows, LANES))
    out = jnp.zeros((rows, LANES), F32)
    for tile, start, shifts in ((0, 0, (0, 2, 4, 6, 7)), (tiles - 1, SUB, (10, 12, 14, 15, 16))):
        for f, (ref, to, shift) in enumerate(zip(stacks, (0, 2, 4, 6, 7), shifts)):
            loads[tile, f].wait()
            value = jnp.concatenate([ref[spread_rows(tile, k), :] for k in range(STEPS)]).astype(F32)
            out = jnp.where(lane >= start + to, pltpu.roll(value, shift, 1) if shift else value, out)
    turned = out.T
    first_y, last_y = turned[0:SUB, :], turned[SUB : 2 * SUB, :]
    even_y = lax.axis_index("gy") % 2 == 0
    ya[0] = jnp.where(even_y, last_y, first_y)
    ya[1] = jnp.where(even_y, first_y, last_y)
    for tile in range(1, tiles - 1):
        for f in range(len(sources)):
            loads[tile, f].wait()


def pack(*fields):
    rows, cols = fields[0].shape
    tiles = cols // LANES
    stacks = [jax.ShapeDtypeStruct((tiles * rows, LANES), v.dtype) for v in fields]
    return pl.pallas_call(
        pack_kernel,
        out_shape=(shape(2, SUB, cols), shape(2, SUB, rows), *stacks),
        in_specs=[HBM] * 5,
        out_specs=(VMEM,) * 7,
        scratch_shapes=[
            pltpu.VMEM((4, SUB, cols), F32),
            pltpu.VMEM((4, SUB, cols), F32),
            pltpu.VMEM((SUB, cols), jnp.int32),
            pltpu.VMEM((SUB, cols), jnp.int32),
            pltpu.SemaphoreType.DMA((10,)),
            pltpu.SemaphoreType.DMA((5 * tiles,)),
        ],
        compiler_params=PARAMS,
        name="pack",
    )(*[pltpu.with_memory_space_constraint(v, pltpu.HBM) for v in fields])


def tie_kernel(both, _, out):
    out[...] = both[1]


def second_of(both, after):
    return pl.pallas_call(
        tie_kernel,
        out_shape=shape(*both.shape[1:]),
        in_specs=[VMEM, VMEM],
        out_specs=VMEM,
        compiler_params=PARAMS,
        name="second_of",
    )(both, after)


def merge_coefficients(one, two):
    t1, gl1, gr1 = one
    t2, gl2, gr2 = two
    shunt = gr1 + gl2
    inverse = 1.0 / (t1 + t2 + shunt)
    w1, w2 = t1 * inverse, t2 * inverse
    return (w1 * t2, gl1 + w1 * shunt, gr2 + w2 * shunt), (w1, w2, inverse)


def merge_sources(one, two, weights):
    w1, w2, inverse = weights
    source = one[1] - two[0]
    return (one[0] - w1 * source, two[1] + w2 * source), source * inverse


def merge(one, two):
    coefficients, weights = merge_coefficients(one[:3], two[:3])
    sources, middle = merge_sources(one[3:], two[3:], weights)
    return coefficients + sources, weights[:2] + (middle,)


def log2(count):
    return (count - 1).bit_length()


def full(ref, step):
    return jnp.concatenate([ref[at(tile, step), :] for tile in range(ref.shape[0] // LANES)])


def march_depth(inv_ref, scale, out_t, out_w, levels):
    count = inv_ref.shape[0] // STEPS
    zero = jnp.zeros((count, LANES), F32)
    alpha, gamma, beta, delta = zero, zero, zero, zero
    for k in range(STEPS):
        inverse = full(inv_ref, k)
        d = scale * (inverse * inverse)
        alpha = alpha + gamma
        gamma = gamma + d * (1.0 + alpha)
        beta = beta + delta
        delta = delta + d * ((k + 1.0) + beta)
    t = 1.0 / (STEPS + beta)
    out_t[0] = t
    out_t[1] = t * alpha
    out_t[2] = 1.0 + delta
    coefficients = (t, t * alpha, t * delta)
    for level in range(levels):
        after = tuple(pltpu.roll(v, count - (1 << level), 0) for v in coefficients)
        coefficients, weights = merge_coefficients(coefficients, after)
        for j, v in enumerate(weights):
            out_w[3 * level + j] = v
    return coefficients


def lay_out(src, xs, ys, turned):
    for tile in range(src.shape[0] // LANES):
        for k in range(STEPS):
            xs[at(tile, k), :] = src[spread_rows(tile, k), :].astype(F32)
        turned[tile_span(tile), :] = xs[tile_span(tile), :].T
        for k in range(STEPS):
            ys[at(tile, k), :] = turned[spread_rows(tile, k), :]


def prepare_depth_kernel(hs, hx, hy, ix, iy, tx, wx, ty, wy, endx, endy, turned, *, inv_cx, inv_cy):
    tiles = hs.shape[0] // LANES
    lay_out(hs, hx, hy, turned)
    ix[...] = 1.0 / hx[...]
    iy[...] = 1.0 / hy[...]
    ends_x = march_depth(ix, inv_cx, tx, wx, log2(SUB))
    ends_y = march_depth(iy, inv_cy, ty, wy, log2(SUB * tiles))
    for i in range(3):
        for tile in range(tiles):
            endx[i : i + 1, tile_span(tile)] = ends_x[i][tile * SUB : tile * SUB + 1, :]
        endy[i : i + 1, :] = ends_y[i][0:1, :]
    endx[3:8, :] = jnp.zeros((5, endx.shape[1]), F32)
    endy[3:8, :] = jnp.zeros((5, endy.shape[1]), F32)


def prepare_depth(hs, inv_cx, inv_cy):
    stack = hs.shape
    count = stack[0] // STEPS
    shapes = [shape(*stack)] * 4 + [
        shape(3, count, LANES),
        shape(3 * log2(SUB), count, LANES),
        shape(3, count, LANES),
        shape(3 * log2(count), count, LANES),
        shape(SUB, stack[0]),
        shape(SUB, LANES),
    ]
    return pl.pallas_call(
        functools.partial(prepare_depth_kernel, inv_cx=inv_cx, inv_cy=inv_cy),
        out_shape=tuple(shapes),
        in_specs=[VMEM],
        out_specs=(VMEM,) * len(shapes),
        scratch_shapes=[pltpu.VMEM(stack, F32)],
        compiler_params=PARAMS,
        cost_estimate=pl.CostEstimate(flops=2_000_000, bytes_accessed=4_000_000, transcendentals=0),
        name="prepare_depth",
    )(hs)


def prepare_rest_kernel(*refs):
    sources, outs, turned = refs[:4], refs[4:12], refs[12]
    for f, src in enumerate(sources):
        lay_out(src, outs[2 * f], outs[2 * f + 1], turned.at[f % 2])


def prepare_rest(*sources):
    stack = sources[0].shape
    return pl.pallas_call(
        prepare_rest_kernel,
        out_shape=(shape(*stack),) * 8,
        in_specs=[VMEM] * 4,
        out_specs=(VMEM,) * 8,
        scratch_shapes=[pltpu.VMEM((2, *stack), F32)],
        compiler_params=PARAMS,
        cost_estimate=pl.CostEstimate(flops=2_000_000, bytes_accessed=6_000_000, transcendentals=0),
        name="prepare_rest",
    )(*sources)


def low_high(axis, near, far):
    index, count = lax.axis_index(axis), lax.axis_size(axis)
    even = index % 2 == 0
    low = jnp.where(index > 0, jnp.where(even, far, near), 0.0)
    high = jnp.where(index < count - 1, jnp.where(even, near, far), 0.0)
    return low, high


def half_slope(a, c):
    return 0.5 * (jnp.maximum(jnp.minimum(a, c), 0.0) + jnp.minimum(jnp.maximum(a, c), 0.0))


def face_flux(left, right, opened):
    is_open = opened > 0.5
    hl = jnp.where(is_open, left[0], 1.0)
    hr = jnp.where(is_open, right[0], 1.0)
    joint = 1.0 / (hl * hr)
    ul = left[1] * (hr * joint)
    ur = right[1] * (hl * joint)
    gl = gravity * hl
    gr = gravity * hr
    fastest = jnp.maximum(jnp.abs(ul) + gl * lax.rsqrt(gl), jnp.abs(ur) + gr * lax.rsqrt(gr))
    scale = (0.5 * ratio) * opened
    mass = (left[1] + right[1]) - fastest * (right[0] - left[0])
    push = 0.5 * (gl * hl + gr * hr) + left[1] * ul + right[1] * ur - fastest * (right[1] - left[1])
    shear = left[2] * ul + right[2] * ur - fastest * (right[2] - left[2])
    return scale * mass, scale * push, scale * shear


def extended(ref, tile, lows, highs):
    sub = row_index((SUB, LANES))
    out = {}
    for n, row in enumerate(lows, 1):
        value = ref[at(tile, STEPS - n), :]
        out[-n] = jnp.where(sub == 0, row, pltpu.roll(value, 1, 0))
    for n, row in enumerate(highs):
        value = ref[at(tile, n), :]
        out[STEPS + n] = jnp.where(sub == SUB - 1, row, pltpu.roll(value, SUB - 1, 0))
    return lambda k: out[k] if k in out else ref[at(tile, k), :]


def tile_fluxes(fields, bed, wet, store):
    def states(k):
        both = []
        for w in fields:
            here = w(k)
            both.append((here, half_slope(here - w(k - 1), w(k + 1) - here)))
        return [w + s for w, s in both], [w - s for w, s in both]

    left, _ = states(-1)
    before = None
    for k in range(-1, STEPS):
        left_next, right = states(k + 1)
        face = face_flux(left, right, wet(k) * wet(k + 1))
        left = left_next
        if k >= 0:
            store(k, [a - c for a, c in zip(face, before)], bed(k + 1) - bed(k - 1))
        before = face


def march_source(inv_ref, scale, r_ref, t_ref, w_ref, s_ref, levels):
    count = inv_ref.shape[0] // STEPS
    c = jnp.zeros((count, LANES), F32)
    e = c
    for k in range(STEPS):
        inverse = full(inv_ref, k)
        c = c + e
        e = e + (scale * (inverse * inverse) * c - full(r_ref, k))
    sl = t_ref[0] * c
    s_ref[0] = sl
    sources = (sl, t_ref[2] * sl - e)
    for level in range(levels):
        after = tuple(pltpu.roll(v, count - (1 << level), 0) for v in sources)
        sources, middle = merge_sources(sources, after, tuple(w_ref[3 * level + j] for j in range(3)))
        s_ref[1 + level] = middle
    return sources


def flux_y_kernel(near, far, hy, py, qy, by, my, mass, shear, normal, across, along):
    tiles = hy.shape[0] // LANES
    low, high = low_high("gy", near[0], far[0:SUB, :])
    for tile in range(tiles):

        def extend(ref, row, layers):
            lows, highs = [], []
            for n in range(layers):
                last = at(tile - 1, STEPS - 1 - n).stop - 1
                first = at(tile + 1, n).start
                lows.append(low[row + layers - 1 - n : row + layers - n, :] if tile == 0 else ref[last : last + 1, :])
                highs.append(high[row + n : row + n + 1, :] if tile == tiles - 1 else ref[first : first + 1, :])
            return extended(ref, tile, lows, highs)

        def store(k, difference, bed):
            here, natural = at(tile, k), spread_rows(tile, k)
            across[natural, :] = difference[0]
            along[natural, :] = difference[2]
            pull = (0.5 * ratio * gravity) * hy[here, :]
            normal[here, :] = qy[here, :] - difference[1] - pull * bed

        tile_fluxes([extend(hy, 0, 2), extend(qy, 4, 2), extend(py, 2, 2)], extend(by, 6, 1), extend(my, 7, 1), store)
        span = tile_span(tile)
        mass[span, :] = across[span, :].T
        shear[span, :] = along[span, :].T


def fluxes_y(*arrays):
    stack = arrays[2].shape
    return pl.pallas_call(
        flux_y_kernel,
        out_shape=(shape(*stack),) * 3,
        in_specs=[VMEM] * len(arrays),
        out_specs=(VMEM,) * 3,
        scratch_shapes=[pltpu.VMEM(stack, F32)] * 2,
        compiler_params=PARAMS,
        cost_estimate=pl.CostEstimate(flops=4_000_000, bytes_accessed=4_000_000, transcendentals=0),
        name="fluxes_y",
    )(*arrays)


def flux_x_kernel(
    near, far, hx, px, qx, bx, mx, ix, iy, my, mass_y, shear_y, normal_y, tx, wx, ty, wy, coefx, coefy,
    depth, rx, ry, sx, sy, endx, endy, tally,
    across, turned,
    *, inv_cx, inv_cy,
):
    tiles = hx.shape[0] // LANES
    low, high = low_high("gx", near[0], far[...])
    for tile in range(tiles):
        span = tile_span(tile)

        def extend(ref, row, layers):
            lows = [low[row + layers - 1 - n : row + layers - n, span] for n in range(layers)]
            highs = [high[row + n : row + n + 1, span] for n in range(layers)]
            return extended(ref, tile, lows, highs)

        def store(k, difference, bed):
            here = at(tile, k)
            h, m, inverse = hx[here, :], mx[here, :], ix[here, :]
            depth[here, :] = h - m * (difference[0] + mass_y[here, :])
            push = px[here, :] - difference[1] - shear_y[here, :] - (0.5 * ratio * gravity) * h * bed
            rx[here, :] = (inv_cx * (inverse * inverse)) * m * push
            across[here, :] = difference[2]

        tile_fluxes([extend(hx, 0, 2), extend(px, 2, 2), extend(qx, 4, 2)], extend(bx, 6, 1), extend(mx, 7, 1), store)
        turned[span, :] = across[span, :].T
        for k in range(STEPS):
            here = at(tile, k)
            inverse = iy[here, :]
            push = normal_y[here, :] - turned[spread_rows(tile, k), :]
            ry[here, :] = (inv_cy * (inverse * inverse)) * my[here, :] * push

    ends_x = march_source(ix, inv_cx, rx, tx, wx, sx, log2(SUB))
    ends_y = march_source(iy, inv_cy, ry, ty, wy, sy, log2(SUB * tiles))
    endx[...] = coefx[...]
    endy[...] = coefy[...]
    for i in range(2):
        for tile in range(tiles):
            endx[3 + i : 4 + i, tile_span(tile)] = ends_x[i][tile * SUB : tile * SUB + 1, :]
        endy[3 + i : 4 + i, :] = ends_y[i][0:1, :]
    tally[...] = jnp.zeros_like(tally)
    tally[0:SUB, :] = endy[...]


def fluxes_x(*arrays, inv_cx, inv_cy):
    stack = arrays[2].shape
    count = stack[0] // STEPS
    shapes = (
        shape(*stack),
        shape(*stack),
        shape(*stack),
        shape(1 + log2(SUB), count, LANES),
        shape(1 + log2(count), count, LANES),
        shape(*arrays[-2].shape),
        shape(*arrays[-1].shape),
        shape(3 * SUB, arrays[-1].shape[1]),
    )
    return pl.pallas_call(
        functools.partial(flux_x_kernel, inv_cx=inv_cx, inv_cy=inv_cy),
        out_shape=shapes,
        in_specs=[VMEM] * len(arrays),
        out_specs=(VMEM,) * len(shapes),
        scratch_shapes=[pltpu.VMEM(stack, F32)] * 2,
        compiler_params=PARAMS,
        name="fluxes_x",
    )(*arrays)


def tile_write(tiled, whole, tile, sems):
    rows = whole.shape[0]
    return pltpu.make_async_copy(
        tiled.at[pl.ds(tile * rows, rows), :], whole.at[:, pl.ds(tile * LANES, LANES)], sems.at[tile]
    )


def write_scratch(cols):
    return [pltpu.VMEM((cols, LANES), F32), pltpu.SemaphoreType.DMA((cols // LANES,))]


def depth_kernel(depth, out, natural, sems):
    writes = []
    for tile in range(depth.shape[0] // LANES):
        for k in range(STEPS):
            natural[spread_rows(tile, k), :] = depth[at(tile, k), :]
        writes.append(tile_write(natural, out, tile, sems))
        writes[-1].start()
    for write in writes:
        write.wait()


def write_depth(depth, block):
    return pl.pallas_call(
        depth_kernel,
        out_shape=shape(*block),
        in_specs=[VMEM],
        out_specs=ANY,
        scratch_shapes=write_scratch(block[1]),
        compiler_params=PARAMS,
        cost_estimate=pl.CostEstimate(flops=100_000, bytes_accessed=2_000_000, transcendentals=0),
        name="write_depth",
    )(depth)


def rows_of(ref):
    return tuple(ref[i : i + 1, :] for i in range(5))


def ordered(axis, stage, mine, theirs):
    is_low = (lax.axis_index(axis) >> stage) % 2 == 0
    one = tuple(jnp.where(is_low, a, b) for a, b in zip(mine, theirs))
    two = tuple(jnp.where(is_low, b, a) for a, b in zip(mine, theirs))
    return is_low, merge(one, two)


def merge_kernel(mine, theirs, *refs, axis, stage):
    out = refs[-1]
    _, (merged, _) = ordered(axis, stage, rows_of(mine), rows_of(theirs))
    for i, v in enumerate(merged):
        out[i : i + 1, :] = v
    out[5:8, :] = jnp.zeros((3, out.shape[1]), F32)


def merge_call(axis, stage, mine, theirs, beside):
    return pl.pallas_call(
        functools.partial(merge_kernel, axis=axis, stage=stage),
        out_shape=shape(*mine.shape),
        in_specs=[VMEM] * (2 + len(beside)),
        out_specs=VMEM,
        compiler_params=PARAMS,
        name="merge",
    )(mine, theirs, *beside)


def line_ends(axis, refs):
    steps = []
    parts = [rows_of(ref) for ref in refs]
    stage = 0
    while len(parts) > 4:
        is_low, (_, weights) = ordered(axis, stage, *parts[:2])
        steps.append((is_low, weights))
        parts = parts[2:]
        stage += 1
    is_low, (own, weights) = ordered(axis, stage, *parts[:2])
    steps.append((is_low, weights))
    _, (other, _) = ordered(axis, stage, *parts[2:])
    is_low, (whole, weights) = ordered(axis, stage + 1, own, other)
    steps.append((is_low, weights))
    t, _, gr, _, sr = whole
    left = jnp.zeros_like(t)
    right = sr / (t + gr + 1.0)
    for is_low, (w1, w2, source) in reversed(steps):
        middle = w1 * left + w2 * right + source
        left = jnp.where(is_low, left, middle)
        right = jnp.where(is_low, middle, right)
    return left, right


def segment_ends(left, right, w_ref, s_ref, levels):
    index = row_index(left.shape)
    for level in reversed(range(levels)):
        stride = 1 << level
        middle = w_ref[3 * level] * left + w_ref[3 * level + 1] * right + s_ref[1 + level]
        upper = (index >> level) % 2 == 1
        left, right = (
            jnp.where(upper, pltpu.roll(middle, stride, 0), left),
            jnp.where(upper, pltpu.roll(right, stride, 0), middle),
        )
    return left, right


def march_values(left, right, t_ref, s_ref, inv_ref, scale, r_ref, store):
    value = left
    change = t_ref[0] * (right - left) - t_ref[1] * left - s_ref[0]
    for k in range(STEPS):
        inverse = full(inv_ref, k)
        value = value + change
        change = change + (scale * (inverse * inverse) * value - full(r_ref, k))
        store(k, value * inverse)


def solve_x_kernel(inv_ref, r_ref, t_ref, w_ref, s_ref, *refs, scale):
    parts, (out, natural, sems) = refs[:-3], refs[-3:]
    tiles = out.shape[1] // LANES
    ends = []
    for row in line_ends("gx", parts[:-3] + parts[:-4:-1]):
        ends.append(
            jnp.concatenate([jnp.broadcast_to(row[:, tile_span(t)], (SUB, LANES)) for t in range(tiles)])
        )
    left, right = segment_ends(*ends, w_ref, s_ref, log2(SUB))

    def store(k, speed):
        for tile in range(tiles):
            natural[spread_rows(tile, k), :] = speed[tile * SUB : (tile + 1) * SUB, :]

    march_values(left, right, t_ref, s_ref, inv_ref, scale, r_ref, store)
    writes = [tile_write(natural, out, tile, sems) for tile in range(tiles)]
    for write in writes:
        write.start()
    for write in writes:
        write.wait()


def solve_y_kernel(inv_ref, r_ref, t_ref, w_ref, s_ref, *refs, scale):
    parts, (out, natural, sems, turned) = refs[:-4], refs[-4:]
    tiles = out.shape[1] // LANES
    ends = line_ends("gy", parts)
    ends = [jnp.broadcast_to(row, (tiles * SUB, LANES)) for row in ends]
    left, right = segment_ends(*ends, w_ref, s_ref, log2(tiles * SUB))

    def store(k, speed):
        for tile in range(tiles):
            turned[spread_rows(tile, k), :] = speed[tile * SUB : (tile + 1) * SUB, :]

    march_values(left, right, t_ref, s_ref, inv_ref, scale, r_ref, store)
    writes = []
    for tile in range(tiles):
        block = turned[tile_span(tile), :].T
        for k in range(STEPS):
            natural[spread_rows(tile, k), :] = block[k * SUB : (k + 1) * SUB, :]
        writes.append(tile_write(natural, out, tile, sems))
        writes[-1].start()
    for write in writes:
        write.wait()


def solve(kernel, name, pieces, parts, block, scale, extra=()):
    return pl.pallas_call(
        functools.partial(kernel, scale=scale),
        out_shape=shape(*block),
        in_specs=[VMEM] * (len(pieces) + len(parts)),
        out_specs=ANY,
        scratch_shapes=write_scratch(block[1]) + list(extra),
        compiler_params=PARAMS,
        cost_estimate=pl.CostEstimate(flops=1_000_000, bytes_accessed=4_000_000, transcendentals=0),
        name=name,
    )(*pieces, *parts)


def hand_on(value, axis):
    count = lax.axis_size(axis)
    far = [i + 2 if i % 2 == 0 else i - 2 for i in range(count)]
    return lax.ppermute(value, axis, [(i, t if 0 <= t < count else i ^ 1) for i, t in enumerate(far)])


def cross(value, axis, mask):
    return lax.ppermute(value, axis, [(i, i ^ mask) for i in range(lax.axis_size(axis))])


def parts_of_line(axis, mine, relay, beside=(), tall=None):
    parts = []
    last = log2(lax.axis_size(axis)) - 2
    for stage in range(last):
        theirs = cross(mine, axis, 1 << stage)
        parts += [mine, theirs]
        mine = merge_call(axis, stage, mine, theirs, beside)
    if relay:
        first = cross(mine, axis, 1 << last)
        second = cross(mine if tall is None else tall, axis, 2 << last)
        both = cross(second[0:SUB], axis, 1 << last)
    else:
        first, second, both = (cross(mine, axis, n << last) for n in (1, 2, 3))
    return parts + [mine] + ([first, second, both] if relay else [both, second, first])


def on_device(h, p, q, b, m):
    block = h.shape
    rows, cols = block
    inv_cx = 3.0 / (rows * lax.axis_size("gx") / 4.0) ** 2
    inv_cy = 3.0 / (cols * lax.axis_size("gy") / 4.0) ** 2
    xa, ya, hs, ps, qs, bs, ms = pack(h, p, q, b, m)
    near_x, near_y = cross(xa, "gx", 1), cross(ya, "gy", 1)
    far_y = hand_on(jnp.pad(near_y[1], ((0, 5 * SUB), (0, 0))), "gy")
    hx, hy, ix, iy, tx, wx, ty, wy, coef_x, coef_y = prepare_depth(hs, inv_cx, inv_cy)
    far_x = hand_on(second_of(near_x, coef_x), "gx")
    px, py, qx, qy, bx, by, mx, my = prepare_rest(ps, qs, bs, ms)
    mass_y, shear_y, normal_y = fluxes_y(near_y, far_y, hy, py, qy, by, my)
    depth, rx, ry, sx, sy, end_x, end_y, tall_y = fluxes_x(
        near_x, far_x, hx, px, qx, bx, mx, ix, iy, my, mass_y, shear_y, normal_y,
        tx, wx, ty, wy, coef_x, coef_y, inv_cx=inv_cx, inv_cy=inv_cy,
    )
    new_depth = write_depth(depth, block)
    parts_y = parts_of_line("gy", end_y, True, tall=tall_y if lax.axis_size("gy") == 4 else None)
    parts_x = parts_of_line("gx", end_x, False, parts_y[1:2])
    turned = [pltpu.VMEM((cols, LANES), F32)]
    vy = solve(solve_y_kernel, "solve_y", (iy, ry, ty, wy, sy), parts_y, block, inv_cy, turned)
    vx = solve(solve_x_kernel, "solve_x", (ix, rx, tx, wx, sx), parts_x, block, inv_cx)
    return new_depth, vx, vy


def solution(mesh):
    spec = P("gx", "gy")
    return jax.shard_map(
        on_device,
        mesh=mesh,
        in_specs=(spec,) * 5,
        out_specs=(spec,) * 3,
        check_vma=False,
    )
```

```python
import functools

import jax
import jax.numpy as jnp
from jax import lax
from jax.experimental import pallas as pl
from jax.experimental.pallas import tpu as pltpu
from jax.sharding import PartitionSpec as P

gravity = 9.81
ratio = 0.05
LANES = 128
SUB = 8
STEPS = LANES // SUB
F32 = jnp.float32
VMEM = pl.BlockSpec(memory_space=pltpu.VMEM)
HBM = pl.BlockSpec(memory_space=pltpu.HBM)
ANY = pl.BlockSpec(memory_space=pl.ANY)
PARAMS = pltpu.CompilerParams(vmem_limit_bytes=16 * 1024 * 1024)


def lane_index(shape):
    return lax.broadcasted_iota(jnp.int32, shape, len(shape) - 1)


def row_index(shape):
    return lax.broadcasted_iota(jnp.int32, shape, len(shape) - 2)


def at(tile, step):
    first = tile * LANES + step * SUB
    return slice(first, first + SUB)


def tile_span(tile):
    return slice(tile * LANES, (tile + 1) * LANES)


def spread_rows(tile, step):
    return pl.ds(tile * LANES + step, SUB, stride=STEPS)


def shape(*dims):
    return jax.ShapeDtypeStruct(dims, F32)


def pack_kernel(h, p, q, b, m, xa, ya, hs, ps, qs, bs, ms, top, bottom, itop, ibottom, sems_x, sems):
    rows, cols = h.shape
    tiles = cols // LANES
    sources = (h, p, q, b, m)
    stacks = (hs, ps, qs, bs, ms)
    edges = []
    for f, src in enumerate(sources):
        for side, (target, whole, row) in enumerate(((top, itop, 0), (bottom, ibottom, rows - SUB))):
            copy = pltpu.make_async_copy(
                src.at[pl.ds(row, SUB), :], target.at[f] if f < 4 else whole, sems_x.at[2 * f + side]
            )
            copy.start()
            edges.append(copy)
    loads = {}
    for place, tile in enumerate((0, tiles - 1)):
        for f, (src, target) in enumerate(zip(sources, stacks)):
            copy = pltpu.make_async_copy(
                src.at[:, pl.ds(tile * LANES, LANES)], target.at[pl.ds(place * rows, rows), :], sems.at[2 * f + place]
            )
            copy.start()
            loads[place, f] = copy
    for copy in edges:
        copy.wait()
    first_x = jnp.concatenate(
        [top[0, 0:2, :], top[1, 0:2, :], top[2, 0:2, :], top[3, 0:1, :], itop[0:1, :].astype(F32)]
    )
    last_x = jnp.concatenate(
        [
            bottom[0, SUB - 2 : SUB, :],
            bottom[1, SUB - 2 : SUB, :],
            bottom[2, SUB - 2 : SUB, :],
            bottom[3, SUB - 1 : SUB, :],
            ibottom[SUB - 1 : SUB, :].astype(F32),
        ]
    )
    even_x = lax.axis_index("gx") % 2 == 0
    xa[0] = jnp.where(even_x, last_x, first_x)
    xa[1] = jnp.where(even_x, first_x, last_x)
    lane = lane_index((rows, LANES))
    out = jnp.zeros((rows, LANES), F32)
    for place, start, shifts in ((0, 0, (0, 2, 4, 6, 7)), (1, SUB, (10, 12, 14, 15, 16))):
        for f, (ref, to, shift) in enumerate(zip(stacks, (0, 2, 4, 6, 7), shifts)):
            loads[place, f].wait()
            value = jnp.concatenate([ref[spread_rows(place, k), :] for k in range(STEPS)]).astype(F32)
            out = jnp.where(lane >= start + to, pltpu.roll(value, shift, 1) if shift else value, out)
    turned = out.T
    first_y, last_y = turned[0:SUB, :], turned[SUB : 2 * SUB, :]
    even_y = lax.axis_index("gy") % 2 == 0
    ya[0] = jnp.where(even_y, last_y, first_y)
    ya[1] = jnp.where(even_y, first_y, last_y)


def pack(*fields):
    rows, cols = fields[0].shape
    stacks = [jax.ShapeDtypeStruct((2 * rows, LANES), v.dtype) for v in fields]
    return pl.pallas_call(
        pack_kernel,
        out_shape=(shape(2, SUB, cols), shape(2, SUB, rows), *stacks),
        in_specs=[HBM] * 5,
        out_specs=(VMEM,) * 7,
        scratch_shapes=[
            pltpu.VMEM((4, SUB, cols), F32),
            pltpu.VMEM((4, SUB, cols), F32),
            pltpu.VMEM((SUB, cols), jnp.int32),
            pltpu.VMEM((SUB, cols), jnp.int32),
            pltpu.SemaphoreType.DMA((10,)),
            pltpu.SemaphoreType.DMA((10,)),
        ],
        compiler_params=PARAMS,
        name="pack",
    )(*[pltpu.with_memory_space_constraint(v, pltpu.HBM) for v in fields])


def load_kernel(*refs):
    sources, targets, sems = refs[:5], refs[5:10], refs[10]
    rows, cols = sources[0].shape
    copies = []
    for f, (src, target) in enumerate(zip(sources, targets)):
        for tile in range(1, cols // LANES - 1):
            copies.append(
                pltpu.make_async_copy(
                    src.at[:, pl.ds(tile * LANES, LANES)],
                    target.at[pl.ds((tile - 1) * rows, rows), :],
                    sems.at[f * (cols // LANES) + tile],
                )
            )
            copies[-1].start()
    for copy in copies:
        copy.wait()


def load_middle(*fields):
    rows, cols = fields[0].shape
    tiles = cols // LANES
    return pl.pallas_call(
        load_kernel,
        out_shape=tuple(jax.ShapeDtypeStruct(((tiles - 2) * rows, LANES), v.dtype) for v in fields),
        in_specs=[HBM] * 5,
        out_specs=(VMEM,) * 5,
        scratch_shapes=[pltpu.SemaphoreType.DMA((5 * tiles,))],
        compiler_params=PARAMS,
        cost_estimate=pl.CostEstimate(flops=0, bytes_accessed=1_300_000, transcendentals=0),
        name="load_middle",
    )(*[pltpu.with_memory_space_constraint(v, pltpu.HBM) for v in fields])


def tie_kernel(both, _, out):
    out[...] = both[1]


def second_of(both, after):
    return pl.pallas_call(
        tie_kernel,
        out_shape=shape(*both.shape[1:]),
        in_specs=[VMEM, VMEM],
        out_specs=VMEM,
        compiler_params=PARAMS,
        name="second_of",
    )(both, after)


def merge_coefficients(one, two):
    t1, gl1, gr1 = one
    t2, gl2, gr2 = two
    shunt = gr1 + gl2
    inverse = 1.0 / (t1 + t2 + shunt)
    w1, w2 = t1 * inverse, t2 * inverse
    return (w1 * t2, gl1 + w1 * shunt, gr2 + w2 * shunt), (w1, w2, inverse)


def merge_sources(one, two, weights):
    w1, w2, inverse = weights
    source = one[1] - two[0]
    return (one[0] - w1 * source, two[1] + w2 * source), source * inverse


def merge(one, two):
    coefficients, weights = merge_coefficients(one[:3], two[:3])
    sources, middle = merge_sources(one[3:], two[3:], weights)
    return coefficients + sources, weights[:2] + (middle,)


def log2(count):
    return (count - 1).bit_length()


def full(ref, step):
    return jnp.concatenate([ref[at(tile, step), :] for tile in range(ref.shape[0] // LANES)])


def march_depth(inv_ref, scale, out_t, out_w, levels):
    count = inv_ref.shape[0] // STEPS
    zero = jnp.zeros((count, LANES), F32)
    alpha, gamma, beta, delta = zero, zero, zero, zero
    for k in range(STEPS):
        inverse = full(inv_ref, k)
        d = scale * (inverse * inverse)
        alpha = alpha + gamma
        gamma = gamma + d * (1.0 + alpha)
        beta = beta + delta
        delta = delta + d * ((k + 1.0) + beta)
    t = 1.0 / (STEPS + beta)
    out_t[0] = t
    out_t[1] = t * alpha
    out_t[2] = 1.0 + delta
    coefficients = (t, t * alpha, t * delta)
    for level in range(levels):
        after = tuple(pltpu.roll(v, count - (1 << level), 0) for v in coefficients)
        coefficients, weights = merge_coefficients(coefficients, after)
        for j, v in enumerate(weights):
            out_w[3 * level + j] = v
    return coefficients


def lay_out(outer, middle, xs, ys, turned):
    tiles = xs.shape[0] // LANES
    for tile in range(tiles):
        src, place = (middle, tile - 1) if 0 < tile < tiles - 1 else (outer, min(tile, 1))
        for k in range(STEPS):
            xs[at(tile, k), :] = src[spread_rows(place, k), :].astype(F32)
        turned[tile_span(tile), :] = xs[tile_span(tile), :].T
        for k in range(STEPS):
            ys[at(tile, k), :] = turned[spread_rows(tile, k), :]


def prepare_depth_kernel(outer, middle, hx, hy, ix, iy, tx, wx, ty, wy, endx, endy, turned, *, inv_cx, inv_cy):
    tiles = hx.shape[0] // LANES
    lay_out(outer, middle, hx, hy, turned)
    ix[...] = 1.0 / hx[...]
    iy[...] = 1.0 / hy[...]
    ends_x = march_depth(ix, inv_cx, tx, wx, log2(SUB))
    ends_y = march_depth(iy, inv_cy, ty, wy, log2(SUB * tiles))
    for i in range(3):
        for tile in range(tiles):
            endx[i : i + 1, tile_span(tile)] = ends_x[i][tile * SUB : tile * SUB + 1, :]
        endy[i : i + 1, :] = ends_y[i][0:1, :]
    endx[3:8, :] = jnp.zeros((5, endx.shape[1]), F32)
    endy[3:8, :] = jnp.zeros((5, endy.shape[1]), F32)


def prepare_depth(outer, middle, inv_cx, inv_cy):
    stack = (outer.shape[0] + middle.shape[0], LANES)
    count = stack[0] // STEPS
    shapes = [shape(*stack)] * 4 + [
        shape(3, count, LANES),
        shape(3 * log2(SUB), count, LANES),
        shape(3, count, LANES),
        shape(3 * log2(count), count, LANES),
        shape(SUB, stack[0]),
        shape(SUB, LANES),
    ]
    return pl.pallas_call(
        functools.partial(prepare_depth_kernel, inv_cx=inv_cx, inv_cy=inv_cy),
        out_shape=tuple(shapes),
        in_specs=[VMEM] * 2,
        out_specs=(VMEM,) * len(shapes),
        scratch_shapes=[pltpu.VMEM(stack, F32)],
        compiler_params=PARAMS,
        cost_estimate=pl.CostEstimate(flops=2_000_000, bytes_accessed=4_000_000, transcendentals=0),
        name="prepare_depth",
    )(outer, middle)


def prepare_rest_kernel(*refs):
    outer, middle, outs, turned = refs[:4], refs[4:8], refs[8:16], refs[16]
    for f in range(4):
        lay_out(outer[f], middle[f], outs[2 * f], outs[2 * f + 1], turned.at[f % 2])


def prepare_rest(outer, middle):
    stack = (outer[0].shape[0] + middle[0].shape[0], LANES)
    return pl.pallas_call(
        prepare_rest_kernel,
        out_shape=(shape(*stack),) * 8,
        in_specs=[VMEM] * 8,
        out_specs=(VMEM,) * 8,
        scratch_shapes=[pltpu.VMEM((2, *stack), F32)],
        compiler_params=PARAMS,
        cost_estimate=pl.CostEstimate(flops=2_000_000, bytes_accessed=6_000_000, transcendentals=0),
        name="prepare_rest",
    )(*outer, *middle)


def low_high(axis, near, far):
    index, count = lax.axis_index(axis), lax.axis_size(axis)
    even = index % 2 == 0
    low = jnp.where(index > 0, jnp.where(even, far, near), 0.0)
    high = jnp.where(index < count - 1, jnp.where(even, near, far), 0.0)
    return low, high


def half_slope(a, c):
    return 0.5 * (jnp.maximum(jnp.minimum(a, c), 0.0) + jnp.minimum(jnp.maximum(a, c), 0.0))


def face_flux(left, right, opened):
    is_open = opened > 0.5
    hl = jnp.where(is_open, left[0], 1.0)
    hr = jnp.where(is_open, right[0], 1.0)
    joint = 1.0 / (hl * hr)
    ul = left[1] * (hr * joint)
    ur = right[1] * (hl * joint)
    gl = gravity * hl
    gr = gravity * hr
    fastest = jnp.maximum(jnp.abs(ul) + gl * lax.rsqrt(gl), jnp.abs(ur) + gr * lax.rsqrt(gr))
    scale = (0.5 * ratio) * opened
    mass = (left[1] + right[1]) - fastest * (right[0] - left[0])
    push = 0.5 * (gl * hl + gr * hr) + left[1] * ul + right[1] * ur - fastest * (right[1] - left[1])
    shear = left[2] * ul + right[2] * ur - fastest * (right[2] - left[2])
    return scale * mass, scale * push, scale * shear


def extended(ref, tile, lows, highs):
    sub = row_index((SUB, LANES))
    out = {}
    for n, row in enumerate(lows, 1):
        value = ref[at(tile, STEPS - n), :]
        out[-n] = jnp.where(sub == 0, row, pltpu.roll(value, 1, 0))
    for n, row in enumerate(highs):
        value = ref[at(tile, n), :]
        out[STEPS + n] = jnp.where(sub == SUB - 1, row, pltpu.roll(value, SUB - 1, 0))
    return lambda k: out[k] if k in out else ref[at(tile, k), :]


def tile_fluxes(fields, bed, wet, store, start=0, stop=STEPS):
    def states(k):
        both = []
        for w in fields:
            here = w(k)
            both.append((here, half_slope(here - w(k - 1), w(k + 1) - here)))
        return [w + s for w, s in both], [w - s for w, s in both]

    left, _ = states(start - 1)
    before = None
    for k in range(start - 1, stop):
        left_next, right = states(k + 1)
        face = face_flux(left, right, wet(k) * wet(k + 1))
        left = left_next
        if k >= start:
            store(k, [a - c for a, c in zip(face, before)], bed(k + 1) - bed(k - 1))
        before = face


def march_source(inv_ref, scale, r_ref, t_ref, w_ref, s_ref, levels):
    count = inv_ref.shape[0] // STEPS
    c = jnp.zeros((count, LANES), F32)
    e = c
    for k in range(STEPS):
        inverse = full(inv_ref, k)
        c = c + e
        e = e + (scale * (inverse * inverse) * c - full(r_ref, k))
    sl = t_ref[0] * c
    s_ref[0] = sl
    sources = (sl, t_ref[2] * sl - e)
    for level in range(levels):
        after = tuple(pltpu.roll(v, count - (1 << level), 0) for v in sources)
        sources, middle = merge_sources(sources, after, tuple(w_ref[3 * level + j] for j in range(3)))
        s_ref[1 + level] = middle
    return sources


def flux_y_kernel(near, far, hy, py, qy, by, my, mass, shear, normal, across, along):
    tiles = hy.shape[0] // LANES
    low, high = low_high("gy", near[0], far[0:SUB, :])
    for tile in range(tiles):

        def extend(ref, row, layers):
            lows, highs = [], []
            for n in range(layers):
                last = at(tile - 1, STEPS - 1 - n).stop - 1
                first = at(tile + 1, n).start
                lows.append(low[row + layers - 1 - n : row + layers - n, :] if tile == 0 else ref[last : last + 1, :])
                highs.append(high[row + n : row + n + 1, :] if tile == tiles - 1 else ref[first : first + 1, :])
            return extended(ref, tile, lows, highs)

        def store(k, difference, bed):
            here, natural = at(tile, k), spread_rows(tile, k)
            across[natural, :] = difference[0]
            along[natural, :] = difference[2]
            pull = (0.5 * ratio * gravity) * hy[here, :]
            normal[here, :] = qy[here, :] - difference[1] - pull * bed

        tile_fluxes([extend(hy, 0, 2), extend(qy, 4, 2), extend(py, 2, 2)], extend(by, 6, 1), extend(my, 7, 1), store)
        span = tile_span(tile)
        mass[span, :] = across[span, :].T
        shear[span, :] = along[span, :].T


def fluxes_y(*arrays):
    stack = arrays[2].shape
    return pl.pallas_call(
        flux_y_kernel,
        out_shape=(shape(*stack),) * 3,
        in_specs=[VMEM] * len(arrays),
        out_specs=(VMEM,) * 3,
        scratch_shapes=[pltpu.VMEM(stack, F32)] * 2,
        compiler_params=PARAMS,
        cost_estimate=pl.CostEstimate(flops=4_000_000, bytes_accessed=4_000_000, transcendentals=0),
        name="fluxes_y",
    )(*arrays)


INNER = (2, STEPS - 2)


def x_store(hx, px, mx, ix, mass_y, shear_y, depth, rx, across, inv_cx):
    def of_tile(tile):
        def store(k, difference, bed):
            here = at(tile, k)
            h, m, inverse = hx[here, :], mx[here, :], ix[here, :]
            depth[here, :] = h - m * (difference[0] + mass_y[here, :])
            push = px[here, :] - difference[1] - shear_y[here, :] - (0.5 * ratio * gravity) * h * bed
            rx[here, :] = (inv_cx * (inverse * inverse)) * m * push
            across[here, :] = difference[2]

        return store

    return of_tile


def flux_x_inner_kernel(hx, px, qx, bx, mx, ix, mass_y, shear_y, depth, rx, across, *, inv_cx):
    store = x_store(hx, px, mx, ix, mass_y, shear_y, depth, rx, across, inv_cx)
    for tile in range(hx.shape[0] // LANES):
        fields, bed, wet = ([extended(v, tile, (), ()) for v in (hx, px, qx)], *(extended(v, tile, (), ()) for v in (bx, mx)))
        tile_fluxes(fields, bed, wet, store(tile), *INNER)
        for k in (*range(INNER[0]), *range(INNER[1], STEPS)):
            for ref in (depth, rx, across):
                ref[at(tile, k), :] = jnp.zeros((SUB, LANES), F32)


def fluxes_x_inner(*arrays, inv_cx):
    stack = arrays[0].shape
    return pl.pallas_call(
        functools.partial(flux_x_inner_kernel, inv_cx=inv_cx),
        out_shape=(shape(*stack),) * 3,
        in_specs=[VMEM] * len(arrays),
        out_specs=(VMEM,) * 3,
        compiler_params=PARAMS,
        cost_estimate=pl.CostEstimate(flops=4_000_000, bytes_accessed=4_000_000, transcendentals=0),
        name="fluxes_x_inner",
    )(*arrays)


def flux_x_kernel(
    near, far, hx, px, qx, bx, mx, ix, iy, my, mass_y, shear_y, normal_y, depth_in, rx_in, across_in,
    tx, wx, ty, wy, coefx, coefy,
    depth, rx, ry, sx, sy, endx, endy, tally,
    across, turned,
    *, inv_cx, inv_cy,
):
    tiles = hx.shape[0] // LANES
    low, high = low_high("gx", near[0], far[...])
    store = x_store(hx, px, mx, ix, mass_y, shear_y, depth, rx, across, inv_cx)
    for tile in range(tiles):
        span = tile_span(tile)

        def extend(ref, row, layers):
            lows = [low[row + layers - 1 - n : row + layers - n, span] for n in range(layers)]
            highs = [high[row + n : row + n + 1, span] for n in range(layers)]
            return extended(ref, tile, lows, highs)

        fields, bed, wet = [extend(hx, 0, 2), extend(px, 2, 2), extend(qx, 4, 2)], extend(bx, 6, 1), extend(mx, 7, 1)
        tile_fluxes(fields, bed, wet, store(tile), 0, INNER[0])
        tile_fluxes(fields, bed, wet, store(tile), INNER[1], STEPS)
        inner = slice(at(tile, INNER[0]).start, at(tile, INNER[1]).start)
        for done, ref in ((depth_in, depth), (rx_in, rx), (across_in, across)):
            ref[inner, :] = done[inner, :]
        turned[span, :] = across[span, :].T
        for k in range(STEPS):
            here = at(tile, k)
            inverse = iy[here, :]
            push = normal_y[here, :] - turned[spread_rows(tile, k), :]
            ry[here, :] = (inv_cy * (inverse * inverse)) * my[here, :] * push

    ends_x = march_source(ix, inv_cx, rx, tx, wx, sx, log2(SUB))
    ends_y = march_source(iy, inv_cy, ry, ty, wy, sy, log2(SUB * tiles))
    endx[...] = coefx[...]
    endy[...] = coefy[...]
    for i in range(2):
        for tile in range(tiles):
            endx[3 + i : 4 + i, tile_span(tile)] = ends_x[i][tile * SUB : tile * SUB + 1, :]
        endy[3 + i : 4 + i, :] = ends_y[i][0:1, :]
    tally[...] = jnp.zeros_like(tally)
    tally[0:SUB, :] = endy[...]


def fluxes_x(*arrays, inv_cx, inv_cy):
    stack = arrays[2].shape
    count = stack[0] // STEPS
    shapes = (
        shape(*stack),
        shape(*stack),
        shape(*stack),
        shape(1 + log2(SUB), count, LANES),
        shape(1 + log2(count), count, LANES),
        shape(*arrays[-2].shape),
        shape(*arrays[-1].shape),
        shape(3 * SUB, arrays[-1].shape[1]),
    )
    return pl.pallas_call(
        functools.partial(flux_x_kernel, inv_cx=inv_cx, inv_cy=inv_cy),
        out_shape=shapes,
        in_specs=[VMEM] * len(arrays),
        out_specs=(VMEM,) * len(shapes),
        scratch_shapes=[pltpu.VMEM(stack, F32)] * 2,
        compiler_params=PARAMS,
        name="fluxes_x",
    )(*arrays)


def tile_write(tiled, whole, tile, sems):
    rows = whole.shape[0]
    return pltpu.make_async_copy(
        tiled.at[pl.ds(tile * rows, rows), :], whole.at[:, pl.ds(tile * LANES, LANES)], sems.at[tile]
    )


def write_scratch(cols):
    return [pltpu.VMEM((cols, LANES), F32), pltpu.SemaphoreType.DMA((cols // LANES,))]


def depth_kernel(depth, out, natural, sems):
    writes = []
    for tile in range(depth.shape[0] // LANES):
        for k in range(STEPS):
            natural[spread_rows(tile, k), :] = depth[at(tile, k), :]
        writes.append(tile_write(natural, out, tile, sems))
        writes[-1].start()
    for write in writes:
        write.wait()


def write_depth(depth, block):
    return pl.pallas_call(
        depth_kernel,
        out_shape=shape(*block),
        in_specs=[VMEM],
        out_specs=ANY,
        scratch_shapes=write_scratch(block[1]),
        compiler_params=PARAMS,
        cost_estimate=pl.CostEstimate(flops=100_000, bytes_accessed=2_000_000, transcendentals=0),
        name="write_depth",
    )(depth)


def rows_of(ref):
    return tuple(ref[i : i + 1, :] for i in range(5))


def ordered(axis, stage, mine, theirs):
    is_low = (lax.axis_index(axis) >> stage) % 2 == 0
    one = tuple(jnp.where(is_low, a, b) for a, b in zip(mine, theirs))
    two = tuple(jnp.where(is_low, b, a) for a, b in zip(mine, theirs))
    return is_low, merge(one, two)


def merge_kernel(mine, theirs, *refs, axis, stage):
    out = refs[-1]
    _, (merged, _) = ordered(axis, stage, rows_of(mine), rows_of(theirs))
    for i, v in enumerate(merged):
        out[i : i + 1, :] = v
    out[5:8, :] = jnp.zeros((3, out.shape[1]), F32)


def merge_call(axis, stage, mine, theirs, beside):
    return pl.pallas_call(
        functools.partial(merge_kernel, axis=axis, stage=stage),
        out_shape=shape(*mine.shape),
        in_specs=[VMEM] * (2 + len(beside)),
        out_specs=VMEM,
        compiler_params=PARAMS,
        name="merge",
    )(mine, theirs, *beside)


def line_ends(axis, refs):
    steps = []
    parts = [rows_of(ref) for ref in refs]
    stage = 0
    while len(parts) > 4:
        is_low, (_, weights) = ordered(axis, stage, *parts[:2])
        steps.append((is_low, weights))
        parts = parts[2:]
        stage += 1
    is_low, (own, weights) = ordered(axis, stage, *parts[:2])
    steps.append((is_low, weights))
    _, (other, _) = ordered(axis, stage, *parts[2:])
    is_low, (whole, weights) = ordered(axis, stage + 1, own, other)
    steps.append((is_low, weights))
    t, _, gr, _, sr = whole
    left = jnp.zeros_like(t)
    right = sr / (t + gr + 1.0)
    for is_low, (w1, w2, source) in reversed(steps):
        middle = w1 * left + w2 * right + source
        left = jnp.where(is_low, left, middle)
        right = jnp.where(is_low, middle, right)
    return left, right


def segment_ends(left, right, w_ref, s_ref, levels):
    index = row_index(left.shape)
    for level in reversed(range(levels)):
        stride = 1 << level
        middle = w_ref[3 * level] * left + w_ref[3 * level + 1] * right + s_ref[1 + level]
        upper = (index >> level) % 2 == 1
        left, right = (
            jnp.where(upper, pltpu.roll(middle, stride, 0), left),
            jnp.where(upper, pltpu.roll(right, stride, 0), middle),
        )
    return left, right


def march_values(left, right, t_ref, s_ref, inv_ref, scale, r_ref, store):
    value = left
    change = t_ref[0] * (right - left) - t_ref[1] * left - s_ref[0]
    for k in range(STEPS):
        inverse = full(inv_ref, k)
        value = value + change
        change = change + (scale * (inverse * inverse) * value - full(r_ref, k))
        store(k, value * inverse)


def solve_x_kernel(inv_ref, r_ref, t_ref, w_ref, s_ref, *refs, scale):
    parts, (out, natural, sems) = refs[:-3], refs[-3:]
    tiles = out.shape[1] // LANES
    ends = []
    for row in line_ends("gx", parts):
        ends.append(
            jnp.concatenate([jnp.broadcast_to(row[:, tile_span(t)], (SUB, LANES)) for t in range(tiles)])
        )
    left, right = segment_ends(*ends, w_ref, s_ref, log2(SUB))

    def store(k, speed):
        for tile in range(tiles):
            natural[spread_rows(tile, k), :] = speed[tile * SUB : (tile + 1) * SUB, :]

    march_values(left, right, t_ref, s_ref, inv_ref, scale, r_ref, store)
    writes = [tile_write(natural, out, tile, sems) for tile in range(tiles)]
    for write in writes:
        write.start()
    for write in writes:
        write.wait()


def solve_y_kernel(inv_ref, r_ref, t_ref, w_ref, s_ref, *refs, scale):
    parts, (out, natural, sems, turned) = refs[:-4], refs[-4:]
    tiles = out.shape[1] // LANES
    ends = line_ends("gy", parts)
    ends = [jnp.broadcast_to(row, (tiles * SUB, LANES)) for row in ends]
    left, right = segment_ends(*ends, w_ref, s_ref, log2(tiles * SUB))

    def store(k, speed):
        for tile in range(tiles):
            turned[spread_rows(tile, k), :] = speed[tile * SUB : (tile + 1) * SUB, :]

    march_values(left, right, t_ref, s_ref, inv_ref, scale, r_ref, store)
    writes = []
    for tile in range(tiles):
        block = turned[tile_span(tile), :].T
        for k in range(STEPS):
            natural[spread_rows(tile, k), :] = block[k * SUB : (k + 1) * SUB, :]
        writes.append(tile_write(natural, out, tile, sems))
        writes[-1].start()
    for write in writes:
        write.wait()


def solve(kernel, name, pieces, parts, block, scale, extra=()):
    return pl.pallas_call(
        functools.partial(kernel, scale=scale),
        out_shape=shape(*block),
        in_specs=[VMEM] * (len(pieces) + len(parts)),
        out_specs=ANY,
        scratch_shapes=write_scratch(block[1]) + list(extra),
        compiler_params=PARAMS,
        cost_estimate=pl.CostEstimate(flops=1_000_000, bytes_accessed=4_000_000, transcendentals=0),
        name=name,
    )(*pieces, *parts)


def hand_on(value, axis):
    count = lax.axis_size(axis)
    far = [i + 2 if i % 2 == 0 else i - 2 for i in range(count)]
    return lax.ppermute(value, axis, [(i, t if 0 <= t < count else i ^ 1) for i, t in enumerate(far)])


def cross(value, axis, mask):
    return lax.ppermute(value, axis, [(i, i ^ mask) for i in range(lax.axis_size(axis))])


def parts_of_line(axis, mine, relay, beside=(), tall=None):
    parts = []
    last = log2(lax.axis_size(axis)) - 2
    for stage in range(last):
        theirs = cross(mine, axis, 1 << stage)
        parts += [mine, theirs]
        mine = merge_call(axis, stage, mine, theirs, beside)
    if relay:
        first = cross(mine, axis, 1 << last)
        second = cross(mine if tall is None else tall, axis, 2 << last)
        both = cross(second[0:SUB], axis, 1 << last)
    else:
        first, second, both = (cross(mine, axis, n << last) for n in (1, 2, 3))
    return parts + [mine, first, second, both]


def on_device(h, p, q, b, m):
    block = h.shape
    rows, cols = block
    inv_cx = 3.0 / (rows * lax.axis_size("gx") / 4.0) ** 2
    inv_cy = 3.0 / (cols * lax.axis_size("gy") / 4.0) ** 2
    xa, ya, *outer = pack(h, p, q, b, m)
    middle = load_middle(h, p, q, b, m)
    near_x, near_y = cross(xa, "gx", 1), cross(ya, "gy", 1)
    far_y = hand_on(jnp.pad(near_y[1], ((0, 5 * SUB), (0, 0))), "gy")
    hx, hy, ix, iy, tx, wx, ty, wy, coef_x, coef_y = prepare_depth(outer[0], middle[0], inv_cx, inv_cy)
    far_x = hand_on(second_of(near_x, coef_x), "gx")
    px, py, qx, qy, bx, by, mx, my = prepare_rest(outer[1:], middle[1:])
    mass_y, shear_y, normal_y = fluxes_y(near_y, far_y, hy, py, qy, by, my)
    inner = fluxes_x_inner(hx, px, qx, bx, mx, ix, mass_y, shear_y, inv_cx=inv_cx)
    depth, rx, ry, sx, sy, end_x, end_y, tall_y = fluxes_x(
        near_x, far_x, hx, px, qx, bx, mx, ix, iy, my, mass_y, shear_y, normal_y, *inner,
        tx, wx, ty, wy, coef_x, coef_y, inv_cx=inv_cx, inv_cy=inv_cy,
    )
    new_depth = write_depth(depth, block)
    parts_y = parts_of_line("gy", end_y, True, tall=tall_y if lax.axis_size("gy") == 4 else None)
    parts_x = parts_of_line("gx", end_x, False, parts_y[1:2])
    turned = [pltpu.VMEM((cols, LANES), F32)]
    vy = solve(solve_y_kernel, "solve_y", (iy, ry, ty, wy, sy), parts_y, block, inv_cy, turned)
    vx = solve(solve_x_kernel, "solve_x", (ix, rx, tx, wx, sx), parts_x, block, inv_cx)
    return new_depth, vx, vy


def solution(mesh):
    spec = P("gx", "gy")
    return jax.shard_map(
        on_device,
        mesh=mesh,
        in_specs=(spec,) * 5,
        out_specs=(spec,) * 3,
        check_vma=False,
    )
```

```python
import functools

import jax
import jax.numpy as jnp
from jax import lax
from jax.experimental import pallas as pl
from jax.experimental.pallas import tpu as pltpu
from jax.sharding import PartitionSpec as P

gravity = 9.81
ratio = 0.05
LANES = 128
SUB = 8
STEPS = LANES // SUB
F32 = jnp.float32
VMEM = pl.BlockSpec(memory_space=pltpu.VMEM)
HBM = pl.BlockSpec(memory_space=pltpu.HBM)
ANY = pl.BlockSpec(memory_space=pl.ANY)
PARAMS = pltpu.CompilerParams(vmem_limit_bytes=16 * 1024 * 1024)


def lane_index(shape):
    return lax.broadcasted_iota(jnp.int32, shape, len(shape) - 1)


def row_index(shape):
    return lax.broadcasted_iota(jnp.int32, shape, len(shape) - 2)


def at(tile, step):
    first = tile * LANES + step * SUB
    return slice(first, first + SUB)


def tile_span(tile):
    return slice(tile * LANES, (tile + 1) * LANES)


def spread_rows(tile, step):
    return pl.ds(tile * LANES + step, SUB, stride=STEPS)


def shape(*dims):
    return jax.ShapeDtypeStruct(dims, F32)


def pack_x_kernel(h, p, q, b, m, slabs, top, bottom, itop, ibottom, sems):
    rows = h.shape[0]
    copies = []
    for f, src in enumerate((h, p, q, b, m)):
        for side, (target, whole, row) in enumerate(((top, itop, 0), (bottom, ibottom, rows - SUB))):
            copy = pltpu.make_async_copy(
                src.at[pl.ds(row, SUB), :], target.at[f] if f < 4 else whole, sems.at[2 * f + side]
            )
            copy.start()
            copies.append(copy)
    for copy in copies:
        copy.wait()
    first = jnp.concatenate(
        [top[0, 0:2, :], top[1, 0:2, :], top[2, 0:2, :], top[3, 0:1, :], itop[0:1, :].astype(F32)]
    )
    last = jnp.concatenate(
        [
            bottom[0, SUB - 2 : SUB, :],
            bottom[1, SUB - 2 : SUB, :],
            bottom[2, SUB - 2 : SUB, :],
            bottom[3, SUB - 1 : SUB, :],
            ibottom[SUB - 1 : SUB, :].astype(F32),
        ]
    )
    even = lax.axis_index("gx") % 2 == 0
    slabs[0] = jnp.where(even, last, first)
    slabs[1] = jnp.where(even, first, last)


def pack_x(*fields):
    cols = fields[0].shape[1]
    return pl.pallas_call(
        pack_x_kernel,
        out_shape=shape(2, SUB, cols),
        in_specs=[HBM] * 5,
        out_specs=VMEM,
        scratch_shapes=[
            pltpu.VMEM((4, SUB, cols), F32),
            pltpu.VMEM((4, SUB, cols), F32),
            pltpu.VMEM((SUB, cols), jnp.int32),
            pltpu.VMEM((SUB, cols), jnp.int32),
            pltpu.SemaphoreType.DMA((10,)),
        ],
        compiler_params=PARAMS,
        name="pack_x",
    )(*[pltpu.with_memory_space_constraint(v, pltpu.HBM) for v in fields])


def pack_y_kernel(h, p, q, b, m, _, slabs, natural):
    rows, cols = h.shape
    lane = lane_index((rows, LANES))
    out = None
    for f, src in enumerate((h, p, q, b, m)):
        both = jnp.where(lane < LANES // 2, src[:, 0:LANES], src[:, cols - LANES : cols]).astype(F32)
        moved = pltpu.roll(both, 4 * f + 2, 1)
        out = moved if out is None else jnp.where(lane >= 4 * f, moved, out)
    natural[...] = out
    turned = jnp.concatenate([natural[spread_rows(0, k), :] for k in range(STEPS)]).T
    last = jnp.concatenate([turned[0:2], turned[4:6], turned[8:10], turned[13:14], turned[17:18]])
    first = jnp.concatenate([turned[2:4], turned[6:8], turned[10:12], turned[14:15], turned[18:19]])
    even = lax.axis_index("gy") % 2 == 0
    slabs[0] = jnp.where(even, last, first)
    slabs[1] = jnp.where(even, first, last)


def pack_y(*fields, after):
    rows = fields[0].shape[0]
    return pl.pallas_call(
        pack_y_kernel,
        out_shape=shape(2, SUB, rows),
        in_specs=[VMEM] * 6,
        out_specs=VMEM,
        scratch_shapes=[pltpu.VMEM((rows, LANES), F32)],
        compiler_params=PARAMS,
        cost_estimate=pl.CostEstimate(flops=500_000, bytes_accessed=1_000_000, transcendentals=0),
        name="pack_y",
    )(*fields, after)


def tie_kernel(both, _, out):
    out[...] = both[1]


def second_of(both, after):
    return pl.pallas_call(
        tie_kernel,
        out_shape=shape(*both.shape[1:]),
        in_specs=[VMEM, VMEM],
        out_specs=VMEM,
        compiler_params=PARAMS,
        name="second_of",
    )(both, after)


def merge_coefficients(one, two):
    t1, gl1, gr1 = one
    t2, gl2, gr2 = two
    shunt = gr1 + gl2
    inverse = 1.0 / (t1 + t2 + shunt)
    w1, w2 = t1 * inverse, t2 * inverse
    return (w1 * t2, gl1 + w1 * shunt, gr2 + w2 * shunt), (w1, w2, inverse)


def merge_sources(one, two, weights):
    w1, w2, inverse = weights
    source = one[1] - two[0]
    return (one[0] - w1 * source, two[1] + w2 * source), source * inverse


def merge(one, two):
    coefficients, weights = merge_coefficients(one[:3], two[:3])
    sources, middle = merge_sources(one[3:], two[3:], weights)
    return coefficients + sources, weights[:2] + (middle,)


def log2(count):
    return (count - 1).bit_length()


def full(ref, step):
    return jnp.concatenate([ref[at(tile, step), :] for tile in range(ref.shape[0] // LANES)])


def march_depth(inv_ref, scale, out_t, out_w, levels):
    count = inv_ref.shape[0] // STEPS
    zero = jnp.zeros((count, LANES), F32)
    alpha, gamma, beta, delta = zero, zero, zero, zero
    for k in range(STEPS):
        inverse = full(inv_ref, k)
        d = scale * (inverse * inverse)
        alpha = alpha + gamma
        gamma = gamma + d * (1.0 + alpha)
        beta = beta + delta
        delta = delta + d * ((k + 1.0) + beta)
    t = 1.0 / (STEPS + beta)
    out_t[0] = t
    out_t[1] = t * alpha
    out_t[2] = 1.0 + delta
    coefficients = (t, t * alpha, t * delta)
    for level in range(levels):
        after = tuple(pltpu.roll(v, count - (1 << level), 0) for v in coefficients)
        coefficients, weights = merge_coefficients(coefficients, after)
        for j, v in enumerate(weights):
            out_w[3 * level + j] = v
    return coefficients


def lay_out(src, xs, ys, natural, turned):
    for tile in range(xs.shape[0] // LANES):
        natural[tile_span(tile), :] = src[:, tile_span(tile)].astype(F32)
        for k in range(STEPS):
            xs[at(tile, k), :] = natural[spread_rows(tile, k), :]
        turned[tile_span(tile), :] = xs[tile_span(tile), :].T
        for k in range(STEPS):
            ys[at(tile, k), :] = turned[spread_rows(tile, k), :]


def prepare_depth_kernel(h, hx, hy, ix, iy, tx, wx, ty, wy, endx, endy, natural, turned, *, inv_cx, inv_cy):
    tiles = hx.shape[0] // LANES
    lay_out(h, hx, hy, natural, turned)
    ix[...] = 1.0 / hx[...]
    iy[...] = 1.0 / hy[...]
    ends_x = march_depth(ix, inv_cx, tx, wx, log2(SUB))
    ends_y = march_depth(iy, inv_cy, ty, wy, log2(SUB * tiles))
    for i in range(3):
        for tile in range(tiles):
            endx[i : i + 1, tile_span(tile)] = ends_x[i][tile * SUB : tile * SUB + 1, :]
        endy[i : i + 1, :] = ends_y[i][0:1, :]
    endx[3:8, :] = jnp.zeros((5, endx.shape[1]), F32)
    endy[3:8, :] = jnp.zeros((5, endy.shape[1]), F32)


def prepare_depth(h, inv_cx, inv_cy):
    stack = (h.shape[1], LANES)
    count = stack[0] // STEPS
    shapes = [shape(*stack)] * 4 + [
        shape(3, count, LANES),
        shape(3 * log2(SUB), count, LANES),
        shape(3, count, LANES),
        shape(3 * log2(count), count, LANES),
        shape(SUB, stack[0]),
        shape(SUB, LANES),
    ]
    return pl.pallas_call(
        functools.partial(prepare_depth_kernel, inv_cx=inv_cx, inv_cy=inv_cy),
        out_shape=tuple(shapes),
        in_specs=[VMEM],
        out_specs=(VMEM,) * len(shapes),
        scratch_shapes=[pltpu.VMEM(stack, F32)] * 2,
        compiler_params=PARAMS,
        cost_estimate=pl.CostEstimate(flops=2_000_000, bytes_accessed=4_000_000, transcendentals=0),
        name="prepare_depth",
    )(h)


def prepare_rest_kernel(*refs):
    fields, outs, natural, turned = refs[:4], refs[4:12], refs[12], refs[13]
    for f, src in enumerate(fields):
        lay_out(src, outs[2 * f], outs[2 * f + 1], natural.at[f % 2], turned.at[f % 2])


def prepare_rest(*fields):
    stack = (fields[0].shape[1], LANES)
    return pl.pallas_call(
        prepare_rest_kernel,
        out_shape=(shape(*stack),) * 8,
        in_specs=[VMEM] * 4,
        out_specs=(VMEM,) * 8,
        scratch_shapes=[pltpu.VMEM((2, *stack), F32)] * 2,
        compiler_params=PARAMS,
        cost_estimate=pl.CostEstimate(flops=2_000_000, bytes_accessed=6_000_000, transcendentals=0),
        name="prepare_rest",
    )(*fields)


def low_high(axis, near, far):
    index, count = lax.axis_index(axis), lax.axis_size(axis)
    even = index % 2 == 0
    low = jnp.where(index > 0, jnp.where(even, far, near), 0.0)
    high = jnp.where(index < count - 1, jnp.where(even, near, far), 0.0)
    return low, high


def half_slope(a, c):
    return 0.5 * (jnp.maximum(jnp.minimum(a, c), 0.0) + jnp.minimum(jnp.maximum(a, c), 0.0))


def face_flux(left, right, opened):
    is_open = opened > 0.5
    hl = jnp.where(is_open, left[0], 1.0)
    hr = jnp.where(is_open, right[0], 1.0)
    joint = 1.0 / (hl * hr)
    ul = left[1] * (hr * joint)
    ur = right[1] * (hl * joint)
    gl = gravity * hl
    gr = gravity * hr
    fastest = jnp.maximum(jnp.abs(ul) + gl * lax.rsqrt(gl), jnp.abs(ur) + gr * lax.rsqrt(gr))
    scale = (0.5 * ratio) * opened
    mass = (left[1] + right[1]) - fastest * (right[0] - left[0])
    push = 0.5 * (gl * hl + gr * hr) + left[1] * ul + right[1] * ur - fastest * (right[1] - left[1])
    shear = left[2] * ul + right[2] * ur - fastest * (right[2] - left[2])
    return scale * mass, scale * push, scale * shear


def extended(ref, tile, lows, highs):
    sub = row_index((SUB, LANES))
    out = {}
    for n, row in enumerate(lows, 1):
        value = ref[at(tile, STEPS - n), :]
        out[-n] = jnp.where(sub == 0, row, pltpu.roll(value, 1, 0))
    for n, row in enumerate(highs):
        value = ref[at(tile, n), :]
        out[STEPS + n] = jnp.where(sub == SUB - 1, row, pltpu.roll(value, SUB - 1, 0))
    return lambda k: out[k] if k in out else ref[at(tile, k), :]


def tile_fluxes(fields, bed, wet, store, start=0, stop=STEPS):
    def states(k):
        both = []
        for w in fields:
            here = w(k)
            both.append((here, half_slope(here - w(k - 1), w(k + 1) - here)))
        return [w + s for w, s in both], [w - s for w, s in both]

    left, _ = states(start - 1)
    before = None
    for k in range(start - 1, stop):
        left_next, right = states(k + 1)
        face = face_flux(left, right, wet(k) * wet(k + 1))
        left = left_next
        if k >= start:
            store(k, [a - c for a, c in zip(face, before)], bed(k + 1) - bed(k - 1))
        before = face


def march_source(inv_ref, scale, r_ref, t_ref, w_ref, s_ref, levels):
    count = inv_ref.shape[0] // STEPS
    c = jnp.zeros((count, LANES), F32)
    e = c
    for k in range(STEPS):
        inverse = full(inv_ref, k)
        c = c + e
        e = e + (scale * (inverse * inverse) * c - full(r_ref, k))
    sl = t_ref[0] * c
    s_ref[0] = sl
    sources = (sl, t_ref[2] * sl - e)
    for level in range(levels):
        after = tuple(pltpu.roll(v, count - (1 << level), 0) for v in sources)
        sources, middle = merge_sources(sources, after, tuple(w_ref[3 * level + j] for j in range(3)))
        s_ref[1 + level] = middle
    return sources


def flux_y_kernel(near, far, hy, py, qy, by, my, mass, shear, normal, across, along):
    tiles = hy.shape[0] // LANES
    low, high = low_high("gy", near[0], far[0:SUB, :])
    for tile in range(tiles):

        def extend(ref, row, layers):
            lows, highs = [], []
            for n in range(layers):
                last = at(tile - 1, STEPS - 1 - n).stop - 1
                first = at(tile + 1, n).start
                lows.append(low[row + layers - 1 - n : row + layers - n, :] if tile == 0 else ref[last : last + 1, :])
                highs.append(high[row + n : row + n + 1, :] if tile == tiles - 1 else ref[first : first + 1, :])
            return extended(ref, tile, lows, highs)

        def store(k, difference, bed):
            here, natural = at(tile, k), spread_rows(tile, k)
            across[natural, :] = difference[0]
            along[natural, :] = difference[2]
            pull = (0.5 * ratio * gravity) * hy[here, :]
            normal[here, :] = qy[here, :] - difference[1] - pull * bed

        tile_fluxes([extend(hy, 0, 2), extend(qy, 4, 2), extend(py, 2, 2)], extend(by, 6, 1), extend(my, 7, 1), store)
        span = tile_span(tile)
        mass[span, :] = across[span, :].T
        shear[span, :] = along[span, :].T


def fluxes_y(*arrays):
    stack = arrays[2].shape
    return pl.pallas_call(
        flux_y_kernel,
        out_shape=(shape(*stack),) * 3,
        in_specs=[VMEM] * len(arrays),
        out_specs=(VMEM,) * 3,
        scratch_shapes=[pltpu.VMEM(stack, F32)] * 2,
        compiler_params=PARAMS,
        cost_estimate=pl.CostEstimate(flops=4_000_000, bytes_accessed=4_000_000, transcendentals=0),
        name="fluxes_y",
    )(*arrays)


INNER = (2, STEPS - 2)


def x_store(hx, px, mx, depth, push, across):
    def of_tile(tile):
        def store(k, difference, bed):
            here = at(tile, k)
            h = hx[here, :]
            depth[here, :] = h - mx[here, :] * difference[0]
            push[here, :] = px[here, :] - difference[1] - (0.5 * ratio * gravity) * h * bed
            across[here, :] = difference[2]

        return store

    return of_tile


def flux_x_inner_kernel(hx, px, qx, bx, mx, depth, push, across):
    store = x_store(hx, px, mx, depth, push, across)
    for tile in range(hx.shape[0] // LANES):
        fields = [extended(v, tile, (), ()) for v in (hx, px, qx, bx, mx)]
        tile_fluxes(fields[:3], fields[3], fields[4], store(tile), *INNER)
        for k in (*range(INNER[0]), *range(INNER[1], STEPS)):
            for ref in (depth, push, across):
                ref[at(tile, k), :] = jnp.zeros((SUB, LANES), F32)


def fluxes_x_inner(*arrays):
    stack = arrays[0].shape
    return pl.pallas_call(
        flux_x_inner_kernel,
        out_shape=(shape(*stack),) * 3,
        in_specs=[VMEM] * len(arrays),
        out_specs=(VMEM,) * 3,
        compiler_params=PARAMS,
        cost_estimate=pl.CostEstimate(flops=4_000_000, bytes_accessed=4_000_000, transcendentals=0),
        name="fluxes_x_inner",
    )(*arrays)


def flux_x_kernel(
    near, far, hx, px, qx, bx, mx, ix, iy, my, mass_y, shear_y, normal_y, depth_in, push_in, across_in,
    tx, wx, ty, wy, coefx, coefy,
    depth, rx, ry, sx, sy, endx, endy, tally,
    outer_depth, push, across, turned,
    *, inv_cx, inv_cy,
):
    tiles = hx.shape[0] // LANES
    low, high = low_high("gx", near[0], far[...])
    store = x_store(hx, px, mx, outer_depth, push, across)
    for tile in range(tiles):
        span = tile_span(tile)

        def extend(ref, row, layers):
            lows = [low[row + layers - 1 - n : row + layers - n, span] for n in range(layers)]
            highs = [high[row + n : row + n + 1, span] for n in range(layers)]
            return extended(ref, tile, lows, highs)

        fields, bed, wet = [extend(hx, 0, 2), extend(px, 2, 2), extend(qx, 4, 2)], extend(bx, 6, 1), extend(mx, 7, 1)
        tile_fluxes(fields, bed, wet, store(tile), 0, INNER[0])
        tile_fluxes(fields, bed, wet, store(tile), INNER[1], STEPS)
        inner = slice(at(tile, INNER[0]).start, at(tile, INNER[1]).start)
        for done, ref in ((depth_in, outer_depth), (push_in, push), (across_in, across)):
            ref[inner, :] = done[inner, :]
        turned[span, :] = across[span, :].T
        m, inverse = mx[span, :], ix[span, :]
        depth[span, :] = outer_depth[span, :] - m * mass_y[span, :]
        rx[span, :] = (inv_cx * (inverse * inverse)) * m * (push[span, :] - shear_y[span, :])
        for k in range(STEPS):
            here = at(tile, k)
            inverse = iy[here, :]
            total = normal_y[here, :] - turned[spread_rows(tile, k), :]
            ry[here, :] = (inv_cy * (inverse * inverse)) * my[here, :] * total

    ends_x = march_source(ix, inv_cx, rx, tx, wx, sx, log2(SUB))
    ends_y = march_source(iy, inv_cy, ry, ty, wy, sy, log2(SUB * tiles))
    endx[...] = coefx[...]
    endy[...] = coefy[...]
    for i in range(2):
        for tile in range(tiles):
            endx[3 + i : 4 + i, tile_span(tile)] = ends_x[i][tile * SUB : tile * SUB + 1, :]
        endy[3 + i : 4 + i, :] = ends_y[i][0:1, :]
    tally[...] = jnp.zeros_like(tally)
    tally[0:SUB, :] = endy[...]


def fluxes_x(*arrays, inv_cx, inv_cy):
    stack = arrays[2].shape
    count = stack[0] // STEPS
    shapes = (
        shape(*stack),
        shape(*stack),
        shape(*stack),
        shape(1 + log2(SUB), count, LANES),
        shape(1 + log2(count), count, LANES),
        shape(*arrays[-2].shape),
        shape(*arrays[-1].shape),
        shape(3 * SUB, arrays[-1].shape[1]),
    )
    return pl.pallas_call(
        functools.partial(flux_x_kernel, inv_cx=inv_cx, inv_cy=inv_cy),
        out_shape=shapes,
        in_specs=[VMEM] * len(arrays),
        out_specs=(VMEM,) * len(shapes),
        scratch_shapes=[pltpu.VMEM(stack, F32)] * 4,
        compiler_params=PARAMS,
        name="fluxes_x",
    )(*arrays)


def tile_write(tiled, whole, tile, sems):
    rows = whole.shape[0]
    return pltpu.make_async_copy(
        tiled.at[pl.ds(tile * rows, rows), :], whole.at[:, pl.ds(tile * LANES, LANES)], sems.at[tile]
    )


def write_scratch(cols):
    return [pltpu.VMEM((cols, LANES), F32), pltpu.SemaphoreType.DMA((cols // LANES,))]


def depth_kernel(depth, out, natural, sems):
    writes = []
    for tile in range(depth.shape[0] // LANES):
        for k in range(STEPS):
            natural[spread_rows(tile, k), :] = depth[at(tile, k), :]
        writes.append(tile_write(natural, out, tile, sems))
        writes[-1].start()
    for write in writes:
        write.wait()


def write_depth(depth, block):
    return pl.pallas_call(
        depth_kernel,
        out_shape=shape(*block),
        in_specs=[VMEM],
        out_specs=ANY,
        scratch_shapes=write_scratch(block[1]),
        compiler_params=PARAMS,
        cost_estimate=pl.CostEstimate(flops=100_000, bytes_accessed=2_000_000, transcendentals=0),
        name="write_depth",
    )(depth)


def rows_of(ref):
    return tuple(ref[i : i + 1, :] for i in range(5))


def ordered(axis, stage, mine, theirs):
    is_low = (lax.axis_index(axis) >> stage) % 2 == 0
    one = tuple(jnp.where(is_low, a, b) for a, b in zip(mine, theirs))
    two = tuple(jnp.where(is_low, b, a) for a, b in zip(mine, theirs))
    return is_low, merge(one, two)


def merge_kernel(mine, theirs, *refs, axis, stage):
    out = refs[-1]
    _, (merged, _) = ordered(axis, stage, rows_of(mine), rows_of(theirs))
    for i, v in enumerate(merged):
        out[i : i + 1, :] = v
    out[5:8, :] = jnp.zeros((3, out.shape[1]), F32)


def merge_call(axis, stage, mine, theirs, beside):
    return pl.pallas_call(
        functools.partial(merge_kernel, axis=axis, stage=stage),
        out_shape=shape(*mine.shape),
        in_specs=[VMEM] * (2 + len(beside)),
        out_specs=VMEM,
        compiler_params=PARAMS,
        name="merge",
    )(mine, theirs, *beside)


def line_ends(axis, refs):
    steps = []
    parts = [rows_of(ref) for ref in refs]
    stage = 0
    while len(parts) > 4:
        is_low, (_, weights) = ordered(axis, stage, *parts[:2])
        steps.append((is_low, weights))
        parts = parts[2:]
        stage += 1
    is_low, (own, weights) = ordered(axis, stage, *parts[:2])
    steps.append((is_low, weights))
    _, (other, _) = ordered(axis, stage, *parts[2:])
    is_low, (whole, weights) = ordered(axis, stage + 1, own, other)
    steps.append((is_low, weights))
    t, _, gr, _, sr = whole
    left = jnp.zeros_like(t)
    right = sr / (t + gr + 1.0)
    for is_low, (w1, w2, source) in reversed(steps):
        middle = w1 * left + w2 * right + source
        left = jnp.where(is_low, left, middle)
        right = jnp.where(is_low, middle, right)
    return left, right


def segment_ends(left, right, w_ref, s_ref, levels):
    index = row_index(left.shape)
    for level in reversed(range(levels)):
        stride = 1 << level
        middle = w_ref[3 * level] * left + w_ref[3 * level + 1] * right + s_ref[1 + level]
        upper = (index >> level) % 2 == 1
        left, right = (
            jnp.where(upper, pltpu.roll(middle, stride, 0), left),
            jnp.where(upper, pltpu.roll(right, stride, 0), middle),
        )
    return left, right


def march_values(left, right, t_ref, s_ref, inv_ref, scale, r_ref, store):
    value = left
    change = t_ref[0] * (right - left) - t_ref[1] * left - s_ref[0]
    for k in range(STEPS):
        inverse = full(inv_ref, k)
        value = value + change
        change = change + (scale * (inverse * inverse) * value - full(r_ref, k))
        store(k, value * inverse)


def solve_x_kernel(inv_ref, r_ref, t_ref, w_ref, s_ref, *refs, scale):
    parts, (out, natural, sems) = refs[:-3], refs[-3:]
    tiles = out.shape[1] // LANES
    ends = []
    for row in line_ends("gx", parts):
        ends.append(
            jnp.concatenate([jnp.broadcast_to(row[:, tile_span(t)], (SUB, LANES)) for t in range(tiles)])
        )
    left, right = segment_ends(*ends, w_ref, s_ref, log2(SUB))

    def store(k, speed):
        for tile in range(tiles):
            natural[spread_rows(tile, k), :] = speed[tile * SUB : (tile + 1) * SUB, :]

    march_values(left, right, t_ref, s_ref, inv_ref, scale, r_ref, store)
    writes = [tile_write(natural, out, tile, sems) for tile in range(tiles)]
    for write in writes:
        write.start()
    for write in writes:
        write.wait()


def solve_y_kernel(inv_ref, r_ref, t_ref, w_ref, s_ref, *refs, scale):
    parts, (out, natural, sems, turned) = refs[:-4], refs[-4:]
    tiles = out.shape[1] // LANES
    ends = line_ends("gy", parts)
    ends = [jnp.broadcast_to(row, (tiles * SUB, LANES)) for row in ends]
    left, right = segment_ends(*ends, w_ref, s_ref, log2(tiles * SUB))

    def store(k, speed):
        for tile in range(tiles):
            turned[spread_rows(tile, k), :] = speed[tile * SUB : (tile + 1) * SUB, :]

    march_values(left, right, t_ref, s_ref, inv_ref, scale, r_ref, store)
    writes = []
    for tile in range(tiles):
        block = turned[tile_span(tile), :].T
        for k in range(STEPS):
            natural[spread_rows(tile, k), :] = block[k * SUB : (k + 1) * SUB, :]
        writes.append(tile_write(natural, out, tile, sems))
        writes[-1].start()
    for write in writes:
        write.wait()


def solve(kernel, name, pieces, parts, block, scale, extra=()):
    return pl.pallas_call(
        functools.partial(kernel, scale=scale),
        out_shape=shape(*block),
        in_specs=[VMEM] * (len(pieces) + len(parts)),
        out_specs=ANY,
        scratch_shapes=write_scratch(block[1]) + list(extra),
        compiler_params=PARAMS,
        cost_estimate=pl.CostEstimate(flops=1_000_000, bytes_accessed=4_000_000, transcendentals=0),
        name=name,
    )(*pieces, *parts)


def hand_on(value, axis):
    count = lax.axis_size(axis)
    far = [i + 2 if i % 2 == 0 else i - 2 for i in range(count)]
    return lax.ppermute(value, axis, [(i, t if 0 <= t < count else i ^ 1) for i, t in enumerate(far)])


def cross(value, axis, mask):
    return lax.ppermute(value, axis, [(i, i ^ mask) for i in range(lax.axis_size(axis))])


def parts_of_line(axis, mine, relay, beside=(), tall=None):
    parts = []
    last = log2(lax.axis_size(axis)) - 2
    for stage in range(last):
        theirs = cross(mine, axis, 1 << stage)
        parts += [mine, theirs]
        mine = merge_call(axis, stage, mine, theirs, beside)
    if relay:
        first = cross(mine, axis, 1 << last)
        second = cross(mine if tall is None else tall, axis, 2 << last)
        both = cross(second[0:SUB], axis, 1 << last)
    else:
        first, second, both = (cross(mine, axis, n << last) for n in (1, 2, 3))
    return parts + [mine, first, second, both]


def on_device(h, p, q, b, m):
    block = h.shape
    rows, cols = block
    inv_cx = 3.0 / (rows * lax.axis_size("gx") / 4.0) ** 2
    inv_cy = 3.0 / (cols * lax.axis_size("gy") / 4.0) ** 2
    slabs_x = pack_x(h, p, q, b, m)
    near_x = cross(slabs_x, "gx", 1)
    near_y = cross(pack_y(h, p, q, b, m, after=slabs_x), "gy", 1)
    far_y = hand_on(jnp.pad(near_y[1], ((0, 5 * SUB), (0, 0))), "gy")
    far_x = hand_on(near_x[1], "gx")
    hx, hy, ix, iy, tx, wx, ty, wy, coef_x, coef_y = prepare_depth(h, inv_cx, inv_cy)
    px, py, qx, qy, bx, by, mx, my = prepare_rest(p, q, b, m)
    inner = fluxes_x_inner(hx, px, qx, bx, mx)
    mass_y, shear_y, normal_y = fluxes_y(near_y, far_y, hy, py, qy, by, my)
    depth, rx, ry, sx, sy, end_x, end_y, tall_y = fluxes_x(
        near_x, far_x, hx, px, qx, bx, mx, ix, iy, my, mass_y, shear_y, normal_y, *inner,
        tx, wx, ty, wy, coef_x, coef_y, inv_cx=inv_cx, inv_cy=inv_cy,
    )
    new_depth = write_depth(depth, block)
    parts_y = parts_of_line("gy", end_y, True, tall=tall_y if lax.axis_size("gy") == 4 else None)
    parts_x = parts_of_line("gx", end_x, False, parts_y[1:2])
    turned = [pltpu.VMEM((cols, LANES), F32)]
    vy = solve(solve_y_kernel, "solve_y", (iy, ry, ty, wy, sy), parts_y, block, inv_cy, turned)
    vx = solve(solve_x_kernel, "solve_x", (ix, rx, tx, wx, sx), parts_x, block, inv_cx)
    return new_depth, vx, vy


def solution(mesh):
    spec = P("gx", "gy")
    return jax.shard_map(
        on_device,
        mesh=mesh,
        in_specs=(spec,) * 5,
        out_specs=(spec,) * 3,
        check_vma=False,
    )
```

```python
import functools

import jax
import jax.numpy as jnp
from jax import lax
from jax.experimental import pallas as pl
from jax.experimental.pallas import tpu as pltpu
from jax.sharding import PartitionSpec as P

gravity = 9.81
ratio = 0.05
LANES = 128
SUB = 8
STEPS = LANES // SUB
F32 = jnp.float32
VMEM = pl.BlockSpec(memory_space=pltpu.VMEM)
HBM = pl.BlockSpec(memory_space=pltpu.HBM)
ANY = pl.BlockSpec(memory_space=pl.ANY)
PARAMS = pltpu.CompilerParams(vmem_limit_bytes=16 * 1024 * 1024)


def lane_index(shape):
    return lax.broadcasted_iota(jnp.int32, shape, len(shape) - 1)


def row_index(shape):
    return lax.broadcasted_iota(jnp.int32, shape, len(shape) - 2)


def at(tile, step):
    first = tile * LANES + step * SUB
    return slice(first, first + SUB)


def tile_span(tile):
    return slice(tile * LANES, (tile + 1) * LANES)


def spread_rows(tile, step):
    return pl.ds(tile * LANES + step, SUB, stride=STEPS)


def shape(*dims):
    return jax.ShapeDtypeStruct(dims, F32)


def pack_x_kernel(h, p, q, b, m, slabs, top, bottom, itop, ibottom, sems):
    rows = h.shape[0]
    copies = []
    for f, src in enumerate((h, p, q, b, m)):
        for side, (target, whole, row) in enumerate(((top, itop, 0), (bottom, ibottom, rows - SUB))):
            copy = pltpu.make_async_copy(
                src.at[pl.ds(row, SUB), :], target.at[f] if f < 4 else whole, sems.at[2 * f + side]
            )
            copy.start()
            copies.append(copy)
    for copy in copies:
        copy.wait()
    first = jnp.concatenate(
        [top[0, 0:2, :], top[1, 0:2, :], top[2, 0:2, :], top[3, 0:1, :], itop[0:1, :].astype(F32)]
    )
    last = jnp.concatenate(
        [
            bottom[0, SUB - 2 : SUB, :],
            bottom[1, SUB - 2 : SUB, :],
            bottom[2, SUB - 2 : SUB, :],
            bottom[3, SUB - 1 : SUB, :],
            ibottom[SUB - 1 : SUB, :].astype(F32),
        ]
    )
    even = lax.axis_index("gx") % 2 == 0
    slabs[0] = jnp.where(even, last, first)
    slabs[1] = jnp.where(even, first, last)


def pack_x(*fields):
    cols = fields[0].shape[1]
    return pl.pallas_call(
        pack_x_kernel,
        out_shape=shape(2, SUB, cols),
        in_specs=[HBM] * 5,
        out_specs=VMEM,
        scratch_shapes=[
            pltpu.VMEM((4, SUB, cols), F32),
            pltpu.VMEM((4, SUB, cols), F32),
            pltpu.VMEM((SUB, cols), jnp.int32),
            pltpu.VMEM((SUB, cols), jnp.int32),
            pltpu.SemaphoreType.DMA((10,)),
        ],
        compiler_params=PARAMS,
        name="pack_x",
    )(*[pltpu.with_memory_space_constraint(v, pltpu.HBM) for v in fields])


def pack_y_kernel(h, p, q, b, m, _, slabs, natural):
    rows, cols = h.shape
    lane = lane_index((rows, LANES))
    out = None
    for f, src in enumerate((h, p, q, b, m)):
        both = jnp.where(lane < LANES // 2, src[:, 0:LANES], src[:, cols - LANES : cols]).astype(F32)
        moved = pltpu.roll(both, 4 * f + 2, 1)
        out = moved if out is None else jnp.where(lane >= 4 * f, moved, out)
    natural[...] = out
    turned = jnp.concatenate([natural[spread_rows(0, k), :] for k in range(STEPS)]).T
    last = jnp.concatenate([turned[0:2], turned[4:6], turned[8:10], turned[13:14], turned[17:18]])
    first = jnp.concatenate([turned[2:4], turned[6:8], turned[10:12], turned[14:15], turned[18:19]])
    even = lax.axis_index("gy") % 2 == 0
    slabs[0] = jnp.where(even, last, first)
    slabs[1] = jnp.where(even, first, last)


def pack_y(*fields, after):
    rows = fields[0].shape[0]
    return pl.pallas_call(
        pack_y_kernel,
        out_shape=shape(2, SUB, rows),
        in_specs=[VMEM] * 6,
        out_specs=VMEM,
        scratch_shapes=[pltpu.VMEM((rows, LANES), F32)],
        compiler_params=PARAMS,
        cost_estimate=pl.CostEstimate(flops=500_000, bytes_accessed=1_000_000, transcendentals=0),
        name="pack_y",
    )(*fields, after)


def tie_kernel(both, _, out):
    out[...] = both[1]


def second_of(both, after):
    return pl.pallas_call(
        tie_kernel,
        out_shape=shape(*both.shape[1:]),
        in_specs=[VMEM, VMEM],
        out_specs=VMEM,
        compiler_params=PARAMS,
        name="second_of",
    )(both, after)


def merge_coefficients(one, two):
    t1, gl1, gr1 = one
    t2, gl2, gr2 = two
    shunt = gr1 + gl2
    inverse = 1.0 / (t1 + t2 + shunt)
    w1, w2 = t1 * inverse, t2 * inverse
    return (w1 * t2, gl1 + w1 * shunt, gr2 + w2 * shunt), (w1, w2, inverse)


def merge_sources(one, two, weights):
    w1, w2, inverse = weights
    source = one[1] - two[0]
    return (one[0] - w1 * source, two[1] + w2 * source), source * inverse


def merge(one, two):
    coefficients, weights = merge_coefficients(one[:3], two[:3])
    sources, middle = merge_sources(one[3:], two[3:], weights)
    return coefficients + sources, weights[:2] + (middle,)


def log2(count):
    return (count - 1).bit_length()


def full(ref, step):
    return jnp.concatenate([ref[at(tile, step), :] for tile in range(ref.shape[0] // LANES)])


def march_depth(inv_ref, scale, out_t, out_w, levels):
    count = inv_ref.shape[0] // STEPS
    zero = jnp.zeros((count, LANES), F32)
    alpha, gamma, beta, delta = zero, zero, zero, zero
    for k in range(STEPS):
        inverse = full(inv_ref, k)
        d = scale * (inverse * inverse)
        alpha = alpha + gamma
        gamma = gamma + d * (1.0 + alpha)
        beta = beta + delta
        delta = delta + d * ((k + 1.0) + beta)
    t = 1.0 / (STEPS + beta)
    out_t[0] = t
    out_t[1] = t * alpha
    out_t[2] = 1.0 + delta
    coefficients = (t, t * alpha, t * delta)
    for level in range(levels):
        after = tuple(pltpu.roll(v, count - (1 << level), 0) for v in coefficients)
        coefficients, weights = merge_coefficients(coefficients, after)
        for j, v in enumerate(weights):
            out_w[3 * level + j] = v
    return coefficients


def lay_out(src, xs, ys, natural, turned):
    for tile in range(xs.shape[0] // LANES):
        natural[tile_span(tile), :] = src[:, tile_span(tile)].astype(F32)
        for k in range(STEPS):
            xs[at(tile, k), :] = natural[spread_rows(tile, k), :]
        turned[tile_span(tile), :] = xs[tile_span(tile), :].T
        for k in range(STEPS):
            ys[at(tile, k), :] = turned[spread_rows(tile, k), :]


def prepare_depth_kernel(h, hx, hy, ix, iy, tx, wx, ty, wy, endx, endy, natural, turned, *, inv_cx, inv_cy):
    tiles = hx.shape[0] // LANES
    lay_out(h, hx, hy, natural, turned)
    ix[...] = 1.0 / hx[...]
    iy[...] = 1.0 / hy[...]
    ends_x = march_depth(ix, inv_cx, tx, wx, log2(SUB))
    ends_y = march_depth(iy, inv_cy, ty, wy, log2(SUB * tiles))
    for i in range(3):
        for tile in range(tiles):
            endx[i : i + 1, tile_span(tile)] = ends_x[i][tile * SUB : tile * SUB + 1, :]
        endy[i : i + 1, :] = ends_y[i][0:1, :]
    endx[3:8, :] = jnp.zeros((5, endx.shape[1]), F32)
    endy[3:8, :] = jnp.zeros((5, endy.shape[1]), F32)


def prepare_depth(h, inv_cx, inv_cy):
    stack = (h.shape[1], LANES)
    count = stack[0] // STEPS
    shapes = [shape(*stack)] * 4 + [
        shape(3, count, LANES),
        shape(3 * log2(SUB), count, LANES),
        shape(3, count, LANES),
        shape(3 * log2(count), count, LANES),
        shape(SUB, stack[0]),
        shape(SUB, LANES),
    ]
    return pl.pallas_call(
        functools.partial(prepare_depth_kernel, inv_cx=inv_cx, inv_cy=inv_cy),
        out_shape=tuple(shapes),
        in_specs=[VMEM],
        out_specs=(VMEM,) * len(shapes),
        scratch_shapes=[pltpu.VMEM(stack, F32)] * 2,
        compiler_params=PARAMS,
        cost_estimate=pl.CostEstimate(flops=2_000_000, bytes_accessed=4_000_000, transcendentals=0),
        name="prepare_depth",
    )(h)


def prepare_rest_kernel(*refs):
    fields, outs, natural, turned = refs[:4], refs[4:12], refs[12], refs[13]
    for f, src in enumerate(fields):
        lay_out(src, outs[2 * f], outs[2 * f + 1], natural.at[f % 2], turned.at[f % 2])


def prepare_rest(*fields):
    stack = (fields[0].shape[1], LANES)
    return pl.pallas_call(
        prepare_rest_kernel,
        out_shape=(shape(*stack),) * 8,
        in_specs=[VMEM] * 4,
        out_specs=(VMEM,) * 8,
        scratch_shapes=[pltpu.VMEM((2, *stack), F32)] * 2,
        compiler_params=PARAMS,
        cost_estimate=pl.CostEstimate(flops=2_000_000, bytes_accessed=6_000_000, transcendentals=0),
        name="prepare_rest",
    )(*fields)


def low_high(axis, near, far):
    index, count = lax.axis_index(axis), lax.axis_size(axis)
    even = index % 2 == 0
    low = jnp.where(index > 0, jnp.where(even, far, near), 0.0)
    high = jnp.where(index < count - 1, jnp.where(even, near, far), 0.0)
    return low, high


def half_slope(a, c):
    return 0.5 * (jnp.maximum(jnp.minimum(a, c), 0.0) + jnp.minimum(jnp.maximum(a, c), 0.0))


def face_flux(left, right, opened):
    is_open = opened > 0.5
    hl = jnp.where(is_open, left[0], 1.0)
    hr = jnp.where(is_open, right[0], 1.0)
    joint = 1.0 / (hl * hr)
    ul = left[1] * (hr * joint)
    ur = right[1] * (hl * joint)
    gl = gravity * hl
    gr = gravity * hr
    fastest = jnp.maximum(jnp.abs(ul) + gl * lax.rsqrt(gl), jnp.abs(ur) + gr * lax.rsqrt(gr))
    scale = (0.5 * ratio) * opened
    mass = (left[1] + right[1]) - fastest * (right[0] - left[0])
    push = 0.5 * (gl * hl + gr * hr) + left[1] * ul + right[1] * ur - fastest * (right[1] - left[1])
    shear = left[2] * ul + right[2] * ur - fastest * (right[2] - left[2])
    return scale * mass, scale * push, scale * shear


def extended(ref, tile, lows, highs):
    sub = row_index((SUB, LANES))
    out = {}
    for n, row in enumerate(lows, 1):
        value = ref[at(tile, STEPS - n), :]
        out[-n] = jnp.where(sub == 0, row, pltpu.roll(value, 1, 0))
    for n, row in enumerate(highs):
        value = ref[at(tile, n), :]
        out[STEPS + n] = jnp.where(sub == SUB - 1, row, pltpu.roll(value, SUB - 1, 0))
    return lambda k: out[k] if k in out else ref[at(tile, k), :]


def tile_fluxes(fields, bed, wet, store, start=0, stop=STEPS):
    def states(k):
        both = []
        for w in fields:
            here = w(k)
            both.append((here, half_slope(here - w(k - 1), w(k + 1) - here)))
        return [w + s for w, s in both], [w - s for w, s in both]

    left, _ = states(start - 1)
    before = None
    for k in range(start - 1, stop):
        left_next, right = states(k + 1)
        face = face_flux(left, right, wet(k) * wet(k + 1))
        left = left_next
        if k >= start:
            store(k, [a - c for a, c in zip(face, before)], bed(k + 1) - bed(k - 1))
        before = face


def march_source(inv_ref, scale, r_ref, t_ref, w_ref, s_ref, levels):
    count = inv_ref.shape[0] // STEPS
    c = jnp.zeros((count, LANES), F32)
    e = c
    for k in range(STEPS):
        inverse = full(inv_ref, k)
        c = c + e
        e = e + (scale * (inverse * inverse) * c - full(r_ref, k))
    sl = t_ref[0] * c
    s_ref[0] = sl
    sources = (sl, t_ref[2] * sl - e)
    for level in range(levels):
        after = tuple(pltpu.roll(v, count - (1 << level), 0) for v in sources)
        sources, middle = merge_sources(sources, after, tuple(w_ref[3 * level + j] for j in range(3)))
        s_ref[1 + level] = middle
    return sources


def flux_y_kernel(near, far, hy, py, qy, by, my, mass, shear, normal, across, along):
    tiles = hy.shape[0] // LANES
    low, high = low_high("gy", near[0], far[0:SUB, :])
    for tile in range(tiles):

        def extend(ref, row, layers):
            lows, highs = [], []
            for n in range(layers):
                last = at(tile - 1, STEPS - 1 - n).stop - 1
                first = at(tile + 1, n).start
                lows.append(low[row + layers - 1 - n : row + layers - n, :] if tile == 0 else ref[last : last + 1, :])
                highs.append(high[row + n : row + n + 1, :] if tile == tiles - 1 else ref[first : first + 1, :])
            return extended(ref, tile, lows, highs)

        def store(k, difference, bed):
            here, natural = at(tile, k), spread_rows(tile, k)
            across[natural, :] = difference[0]
            along[natural, :] = difference[2]
            pull = (0.5 * ratio * gravity) * hy[here, :]
            normal[here, :] = qy[here, :] - difference[1] - pull * bed

        tile_fluxes([extend(hy, 0, 2), extend(qy, 4, 2), extend(py, 2, 2)], extend(by, 6, 1), extend(my, 7, 1), store)
        span = tile_span(tile)
        mass[span, :] = across[span, :].T
        shear[span, :] = along[span, :].T


def fluxes_y(*arrays):
    stack = arrays[2].shape
    return pl.pallas_call(
        flux_y_kernel,
        out_shape=(shape(*stack),) * 3,
        in_specs=[VMEM] * len(arrays),
        out_specs=(VMEM,) * 3,
        scratch_shapes=[pltpu.VMEM(stack, F32)] * 2,
        compiler_params=PARAMS,
        cost_estimate=pl.CostEstimate(flops=4_000_000, bytes_accessed=4_000_000, transcendentals=0),
        name="fluxes_y",
    )(*arrays)


INNER = (2, STEPS - 2)


def x_store(hx, px, mx, depth, push, across):
    def of_tile(tile):
        def store(k, difference, bed):
            here = at(tile, k)
            h = hx[here, :]
            depth[here, :] = h - mx[here, :] * difference[0]
            push[here, :] = px[here, :] - difference[1] - (0.5 * ratio * gravity) * h * bed
            across[here, :] = difference[2]

        return store

    return of_tile


def flux_x_inner_kernel(hx, px, qx, bx, mx, depth, push, across):
    store = x_store(hx, px, mx, depth, push, across)
    for tile in range(hx.shape[0] // LANES):
        fields = [extended(v, tile, (), ()) for v in (hx, px, qx, bx, mx)]
        tile_fluxes(fields[:3], fields[3], fields[4], store(tile), *INNER)
        for k in (*range(INNER[0]), *range(INNER[1], STEPS)):
            for ref in (depth, push, across):
                ref[at(tile, k), :] = jnp.zeros((SUB, LANES), F32)


def fluxes_x_inner(*arrays):
    stack = arrays[0].shape
    return pl.pallas_call(
        flux_x_inner_kernel,
        out_shape=(shape(*stack),) * 3,
        in_specs=[VMEM] * len(arrays),
        out_specs=(VMEM,) * 3,
        compiler_params=PARAMS,
        cost_estimate=pl.CostEstimate(flops=4_000_000, bytes_accessed=4_000_000, transcendentals=0),
        name="fluxes_x_inner",
    )(*arrays)


def flux_x_kernel(
    near, far, hx, px, qx, bx, mx, ix, shear_y, push_in, tx, wx, coef,
    depth, across, rx, sx, ends,
    push,
    *, inv_cx,
):
    tiles = hx.shape[0] // LANES
    low, high = low_high("gx", near[0], far[...])
    store = x_store(hx, px, mx, depth, push, across)
    for tile in range(tiles):
        span = tile_span(tile)

        def extend(ref, row, layers):
            lows = [low[row + layers - 1 - n : row + layers - n, span] for n in range(layers)]
            highs = [high[row + n : row + n + 1, span] for n in range(layers)]
            return extended(ref, tile, lows, highs)

        fields, bed, wet = [extend(hx, 0, 2), extend(px, 2, 2), extend(qx, 4, 2)], extend(bx, 6, 1), extend(mx, 7, 1)
        tile_fluxes(fields, bed, wet, store(tile), 0, INNER[0])
        tile_fluxes(fields, bed, wet, store(tile), INNER[1], STEPS)
        for k in range(STEPS):
            here = at(tile, k)
            inverse = ix[here, :]
            total = (push_in if INNER[0] <= k < INNER[1] else push)[here, :] - shear_y[here, :]
            rx[here, :] = (inv_cx * (inverse * inverse)) * mx[here, :] * total
    sources = march_source(ix, inv_cx, rx, tx, wx, sx, log2(SUB))
    ends[...] = coef[...]
    for i in range(2):
        for tile in range(tiles):
            ends[3 + i : 4 + i, tile_span(tile)] = sources[i][tile * SUB : tile * SUB + 1, :]


def fluxes_x(*arrays, inv_cx):
    stack = arrays[2].shape
    count = stack[0] // STEPS
    shapes = (
        shape(*stack),
        shape(*stack),
        shape(*stack),
        shape(1 + log2(SUB), count, LANES),
        shape(*arrays[-1].shape),
    )
    return pl.pallas_call(
        functools.partial(flux_x_kernel, inv_cx=inv_cx),
        out_shape=shapes,
        in_specs=[VMEM] * len(arrays),
        out_specs=(VMEM,) * len(shapes),
        scratch_shapes=[pltpu.VMEM(stack, F32)],
        compiler_params=PARAMS,
        name="fluxes_x",
    )(*arrays)


def join_y_kernel(
    depth_inner, across_inner, depth_outer, across_outer, mass_y, mx, normal_y, iy, my, ty, wy, coef,
    depth, ry, sy, ends, tall,
    across, turned,
    *, inv_cy,
):
    tiles = mx.shape[0] // LANES
    for tile in range(tiles):
        span = tile_span(tile)
        for k in range(STEPS):
            here = at(tile, k)
            inner = INNER[0] <= k < INNER[1]
            across[here, :] = (across_inner if inner else across_outer)[here, :]
            depth[here, :] = (depth_inner if inner else depth_outer)[here, :] - mx[here, :] * mass_y[here, :]
        turned[span, :] = across[span, :].T
        for k in range(STEPS):
            here = at(tile, k)
            inverse = iy[here, :]
            total = normal_y[here, :] - turned[spread_rows(tile, k), :]
            ry[here, :] = (inv_cy * (inverse * inverse)) * my[here, :] * total
    sources = march_source(iy, inv_cy, ry, ty, wy, sy, log2(SUB * tiles))
    ends[...] = coef[...]
    for i in range(2):
        ends[3 + i : 4 + i, :] = sources[i][0:1, :]
    tall[...] = jnp.zeros_like(tall)
    tall[0:SUB, :] = ends[...]


def join_y(*arrays, inv_cy):
    stack = arrays[0].shape
    count = stack[0] // STEPS
    shapes = (
        shape(*stack),
        shape(*stack),
        shape(1 + log2(count), count, LANES),
        shape(*arrays[-1].shape),
        shape(3 * SUB, arrays[-1].shape[1]),
    )
    return pl.pallas_call(
        functools.partial(join_y_kernel, inv_cy=inv_cy),
        out_shape=shapes,
        in_specs=[VMEM] * len(arrays),
        out_specs=(VMEM,) * len(shapes),
        scratch_shapes=[pltpu.VMEM(stack, F32)] * 2,
        compiler_params=PARAMS,
        cost_estimate=pl.CostEstimate(flops=2_000_000, bytes_accessed=2_000_000, transcendentals=0),
        name="join_y",
    )(*arrays)


def tile_write(tiled, whole, tile, sems):
    rows = whole.shape[0]
    return pltpu.make_async_copy(
        tiled.at[pl.ds(tile * rows, rows), :], whole.at[:, pl.ds(tile * LANES, LANES)], sems.at[tile]
    )


def write_scratch(cols):
    return [pltpu.VMEM((cols, LANES), F32), pltpu.SemaphoreType.DMA((cols // LANES,))]


def depth_kernel(depth, out, natural, sems):
    writes = []
    for tile in range(depth.shape[0] // LANES):
        for k in range(STEPS):
            natural[spread_rows(tile, k), :] = depth[at(tile, k), :]
        writes.append(tile_write(natural, out, tile, sems))
        writes[-1].start()
    for write in writes:
        write.wait()


def write_depth(depth, block):
    return pl.pallas_call(
        depth_kernel,
        out_shape=shape(*block),
        in_specs=[VMEM],
        out_specs=ANY,
        scratch_shapes=write_scratch(block[1]),
        compiler_params=PARAMS,
        cost_estimate=pl.CostEstimate(flops=100_000, bytes_accessed=2_000_000, transcendentals=0),
        name="write_depth",
    )(depth)


def rows_of(ref):
    return tuple(ref[i : i + 1, :] for i in range(5))


def ordered(axis, stage, mine, theirs):
    is_low = (lax.axis_index(axis) >> stage) % 2 == 0
    one = tuple(jnp.where(is_low, a, b) for a, b in zip(mine, theirs))
    two = tuple(jnp.where(is_low, b, a) for a, b in zip(mine, theirs))
    return is_low, merge(one, two)


def merge_kernel(mine, theirs, *refs, axis, stage):
    out = refs[-1]
    _, (merged, _) = ordered(axis, stage, rows_of(mine), rows_of(theirs))
    for i, v in enumerate(merged):
        out[i : i + 1, :] = v
    out[5:8, :] = jnp.zeros((3, out.shape[1]), F32)


def merge_call(axis, stage, mine, theirs, beside):
    return pl.pallas_call(
        functools.partial(merge_kernel, axis=axis, stage=stage),
        out_shape=shape(*mine.shape),
        in_specs=[VMEM] * (2 + len(beside)),
        out_specs=VMEM,
        compiler_params=PARAMS,
        name="merge",
    )(mine, theirs, *beside)


def line_ends(axis, refs):
    steps = []
    parts = [rows_of(ref) for ref in refs]
    stage = 0
    while len(parts) > 4:
        is_low, (_, weights) = ordered(axis, stage, *parts[:2])
        steps.append((is_low, weights))
        parts = parts[2:]
        stage += 1
    is_low, (own, weights) = ordered(axis, stage, *parts[:2])
    steps.append((is_low, weights))
    _, (other, _) = ordered(axis, stage, *parts[2:])
    is_low, (whole, weights) = ordered(axis, stage + 1, own, other)
    steps.append((is_low, weights))
    t, _, gr, _, sr = whole
    left = jnp.zeros_like(t)
    right = sr / (t + gr + 1.0)
    for is_low, (w1, w2, source) in reversed(steps):
        middle = w1 * left + w2 * right + source
        left = jnp.where(is_low, left, middle)
        right = jnp.where(is_low, middle, right)
    return left, right


def segment_ends(left, right, w_ref, s_ref, levels):
    index = row_index(left.shape)
    for level in reversed(range(levels)):
        stride = 1 << level
        middle = w_ref[3 * level] * left + w_ref[3 * level + 1] * right + s_ref[1 + level]
        upper = (index >> level) % 2 == 1
        left, right = (
            jnp.where(upper, pltpu.roll(middle, stride, 0), left),
            jnp.where(upper, pltpu.roll(right, stride, 0), middle),
        )
    return left, right


def march_values(left, right, t_ref, s_ref, inv_ref, scale, r_ref, store):
    value = left
    change = t_ref[0] * (right - left) - t_ref[1] * left - s_ref[0]
    for k in range(STEPS):
        inverse = full(inv_ref, k)
        value = value + change
        change = change + (scale * (inverse * inverse) * value - full(r_ref, k))
        store(k, value * inverse)


def solve_x_kernel(inv_ref, r_ref, t_ref, w_ref, s_ref, *refs, scale):
    parts, (out, natural, sems) = refs[:-3], refs[-3:]
    tiles = out.shape[1] // LANES
    ends = []
    for row in line_ends("gx", parts):
        ends.append(
            jnp.concatenate([jnp.broadcast_to(row[:, tile_span(t)], (SUB, LANES)) for t in range(tiles)])
        )
    left, right = segment_ends(*ends, w_ref, s_ref, log2(SUB))

    def store(k, speed):
        for tile in range(tiles):
            natural[spread_rows(tile, k), :] = speed[tile * SUB : (tile + 1) * SUB, :]

    march_values(left, right, t_ref, s_ref, inv_ref, scale, r_ref, store)
    writes = [tile_write(natural, out, tile, sems) for tile in range(tiles)]
    for write in writes:
        write.start()
    for write in writes:
        write.wait()


def solve_y_kernel(inv_ref, r_ref, t_ref, w_ref, s_ref, *refs, scale):
    parts, (out, natural, sems, turned) = refs[:-4], refs[-4:]
    tiles = out.shape[1] // LANES
    ends = line_ends("gy", parts)
    ends = [jnp.broadcast_to(row, (tiles * SUB, LANES)) for row in ends]
    left, right = segment_ends(*ends, w_ref, s_ref, log2(tiles * SUB))

    def store(k, speed):
        for tile in range(tiles):
            turned[spread_rows(tile, k), :] = speed[tile * SUB : (tile + 1) * SUB, :]

    march_values(left, right, t_ref, s_ref, inv_ref, scale, r_ref, store)
    writes = []
    for tile in range(tiles):
        block = turned[tile_span(tile), :].T
        for k in range(STEPS):
            natural[spread_rows(tile, k), :] = block[k * SUB : (k + 1) * SUB, :]
        writes.append(tile_write(natural, out, tile, sems))
        writes[-1].start()
    for write in writes:
        write.wait()


def solve(kernel, name, pieces, parts, block, scale, extra=()):
    return pl.pallas_call(
        functools.partial(kernel, scale=scale),
        out_shape=shape(*block),
        in_specs=[VMEM] * (len(pieces) + len(parts)),
        out_specs=ANY,
        scratch_shapes=write_scratch(block[1]) + list(extra),
        compiler_params=PARAMS,
        cost_estimate=pl.CostEstimate(flops=1_000_000, bytes_accessed=4_000_000, transcendentals=0),
        name=name,
    )(*pieces, *parts)


def hand_on(value, axis):
    count = lax.axis_size(axis)
    far = [i + 2 if i % 2 == 0 else i - 2 for i in range(count)]
    return lax.ppermute(value, axis, [(i, t if 0 <= t < count else i ^ 1) for i, t in enumerate(far)])


def cross(value, axis, mask):
    return lax.ppermute(value, axis, [(i, i ^ mask) for i in range(lax.axis_size(axis))])


def parts_of_line(axis, mine, relay, beside=(), tall=None):
    parts = []
    last = log2(lax.axis_size(axis)) - 2
    for stage in range(last):
        theirs = cross(mine, axis, 1 << stage)
        parts += [mine, theirs]
        mine = merge_call(axis, stage, mine, theirs, beside)
    if relay:
        first = cross(mine, axis, 1 << last)
        second = cross(mine if tall is None else tall, axis, 2 << last)
        both = cross(second[0:SUB], axis, 1 << last)
    else:
        first, second, both = (cross(mine, axis, n << last) for n in (1, 2, 3))
    return parts + [mine, first, second, both]


def on_device(h, p, q, b, m):
    block = h.shape
    rows, cols = block
    inv_cx = 3.0 / (rows * lax.axis_size("gx") / 4.0) ** 2
    inv_cy = 3.0 / (cols * lax.axis_size("gy") / 4.0) ** 2
    slabs_x = pack_x(h, p, q, b, m)
    near_x = cross(slabs_x, "gx", 1)
    near_y = cross(pack_y(h, p, q, b, m, after=slabs_x), "gy", 1)
    far_y = hand_on(jnp.pad(near_y[1], ((0, 5 * SUB), (0, 0))), "gy")
    hx, hy, ix, iy, tx, wx, ty, wy, coef_x, coef_y = prepare_depth(h, inv_cx, inv_cy)
    far_x = hand_on(second_of(near_x, coef_x), "gx")
    px, py, qx, qy, bx, by, mx, my = prepare_rest(p, q, b, m)
    depth_inner, push_inner, across_inner = fluxes_x_inner(hx, px, qx, bx, mx)
    mass_y, shear_y, normal_y = fluxes_y(near_y, far_y, hy, py, qy, by, my)
    depth_outer, across_outer, rx, sx, end_x = fluxes_x(
        near_x, far_x, hx, px, qx, bx, mx, ix, shear_y, push_inner, tx, wx, coef_x, inv_cx=inv_cx
    )
    depth, ry, sy, end_y, tall_y = join_y(
        depth_inner, across_inner, depth_outer, across_outer, mass_y, mx, normal_y, iy, my, ty, wy, coef_y, inv_cy=inv_cy
    )
    new_depth = write_depth(depth, block)
    parts_y = parts_of_line("gy", end_y, True, tall=tall_y if lax.axis_size("gy") == 4 else None)
    parts_x = parts_of_line("gx", end_x, False, parts_y[1:2])
    turned = [pltpu.VMEM((cols, LANES), F32)]
    vy = solve(solve_y_kernel, "solve_y", (iy, ry, ty, wy, sy), parts_y, block, inv_cy, turned)
    vx = solve(solve_x_kernel, "solve_x", (ix, rx, tx, wx, sx), parts_x, block, inv_cx)
    return new_depth, vx, vy


def solution(mesh):
    spec = P("gx", "gy")
    return jax.shard_map(
        on_device,
        mesh=mesh,
        in_specs=(spec,) * 5,
        out_specs=(spec,) * 3,
        check_vma=False,
    )
```

```python
import functools

import jax
import jax.numpy as jnp
from jax import lax
from jax.experimental import pallas as pl
from jax.experimental.pallas import tpu as pltpu
from jax.sharding import PartitionSpec as P

gravity = 9.81
ratio = 0.05
LANES = 128
SUB = 8
STEPS = LANES // SUB
F32 = jnp.float32
VMEM = pl.BlockSpec(memory_space=pltpu.VMEM)
HBM = pl.BlockSpec(memory_space=pltpu.HBM)
ANY = pl.BlockSpec(memory_space=pl.ANY)
PARAMS = pltpu.CompilerParams(vmem_limit_bytes=16 * 1024 * 1024)


def lane_index(shape):
    return lax.broadcasted_iota(jnp.int32, shape, len(shape) - 1)


def row_index(shape):
    return lax.broadcasted_iota(jnp.int32, shape, len(shape) - 2)


def at(tile, step):
    first = tile * LANES + step * SUB
    return slice(first, first + SUB)


def tile_span(tile):
    return slice(tile * LANES, (tile + 1) * LANES)


def spread_rows(tile, step):
    return pl.ds(tile * LANES + step, SUB, stride=STEPS)


def shape(*dims):
    return jax.ShapeDtypeStruct(dims, F32)


def pack_x_kernel(h, p, q, b, m, slabs, top, bottom, itop, ibottom, sems):
    rows = h.shape[0]
    copies = []
    for f, src in enumerate((h, p, q, b, m)):
        for side, (target, whole, row) in enumerate(((top, itop, 0), (bottom, ibottom, rows - SUB))):
            copy = pltpu.make_async_copy(
                src.at[pl.ds(row, SUB), :], target.at[f] if f < 4 else whole, sems.at[2 * f + side]
            )
            copy.start()
            copies.append(copy)
    for copy in copies:
        copy.wait()
    first = jnp.concatenate(
        [top[0, 0:2, :], top[1, 0:2, :], top[2, 0:2, :], top[3, 0:1, :], itop[0:1, :].astype(F32)]
    )
    last = jnp.concatenate(
        [
            bottom[0, SUB - 2 : SUB, :],
            bottom[1, SUB - 2 : SUB, :],
            bottom[2, SUB - 2 : SUB, :],
            bottom[3, SUB - 1 : SUB, :],
            ibottom[SUB - 1 : SUB, :].astype(F32),
        ]
    )
    even = lax.axis_index("gx") % 2 == 0
    slabs[0] = jnp.where(even, last, first)
    slabs[1] = jnp.where(even, first, last)


def pack_x(*fields):
    cols = fields[0].shape[1]
    return pl.pallas_call(
        pack_x_kernel,
        out_shape=shape(2, SUB, cols),
        in_specs=[HBM] * 5,
        out_specs=VMEM,
        scratch_shapes=[
            pltpu.VMEM((4, SUB, cols), F32),
            pltpu.VMEM((4, SUB, cols), F32),
            pltpu.VMEM((SUB, cols), jnp.int32),
            pltpu.VMEM((SUB, cols), jnp.int32),
            pltpu.SemaphoreType.DMA((10,)),
        ],
        compiler_params=PARAMS,
        name="pack_x",
    )(*[pltpu.with_memory_space_constraint(v, pltpu.HBM) for v in fields])


def pack_y_kernel(h, p, q, b, m, _, slabs, natural):
    rows, cols = h.shape
    lane = lane_index((rows, LANES))
    out = None
    for f, src in enumerate((h, p, q, b, m)):
        both = jnp.where(lane < LANES // 2, src[:, 0:LANES], src[:, cols - LANES : cols]).astype(F32)
        moved = pltpu.roll(both, 4 * f + 2, 1)
        out = moved if out is None else jnp.where(lane >= 4 * f, moved, out)
    natural[...] = out
    turned = jnp.concatenate([natural[spread_rows(0, k), :] for k in range(STEPS)]).T
    last = jnp.concatenate([turned[0:2], turned[4:6], turned[8:10], turned[13:14], turned[17:18]])
    first = jnp.concatenate([turned[2:4], turned[6:8], turned[10:12], turned[14:15], turned[18:19]])
    even = lax.axis_index("gy") % 2 == 0
    slabs[0] = jnp.where(even, last, first)
    slabs[1] = jnp.where(even, first, last)


def pack_y(*fields, after):
    rows = fields[0].shape[0]
    return pl.pallas_call(
        pack_y_kernel,
        out_shape=shape(2, SUB, rows),
        in_specs=[VMEM] * 6,
        out_specs=VMEM,
        scratch_shapes=[pltpu.VMEM((rows, LANES), F32)],
        compiler_params=PARAMS,
        cost_estimate=pl.CostEstimate(flops=500_000, bytes_accessed=1_000_000, transcendentals=0),
        name="pack_y",
    )(*fields, after)


def tie_kernel(both, _, out):
    out[...] = both[1]


def second_of(both, after):
    return pl.pallas_call(
        tie_kernel,
        out_shape=shape(*both.shape[1:]),
        in_specs=[VMEM, VMEM],
        out_specs=VMEM,
        compiler_params=PARAMS,
        name="second_of",
    )(both, after)


def merge_coefficients(one, two):
    t1, gl1, gr1 = one
    t2, gl2, gr2 = two
    shunt = gr1 + gl2
    inverse = 1.0 / (t1 + t2 + shunt)
    w1, w2 = t1 * inverse, t2 * inverse
    return (w1 * t2, gl1 + w1 * shunt, gr2 + w2 * shunt), (w1, w2, inverse)


def merge_sources(one, two, weights):
    w1, w2, inverse = weights
    source = one[1] - two[0]
    return (one[0] - w1 * source, two[1] + w2 * source), source * inverse


def merge(one, two):
    coefficients, weights = merge_coefficients(one[:3], two[:3])
    sources, middle = merge_sources(one[3:], two[3:], weights)
    return coefficients + sources, weights[:2] + (middle,)


def log2(count):
    return (count - 1).bit_length()


def full(ref, step):
    return jnp.concatenate([ref[at(tile, step), :] for tile in range(ref.shape[0] // LANES)])


def march_depth(inv_ref, scale, out_t, out_w, levels):
    count = inv_ref.shape[0] // STEPS
    zero = jnp.zeros((count, LANES), F32)
    alpha, gamma, beta, delta = zero, zero, zero, zero
    for k in range(STEPS):
        inverse = full(inv_ref, k)
        d = scale * (inverse * inverse)
        alpha = alpha + gamma
        gamma = gamma + d * (1.0 + alpha)
        beta = beta + delta
        delta = delta + d * ((k + 1.0) + beta)
    t = 1.0 / (STEPS + beta)
    out_t[0] = t
    out_t[1] = t * alpha
    out_t[2] = 1.0 + delta
    coefficients = (t, t * alpha, t * delta)
    for level in range(levels):
        after = tuple(pltpu.roll(v, count - (1 << level), 0) for v in coefficients)
        coefficients, weights = merge_coefficients(coefficients, after)
        for j, v in enumerate(weights):
            out_w[3 * level + j] = v
    return coefficients


def lay_out(src, xs, ys, natural, turned):
    for tile in range(xs.shape[0] // LANES):
        natural[tile_span(tile), :] = src[:, tile_span(tile)].astype(F32)
        for k in range(STEPS):
            xs[at(tile, k), :] = natural[spread_rows(tile, k), :]
        turned[tile_span(tile), :] = xs[tile_span(tile), :].T
        for k in range(STEPS):
            ys[at(tile, k), :] = turned[spread_rows(tile, k), :]


def prepare_depth_kernel(
    h, hx, hy, ix, iy, tx, wx, ty, wy, endx, endy, from_left, from_right, natural, turned, *, inv_cx, inv_cy
):
    tiles = hx.shape[0] // LANES
    lay_out(h, hx, hy, natural, turned)
    ix[...] = 1.0 / hx[...]
    iy[...] = 1.0 / hy[...]
    ends_x = march_depth(ix, inv_cx, tx, wx, log2(SUB))
    ends_y = march_depth(iy, inv_cy, ty, wy, log2(SUB * tiles))
    for i in range(3):
        for tile in range(tiles):
            first = (i * tiles + tile) * LANES
            endx[0:1, first : first + LANES] = ends_x[i][tile * SUB : tile * SUB + 1, :]
        endy[0:1, i * LANES : (i + 1) * LANES] = ends_y[i][0:1, :]
    one = jnp.ones((tiles * SUB, LANES), F32)
    zero = jnp.zeros_like(one)
    for out, left, right in ((from_left, one, zero), (from_right, zero, one)):

        def store(k, speed):
            for tile in range(tiles):
                out[at(tile, k), :] = speed[tile * SUB : (tile + 1) * SUB, :]

        left, right = segment_ends(left, right, wx, None, log2(SUB))
        march_values(left, right, tx, None, ix, inv_cx, None, store)


def prepare_depth(h, inv_cx, inv_cy):
    stack = (h.shape[1], LANES)
    count = stack[0] // STEPS
    shapes = [shape(*stack)] * 4 + [
        shape(3, count, LANES),
        shape(3 * log2(SUB), count, LANES),
        shape(3, count, LANES),
        shape(3 * log2(count), count, LANES),
        shape(1, 3 * stack[0]),
        shape(1, 3 * LANES),
        shape(*stack),
        shape(*stack),
    ]
    return pl.pallas_call(
        functools.partial(prepare_depth_kernel, inv_cx=inv_cx, inv_cy=inv_cy),
        out_shape=tuple(shapes),
        in_specs=[VMEM],
        out_specs=(VMEM,) * len(shapes),
        scratch_shapes=[pltpu.VMEM(stack, F32)] * 2,
        compiler_params=PARAMS,
        cost_estimate=pl.CostEstimate(flops=2_000_000, bytes_accessed=4_000_000, transcendentals=0),
        name="prepare_depth",
    )(h)


def prepare_rest_kernel(*refs):
    fields, outs, natural, turned = refs[:4], refs[4:12], refs[12], refs[13]
    for f, src in enumerate(fields):
        lay_out(src, outs[2 * f], outs[2 * f + 1], natural.at[f % 2], turned.at[f % 2])


def prepare_rest(*fields):
    stack = (fields[0].shape[1], LANES)
    return pl.pallas_call(
        prepare_rest_kernel,
        out_shape=(shape(*stack),) * 8,
        in_specs=[VMEM] * 4,
        out_specs=(VMEM,) * 8,
        scratch_shapes=[pltpu.VMEM((2, *stack), F32)] * 2,
        compiler_params=PARAMS,
        cost_estimate=pl.CostEstimate(flops=2_000_000, bytes_accessed=6_000_000, transcendentals=0),
        name="prepare_rest",
    )(*fields)


def low_high(axis, near, far):
    index, count = lax.axis_index(axis), lax.axis_size(axis)
    even = index % 2 == 0
    low = jnp.where(index > 0, jnp.where(even, far, near), 0.0)
    high = jnp.where(index < count - 1, jnp.where(even, near, far), 0.0)
    return low, high


def half_slope(a, c):
    return 0.5 * (jnp.maximum(jnp.minimum(a, c), 0.0) + jnp.minimum(jnp.maximum(a, c), 0.0))


def face_flux(left, right, opened):
    is_open = opened > 0.5
    hl = jnp.where(is_open, left[0], 1.0)
    hr = jnp.where(is_open, right[0], 1.0)
    joint = 1.0 / (hl * hr)
    ul = left[1] * (hr * joint)
    ur = right[1] * (hl * joint)
    gl = gravity * hl
    gr = gravity * hr
    fastest = jnp.maximum(jnp.abs(ul) + gl * lax.rsqrt(gl), jnp.abs(ur) + gr * lax.rsqrt(gr))
    scale = (0.5 * ratio) * opened
    mass = (left[1] + right[1]) - fastest * (right[0] - left[0])
    push = 0.5 * (gl * hl + gr * hr) + left[1] * ul + right[1] * ur - fastest * (right[1] - left[1])
    shear = left[2] * ul + right[2] * ur - fastest * (right[2] - left[2])
    return scale * mass, scale * push, scale * shear


def extended(ref, tile, lows, highs):
    sub = row_index((SUB, LANES))
    out = {}
    for n, row in enumerate(lows, 1):
        value = ref[at(tile, STEPS - n), :]
        out[-n] = jnp.where(sub == 0, row, pltpu.roll(value, 1, 0))
    for n, row in enumerate(highs):
        value = ref[at(tile, n), :]
        out[STEPS + n] = jnp.where(sub == SUB - 1, row, pltpu.roll(value, SUB - 1, 0))
    return lambda k: out[k] if k in out else ref[at(tile, k), :]


def tile_fluxes(fields, bed, wet, store, start=0, stop=STEPS):
    def states(k):
        both = []
        for w in fields:
            here = w(k)
            both.append((here, half_slope(here - w(k - 1), w(k + 1) - here)))
        return [w + s for w, s in both], [w - s for w, s in both]

    left, _ = states(start - 1)
    before = None
    for k in range(start - 1, stop):
        left_next, right = states(k + 1)
        face = face_flux(left, right, wet(k) * wet(k + 1))
        left = left_next
        if k >= start:
            store(k, [a - c for a, c in zip(face, before)], bed(k + 1) - bed(k - 1))
        before = face


def march_source(inv_ref, scale, r_ref, t_ref, w_ref, s_ref, levels):
    count = inv_ref.shape[0] // STEPS
    c = jnp.zeros((count, LANES), F32)
    e = c
    for k in range(STEPS):
        inverse = full(inv_ref, k)
        c = c + e
        e = e + (scale * (inverse * inverse) * c - full(r_ref, k))
    sl = t_ref[0] * c
    s_ref[0] = sl
    sources = (sl, t_ref[2] * sl - e)
    for level in range(levels):
        after = tuple(pltpu.roll(v, count - (1 << level), 0) for v in sources)
        sources, middle = merge_sources(sources, after, tuple(w_ref[3 * level + j] for j in range(3)))
        s_ref[1 + level] = middle
    return sources


def flux_y_kernel(near, far, hy, py, qy, by, my, mass, shear, normal, across, along):
    tiles = hy.shape[0] // LANES
    low, high = low_high("gy", near[0], far[0:SUB, :])
    for tile in range(tiles):

        def extend(ref, row, layers):
            lows, highs = [], []
            for n in range(layers):
                last = at(tile - 1, STEPS - 1 - n).stop - 1
                first = at(tile + 1, n).start
                lows.append(low[row + layers - 1 - n : row + layers - n, :] if tile == 0 else ref[last : last + 1, :])
                highs.append(high[row + n : row + n + 1, :] if tile == tiles - 1 else ref[first : first + 1, :])
            return extended(ref, tile, lows, highs)

        def store(k, difference, bed):
            here, natural = at(tile, k), spread_rows(tile, k)
            across[natural, :] = difference[0]
            along[natural, :] = difference[2]
            pull = (0.5 * ratio * gravity) * hy[here, :]
            normal[here, :] = qy[here, :] - difference[1] - pull * bed

        tile_fluxes([extend(hy, 0, 2), extend(qy, 4, 2), extend(py, 2, 2)], extend(by, 6, 1), extend(my, 7, 1), store)
        span = tile_span(tile)
        mass[span, :] = across[span, :].T
        shear[span, :] = along[span, :].T


def fluxes_y(*arrays):
    stack = arrays[2].shape
    return pl.pallas_call(
        flux_y_kernel,
        out_shape=(shape(*stack),) * 3,
        in_specs=[VMEM] * len(arrays),
        out_specs=(VMEM,) * 3,
        scratch_shapes=[pltpu.VMEM(stack, F32)] * 2,
        compiler_params=PARAMS,
        cost_estimate=pl.CostEstimate(flops=4_000_000, bytes_accessed=4_000_000, transcendentals=0),
        name="fluxes_y",
    )(*arrays)


INNER = (2, STEPS - 2)
TALL = 16


def x_store(hx, px, mx, depth, push, across):
    def of_tile(tile):
        def store(k, difference, bed):
            here = at(tile, k)
            h = hx[here, :]
            depth[here, :] = h - mx[here, :] * difference[0]
            push[here, :] = px[here, :] - difference[1] - (0.5 * ratio * gravity) * h * bed
            across[here, :] = difference[2]

        return store

    return of_tile


def flux_x_inner_kernel(hx, px, qx, bx, mx, depth, push, across):
    store = x_store(hx, px, mx, depth, push, across)
    for tile in range(hx.shape[0] // LANES):
        fields = [extended(v, tile, (), ()) for v in (hx, px, qx, bx, mx)]
        tile_fluxes(fields[:3], fields[3], fields[4], store(tile), *INNER)
        for k in (*range(INNER[0]), *range(INNER[1], STEPS)):
            for ref in (depth, push, across):
                ref[at(tile, k), :] = jnp.zeros((SUB, LANES), F32)


def fluxes_x_inner(*arrays):
    stack = arrays[0].shape
    return pl.pallas_call(
        flux_x_inner_kernel,
        out_shape=(shape(*stack),) * 3,
        in_specs=[VMEM] * len(arrays),
        out_specs=(VMEM,) * 3,
        compiler_params=PARAMS,
        cost_estimate=pl.CostEstimate(flops=4_000_000, bytes_accessed=4_000_000, transcendentals=0),
        name="fluxes_x_inner",
    )(*arrays)


def flux_x_kernel(
    near, far, hx, px, qx, bx, mx, ix, shear_y, push_in, tx, wx, coef,
    depth, across, rx, sx, ends,
    push,
    *, inv_cx,
):
    tiles = hx.shape[0] // LANES
    low, high = low_high("gx", near[0], far[...])
    store = x_store(hx, px, mx, depth, push, across)
    for tile in range(tiles):
        span = tile_span(tile)

        def extend(ref, row, layers):
            lows = [low[row + layers - 1 - n : row + layers - n, span] for n in range(layers)]
            highs = [high[row + n : row + n + 1, span] for n in range(layers)]
            return extended(ref, tile, lows, highs)

        fields, bed, wet = [extend(hx, 0, 2), extend(px, 2, 2), extend(qx, 4, 2)], extend(bx, 6, 1), extend(mx, 7, 1)
        tile_fluxes(fields, bed, wet, store(tile), 0, INNER[0])
        tile_fluxes(fields, bed, wet, store(tile), INNER[1], STEPS)
        for k in range(STEPS):
            here = at(tile, k)
            inverse = ix[here, :]
            total = (push_in if INNER[0] <= k < INNER[1] else push)[here, :] - shear_y[here, :]
            rx[here, :] = (inv_cx * (inverse * inverse)) * mx[here, :] * total
    sources = march_source(ix, inv_cx, rx, tx, wx, sx, log2(SUB))
    count = tiles * LANES
    ends[0:1, 0 : 3 * count] = coef[...]
    for i in range(2):
        for tile in range(tiles):
            first = (3 + i) * count + tile * LANES
            ends[0:1, first : first + LANES] = sources[i][tile * SUB : tile * SUB + 1, :]


def fluxes_x(*arrays, inv_cx):
    stack = arrays[2].shape
    count = stack[0] // STEPS
    shapes = (
        shape(*stack),
        shape(*stack),
        shape(*stack),
        shape(1 + log2(SUB), count, LANES),
        shape(1, 5 * stack[0]),
    )
    return pl.pallas_call(
        functools.partial(flux_x_kernel, inv_cx=inv_cx),
        out_shape=shapes,
        in_specs=[VMEM] * len(arrays),
        out_specs=(VMEM,) * len(shapes),
        scratch_shapes=[pltpu.VMEM(stack, F32)],
        compiler_params=PARAMS,
        name="fluxes_x",
    )(*arrays)


def join_y_kernel(
    depth_inner, across_inner, depth_outer, across_outer, mass_y, mx, normal_y, iy, my, ty, wy, coef,
    depth, ry, sy, ends, tall,
    across, turned,
    *, inv_cy,
):
    tiles = mx.shape[0] // LANES
    for tile in range(tiles):
        span = tile_span(tile)
        for k in range(STEPS):
            here = at(tile, k)
            inner = INNER[0] <= k < INNER[1]
            across[here, :] = (across_inner if inner else across_outer)[here, :]
            depth[here, :] = (depth_inner if inner else depth_outer)[here, :] - mx[here, :] * mass_y[here, :]
        turned[span, :] = across[span, :].T
        for k in range(STEPS):
            here = at(tile, k)
            inverse = iy[here, :]
            total = normal_y[here, :] - turned[spread_rows(tile, k), :]
            ry[here, :] = (inv_cy * (inverse * inverse)) * my[here, :] * total
    sources = march_source(iy, inv_cy, ry, ty, wy, sy, log2(SUB * tiles))
    ends[0:1, 0 : 3 * LANES] = coef[...]
    for i in range(2):
        ends[0:1, (3 + i) * LANES : (4 + i) * LANES] = sources[i][0:1, :]
    tall[...] = jnp.zeros_like(tall)
    tall[0:1, 0 : 5 * LANES] = ends[...]


def join_y(*arrays, inv_cy):
    stack = arrays[0].shape
    count = stack[0] // STEPS
    shapes = (
        shape(*stack),
        shape(*stack),
        shape(1 + log2(count), count, LANES),
        shape(1, 5 * LANES),
        shape(1, TALL * LANES),
    )
    return pl.pallas_call(
        functools.partial(join_y_kernel, inv_cy=inv_cy),
        out_shape=shapes,
        in_specs=[VMEM] * len(arrays),
        out_specs=(VMEM,) * len(shapes),
        scratch_shapes=[pltpu.VMEM(stack, F32)] * 2,
        compiler_params=PARAMS,
        cost_estimate=pl.CostEstimate(flops=2_000_000, bytes_accessed=2_000_000, transcendentals=0),
        name="join_y",
    )(*arrays)


def tile_write(tiled, whole, tile, sems):
    rows = whole.shape[0]
    return pltpu.make_async_copy(
        tiled.at[pl.ds(tile * rows, rows), :], whole.at[:, pl.ds(tile * LANES, LANES)], sems.at[tile]
    )


def write_scratch(cols):
    return [pltpu.VMEM((cols, LANES), F32), pltpu.SemaphoreType.DMA((cols // LANES,))]


def depth_kernel(depth, out, natural, sems):
    writes = []
    for tile in range(depth.shape[0] // LANES):
        for k in range(STEPS):
            natural[spread_rows(tile, k), :] = depth[at(tile, k), :]
        writes.append(tile_write(natural, out, tile, sems))
        writes[-1].start()
    for write in writes:
        write.wait()


def write_depth(depth, block):
    return pl.pallas_call(
        depth_kernel,
        out_shape=shape(*block),
        in_specs=[VMEM],
        out_specs=ANY,
        scratch_shapes=write_scratch(block[1]),
        compiler_params=PARAMS,
        cost_estimate=pl.CostEstimate(flops=100_000, bytes_accessed=2_000_000, transcendentals=0),
        name="write_depth",
    )(depth)


def rows_of(ref, count):
    return tuple(ref[0:1, i * count : (i + 1) * count] for i in range(5))


def ordered(axis, stage, mine, theirs):
    is_low = (lax.axis_index(axis) >> stage) % 2 == 0
    one = tuple(jnp.where(is_low, a, b) for a, b in zip(mine, theirs))
    two = tuple(jnp.where(is_low, b, a) for a, b in zip(mine, theirs))
    return is_low, merge(one, two)


def merge_kernel(mine, theirs, *refs, axis, stage):
    out = refs[-1]
    count = mine.shape[1] // 5
    _, (merged, _) = ordered(axis, stage, rows_of(mine, count), rows_of(theirs, count))
    for i, v in enumerate(merged):
        out[0:1, i * v.shape[1] : (i + 1) * v.shape[1]] = v


def merge_call(axis, stage, mine, theirs, beside):
    return pl.pallas_call(
        functools.partial(merge_kernel, axis=axis, stage=stage),
        out_shape=shape(*mine.shape),
        in_specs=[VMEM] * (2 + len(beside)),
        out_specs=VMEM,
        compiler_params=PARAMS,
        name="merge",
    )(mine, theirs, *beside)


def line_ends(axis, refs):
    steps = []
    parts = [rows_of(ref, refs[0].shape[1] // 5) for ref in refs]
    stage = 0
    while len(parts) > 4:
        is_low, (_, weights) = ordered(axis, stage, *parts[:2])
        steps.append((is_low, weights))
        parts = parts[2:]
        stage += 1
    is_low, (own, weights) = ordered(axis, stage, *parts[:2])
    steps.append((is_low, weights))
    _, (other, _) = ordered(axis, stage, *parts[2:])
    is_low, (whole, weights) = ordered(axis, stage + 1, own, other)
    steps.append((is_low, weights))
    t, _, gr, _, sr = whole
    left = jnp.zeros_like(t)
    right = sr / (t + gr + 1.0)
    for is_low, (w1, w2, source) in reversed(steps):
        middle = w1 * left + w2 * right + source
        left = jnp.where(is_low, left, middle)
        right = jnp.where(is_low, middle, right)
    return left, right


def segment_ends(left, right, w_ref, s_ref, levels):
    index = row_index(left.shape)
    for level in reversed(range(levels)):
        stride = 1 << level
        middle = w_ref[3 * level] * left + w_ref[3 * level + 1] * right
        if s_ref is not None:
            middle = middle + s_ref[1 + level]
        upper = (index >> level) % 2 == 1
        left, right = (
            jnp.where(upper, pltpu.roll(middle, stride, 0), left),
            jnp.where(upper, pltpu.roll(right, stride, 0), middle),
        )
    return left, right


def march_values(left, right, t_ref, s_ref, inv_ref, scale, r_ref, store):
    value = left
    change = t_ref[0] * (right - left) - t_ref[1] * left
    if s_ref is not None:
        change = change - s_ref[0]
    for k in range(STEPS):
        inverse = full(inv_ref, k)
        value = value + change
        push = scale * (inverse * inverse) * value
        change = change + (push if r_ref is None else push - full(r_ref, k))
        store(k, value * inverse)


def rest_x_kernel(inv_ref, r_ref, t_ref, w_ref, s_ref, out, *, scale):
    tiles = out.shape[0] // LANES
    zero = jnp.zeros((tiles * SUB, LANES), F32)

    def store(k, speed):
        for tile in range(tiles):
            out[at(tile, k), :] = speed[tile * SUB : (tile + 1) * SUB, :]

    left, right = segment_ends(zero, zero, w_ref, s_ref, log2(SUB))
    march_values(left, right, t_ref, s_ref, inv_ref, scale, r_ref, store)


def rest_x(*pieces, scale):
    return pl.pallas_call(
        functools.partial(rest_x_kernel, scale=scale),
        out_shape=shape(*pieces[0].shape),
        in_specs=[VMEM] * len(pieces),
        out_specs=VMEM,
        compiler_params=PARAMS,
        cost_estimate=pl.CostEstimate(flops=1_000_000, bytes_accessed=2_000_000, transcendentals=0),
        name="rest_x",
    )(*pieces)


def solve_x_kernel(from_left, from_right, rest, *refs):
    parts, (out, natural, sems) = refs[:-3], refs[-3:]
    left, right = line_ends("gx", parts)
    writes = []
    for tile in range(out.shape[1] // LANES):
        span = tile_span(tile)
        for k in range(STEPS):
            here = at(tile, k)
            natural[spread_rows(tile, k), :] = (
                from_left[here, :] * left[:, span] + from_right[here, :] * right[:, span] + rest[here, :]
            )
        writes.append(tile_write(natural, out, tile, sems))
        writes[-1].start()
    for write in writes:
        write.wait()


def solve_y_kernel(inv_ref, r_ref, t_ref, w_ref, s_ref, *refs, scale):
    parts, (out, natural, sems, turned) = refs[:-4], refs[-4:]
    tiles = out.shape[1] // LANES
    ends = line_ends("gy", parts)
    ends = [jnp.broadcast_to(row, (tiles * SUB, LANES)) for row in ends]
    left, right = segment_ends(*ends, w_ref, s_ref, log2(tiles * SUB))

    def store(k, speed):
        for tile in range(tiles):
            turned[spread_rows(tile, k), :] = speed[tile * SUB : (tile + 1) * SUB, :]

    march_values(left, right, t_ref, s_ref, inv_ref, scale, r_ref, store)
    writes = []
    for tile in range(tiles):
        block = turned[tile_span(tile), :].T
        for k in range(STEPS):
            natural[spread_rows(tile, k), :] = block[k * SUB : (k + 1) * SUB, :]
        writes.append(tile_write(natural, out, tile, sems))
        writes[-1].start()
    for write in writes:
        write.wait()


def solve(kernel, name, pieces, parts, block, extra=()):
    return pl.pallas_call(
        kernel,
        out_shape=shape(*block),
        in_specs=[VMEM] * (len(pieces) + len(parts)),
        out_specs=ANY,
        scratch_shapes=write_scratch(block[1]) + list(extra),
        compiler_params=PARAMS,
        cost_estimate=pl.CostEstimate(flops=1_000_000, bytes_accessed=4_000_000, transcendentals=0),
        name=name,
    )(*pieces, *parts)


def hand_on(value, axis):
    count = lax.axis_size(axis)
    far = [i + 2 if i % 2 == 0 else i - 2 for i in range(count)]
    return lax.ppermute(value, axis, [(i, t if 0 <= t < count else i ^ 1) for i, t in enumerate(far)])


def cross(value, axis, mask):
    return lax.ppermute(value, axis, [(i, i ^ mask) for i in range(lax.axis_size(axis))])


def parts_of_line(axis, mine, relay, beside=(), tall=None):
    parts = []
    last = log2(lax.axis_size(axis)) - 2
    for stage in range(last):
        theirs = cross(mine, axis, 1 << stage)
        parts += [mine, theirs]
        mine = merge_call(axis, stage, mine, theirs, beside)
    if relay:
        first = cross(mine, axis, 1 << last)
        second = cross(mine if tall is None else tall, axis, 2 << last)
        both = cross(second[:, 0 : mine.shape[1]], axis, 1 << last)
    else:
        first, second, both = (cross(mine, axis, n << last) for n in (1, 2, 3))
    return parts + [mine, first, second, both]


def on_device(h, p, q, b, m):
    block = h.shape
    rows, cols = block
    inv_cx = 3.0 / (rows * lax.axis_size("gx") / 4.0) ** 2
    inv_cy = 3.0 / (cols * lax.axis_size("gy") / 4.0) ** 2
    slabs_x = pack_x(h, p, q, b, m)
    near_x = cross(slabs_x, "gx", 1)
    near_y = cross(pack_y(h, p, q, b, m, after=slabs_x), "gy", 1)
    far_y = hand_on(jnp.pad(near_y[1], ((0, 5 * SUB), (0, 0))), "gy")
    hx, hy, ix, iy, tx, wx, ty, wy, coef_x, coef_y, left_x, right_x = prepare_depth(h, inv_cx, inv_cy)
    far_x = hand_on(second_of(near_x, coef_x), "gx")
    px, py, qx, qy, bx, by, mx, my = prepare_rest(p, q, b, m)
    depth_inner, push_inner, across_inner = fluxes_x_inner(hx, px, qx, bx, mx)
    mass_y, shear_y, normal_y = fluxes_y(near_y, far_y, hy, py, qy, by, my)
    depth_outer, across_outer, rx, sx, end_x = fluxes_x(
        near_x, far_x, hx, px, qx, bx, mx, ix, shear_y, push_inner, tx, wx, coef_x, inv_cx=inv_cx
    )
    depth, ry, sy, end_y, tall_y = join_y(
        depth_inner, across_inner, depth_outer, across_outer, mass_y, mx, normal_y, iy, my, ty, wy, coef_y, inv_cy=inv_cy
    )
    new_depth = write_depth(depth, block)
    parts_y = parts_of_line("gy", end_y, True, tall=tall_y if lax.axis_size("gy") == 4 else None)
    parts_x = parts_of_line("gx", end_x, False, parts_y[1:2])
    turned = [pltpu.VMEM((cols, LANES), F32)]
    solve_y_scaled = functools.partial(solve_y_kernel, scale=inv_cy)
    vy = solve(solve_y_scaled, "solve_y", (iy, ry, ty, wy, sy), parts_y, block, turned)
    own_x = rest_x(ix, rx, tx, wx, sx, scale=inv_cx)
    vx = solve(solve_x_kernel, "solve_x", (left_x, right_x, own_x), parts_x, block)
    return new_depth, vx, vy


def solution(mesh):
    spec = P("gx", "gy")
    return jax.shard_map(
        on_device,
        mesh=mesh,
        in_specs=(spec,) * 5,
        out_specs=(spec,) * 3,
        check_vma=False,
    )
```

```python
import functools

import jax
import jax.numpy as jnp
from jax import lax
from jax.experimental import pallas as pl
from jax.experimental.pallas import tpu as pltpu
from jax.sharding import PartitionSpec as P

gravity = 9.81
ratio = 0.05
LANES = 128
SUB = 8
STEPS = LANES // SUB
F32 = jnp.float32
VMEM = pl.BlockSpec(memory_space=pltpu.VMEM)
HBM = pl.BlockSpec(memory_space=pltpu.HBM)
ANY = pl.BlockSpec(memory_space=pl.ANY)
PARAMS = pltpu.CompilerParams(vmem_limit_bytes=16 * 1024 * 1024)


def lane_index(shape):
    return lax.broadcasted_iota(jnp.int32, shape, len(shape) - 1)


def row_index(shape):
    return lax.broadcasted_iota(jnp.int32, shape, len(shape) - 2)


def at(tile, step):
    first = tile * LANES + step * SUB
    return slice(first, first + SUB)


def tile_span(tile):
    return slice(tile * LANES, (tile + 1) * LANES)


def spread_rows(tile, step):
    return pl.ds(tile * LANES + step, SUB, stride=STEPS)


def shape(*dims):
    return jax.ShapeDtypeStruct(dims, F32)


def pack_x_kernel(h, p, q, b, m, near, outer, top, bottom, itop, ibottom, sems):
    rows = h.shape[0]
    copies = []
    for f, src in enumerate((h, p, q, b, m)):
        for side, (target, whole, row) in enumerate(((top, itop, 0), (bottom, ibottom, rows - SUB))):
            copy = pltpu.make_async_copy(
                src.at[pl.ds(row, SUB), :], target.at[f] if f < 4 else whole, sems.at[2 * f + side]
            )
            copy.start()
            copies.append(copy)
    for copy in copies:
        copy.wait()
    first = jnp.concatenate(
        [top[0, 0:2, :], top[1, 0:2, :], top[2, 0:2, :], top[3, 0:1, :], itop[0:1, :].astype(F32)]
    )
    last = jnp.concatenate(
        [
            bottom[0, SUB - 2 : SUB, :],
            bottom[1, SUB - 2 : SUB, :],
            bottom[2, SUB - 2 : SUB, :],
            bottom[3, SUB - 1 : SUB, :],
            ibottom[SUB - 1 : SUB, :].astype(F32),
        ]
    )
    even = lax.axis_index("gx") % 2 == 0
    near[...] = jnp.where(even, last, first)
    outer[...] = jnp.where(even, first, last)


def pack_x(*fields):
    cols = fields[0].shape[1]
    return pl.pallas_call(
        pack_x_kernel,
        out_shape=(shape(SUB, cols), shape(SUB, cols)),
        in_specs=[HBM] * 5,
        out_specs=(VMEM, VMEM),
        scratch_shapes=[
            pltpu.VMEM((4, SUB, cols), F32),
            pltpu.VMEM((4, SUB, cols), F32),
            pltpu.VMEM((SUB, cols), jnp.int32),
            pltpu.VMEM((SUB, cols), jnp.int32),
            pltpu.SemaphoreType.DMA((10,)),
        ],
        compiler_params=PARAMS,
        name="pack_x",
    )(*[pltpu.with_memory_space_constraint(v, pltpu.HBM) for v in fields])


def pack_y_kernel(h, p, q, b, m, _, slabs, natural):
    rows, cols = h.shape
    lane = lane_index((rows, LANES))
    out = None
    for f, src in enumerate((h, p, q, b, m)):
        both = jnp.where(lane < LANES // 2, src[:, 0:LANES], src[:, cols - LANES : cols]).astype(F32)
        moved = pltpu.roll(both, 4 * f + 2, 1)
        out = moved if out is None else jnp.where(lane >= 4 * f, moved, out)
    natural[...] = out
    turned = jnp.concatenate([natural[spread_rows(0, k), :] for k in range(STEPS)]).T
    last = jnp.concatenate([turned[0:2], turned[4:6], turned[8:10], turned[13:14], turned[17:18]])
    first = jnp.concatenate([turned[2:4], turned[6:8], turned[10:12], turned[14:15], turned[18:19]])
    even = lax.axis_index("gy") % 2 == 0
    slabs[0] = jnp.where(even, last, first)
    slabs[1] = jnp.where(even, first, last)


def pack_y(*fields, after):
    rows = fields[0].shape[0]
    return pl.pallas_call(
        pack_y_kernel,
        out_shape=shape(2, SUB, rows),
        in_specs=[VMEM] * 6,
        out_specs=VMEM,
        scratch_shapes=[pltpu.VMEM((rows, LANES), F32)],
        compiler_params=PARAMS,
        cost_estimate=pl.CostEstimate(flops=500_000, bytes_accessed=1_000_000, transcendentals=0),
        name="pack_y",
    )(*fields, after)


def tie_kernel(value, _, out):
    out[...] = value[...]


def once(value, after):
    return pl.pallas_call(
        tie_kernel,
        out_shape=shape(*value.shape),
        in_specs=[VMEM, VMEM],
        out_specs=VMEM,
        compiler_params=PARAMS,
        name="once",
    )(value, after)


def merge_coefficients(one, two):
    t1, gl1, gr1 = one
    t2, gl2, gr2 = two
    shunt = gr1 + gl2
    inverse = 1.0 / (t1 + t2 + shunt)
    w1, w2 = t1 * inverse, t2 * inverse
    return (w1 * t2, gl1 + w1 * shunt, gr2 + w2 * shunt), (w1, w2, inverse)


def merge_sources(one, two, weights):
    w1, w2, inverse = weights
    source = one[1] - two[0]
    return (one[0] - w1 * source, two[1] + w2 * source), source * inverse


def merge(one, two):
    coefficients, weights = merge_coefficients(one[:3], two[:3])
    sources, middle = merge_sources(one[3:], two[3:], weights)
    return coefficients + sources, weights[:2] + (middle,)


def log2(count):
    return (count - 1).bit_length()


def full(ref, step):
    return jnp.concatenate([ref[at(tile, step), :] for tile in range(ref.shape[0] // LANES)])


def march_depth(inv_ref, scale, out_t, out_w, levels):
    count = inv_ref.shape[0] // STEPS
    zero = jnp.zeros((count, LANES), F32)
    alpha, gamma, beta, delta = zero, zero, zero, zero
    for k in range(STEPS):
        inverse = full(inv_ref, k)
        d = scale * (inverse * inverse)
        alpha = alpha + gamma
        gamma = gamma + d * (1.0 + alpha)
        beta = beta + delta
        delta = delta + d * ((k + 1.0) + beta)
    t = 1.0 / (STEPS + beta)
    out_t[0] = t
    out_t[1] = t * alpha
    out_t[2] = 1.0 + delta
    coefficients = (t, t * alpha, t * delta)
    for level in range(levels):
        after = tuple(pltpu.roll(v, count - (1 << level), 0) for v in coefficients)
        coefficients, weights = merge_coefficients(coefficients, after)
        for j, v in enumerate(weights):
            out_w[3 * level + j] = v
    return coefficients


def lay_out(src, xs, ys, natural, turned):
    for tile in range(xs.shape[0] // LANES):
        natural[tile_span(tile), :] = src[:, tile_span(tile)].astype(F32)
        for k in range(STEPS):
            xs[at(tile, k), :] = natural[spread_rows(tile, k), :]
        turned[tile_span(tile), :] = xs[tile_span(tile), :].T
        for k in range(STEPS):
            ys[at(tile, k), :] = turned[spread_rows(tile, k), :]


def prepare_depth_kernel(
    h, hx, hy, ix, iy, tx, wx, ty, wy, endx, endy, from_left, from_right, natural, turned, *, inv_cx, inv_cy
):
    tiles = hx.shape[0] // LANES
    lay_out(h, hx, hy, natural, turned)
    ix[...] = 1.0 / hx[...]
    iy[...] = 1.0 / hy[...]
    ends_x = march_depth(ix, inv_cx, tx, wx, log2(SUB))
    ends_y = march_depth(iy, inv_cy, ty, wy, log2(SUB * tiles))
    for i in range(3):
        for tile in range(tiles):
            first = (i * tiles + tile) * LANES
            endx[0:1, first : first + LANES] = ends_x[i][tile * SUB : tile * SUB + 1, :]
        endy[0:1, i * LANES : (i + 1) * LANES] = ends_y[i][0:1, :]
    one = jnp.ones((tiles * SUB, LANES), F32)
    zero = jnp.zeros_like(one)
    for out, left, right in ((from_left, one, zero), (from_right, zero, one)):

        def store(k, speed):
            for tile in range(tiles):
                out[at(tile, k), :] = speed[tile * SUB : (tile + 1) * SUB, :]

        left, right = segment_ends(left, right, wx, None, log2(SUB))
        march_values(left, right, tx, None, ix, inv_cx, None, store)


def prepare_depth(h, inv_cx, inv_cy):
    stack = (h.shape[1], LANES)
    count = stack[0] // STEPS
    shapes = [shape(*stack)] * 4 + [
        shape(3, count, LANES),
        shape(3 * log2(SUB), count, LANES),
        shape(3, count, LANES),
        shape(3 * log2(count), count, LANES),
        shape(1, 3 * stack[0]),
        shape(1, 3 * LANES),
        shape(*stack),
        shape(*stack),
    ]
    return pl.pallas_call(
        functools.partial(prepare_depth_kernel, inv_cx=inv_cx, inv_cy=inv_cy),
        out_shape=tuple(shapes),
        in_specs=[VMEM],
        out_specs=(VMEM,) * len(shapes),
        scratch_shapes=[pltpu.VMEM(stack, F32)] * 2,
        compiler_params=PARAMS,
        cost_estimate=pl.CostEstimate(flops=2_000_000, bytes_accessed=4_000_000, transcendentals=0),
        name="prepare_depth",
    )(h)


def prepare_rest_kernel(*refs):
    fields, outs, natural, turned = refs[:4], refs[4:12], refs[12], refs[13]
    for f, src in enumerate(fields):
        lay_out(src, outs[2 * f], outs[2 * f + 1], natural.at[f % 2], turned.at[f % 2])


def prepare_rest(*fields):
    stack = (fields[0].shape[1], LANES)
    return pl.pallas_call(
        prepare_rest_kernel,
        out_shape=(shape(*stack),) * 8,
        in_specs=[VMEM] * 4,
        out_specs=(VMEM,) * 8,
        scratch_shapes=[pltpu.VMEM((2, *stack), F32)] * 2,
        compiler_params=PARAMS,
        cost_estimate=pl.CostEstimate(flops=2_000_000, bytes_accessed=6_000_000, transcendentals=0),
        name="prepare_rest",
    )(*fields)


def low_high(axis, near, far):
    index, count = lax.axis_index(axis), lax.axis_size(axis)
    even = index % 2 == 0
    low = jnp.where(index > 0, jnp.where(even, far, near), 0.0)
    high = jnp.where(index < count - 1, jnp.where(even, near, far), 0.0)
    return low, high


def half_slope(a, c):
    return 0.5 * (jnp.maximum(jnp.minimum(a, c), 0.0) + jnp.minimum(jnp.maximum(a, c), 0.0))


def face_flux(left, right, opened):
    is_open = opened > 0.5
    hl = jnp.where(is_open, left[0], 1.0)
    hr = jnp.where(is_open, right[0], 1.0)
    joint = 1.0 / (hl * hr)
    ul = left[1] * (hr * joint)
    ur = right[1] * (hl * joint)
    gl = gravity * hl
    gr = gravity * hr
    fastest = jnp.maximum(jnp.abs(ul) + gl * lax.rsqrt(gl), jnp.abs(ur) + gr * lax.rsqrt(gr))
    scale = (0.5 * ratio) * opened
    mass = (left[1] + right[1]) - fastest * (right[0] - left[0])
    push = 0.5 * (gl * hl + gr * hr) + left[1] * ul + right[1] * ur - fastest * (right[1] - left[1])
    shear = left[2] * ul + right[2] * ur - fastest * (right[2] - left[2])
    return scale * mass, scale * push, scale * shear


def extended(ref, tile, lows, highs):
    sub = row_index((SUB, LANES))
    out = {}
    for n, row in enumerate(lows, 1):
        value = ref[at(tile, STEPS - n), :]
        out[-n] = jnp.where(sub == 0, row, pltpu.roll(value, 1, 0))
    for n, row in enumerate(highs):
        value = ref[at(tile, n), :]
        out[STEPS + n] = jnp.where(sub == SUB - 1, row, pltpu.roll(value, SUB - 1, 0))
    return lambda k: out[k] if k in out else ref[at(tile, k), :]


def tile_fluxes(fields, bed, wet, store, start=0, stop=STEPS):
    def states(k):
        both = []
        for w in fields:
            here = w(k)
            both.append((here, half_slope(here - w(k - 1), w(k + 1) - here)))
        return [w + s for w, s in both], [w - s for w, s in both]

    left, _ = states(start - 1)
    before = None
    for k in range(start - 1, stop):
        left_next, right = states(k + 1)
        face = face_flux(left, right, wet(k) * wet(k + 1))
        left = left_next
        if k >= start:
            store(k, [a - c for a, c in zip(face, before)], bed(k + 1) - bed(k - 1))
        before = face


def march_source(inv_ref, scale, r_ref, t_ref, w_ref, s_ref, levels):
    count = inv_ref.shape[0] // STEPS
    c = jnp.zeros((count, LANES), F32)
    e = c
    for k in range(STEPS):
        inverse = full(inv_ref, k)
        c = c + e
        e = e + (scale * (inverse * inverse) * c - full(r_ref, k))
    sl = t_ref[0] * c
    s_ref[0] = sl
    sources = (sl, t_ref[2] * sl - e)
    for level in range(levels):
        after = tuple(pltpu.roll(v, count - (1 << level), 0) for v in sources)
        sources, middle = merge_sources(sources, after, tuple(w_ref[3 * level + j] for j in range(3)))
        s_ref[1 + level] = middle
    return sources


def flux_y_kernel(near, far, hy, py, qy, by, my, mass, shear, normal, across, along):
    tiles = hy.shape[0] // LANES
    low, high = low_high("gy", near[0], far[0:SUB, :])
    for tile in range(tiles):

        def extend(ref, row, layers):
            lows, highs = [], []
            for n in range(layers):
                last = at(tile - 1, STEPS - 1 - n).stop - 1
                first = at(tile + 1, n).start
                lows.append(low[row + layers - 1 - n : row + layers - n, :] if tile == 0 else ref[last : last + 1, :])
                highs.append(high[row + n : row + n + 1, :] if tile == tiles - 1 else ref[first : first + 1, :])
            return extended(ref, tile, lows, highs)

        def store(k, difference, bed):
            here, natural = at(tile, k), spread_rows(tile, k)
            across[natural, :] = difference[0]
            along[natural, :] = difference[2]
            pull = (0.5 * ratio * gravity) * hy[here, :]
            normal[here, :] = qy[here, :] - difference[1] - pull * bed

        tile_fluxes([extend(hy, 0, 2), extend(qy, 4, 2), extend(py, 2, 2)], extend(by, 6, 1), extend(my, 7, 1), store)
        span = tile_span(tile)
        mass[span, :] = across[span, :].T
        shear[span, :] = along[span, :].T


def fluxes_y(*arrays):
    stack = arrays[2].shape
    return pl.pallas_call(
        flux_y_kernel,
        out_shape=(shape(*stack),) * 3,
        in_specs=[VMEM] * len(arrays),
        out_specs=(VMEM,) * 3,
        scratch_shapes=[pltpu.VMEM(stack, F32)] * 2,
        compiler_params=PARAMS,
        cost_estimate=pl.CostEstimate(flops=4_000_000, bytes_accessed=4_000_000, transcendentals=0),
        name="fluxes_y",
    )(*arrays)


INNER = (2, STEPS - 2)
TALL = 16


def x_store(hx, px, mx, depth, push, across):
    def of_tile(tile):
        def store(k, difference, bed):
            here = at(tile, k)
            h = hx[here, :]
            depth[here, :] = h - mx[here, :] * difference[0]
            push[here, :] = px[here, :] - difference[1] - (0.5 * ratio * gravity) * h * bed
            across[here, :] = difference[2]

        return store

    return of_tile


def flux_x_inner_kernel(hx, px, qx, bx, mx, depth, push, across):
    store = x_store(hx, px, mx, depth, push, across)
    for tile in range(hx.shape[0] // LANES):
        fields = [extended(v, tile, (), ()) for v in (hx, px, qx, bx, mx)]
        tile_fluxes(fields[:3], fields[3], fields[4], store(tile), *INNER)
        for k in (*range(INNER[0]), *range(INNER[1], STEPS)):
            for ref in (depth, push, across):
                ref[at(tile, k), :] = jnp.zeros((SUB, LANES), F32)


def fluxes_x_inner(*arrays):
    stack = arrays[0].shape
    return pl.pallas_call(
        flux_x_inner_kernel,
        out_shape=(shape(*stack),) * 3,
        in_specs=[VMEM] * len(arrays),
        out_specs=(VMEM,) * 3,
        compiler_params=PARAMS,
        cost_estimate=pl.CostEstimate(flops=4_000_000, bytes_accessed=4_000_000, transcendentals=0),
        name="fluxes_x_inner",
    )(*arrays)


def flux_x_kernel(
    near, far, hx, px, qx, bx, mx, ix, shear_y, push_in, tx, wx, coef,
    depth, across, rx, sx, ends,
    push,
    *, inv_cx,
):
    tiles = hx.shape[0] // LANES
    low, high = low_high("gx", near[...], far[...])
    store = x_store(hx, px, mx, depth, push, across)
    for tile in range(tiles):
        span = tile_span(tile)

        def extend(ref, row, layers):
            lows = [low[row + layers - 1 - n : row + layers - n, span] for n in range(layers)]
            highs = [high[row + n : row + n + 1, span] for n in range(layers)]
            return extended(ref, tile, lows, highs)

        fields, bed, wet = [extend(hx, 0, 2), extend(px, 2, 2), extend(qx, 4, 2)], extend(bx, 6, 1), extend(mx, 7, 1)
        tile_fluxes(fields, bed, wet, store(tile), 0, INNER[0])
        tile_fluxes(fields, bed, wet, store(tile), INNER[1], STEPS)
        for k in range(STEPS):
            here = at(tile, k)
            inverse = ix[here, :]
            total = (push_in if INNER[0] <= k < INNER[1] else push)[here, :] - shear_y[here, :]
            rx[here, :] = (inv_cx * (inverse * inverse)) * mx[here, :] * total
    sources = march_source(ix, inv_cx, rx, tx, wx, sx, log2(SUB))
    count = tiles * LANES
    ends[0:1, 0 : 3 * count] = coef[...]
    for i in range(2):
        for tile in range(tiles):
            first = (3 + i) * count + tile * LANES
            ends[0:1, first : first + LANES] = sources[i][tile * SUB : tile * SUB + 1, :]


def fluxes_x(*arrays, inv_cx):
    stack = arrays[2].shape
    count = stack[0] // STEPS
    shapes = (
        shape(*stack),
        shape(*stack),
        shape(*stack),
        shape(1 + log2(SUB), count, LANES),
        shape(1, 5 * stack[0]),
    )
    return pl.pallas_call(
        functools.partial(flux_x_kernel, inv_cx=inv_cx),
        out_shape=shapes,
        in_specs=[VMEM] * len(arrays),
        out_specs=(VMEM,) * len(shapes),
        scratch_shapes=[pltpu.VMEM(stack, F32)],
        compiler_params=PARAMS,
        name="fluxes_x",
    )(*arrays)


def join_y_kernel(
    depth_inner, across_inner, depth_outer, across_outer, mass_y, mx, normal_y, iy, my, ty, wy, coef,
    depth, ry, sy, ends, tall,
    across, turned,
    *, inv_cy,
):
    tiles = mx.shape[0] // LANES
    for tile in range(tiles):
        span = tile_span(tile)
        for k in range(STEPS):
            here = at(tile, k)
            inner = INNER[0] <= k < INNER[1]
            across[here, :] = (across_inner if inner else across_outer)[here, :]
            depth[here, :] = (depth_inner if inner else depth_outer)[here, :] - mx[here, :] * mass_y[here, :]
        turned[span, :] = across[span, :].T
        for k in range(STEPS):
            here = at(tile, k)
            inverse = iy[here, :]
            total = normal_y[here, :] - turned[spread_rows(tile, k), :]
            ry[here, :] = (inv_cy * (inverse * inverse)) * my[here, :] * total
    sources = march_source(iy, inv_cy, ry, ty, wy, sy, log2(SUB * tiles))
    ends[0:1, 0 : 3 * LANES] = coef[...]
    for i in range(2):
        ends[0:1, (3 + i) * LANES : (4 + i) * LANES] = sources[i][0:1, :]
    tall[...] = jnp.zeros_like(tall)
    tall[0:1, 0 : 5 * LANES] = ends[...]


def join_y(*arrays, inv_cy):
    stack = arrays[0].shape
    count = stack[0] // STEPS
    shapes = (
        shape(*stack),
        shape(*stack),
        shape(1 + log2(count), count, LANES),
        shape(1, 5 * LANES),
        shape(1, TALL * LANES),
    )
    return pl.pallas_call(
        functools.partial(join_y_kernel, inv_cy=inv_cy),
        out_shape=shapes,
        in_specs=[VMEM] * len(arrays),
        out_specs=(VMEM,) * len(shapes),
        scratch_shapes=[pltpu.VMEM(stack, F32)] * 2,
        compiler_params=PARAMS,
        cost_estimate=pl.CostEstimate(flops=2_000_000, bytes_accessed=2_000_000, transcendentals=0),
        name="join_y",
    )(*arrays)


def tile_write(tiled, whole, tile, sems):
    rows = whole.shape[0]
    return pltpu.make_async_copy(
        tiled.at[pl.ds(tile * rows, rows), :], whole.at[:, pl.ds(tile * LANES, LANES)], sems.at[tile]
    )


def write_scratch(cols):
    return [pltpu.VMEM((cols, LANES), F32), pltpu.SemaphoreType.DMA((cols // LANES,))]


def depth_kernel(depth, out, natural, sems):
    writes = []
    for tile in range(depth.shape[0] // LANES):
        for k in range(STEPS):
            natural[spread_rows(tile, k), :] = depth[at(tile, k), :]
        writes.append(tile_write(natural, out, tile, sems))
        writes[-1].start()
    for write in writes:
        write.wait()


def write_depth(depth, block):
    return pl.pallas_call(
        depth_kernel,
        out_shape=shape(*block),
        in_specs=[VMEM],
        out_specs=ANY,
        scratch_shapes=write_scratch(block[1]),
        compiler_params=PARAMS,
        cost_estimate=pl.CostEstimate(flops=100_000, bytes_accessed=2_000_000, transcendentals=0),
        name="write_depth",
    )(depth)


def rows_of(ref, count):
    return tuple(ref[0:1, i * count : (i + 1) * count] for i in range(5))


def ordered(axis, stage, mine, theirs):
    is_low = (lax.axis_index(axis) >> stage) % 2 == 0
    one = tuple(jnp.where(is_low, a, b) for a, b in zip(mine, theirs))
    two = tuple(jnp.where(is_low, b, a) for a, b in zip(mine, theirs))
    return is_low, merge(one, two)


def merge_kernel(mine, theirs, *refs, axis, stage):
    out = refs[-1]
    count = mine.shape[1] // 5
    _, (merged, _) = ordered(axis, stage, rows_of(mine, count), rows_of(theirs, count))
    for i, v in enumerate(merged):
        out[0:1, i * v.shape[1] : (i + 1) * v.shape[1]] = v


def merge_call(axis, stage, mine, theirs, beside):
    return pl.pallas_call(
        functools.partial(merge_kernel, axis=axis, stage=stage),
        out_shape=shape(*mine.shape),
        in_specs=[VMEM] * (2 + len(beside)),
        out_specs=VMEM,
        compiler_params=PARAMS,
        name="merge",
    )(mine, theirs, *beside)


def line_ends(axis, refs):
    steps = []
    parts = [rows_of(ref, refs[0].shape[1] // 5) for ref in refs]
    stage = 0
    while len(parts) > 4:
        is_low, (_, weights) = ordered(axis, stage, *parts[:2])
        steps.append((is_low, weights))
        parts = parts[2:]
        stage += 1
    is_low, (own, weights) = ordered(axis, stage, *parts[:2])
    steps.append((is_low, weights))
    _, (other, _) = ordered(axis, stage, *parts[2:])
    is_low, (whole, weights) = ordered(axis, stage + 1, own, other)
    steps.append((is_low, weights))
    t, _, gr, _, sr = whole
    left = jnp.zeros_like(t)
    right = sr / (t + gr + 1.0)
    for is_low, (w1, w2, source) in reversed(steps):
        middle = w1 * left + w2 * right + source
        left = jnp.where(is_low, left, middle)
        right = jnp.where(is_low, middle, right)
    return left, right


def segment_ends(left, right, w_ref, s_ref, levels):
    index = row_index(left.shape)
    for level in reversed(range(levels)):
        stride = 1 << level
        middle = w_ref[3 * level] * left + w_ref[3 * level + 1] * right
        if s_ref is not None:
            middle = middle + s_ref[1 + level]
        upper = (index >> level) % 2 == 1
        left, right = (
            jnp.where(upper, pltpu.roll(middle, stride, 0), left),
            jnp.where(upper, pltpu.roll(right, stride, 0), middle),
        )
    return left, right


def march_values(left, right, t_ref, s_ref, inv_ref, scale, r_ref, store):
    value = left
    change = t_ref[0] * (right - left) - t_ref[1] * left
    if s_ref is not None:
        change = change - s_ref[0]
    for k in range(STEPS):
        inverse = full(inv_ref, k)
        value = value + change
        push = scale * (inverse * inverse) * value
        change = change + (push if r_ref is None else push - full(r_ref, k))
        store(k, value * inverse)


def rest_x_kernel(inv_ref, r_ref, t_ref, w_ref, s_ref, out, *, scale):
    tiles = out.shape[0] // LANES
    zero = jnp.zeros((tiles * SUB, LANES), F32)

    def store(k, speed):
        for tile in range(tiles):
            out[at(tile, k), :] = speed[tile * SUB : (tile + 1) * SUB, :]

    left, right = segment_ends(zero, zero, w_ref, s_ref, log2(SUB))
    march_values(left, right, t_ref, s_ref, inv_ref, scale, r_ref, store)


def rest_x(*pieces, scale):
    return pl.pallas_call(
        functools.partial(rest_x_kernel, scale=scale),
        out_shape=shape(*pieces[0].shape),
        in_specs=[VMEM] * len(pieces),
        out_specs=VMEM,
        compiler_params=PARAMS,
        cost_estimate=pl.CostEstimate(flops=1_000_000, bytes_accessed=2_000_000, transcendentals=0),
        name="rest_x",
    )(*pieces)


def solve_x_kernel(from_left, from_right, rest, *refs):
    parts, (out, natural, sems) = refs[:-3], refs[-3:]
    left, right = line_ends("gx", parts)
    writes = []
    for tile in range(out.shape[1] // LANES):
        span = tile_span(tile)
        for k in range(STEPS):
            here = at(tile, k)
            natural[spread_rows(tile, k), :] = (
                from_left[here, :] * left[:, span] + from_right[here, :] * right[:, span] + rest[here, :]
            )
        writes.append(tile_write(natural, out, tile, sems))
        writes[-1].start()
    for write in writes:
        write.wait()


def solve_y_kernel(inv_ref, r_ref, t_ref, w_ref, s_ref, *refs, scale):
    parts, (out, natural, sems, turned) = refs[:-4], refs[-4:]
    tiles = out.shape[1] // LANES
    ends = line_ends("gy", parts)
    ends = [jnp.broadcast_to(row, (tiles * SUB, LANES)) for row in ends]
    left, right = segment_ends(*ends, w_ref, s_ref, log2(tiles * SUB))

    def store(k, speed):
        for tile in range(tiles):
            turned[spread_rows(tile, k), :] = speed[tile * SUB : (tile + 1) * SUB, :]

    march_values(left, right, t_ref, s_ref, inv_ref, scale, r_ref, store)
    writes = []
    for tile in range(tiles):
        block = turned[tile_span(tile), :].T
        for k in range(STEPS):
            natural[spread_rows(tile, k), :] = block[k * SUB : (k + 1) * SUB, :]
        writes.append(tile_write(natural, out, tile, sems))
        writes[-1].start()
    for write in writes:
        write.wait()


def solve(kernel, name, pieces, parts, block, extra=()):
    return pl.pallas_call(
        kernel,
        out_shape=shape(*block),
        in_specs=[VMEM] * (len(pieces) + len(parts)),
        out_specs=ANY,
        scratch_shapes=write_scratch(block[1]) + list(extra),
        compiler_params=PARAMS,
        cost_estimate=pl.CostEstimate(flops=1_000_000, bytes_accessed=4_000_000, transcendentals=0),
        name=name,
    )(*pieces, *parts)


def hand_on(value, axis):
    count = lax.axis_size(axis)
    far = [i + 2 if i % 2 == 0 else i - 2 for i in range(count)]
    return lax.ppermute(value, axis, [(i, t if 0 <= t < count else i ^ 1) for i, t in enumerate(far)])


def cross(value, axis, mask):
    return lax.ppermute(value, axis, [(i, i ^ mask) for i in range(lax.axis_size(axis))])


def parts_of_line(axis, mine, relay, beside=(), tall=None):
    parts = []
    last = log2(lax.axis_size(axis)) - 2
    for stage in range(last):
        theirs = cross(mine, axis, 1 << stage)
        parts += [mine, theirs]
        mine = merge_call(axis, stage, mine, theirs, beside)
    if relay:
        first = cross(mine, axis, 1 << last)
        second = cross(mine if tall is None else tall, axis, 2 << last)
        both = cross(second[:, 0 : mine.shape[1]], axis, 1 << last)
    else:
        first, second, both = (cross(mine, axis, n << last) for n in (1, 2, 3))
    return parts + [mine, first, second, both]


def on_device(h, p, q, b, m):
    block = h.shape
    rows, cols = block
    inv_cx = 3.0 / (rows * lax.axis_size("gx") / 4.0) ** 2
    inv_cy = 3.0 / (cols * lax.axis_size("gy") / 4.0) ** 2
    near_x, outer_x = pack_x(h, p, q, b, m)
    near_y = cross(pack_y(h, p, q, b, m, after=outer_x), "gy", 1)
    outer_x, near_x = cross(outer_x, "gx", 1), cross(near_x, "gx", 1)
    far_y = hand_on(jnp.pad(near_y[1], ((0, 5 * SUB), (0, 0))), "gy")
    hx, hy, ix, iy, tx, wx, ty, wy, coef_x, coef_y, left_x, right_x = prepare_depth(h, inv_cx, inv_cy)
    far_x = hand_on(once(outer_x, coef_x), "gx")
    px, py, qx, qy, bx, by, mx, my = prepare_rest(p, q, b, m)
    depth_inner, push_inner, across_inner = fluxes_x_inner(hx, px, qx, bx, mx)
    mass_y, shear_y, normal_y = fluxes_y(near_y, far_y, hy, py, qy, by, my)
    depth_outer, across_outer, rx, sx, end_x = fluxes_x(
        near_x, far_x, hx, px, qx, bx, mx, ix, shear_y, push_inner, tx, wx, coef_x, inv_cx=inv_cx
    )
    depth, ry, sy, end_y, tall_y = join_y(
        depth_inner, across_inner, depth_outer, across_outer, mass_y, mx, normal_y, iy, my, ty, wy, coef_y, inv_cy=inv_cy
    )
    new_depth = write_depth(depth, block)
    parts_y = parts_of_line("gy", end_y, True, tall=tall_y if lax.axis_size("gy") == 4 else None)
    parts_x = parts_of_line("gx", end_x, False, parts_y[1:2])
    turned = [pltpu.VMEM((cols, LANES), F32)]
    solve_y_scaled = functools.partial(solve_y_kernel, scale=inv_cy)
    vy = solve(solve_y_scaled, "solve_y", (iy, ry, ty, wy, sy), parts_y, block, turned)
    own_x = rest_x(ix, rx, tx, wx, sx, scale=inv_cx)
    vx = solve(solve_x_kernel, "solve_x", (left_x, right_x, own_x), parts_x, block)
    return new_depth, vx, vy


def solution(mesh):
    spec = P("gx", "gy")
    return jax.shard_map(
        on_device,
        mesh=mesh,
        in_specs=(spec,) * 5,
        out_specs=(spec,) * 3,
        check_vma=False,
    )
```

```python
import functools

import jax
import jax.numpy as jnp
from jax import lax
from jax.experimental import pallas as pl
from jax.experimental.pallas import tpu as pltpu
from jax.sharding import PartitionSpec as P

gravity = 9.81
ratio = 0.05
LANES = 128
SUB = 8
STEPS = LANES // SUB
F32 = jnp.float32
VMEM = pl.BlockSpec(memory_space=pltpu.VMEM)
HBM = pl.BlockSpec(memory_space=pltpu.HBM)
ANY = pl.BlockSpec(memory_space=pl.ANY)
PARAMS = pltpu.CompilerParams(vmem_limit_bytes=16 * 1024 * 1024)


def lane_index(shape):
    return lax.broadcasted_iota(jnp.int32, shape, len(shape) - 1)


def row_index(shape):
    return lax.broadcasted_iota(jnp.int32, shape, len(shape) - 2)


def at(tile, step):
    first = tile * LANES + step * SUB
    return slice(first, first + SUB)


def tile_span(tile):
    return slice(tile * LANES, (tile + 1) * LANES)


def spread_rows(tile, step):
    return pl.ds(tile * LANES + step, SUB, stride=STEPS)


def shape(*dims):
    return jax.ShapeDtypeStruct(dims, F32)


def pack_x_kernel(h, p, q, b, m, slabs, top, bottom, itop, ibottom, sems):
    rows = h.shape[0]
    copies = []
    for f, src in enumerate((h, p, q, b, m)):
        for side, (target, whole, row) in enumerate(((top, itop, 0), (bottom, ibottom, rows - SUB))):
            copy = pltpu.make_async_copy(
                src.at[pl.ds(row, SUB), :], target.at[f] if f < 4 else whole, sems.at[2 * f + side]
            )
            copy.start()
            copies.append(copy)
    for copy in copies:
        copy.wait()
    first = jnp.concatenate(
        [top[0, 0:2, :], top[1, 0:2, :], top[2, 0:2, :], top[3, 0:1, :], itop[0:1, :].astype(F32)]
    )
    last = jnp.concatenate(
        [
            bottom[0, SUB - 2 : SUB, :],
            bottom[1, SUB - 2 : SUB, :],
            bottom[2, SUB - 2 : SUB, :],
            bottom[3, SUB - 1 : SUB, :],
            ibottom[SUB - 1 : SUB, :].astype(F32),
        ]
    )
    even = lax.axis_index("gx") % 2 == 0
    slabs[0] = jnp.where(even, last, first)
    slabs[1] = jnp.where(even, first, last)


def pack_x(*fields):
    cols = fields[0].shape[1]
    return pl.pallas_call(
        pack_x_kernel,
        out_shape=shape(2, SUB, cols),
        in_specs=[HBM] * 5,
        out_specs=VMEM,
        scratch_shapes=[
            pltpu.VMEM((4, SUB, cols), F32),
            pltpu.VMEM((4, SUB, cols), F32),
            pltpu.VMEM((SUB, cols), jnp.int32),
            pltpu.VMEM((SUB, cols), jnp.int32),
            pltpu.SemaphoreType.DMA((10,)),
        ],
        compiler_params=PARAMS,
        name="pack_x",
    )(*[pltpu.with_memory_space_constraint(v, pltpu.HBM) for v in fields])


def pack_y_kernel(h, p, q, b, m, _, slabs, natural):
    rows, cols = h.shape
    lane = lane_index((rows, LANES))
    out = None
    for f, src in enumerate((h, p, q, b, m)):
        both = jnp.where(lane < LANES // 2, src[:, 0:LANES], src[:, cols - LANES : cols]).astype(F32)
        moved = pltpu.roll(both, 4 * f + 2, 1)
        out = moved if out is None else jnp.where(lane >= 4 * f, moved, out)
    natural[...] = out
    turned = jnp.concatenate([natural[spread_rows(0, k), :] for k in range(STEPS)]).T
    last = jnp.concatenate([turned[0:2], turned[4:6], turned[8:10], turned[13:14], turned[17:18]])
    first = jnp.concatenate([turned[2:4], turned[6:8], turned[10:12], turned[14:15], turned[18:19]])
    even = lax.axis_index("gy") % 2 == 0
    slabs[0] = jnp.where(even, last, first)
    slabs[1] = jnp.where(even, first, last)


def pack_y(*fields, after):
    rows = fields[0].shape[0]
    return pl.pallas_call(
        pack_y_kernel,
        out_shape=shape(2, SUB, rows),
        in_specs=[VMEM] * 6,
        out_specs=VMEM,
        scratch_shapes=[pltpu.VMEM((rows, LANES), F32)],
        compiler_params=PARAMS,
        cost_estimate=pl.CostEstimate(flops=500_000, bytes_accessed=1_000_000, transcendentals=0),
        name="pack_y",
    )(*fields, after)


def tie_kernel(both, _, out):
    out[...] = both[1]


def second_of(both, after):
    return pl.pallas_call(
        tie_kernel,
        out_shape=shape(*both.shape[1:]),
        in_specs=[VMEM, VMEM],
        out_specs=VMEM,
        compiler_params=PARAMS,
        name="second_of",
    )(both, after)


def merge_coefficients(one, two):
    t1, gl1, gr1 = one
    t2, gl2, gr2 = two
    shunt = gr1 + gl2
    inverse = 1.0 / (t1 + t2 + shunt)
    w1, w2 = t1 * inverse, t2 * inverse
    return (w1 * t2, gl1 + w1 * shunt, gr2 + w2 * shunt), (w1, w2, inverse)


def merge_sources(one, two, weights):
    w1, w2, inverse = weights
    source = one[1] - two[0]
    return (one[0] - w1 * source, two[1] + w2 * source), source * inverse


def merge(one, two):
    coefficients, weights = merge_coefficients(one[:3], two[:3])
    sources, middle = merge_sources(one[3:], two[3:], weights)
    return coefficients + sources, weights[:2] + (middle,)


def log2(count):
    return (count - 1).bit_length()


def full(ref, step):
    return jnp.concatenate([ref[at(tile, step), :] for tile in range(ref.shape[0] // LANES)])


def march_depth(inv_ref, scale, out_t, out_w, levels):
    count = inv_ref.shape[0] // STEPS
    zero = jnp.zeros((count, LANES), F32)
    alpha, gamma, beta, delta = zero, zero, zero, zero
    for k in range(STEPS):
        inverse = full(inv_ref, k)
        d = scale * (inverse * inverse)
        alpha = alpha + gamma
        gamma = gamma + d * (1.0 + alpha)
        beta = beta + delta
        delta = delta + d * ((k + 1.0) + beta)
    t = 1.0 / (STEPS + beta)
    out_t[0] = t
    out_t[1] = t * alpha
    out_t[2] = 1.0 + delta
    coefficients = (t, t * alpha, t * delta)
    for level in range(levels):
        after = tuple(pltpu.roll(v, count - (1 << level), 0) for v in coefficients)
        coefficients, weights = merge_coefficients(coefficients, after)
        for j, v in enumerate(weights):
            out_w[3 * level + j] = v
    return coefficients


def lay_out(src, xs, ys, natural, turned):
    for tile in range(xs.shape[0] // LANES):
        natural[tile_span(tile), :] = src[:, tile_span(tile)].astype(F32)
        for k in range(STEPS):
            xs[at(tile, k), :] = natural[spread_rows(tile, k), :]
        turned[tile_span(tile), :] = xs[tile_span(tile), :].T
        for k in range(STEPS):
            ys[at(tile, k), :] = turned[spread_rows(tile, k), :]


def prepare_depth_kernel(
    h, hx, hy, ix, iy, tx, wx, ty, wy, endx, endy, from_left, from_right, natural, turned, *, inv_cx, inv_cy
):
    tiles = hx.shape[0] // LANES
    lay_out(h, hx, hy, natural, turned)
    ix[...] = 1.0 / hx[...]
    iy[...] = 1.0 / hy[...]
    ends_x = march_depth(ix, inv_cx, tx, wx, log2(SUB))
    ends_y = march_depth(iy, inv_cy, ty, wy, log2(SUB * tiles))
    for i in range(3):
        for tile in range(tiles):
            first = (i * tiles + tile) * LANES
            endx[0:1, first : first + LANES] = ends_x[i][tile * SUB : tile * SUB + 1, :]
        endy[0:1, i * LANES : (i + 1) * LANES] = ends_y[i][0:1, :]
    one = jnp.ones((tiles * SUB, LANES), F32)
    zero = jnp.zeros_like(one)
    for out, left, right in ((from_left, one, zero), (from_right, zero, one)):

        def store(k, speed):
            for tile in range(tiles):
                out[at(tile, k), :] = speed[tile * SUB : (tile + 1) * SUB, :]

        left, right = segment_ends(left, right, wx, None, log2(SUB))
        march_values(left, right, tx, None, ix, inv_cx, None, store)


def prepare_depth(h, inv_cx, inv_cy):
    stack = (h.shape[1], LANES)
    count = stack[0] // STEPS
    shapes = [shape(*stack)] * 4 + [
        shape(3, count, LANES),
        shape(3 * log2(SUB), count, LANES),
        shape(3, count, LANES),
        shape(3 * log2(count), count, LANES),
        shape(1, 3 * stack[0]),
        shape(1, 3 * LANES),
        shape(*stack),
        shape(*stack),
    ]
    return pl.pallas_call(
        functools.partial(prepare_depth_kernel, inv_cx=inv_cx, inv_cy=inv_cy),
        out_shape=tuple(shapes),
        in_specs=[VMEM],
        out_specs=(VMEM,) * len(shapes),
        scratch_shapes=[pltpu.VMEM(stack, F32)] * 2,
        compiler_params=PARAMS,
        cost_estimate=pl.CostEstimate(flops=2_000_000, bytes_accessed=4_000_000, transcendentals=0),
        name="prepare_depth",
    )(h)


def prepare_rest_kernel(*refs):
    fields, outs, natural, turned = refs[:4], refs[4:12], refs[12], refs[13]
    for f, src in enumerate(fields):
        lay_out(src, outs[2 * f], outs[2 * f + 1], natural.at[f % 2], turned.at[f % 2])


def prepare_rest(*fields):
    stack = (fields[0].shape[1], LANES)
    return pl.pallas_call(
        prepare_rest_kernel,
        out_shape=(shape(*stack),) * 8,
        in_specs=[VMEM] * 4,
        out_specs=(VMEM,) * 8,
        scratch_shapes=[pltpu.VMEM((2, *stack), F32)] * 2,
        compiler_params=PARAMS,
        cost_estimate=pl.CostEstimate(flops=2_000_000, bytes_accessed=6_000_000, transcendentals=0),
        name="prepare_rest",
    )(*fields)


def low_high(axis, near, far):
    index, count = lax.axis_index(axis), lax.axis_size(axis)
    even = index % 2 == 0
    low = jnp.where(index > 0, jnp.where(even, far, near), 0.0)
    high = jnp.where(index < count - 1, jnp.where(even, near, far), 0.0)
    return low, high


def half_slope(a, c):
    return 0.5 * (jnp.maximum(jnp.minimum(a, c), 0.0) + jnp.minimum(jnp.maximum(a, c), 0.0))


def face_flux(left, right, opened):
    is_open = opened > 0.5
    hl = jnp.where(is_open, left[0], 1.0)
    hr = jnp.where(is_open, right[0], 1.0)
    joint = 1.0 / (hl * hr)
    ul = left[1] * (hr * joint)
    ur = right[1] * (hl * joint)
    gl = gravity * hl
    gr = gravity * hr
    fastest = jnp.maximum(jnp.abs(ul) + gl * lax.rsqrt(gl), jnp.abs(ur) + gr * lax.rsqrt(gr))
    scale = (0.5 * ratio) * opened
    mass = (left[1] + right[1]) - fastest * (right[0] - left[0])
    push = 0.5 * (gl * hl + gr * hr) + left[1] * ul + right[1] * ur - fastest * (right[1] - left[1])
    shear = left[2] * ul + right[2] * ur - fastest * (right[2] - left[2])
    return scale * mass, scale * push, scale * shear


def extended(ref, tile, lows, highs):
    sub = row_index((SUB, LANES))
    out = {}
    for n, row in enumerate(lows, 1):
        value = ref[at(tile, STEPS - n), :]
        out[-n] = jnp.where(sub == 0, row, pltpu.roll(value, 1, 0))
    for n, row in enumerate(highs):
        value = ref[at(tile, n), :]
        out[STEPS + n] = jnp.where(sub == SUB - 1, row, pltpu.roll(value, SUB - 1, 0))
    return lambda k: out[k] if k in out else ref[at(tile, k), :]


def tile_fluxes(fields, bed, wet, store, start=0, stop=STEPS):
    def states(k):
        both = []
        for w in fields:
            here = w(k)
            both.append((here, half_slope(here - w(k - 1), w(k + 1) - here)))
        return [w + s for w, s in both], [w - s for w, s in both]

    left, _ = states(start - 1)
    before = None
    for k in range(start - 1, stop):
        left_next, right = states(k + 1)
        face = face_flux(left, right, wet(k) * wet(k + 1))
        left = left_next
        if k >= start:
            store(k, [a - c for a, c in zip(face, before)], bed(k + 1) - bed(k - 1))
        before = face


def march_source(inv_ref, scale, r_ref, t_ref, w_ref, s_ref, levels):
    count = inv_ref.shape[0] // STEPS
    c = jnp.zeros((count, LANES), F32)
    e = c
    for k in range(STEPS):
        inverse = full(inv_ref, k)
        c = c + e
        e = e + (scale * (inverse * inverse) * c - full(r_ref, k))
    sl = t_ref[0] * c
    s_ref[0] = sl
    sources = (sl, t_ref[2] * sl - e)
    for level in range(levels):
        after = tuple(pltpu.roll(v, count - (1 << level), 0) for v in sources)
        sources, middle = merge_sources(sources, after, tuple(w_ref[3 * level + j] for j in range(3)))
        s_ref[1 + level] = middle
    return sources


def flux_y_kernel(near, far, hy, py, qy, by, my, mass, shear, normal, across, along):
    tiles = hy.shape[0] // LANES
    low, high = low_high("gy", near[0], far[0:SUB, :])
    for tile in range(tiles):

        def extend(ref, row, layers):
            lows, highs = [], []
            for n in range(layers):
                last = at(tile - 1, STEPS - 1 - n).stop - 1
                first = at(tile + 1, n).start
                lows.append(low[row + layers - 1 - n : row + layers - n, :] if tile == 0 else ref[last : last + 1, :])
                highs.append(high[row + n : row + n + 1, :] if tile == tiles - 1 else ref[first : first + 1, :])
            return extended(ref, tile, lows, highs)

        def store(k, difference, bed):
            here, natural = at(tile, k), spread_rows(tile, k)
            across[natural, :] = difference[0]
            along[natural, :] = difference[2]
            pull = (0.5 * ratio * gravity) * hy[here, :]
            normal[here, :] = qy[here, :] - difference[1] - pull * bed

        tile_fluxes([extend(hy, 0, 2), extend(qy, 4, 2), extend(py, 2, 2)], extend(by, 6, 1), extend(my, 7, 1), store)
        span = tile_span(tile)
        mass[span, :] = across[span, :].T
        shear[span, :] = along[span, :].T


def fluxes_y(*arrays):
    stack = arrays[2].shape
    return pl.pallas_call(
        flux_y_kernel,
        out_shape=(shape(*stack),) * 3,
        in_specs=[VMEM] * len(arrays),
        out_specs=(VMEM,) * 3,
        scratch_shapes=[pltpu.VMEM(stack, F32)] * 2,
        compiler_params=PARAMS,
        cost_estimate=pl.CostEstimate(flops=4_000_000, bytes_accessed=4_000_000, transcendentals=0),
        name="fluxes_y",
    )(*arrays)


INNER = (2, STEPS - 2)
TALL = 16


def x_store(hx, px, mx, depth, push, across):
    def of_tile(tile):
        def store(k, difference, bed):
            here = at(tile, k)
            h = hx[here, :]
            depth[here, :] = h - mx[here, :] * difference[0]
            push[here, :] = px[here, :] - difference[1] - (0.5 * ratio * gravity) * h * bed
            across[here, :] = difference[2]

        return store

    return of_tile


def flux_x_inner_kernel(hx, px, qx, bx, mx, depth, push, across):
    store = x_store(hx, px, mx, depth, push, across)
    for tile in range(hx.shape[0] // LANES):
        fields = [extended(v, tile, (), ()) for v in (hx, px, qx, bx, mx)]
        tile_fluxes(fields[:3], fields[3], fields[4], store(tile), *INNER)
        for k in (*range(INNER[0]), *range(INNER[1], STEPS)):
            for ref in (depth, push, across):
                ref[at(tile, k), :] = jnp.zeros((SUB, LANES), F32)


def fluxes_x_inner(*arrays):
    stack = arrays[0].shape
    return pl.pallas_call(
        flux_x_inner_kernel,
        out_shape=(shape(*stack),) * 3,
        in_specs=[VMEM] * len(arrays),
        out_specs=(VMEM,) * 3,
        compiler_params=PARAMS,
        cost_estimate=pl.CostEstimate(flops=4_000_000, bytes_accessed=4_000_000, transcendentals=0),
        name="fluxes_x_inner",
    )(*arrays)


def flux_x_kernel(
    near, far, hx, px, qx, bx, mx, ix, shear_y, push_in, tx, wx, coef,
    depth, across, rx, sx, ends,
    push,
    *, inv_cx,
):
    tiles = hx.shape[0] // LANES
    low, high = low_high("gx", near[0], far[...])
    store = x_store(hx, px, mx, depth, push, across)
    for tile in range(tiles):
        span = tile_span(tile)

        def extend(ref, row, layers):
            lows = [low[row + layers - 1 - n : row + layers - n, span] for n in range(layers)]
            highs = [high[row + n : row + n + 1, span] for n in range(layers)]
            return extended(ref, tile, lows, highs)

        fields, bed, wet = [extend(hx, 0, 2), extend(px, 2, 2), extend(qx, 4, 2)], extend(bx, 6, 1), extend(mx, 7, 1)
        tile_fluxes(fields, bed, wet, store(tile), 0, INNER[0])
        tile_fluxes(fields, bed, wet, store(tile), INNER[1], STEPS)
        for k in range(STEPS):
            here = at(tile, k)
            inverse = ix[here, :]
            total = (push_in if INNER[0] <= k < INNER[1] else push)[here, :] - shear_y[here, :]
            rx[here, :] = (inv_cx * (inverse * inverse)) * mx[here, :] * total
    sources = march_source(ix, inv_cx, rx, tx, wx, sx, log2(SUB))
    count = tiles * LANES
    ends[0:1, 0 : 3 * count] = coef[...]
    for i in range(2):
        for tile in range(tiles):
            first = (3 + i) * count + tile * LANES
            ends[0:1, first : first + LANES] = sources[i][tile * SUB : tile * SUB + 1, :]


def fluxes_x(*arrays, inv_cx):
    stack = arrays[2].shape
    count = stack[0] // STEPS
    shapes = (
        shape(*stack),
        shape(*stack),
        shape(*stack),
        shape(1 + log2(SUB), count, LANES),
        shape(1, 5 * stack[0]),
    )
    return pl.pallas_call(
        functools.partial(flux_x_kernel, inv_cx=inv_cx),
        out_shape=shapes,
        in_specs=[VMEM] * len(arrays),
        out_specs=(VMEM,) * len(shapes),
        scratch_shapes=[pltpu.VMEM(stack, F32)],
        compiler_params=PARAMS,
        name="fluxes_x",
    )(*arrays)


def join_y_kernel(
    depth_inner, across_inner, depth_outer, across_outer, mass_y, mx, normal_y, iy, my, ty, wy, coef,
    depth, ry, sy, ends, tall,
    across, turned,
    *, inv_cy,
):
    tiles = mx.shape[0] // LANES
    for tile in range(tiles):
        span = tile_span(tile)
        for k in range(STEPS):
            here = at(tile, k)
            inner = INNER[0] <= k < INNER[1]
            across[here, :] = (across_inner if inner else across_outer)[here, :]
            depth[here, :] = (depth_inner if inner else depth_outer)[here, :] - mx[here, :] * mass_y[here, :]
        turned[span, :] = across[span, :].T
        for k in range(STEPS):
            here = at(tile, k)
            inverse = iy[here, :]
            total = normal_y[here, :] - turned[spread_rows(tile, k), :]
            ry[here, :] = (inv_cy * (inverse * inverse)) * my[here, :] * total
    sources = march_source(iy, inv_cy, ry, ty, wy, sy, log2(SUB * tiles))
    ends[0:1, 0 : 3 * LANES] = coef[...]
    for i in range(2):
        ends[0:1, (3 + i) * LANES : (4 + i) * LANES] = sources[i][0:1, :]
    tall[...] = jnp.zeros_like(tall)
    tall[0:1, 0 : 5 * LANES] = ends[...]


def join_y(*arrays, inv_cy):
    stack = arrays[0].shape
    count = stack[0] // STEPS
    shapes = (
        shape(*stack),
        shape(*stack),
        shape(1 + log2(count), count, LANES),
        shape(1, 5 * LANES),
        shape(1, TALL * LANES),
    )
    return pl.pallas_call(
        functools.partial(join_y_kernel, inv_cy=inv_cy),
        out_shape=shapes,
        in_specs=[VMEM] * len(arrays),
        out_specs=(VMEM,) * len(shapes),
        scratch_shapes=[pltpu.VMEM(stack, F32)] * 2,
        compiler_params=PARAMS,
        cost_estimate=pl.CostEstimate(flops=2_000_000, bytes_accessed=2_000_000, transcendentals=0),
        name="join_y",
    )(*arrays)


def tile_write(tiled, whole, tile, sems):
    rows = whole.shape[0]
    return pltpu.make_async_copy(
        tiled.at[pl.ds(tile * rows, rows), :], whole.at[:, pl.ds(tile * LANES, LANES)], sems.at[tile]
    )


def write_scratch(cols):
    return [pltpu.VMEM((cols, LANES), F32), pltpu.SemaphoreType.DMA((cols // LANES,))]


def depth_kernel(depth, out, natural, sems):
    writes = []
    for tile in range(depth.shape[0] // LANES):
        for k in range(STEPS):
            natural[spread_rows(tile, k), :] = depth[at(tile, k), :]
        writes.append(tile_write(natural, out, tile, sems))
        writes[-1].start()
    for write in writes:
        write.wait()


def write_depth(depth, block):
    return pl.pallas_call(
        depth_kernel,
        out_shape=shape(*block),
        in_specs=[VMEM],
        out_specs=ANY,
        scratch_shapes=write_scratch(block[1]),
        compiler_params=PARAMS,
        cost_estimate=pl.CostEstimate(flops=100_000, bytes_accessed=2_000_000, transcendentals=0),
        name="write_depth",
    )(depth)


def rows_of(ref, count):
    return tuple(ref[0:1, i * count : (i + 1) * count] for i in range(5))


def ordered(axis, stage, mine, theirs):
    is_low = (lax.axis_index(axis) >> stage) % 2 == 0
    one = tuple(jnp.where(is_low, a, b) for a, b in zip(mine, theirs))
    two = tuple(jnp.where(is_low, b, a) for a, b in zip(mine, theirs))
    return is_low, merge(one, two)


def merge_kernel(mine, theirs, *refs, axis, stage):
    out = refs[-1]
    count = mine.shape[1] // 5
    _, (merged, _) = ordered(axis, stage, rows_of(mine, count), rows_of(theirs, count))
    for i, v in enumerate(merged):
        out[0:1, i * v.shape[1] : (i + 1) * v.shape[1]] = v


def merge_call(axis, stage, mine, theirs, beside):
    return pl.pallas_call(
        functools.partial(merge_kernel, axis=axis, stage=stage),
        out_shape=shape(*mine.shape),
        in_specs=[VMEM] * (2 + len(beside)),
        out_specs=VMEM,
        compiler_params=PARAMS,
        name="merge",
    )(mine, theirs, *beside)


def line_ends(axis, refs, is_crossed=False):
    steps = []
    parts = [rows_of(ref, refs[0].shape[1] // 5) for ref in refs]
    stage = 0
    while len(parts) > 4:
        is_low, (_, weights) = ordered(axis, stage, *parts[:2])
        steps.append((is_low, weights))
        parts = parts[2:]
        stage += 1
    if is_crossed:
        lower = (lax.axis_index(axis) >> (stage + 1)) % 2 == 0
        both = list(zip(*parts[2:]))
        parts[2] = tuple(jnp.where(lower, a, b) for a, b in both)
        parts[3] = tuple(jnp.where(lower, b, a) for a, b in both)
    is_low, (own, weights) = ordered(axis, stage, *parts[:2])
    steps.append((is_low, weights))
    _, (other, _) = ordered(axis, stage, *parts[2:])
    is_low, (whole, weights) = ordered(axis, stage + 1, own, other)
    steps.append((is_low, weights))
    t, _, gr, _, sr = whole
    left = jnp.zeros_like(t)
    right = sr / (t + gr + 1.0)
    for is_low, (w1, w2, source) in reversed(steps):
        middle = w1 * left + w2 * right + source
        left = jnp.where(is_low, left, middle)
        right = jnp.where(is_low, middle, right)
    return left, right


def segment_ends(left, right, w_ref, s_ref, levels):
    index = row_index(left.shape)
    for level in reversed(range(levels)):
        stride = 1 << level
        middle = w_ref[3 * level] * left + w_ref[3 * level + 1] * right
        if s_ref is not None:
            middle = middle + s_ref[1 + level]
        upper = (index >> level) % 2 == 1
        left, right = (
            jnp.where(upper, pltpu.roll(middle, stride, 0), left),
            jnp.where(upper, pltpu.roll(right, stride, 0), middle),
        )
    return left, right


def march_values(left, right, t_ref, s_ref, inv_ref, scale, r_ref, store):
    value = left
    change = t_ref[0] * (right - left) - t_ref[1] * left
    if s_ref is not None:
        change = change - s_ref[0]
    for k in range(STEPS):
        inverse = full(inv_ref, k)
        value = value + change
        push = scale * (inverse * inverse) * value
        change = change + (push if r_ref is None else push - full(r_ref, k))
        store(k, value * inverse)


def rest_x_kernel(inv_ref, r_ref, t_ref, w_ref, s_ref, out, *, scale):
    tiles = out.shape[0] // LANES
    zero = jnp.zeros((tiles * SUB, LANES), F32)

    def store(k, speed):
        for tile in range(tiles):
            out[at(tile, k), :] = speed[tile * SUB : (tile + 1) * SUB, :]

    left, right = segment_ends(zero, zero, w_ref, s_ref, log2(SUB))
    march_values(left, right, t_ref, s_ref, inv_ref, scale, r_ref, store)


def rest_x(*pieces, scale):
    return pl.pallas_call(
        functools.partial(rest_x_kernel, scale=scale),
        out_shape=shape(*pieces[0].shape),
        in_specs=[VMEM] * len(pieces),
        out_specs=VMEM,
        compiler_params=PARAMS,
        cost_estimate=pl.CostEstimate(flops=1_000_000, bytes_accessed=2_000_000, transcendentals=0),
        name="rest_x",
    )(*pieces)


def solve_x_kernel(from_left, from_right, rest, *refs):
    parts, (out, natural, sems) = refs[:-3], refs[-3:]
    left, right = line_ends("gx", parts, True)
    writes = []
    for tile in range(out.shape[1] // LANES):
        span = tile_span(tile)
        for k in range(STEPS):
            here = at(tile, k)
            natural[spread_rows(tile, k), :] = (
                from_left[here, :] * left[:, span] + from_right[here, :] * right[:, span] + rest[here, :]
            )
        writes.append(tile_write(natural, out, tile, sems))
        writes[-1].start()
    for write in writes:
        write.wait()


def solve_y_kernel(inv_ref, r_ref, t_ref, w_ref, s_ref, *refs, scale):
    parts, (out, natural, sems, turned) = refs[:-4], refs[-4:]
    tiles = out.shape[1] // LANES
    ends = line_ends("gy", parts)
    ends = [jnp.broadcast_to(row, (tiles * SUB, LANES)) for row in ends]
    left, right = segment_ends(*ends, w_ref, s_ref, log2(tiles * SUB))

    def store(k, speed):
        for tile in range(tiles):
            turned[spread_rows(tile, k), :] = speed[tile * SUB : (tile + 1) * SUB, :]

    march_values(left, right, t_ref, s_ref, inv_ref, scale, r_ref, store)
    writes = []
    for tile in range(tiles):
        block = turned[tile_span(tile), :].T
        for k in range(STEPS):
            natural[spread_rows(tile, k), :] = block[k * SUB : (k + 1) * SUB, :]
        writes.append(tile_write(natural, out, tile, sems))
        writes[-1].start()
    for write in writes:
        write.wait()


def solve(kernel, name, pieces, parts, block, extra=()):
    return pl.pallas_call(
        kernel,
        out_shape=shape(*block),
        in_specs=[VMEM] * (len(pieces) + len(parts)),
        out_specs=ANY,
        scratch_shapes=write_scratch(block[1]) + list(extra),
        compiler_params=PARAMS,
        cost_estimate=pl.CostEstimate(flops=1_000_000, bytes_accessed=4_000_000, transcendentals=0),
        name=name,
    )(*pieces, *parts)


def hand_on(value, axis):
    count = lax.axis_size(axis)
    far = [i + 2 if i % 2 == 0 else i - 2 for i in range(count)]
    return lax.ppermute(value, axis, [(i, t if 0 <= t < count else i ^ 1) for i, t in enumerate(far)])


def cross(value, axis, mask):
    return lax.ppermute(value, axis, [(i, i ^ mask) for i in range(lax.axis_size(axis))])


def crossed(value, axis, stage, half):
    pairs = []
    for i in range(lax.axis_size(axis)):
        upper = (i >> (stage + 1)) & 1
        pairs.append((i, i ^ ((2 if upper == half else 3) << stage)))
    return lax.ppermute(value, axis, pairs)


def parts_of_line(axis, mine, relay, beside=(), tall=None):
    parts = []
    last = log2(lax.axis_size(axis)) - 2
    for stage in range(last):
        theirs = cross(mine, axis, 1 << stage)
        parts += [mine, theirs]
        mine = merge_call(axis, stage, mine, theirs, beside)
    if relay:
        first = cross(mine, axis, 1 << last)
        second = cross(mine if tall is None else tall, axis, 2 << last)
        both = cross(second[:, 0 : mine.shape[1]], axis, 1 << last)
    else:
        first = cross(mine, axis, 1 << last)
        second, both = (crossed(mine, axis, last, n) for n in (1, 0))
    return parts + [mine, first, second, both]


def on_device(h, p, q, b, m):
    block = h.shape
    rows, cols = block
    inv_cx = 3.0 / (rows * lax.axis_size("gx") / 4.0) ** 2
    inv_cy = 3.0 / (cols * lax.axis_size("gy") / 4.0) ** 2
    slabs_x = pack_x(h, p, q, b, m)
    near_x = cross(slabs_x, "gx", 1)
    near_y = cross(pack_y(h, p, q, b, m, after=slabs_x), "gy", 1)
    far_y = hand_on(jnp.pad(near_y[1], ((0, 5 * SUB), (0, 0))), "gy")
    hx, hy, ix, iy, tx, wx, ty, wy, coef_x, coef_y, left_x, right_x = prepare_depth(h, inv_cx, inv_cy)
    far_x = hand_on(second_of(near_x, coef_x), "gx")
    px, py, qx, qy, bx, by, mx, my = prepare_rest(p, q, b, m)
    depth_inner, push_inner, across_inner = fluxes_x_inner(hx, px, qx, bx, mx)
    mass_y, shear_y, normal_y = fluxes_y(near_y, far_y, hy, py, qy, by, my)
    depth_outer, across_outer, rx, sx, end_x = fluxes_x(
        near_x, far_x, hx, px, qx, bx, mx, ix, shear_y, push_inner, tx, wx, coef_x, inv_cx=inv_cx
    )
    depth, ry, sy, end_y, tall_y = join_y(
        depth_inner, across_inner, depth_outer, across_outer, mass_y, mx, normal_y, iy, my, ty, wy, coef_y, inv_cy=inv_cy
    )
    new_depth = write_depth(depth, block)
    parts_y = parts_of_line("gy", end_y, True, tall=tall_y if lax.axis_size("gy") == 4 else None)
    parts_x = parts_of_line("gx", end_x, False, parts_y[1:2])
    turned = [pltpu.VMEM((cols, LANES), F32)]
    solve_y_scaled = functools.partial(solve_y_kernel, scale=inv_cy)
    vy = solve(solve_y_scaled, "solve_y", (iy, ry, ty, wy, sy), parts_y, block, turned)
    own_x = rest_x(ix, rx, tx, wx, sx, scale=inv_cx)
    vx = solve(solve_x_kernel, "solve_x", (left_x, right_x, own_x), parts_x, block)
    return new_depth, vx, vy


def solution(mesh):
    spec = P("gx", "gy")
    return jax.shard_map(
        on_device,
        mesh=mesh,
        in_specs=(spec,) * 5,
        out_specs=(spec,) * 3,
        check_vma=False,
    )
```

```python
import functools

import jax
import jax.numpy as jnp
from jax import lax
from jax.experimental import pallas as pl
from jax.experimental.pallas import tpu as pltpu
from jax.sharding import PartitionSpec as P

gravity = 9.81
ratio = 0.05
LANES = 128
SUB = 8
STEPS = LANES // SUB
F32 = jnp.float32
VMEM = pl.BlockSpec(memory_space=pltpu.VMEM)
HBM = pl.BlockSpec(memory_space=pltpu.HBM)
ANY = pl.BlockSpec(memory_space=pl.ANY)
PARAMS = pltpu.CompilerParams(vmem_limit_bytes=16 * 1024 * 1024)


def lane_index(shape):
    return lax.broadcasted_iota(jnp.int32, shape, len(shape) - 1)


def row_index(shape):
    return lax.broadcasted_iota(jnp.int32, shape, len(shape) - 2)


def at(tile, step):
    first = tile * LANES + step * SUB
    return slice(first, first + SUB)


def tile_span(tile):
    return slice(tile * LANES, (tile + 1) * LANES)


def spread_rows(tile, step):
    return pl.ds(tile * LANES + step, SUB, stride=STEPS)


def shape(*dims):
    return jax.ShapeDtypeStruct(dims, F32)


def pack_x_kernel(h, p, q, b, m, slabs, top, bottom, itop, ibottom, sems):
    rows = h.shape[0]
    copies = []
    for f, src in enumerate((h, p, q, b, m)):
        for side, (target, whole, row) in enumerate(((top, itop, 0), (bottom, ibottom, rows - SUB))):
            copy = pltpu.make_async_copy(
                src.at[pl.ds(row, SUB), :], target.at[f] if f < 4 else whole, sems.at[2 * f + side]
            )
            copy.start()
            copies.append(copy)
    for copy in copies:
        copy.wait()
    first = jnp.concatenate(
        [top[0, 0:2, :], top[1, 0:2, :], top[2, 0:2, :], top[3, 0:1, :], itop[0:1, :].astype(F32)]
    )
    last = jnp.concatenate(
        [
            bottom[0, SUB - 2 : SUB, :],
            bottom[1, SUB - 2 : SUB, :],
            bottom[2, SUB - 2 : SUB, :],
            bottom[3, SUB - 1 : SUB, :],
            ibottom[SUB - 1 : SUB, :].astype(F32),
        ]
    )
    even = lax.axis_index("gx") % 2 == 0
    slabs[0] = jnp.where(even, last, first)
    slabs[1] = jnp.where(even, first, last)


def pack_x(*fields):
    cols = fields[0].shape[1]
    return pl.pallas_call(
        pack_x_kernel,
        out_shape=shape(2, SUB, cols),
        in_specs=[HBM] * 5,
        out_specs=VMEM,
        scratch_shapes=[
            pltpu.VMEM((4, SUB, cols), F32),
            pltpu.VMEM((4, SUB, cols), F32),
            pltpu.VMEM((SUB, cols), jnp.int32),
            pltpu.VMEM((SUB, cols), jnp.int32),
            pltpu.SemaphoreType.DMA((10,)),
        ],
        compiler_params=PARAMS,
        name="pack_x",
    )(*[pltpu.with_memory_space_constraint(v, pltpu.HBM) for v in fields])


def pack_y_kernel(h, p, q, b, m, _, near, far, natural):
    rows, cols = h.shape
    lane = lane_index((rows, LANES))
    out = None
    for f, src in enumerate((h, p, q, b, m)):
        both = jnp.where(lane < LANES // 2, src[:, 0:LANES], src[:, cols - LANES : cols]).astype(F32)
        moved = pltpu.roll(both, 4 * f + 2, 1)
        out = moved if out is None else jnp.where(lane >= 4 * f, moved, out)
    natural[...] = out
    turned = jnp.concatenate([natural[spread_rows(0, k), :] for k in range(STEPS)]).T
    last = jnp.concatenate([turned[0:2], turned[4:6], turned[8:10], turned[13:14], turned[17:18]])
    first = jnp.concatenate([turned[2:4], turned[6:8], turned[10:12], turned[14:15], turned[18:19]])
    even = lax.axis_index("gy") % 2 == 0
    for slab, value in ((near, jnp.where(even, last, first)), (far, jnp.where(even, first, last))):
        slab[...] = jnp.zeros_like(slab)
        slab[0:SUB, :] = value


def pack_y(*fields, after):
    rows = fields[0].shape[0]
    return pl.pallas_call(
        pack_y_kernel,
        out_shape=(shape(1 * SUB, rows), shape(4 * SUB, rows)),
        in_specs=[VMEM] * 6,
        out_specs=(VMEM, VMEM),
        scratch_shapes=[pltpu.VMEM((rows, LANES), F32)],
        compiler_params=PARAMS,
        cost_estimate=pl.CostEstimate(flops=500_000, bytes_accessed=1_000_000, transcendentals=0),
        name="pack_y",
    )(*fields, after)


def tie_kernel(both, *refs):
    refs[-1][...] = both[1]


def second_of(both, *after):
    return pl.pallas_call(
        tie_kernel,
        out_shape=shape(*both.shape[1:]),
        in_specs=[VMEM] * (1 + len(after)),
        out_specs=VMEM,
        compiler_params=PARAMS,
        name="second_of",
    )(both, *after)


def merge_coefficients(one, two):
    t1, gl1, gr1 = one
    t2, gl2, gr2 = two
    shunt = gr1 + gl2
    inverse = 1.0 / (t1 + t2 + shunt)
    w1, w2 = t1 * inverse, t2 * inverse
    return (w1 * t2, gl1 + w1 * shunt, gr2 + w2 * shunt), (w1, w2, inverse)


def merge_sources(one, two, weights):
    w1, w2, inverse = weights
    source = one[1] - two[0]
    return (one[0] - w1 * source, two[1] + w2 * source), source * inverse


def merge(one, two):
    coefficients, weights = merge_coefficients(one[:3], two[:3])
    sources, middle = merge_sources(one[3:], two[3:], weights)
    return coefficients + sources, weights[:2] + (middle,)


def log2(count):
    return (count - 1).bit_length()


def full(ref, step):
    return jnp.concatenate([ref[at(tile, step), :] for tile in range(ref.shape[0] // LANES)])


def march_depth(inv_ref, scale, out_t, out_w, levels):
    count = inv_ref.shape[0] // STEPS
    zero = jnp.zeros((count, LANES), F32)
    alpha, gamma, beta, delta = zero, zero, zero, zero
    for k in range(STEPS):
        inverse = full(inv_ref, k)
        d = scale * (inverse * inverse)
        alpha = alpha + gamma
        gamma = gamma + d * (1.0 + alpha)
        beta = beta + delta
        delta = delta + d * ((k + 1.0) + beta)
    t = 1.0 / (STEPS + beta)
    out_t[0] = t
    out_t[1] = t * alpha
    out_t[2] = 1.0 + delta
    coefficients = (t, t * alpha, t * delta)
    for level in range(levels):
        after = tuple(pltpu.roll(v, count - (1 << level), 0) for v in coefficients)
        coefficients, weights = merge_coefficients(coefficients, after)
        for j, v in enumerate(weights):
            out_w[3 * level + j] = v
    return coefficients


def lay_out(src, xs, ys, natural, turned):
    for tile in range(xs.shape[0] // LANES):
        natural[tile_span(tile), :] = src[:, tile_span(tile)].astype(F32)
        for k in range(STEPS):
            xs[at(tile, k), :] = natural[spread_rows(tile, k), :]
        turned[tile_span(tile), :] = xs[tile_span(tile), :].T
        for k in range(STEPS):
            ys[at(tile, k), :] = turned[spread_rows(tile, k), :]


def prepare_depth_kernel(
    h, hx, hy, ix, iy, tx, wx, ty, wy, endx, endy, from_left, from_right, natural, turned, *, inv_cx, inv_cy
):
    tiles = hx.shape[0] // LANES
    lay_out(h, hx, hy, natural, turned)
    ix[...] = 1.0 / hx[...]
    iy[...] = 1.0 / hy[...]
    ends_x = march_depth(ix, inv_cx, tx, wx, log2(SUB))
    ends_y = march_depth(iy, inv_cy, ty, wy, log2(SUB * tiles))
    for i in range(3):
        for tile in range(tiles):
            first = (i * tiles + tile) * LANES
            endx[0:1, first : first + LANES] = ends_x[i][tile * SUB : tile * SUB + 1, :]
        endy[0:1, i * LANES : (i + 1) * LANES] = ends_y[i][0:1, :]
    one = jnp.ones((tiles * SUB, LANES), F32)
    zero = jnp.zeros_like(one)
    for out, left, right in ((from_left, one, zero), (from_right, zero, one)):

        def store(k, speed):
            for tile in range(tiles):
                out[at(tile, k), :] = speed[tile * SUB : (tile + 1) * SUB, :]

        left, right = segment_ends(left, right, wx, None, log2(SUB))
        march_values(left, right, tx, None, ix, inv_cx, None, store)


def prepare_depth(h, inv_cx, inv_cy):
    stack = (h.shape[1], LANES)
    count = stack[0] // STEPS
    shapes = [shape(*stack)] * 4 + [
        shape(3, count, LANES),
        shape(3 * log2(SUB), count, LANES),
        shape(3, count, LANES),
        shape(3 * log2(count), count, LANES),
        shape(1, 3 * stack[0]),
        shape(1, 3 * LANES),
        shape(*stack),
        shape(*stack),
    ]
    return pl.pallas_call(
        functools.partial(prepare_depth_kernel, inv_cx=inv_cx, inv_cy=inv_cy),
        out_shape=tuple(shapes),
        in_specs=[VMEM],
        out_specs=(VMEM,) * len(shapes),
        scratch_shapes=[pltpu.VMEM(stack, F32)] * 2,
        compiler_params=PARAMS,
        cost_estimate=pl.CostEstimate(flops=2_000_000, bytes_accessed=4_000_000, transcendentals=0),
        name="prepare_depth",
    )(h)


def prepare_rest_kernel(*refs):
    fields, outs, natural, turned = refs[:4], refs[4:12], refs[12], refs[13]
    for f, src in enumerate(fields):
        lay_out(src, outs[2 * f], outs[2 * f + 1], natural.at[f % 2], turned.at[f % 2])


def prepare_rest(*fields):
    stack = (fields[0].shape[1], LANES)
    return pl.pallas_call(
        prepare_rest_kernel,
        out_shape=(shape(*stack),) * 8,
        in_specs=[VMEM] * 4,
        out_specs=(VMEM,) * 8,
        scratch_shapes=[pltpu.VMEM((2, *stack), F32)] * 2,
        compiler_params=PARAMS,
        cost_estimate=pl.CostEstimate(flops=2_000_000, bytes_accessed=6_000_000, transcendentals=0),
        name="prepare_rest",
    )(*fields)


def low_high(axis, near, far):
    index, count = lax.axis_index(axis), lax.axis_size(axis)
    even = index % 2 == 0
    low = jnp.where(index > 0, jnp.where(even, far, near), 0.0)
    high = jnp.where(index < count - 1, jnp.where(even, near, far), 0.0)
    return low, high


def half_slope(a, c):
    return 0.5 * (jnp.maximum(jnp.minimum(a, c), 0.0) + jnp.minimum(jnp.maximum(a, c), 0.0))


def face_flux(left, right, opened):
    is_open = opened > 0.5
    hl = jnp.where(is_open, left[0], 1.0)
    hr = jnp.where(is_open, right[0], 1.0)
    joint = 1.0 / (hl * hr)
    ul = left[1] * (hr * joint)
    ur = right[1] * (hl * joint)
    gl = gravity * hl
    gr = gravity * hr
    fastest = jnp.maximum(jnp.abs(ul) + gl * lax.rsqrt(gl), jnp.abs(ur) + gr * lax.rsqrt(gr))
    scale = (0.5 * ratio) * opened
    mass = (left[1] + right[1]) - fastest * (right[0] - left[0])
    push = 0.5 * (gl * hl + gr * hr) + left[1] * ul + right[1] * ur - fastest * (right[1] - left[1])
    shear = left[2] * ul + right[2] * ur - fastest * (right[2] - left[2])
    return scale * mass, scale * push, scale * shear


def extended(ref, tile, lows, highs):
    sub = row_index((SUB, LANES))
    out = {}
    for n, row in enumerate(lows, 1):
        value = ref[at(tile, STEPS - n), :]
        out[-n] = jnp.where(sub == 0, row, pltpu.roll(value, 1, 0))
    for n, row in enumerate(highs):
        value = ref[at(tile, n), :]
        out[STEPS + n] = jnp.where(sub == SUB - 1, row, pltpu.roll(value, SUB - 1, 0))
    return lambda k: out[k] if k in out else ref[at(tile, k), :]


def tile_fluxes(fields, bed, wet, store, start=0, stop=STEPS):
    def states(k):
        both = []
        for w in fields:
            here = w(k)
            both.append((here, half_slope(here - w(k - 1), w(k + 1) - here)))
        return [w + s for w, s in both], [w - s for w, s in both]

    left, _ = states(start - 1)
    before = None
    for k in range(start - 1, stop):
        left_next, right = states(k + 1)
        face = face_flux(left, right, wet(k) * wet(k + 1))
        left = left_next
        if k >= start:
            store(k, [a - c for a, c in zip(face, before)], bed(k + 1) - bed(k - 1))
        before = face


def march_source(inv_ref, scale, r_ref, t_ref, w_ref, s_ref, levels):
    count = inv_ref.shape[0] // STEPS
    c = jnp.zeros((count, LANES), F32)
    e = c
    for k in range(STEPS):
        inverse = full(inv_ref, k)
        c = c + e
        e = e + (scale * (inverse * inverse) * c - full(r_ref, k))
    sl = t_ref[0] * c
    s_ref[0] = sl
    sources = (sl, t_ref[2] * sl - e)
    for level in range(levels):
        after = tuple(pltpu.roll(v, count - (1 << level), 0) for v in sources)
        sources, middle = merge_sources(sources, after, tuple(w_ref[3 * level + j] for j in range(3)))
        s_ref[1 + level] = middle
    return sources


def flux_y_kernel(near, far, hy, py, qy, by, my, mass, shear, normal, across, along):
    tiles = hy.shape[0] // LANES
    low, high = low_high("gy", near[0:SUB, :], far[0:SUB, :])
    for tile in range(tiles):

        def extend(ref, row, layers):
            lows, highs = [], []
            for n in range(layers):
                last = at(tile - 1, STEPS - 1 - n).stop - 1
                first = at(tile + 1, n).start
                lows.append(low[row + layers - 1 - n : row + layers - n, :] if tile == 0 else ref[last : last + 1, :])
                highs.append(high[row + n : row + n + 1, :] if tile == tiles - 1 else ref[first : first + 1, :])
            return extended(ref, tile, lows, highs)

        def store(k, difference, bed):
            here, natural = at(tile, k), spread_rows(tile, k)
            across[natural, :] = difference[0]
            along[natural, :] = difference[2]
            pull = (0.5 * ratio * gravity) * hy[here, :]
            normal[here, :] = qy[here, :] - difference[1] - pull * bed

        tile_fluxes([extend(hy, 0, 2), extend(qy, 4, 2), extend(py, 2, 2)], extend(by, 6, 1), extend(my, 7, 1), store)
        span = tile_span(tile)
        mass[span, :] = across[span, :].T
        shear[span, :] = along[span, :].T


def fluxes_y(*arrays):
    stack = arrays[2].shape
    return pl.pallas_call(
        flux_y_kernel,
        out_shape=(shape(*stack),) * 3,
        in_specs=[VMEM] * len(arrays),
        out_specs=(VMEM,) * 3,
        scratch_shapes=[pltpu.VMEM(stack, F32)] * 2,
        compiler_params=PARAMS,
        cost_estimate=pl.CostEstimate(flops=4_000_000, bytes_accessed=4_000_000, transcendentals=0),
        name="fluxes_y",
    )(*arrays)


INNER = (2, STEPS - 2)
TALL = 16


def x_store(hx, px, mx, depth, push, across):
    def of_tile(tile):
        def store(k, difference, bed):
            here = at(tile, k)
            h = hx[here, :]
            depth[here, :] = h - mx[here, :] * difference[0]
            push[here, :] = px[here, :] - difference[1] - (0.5 * ratio * gravity) * h * bed
            across[here, :] = difference[2]

        return store

    return of_tile


def flux_x_inner_kernel(hx, px, qx, bx, mx, depth, push, across):
    store = x_store(hx, px, mx, depth, push, across)
    for tile in range(hx.shape[0] // LANES):
        fields = [extended(v, tile, (), ()) for v in (hx, px, qx, bx, mx)]
        tile_fluxes(fields[:3], fields[3], fields[4], store(tile), *INNER)
        for k in (*range(INNER[0]), *range(INNER[1], STEPS)):
            for ref in (depth, push, across):
                ref[at(tile, k), :] = jnp.zeros((SUB, LANES), F32)


def fluxes_x_inner(*arrays):
    stack = arrays[0].shape
    return pl.pallas_call(
        flux_x_inner_kernel,
        out_shape=(shape(*stack),) * 3,
        in_specs=[VMEM] * len(arrays),
        out_specs=(VMEM,) * 3,
        compiler_params=PARAMS,
        cost_estimate=pl.CostEstimate(flops=4_000_000, bytes_accessed=4_000_000, transcendentals=0),
        name="fluxes_x_inner",
    )(*arrays)


def flux_x_kernel(
    near, far, hx, px, qx, bx, mx, ix, shear_y, push_in, tx, wx, coef,
    depth, across, rx, sx, ends,
    push,
    *, inv_cx,
):
    tiles = hx.shape[0] // LANES
    low, high = low_high("gx", near[0], far[...])
    store = x_store(hx, px, mx, depth, push, across)
    for tile in range(tiles):
        span = tile_span(tile)

        def extend(ref, row, layers):
            lows = [low[row + layers - 1 - n : row + layers - n, span] for n in range(layers)]
            highs = [high[row + n : row + n + 1, span] for n in range(layers)]
            return extended(ref, tile, lows, highs)

        fields, bed, wet = [extend(hx, 0, 2), extend(px, 2, 2), extend(qx, 4, 2)], extend(bx, 6, 1), extend(mx, 7, 1)
        tile_fluxes(fields, bed, wet, store(tile), 0, INNER[0])
        tile_fluxes(fields, bed, wet, store(tile), INNER[1], STEPS)
        for k in range(STEPS):
            here = at(tile, k)
            inverse = ix[here, :]
            total = (push_in if INNER[0] <= k < INNER[1] else push)[here, :] - shear_y[here, :]
            rx[here, :] = (inv_cx * (inverse * inverse)) * mx[here, :] * total
    sources = march_source(ix, inv_cx, rx, tx, wx, sx, log2(SUB))
    count = tiles * LANES
    ends[0:1, 0 : 3 * count] = coef[...]
    for i in range(2):
        for tile in range(tiles):
            first = (3 + i) * count + tile * LANES
            ends[0:1, first : first + LANES] = sources[i][tile * SUB : tile * SUB + 1, :]


def fluxes_x(*arrays, inv_cx):
    stack = arrays[2].shape
    count = stack[0] // STEPS
    shapes = (
        shape(*stack),
        shape(*stack),
        shape(*stack),
        shape(1 + log2(SUB), count, LANES),
        shape(1, 5 * stack[0]),
    )
    return pl.pallas_call(
        functools.partial(flux_x_kernel, inv_cx=inv_cx),
        out_shape=shapes,
        in_specs=[VMEM] * len(arrays),
        out_specs=(VMEM,) * len(shapes),
        scratch_shapes=[pltpu.VMEM(stack, F32)],
        compiler_params=PARAMS,
        name="fluxes_x",
    )(*arrays)


def join_y_kernel(
    depth_inner, across_inner, depth_outer, across_outer, mass_y, mx, normal_y, iy, my, ty, wy, coef,
    depth, ry, sy, ends, tall,
    across, turned,
    *, inv_cy,
):
    tiles = mx.shape[0] // LANES
    for tile in range(tiles):
        span = tile_span(tile)
        for k in range(STEPS):
            here = at(tile, k)
            inner = INNER[0] <= k < INNER[1]
            across[here, :] = (across_inner if inner else across_outer)[here, :]
            depth[here, :] = (depth_inner if inner else depth_outer)[here, :] - mx[here, :] * mass_y[here, :]
        turned[span, :] = across[span, :].T
        for k in range(STEPS):
            here = at(tile, k)
            inverse = iy[here, :]
            total = normal_y[here, :] - turned[spread_rows(tile, k), :]
            ry[here, :] = (inv_cy * (inverse * inverse)) * my[here, :] * total
    sources = march_source(iy, inv_cy, ry, ty, wy, sy, log2(SUB * tiles))
    ends[0:1, 0 : 3 * LANES] = coef[...]
    for i in range(2):
        ends[0:1, (3 + i) * LANES : (4 + i) * LANES] = sources[i][0:1, :]
    tall[...] = jnp.zeros_like(tall)
    tall[0:1, 0 : 5 * LANES] = ends[...]


def join_y(*arrays, inv_cy):
    stack = arrays[0].shape
    count = stack[0] // STEPS
    shapes = (
        shape(*stack),
        shape(*stack),
        shape(1 + log2(count), count, LANES),
        shape(1, 5 * LANES),
        shape(1, TALL * LANES),
    )
    return pl.pallas_call(
        functools.partial(join_y_kernel, inv_cy=inv_cy),
        out_shape=shapes,
        in_specs=[VMEM] * len(arrays),
        out_specs=(VMEM,) * len(shapes),
        scratch_shapes=[pltpu.VMEM(stack, F32)] * 2,
        compiler_params=PARAMS,
        cost_estimate=pl.CostEstimate(flops=2_000_000, bytes_accessed=2_000_000, transcendentals=0),
        name="join_y",
    )(*arrays)


def tile_write(tiled, whole, tile, sems):
    rows = whole.shape[0]
    return pltpu.make_async_copy(
        tiled.at[pl.ds(tile * rows, rows), :], whole.at[:, pl.ds(tile * LANES, LANES)], sems.at[tile]
    )


def write_scratch(cols):
    return [pltpu.VMEM((cols, LANES), F32), pltpu.SemaphoreType.DMA((cols // LANES,))]


def depth_kernel(depth, out, natural, sems):
    writes = []
    for tile in range(depth.shape[0] // LANES):
        for k in range(STEPS):
            natural[spread_rows(tile, k), :] = depth[at(tile, k), :]
        writes.append(tile_write(natural, out, tile, sems))
        writes[-1].start()
    for write in writes:
        write.wait()


def write_depth(depth, block):
    return pl.pallas_call(
        depth_kernel,
        out_shape=shape(*block),
        in_specs=[VMEM],
        out_specs=ANY,
        scratch_shapes=write_scratch(block[1]),
        compiler_params=PARAMS,
        cost_estimate=pl.CostEstimate(flops=100_000, bytes_accessed=2_000_000, transcendentals=0),
        name="write_depth",
    )(depth)


def rows_of(ref, count):
    return tuple(ref[0:1, i * count : (i + 1) * count] for i in range(5))


def ordered(axis, stage, mine, theirs):
    is_low = (lax.axis_index(axis) >> stage) % 2 == 0
    one = tuple(jnp.where(is_low, a, b) for a, b in zip(mine, theirs))
    two = tuple(jnp.where(is_low, b, a) for a, b in zip(mine, theirs))
    return is_low, merge(one, two)


def merge_kernel(mine, theirs, *refs, axis, stage):
    out = refs[-1]
    count = mine.shape[1] // 5
    _, (merged, _) = ordered(axis, stage, rows_of(mine, count), rows_of(theirs, count))
    for i, v in enumerate(merged):
        out[0:1, i * v.shape[1] : (i + 1) * v.shape[1]] = v


def merge_call(axis, stage, mine, theirs, beside):
    return pl.pallas_call(
        functools.partial(merge_kernel, axis=axis, stage=stage),
        out_shape=shape(*mine.shape),
        in_specs=[VMEM] * (2 + len(beside)),
        out_specs=VMEM,
        compiler_params=PARAMS,
        name="merge",
    )(mine, theirs, *beside)


def line_ends(axis, refs, is_crossed=False):
    steps = []
    parts = [rows_of(ref, refs[0].shape[1] // 5) for ref in refs]
    stage = 0
    while len(parts) > 4:
        is_low, (_, weights) = ordered(axis, stage, *parts[:2])
        steps.append((is_low, weights))
        parts = parts[2:]
        stage += 1
    if is_crossed:
        lower = (lax.axis_index(axis) >> (stage + 1)) % 2 == 0
        both = list(zip(*parts[2:]))
        parts[2] = tuple(jnp.where(lower, a, b) for a, b in both)
        parts[3] = tuple(jnp.where(lower, b, a) for a, b in both)
    is_low, (own, weights) = ordered(axis, stage, *parts[:2])
    steps.append((is_low, weights))
    _, (other, _) = ordered(axis, stage, *parts[2:])
    is_low, (whole, weights) = ordered(axis, stage + 1, own, other)
    steps.append((is_low, weights))
    t, _, gr, _, sr = whole
    left = jnp.zeros_like(t)
    right = sr / (t + gr + 1.0)
    for is_low, (w1, w2, source) in reversed(steps):
        middle = w1 * left + w2 * right + source
        left = jnp.where(is_low, left, middle)
        right = jnp.where(is_low, middle, right)
    return left, right


def segment_ends(left, right, w_ref, s_ref, levels):
    index = row_index(left.shape)
    for level in reversed(range(levels)):
        stride = 1 << level
        middle = w_ref[3 * level] * left + w_ref[3 * level + 1] * right
        if s_ref is not None:
            middle = middle + s_ref[1 + level]
        upper = (index >> level) % 2 == 1
        left, right = (
            jnp.where(upper, pltpu.roll(middle, stride, 0), left),
            jnp.where(upper, pltpu.roll(right, stride, 0), middle),
        )
    return left, right


def march_values(left, right, t_ref, s_ref, inv_ref, scale, r_ref, store):
    value = left
    change = t_ref[0] * (right - left) - t_ref[1] * left
    if s_ref is not None:
        change = change - s_ref[0]
    for k in range(STEPS):
        inverse = full(inv_ref, k)
        value = value + change
        push = scale * (inverse * inverse) * value
        change = change + (push if r_ref is None else push - full(r_ref, k))
        store(k, value * inverse)


def rest_x_kernel(inv_ref, r_ref, t_ref, w_ref, s_ref, out, *, scale):
    tiles = out.shape[0] // LANES
    zero = jnp.zeros((tiles * SUB, LANES), F32)

    def store(k, speed):
        for tile in range(tiles):
            out[at(tile, k), :] = speed[tile * SUB : (tile + 1) * SUB, :]

    left, right = segment_ends(zero, zero, w_ref, s_ref, log2(SUB))
    march_values(left, right, t_ref, s_ref, inv_ref, scale, r_ref, store)


def rest_x(*pieces, scale):
    return pl.pallas_call(
        functools.partial(rest_x_kernel, scale=scale),
        out_shape=shape(*pieces[0].shape),
        in_specs=[VMEM] * len(pieces),
        out_specs=VMEM,
        compiler_params=PARAMS,
        cost_estimate=pl.CostEstimate(flops=1_000_000, bytes_accessed=2_000_000, transcendentals=0),
        name="rest_x",
    )(*pieces)


def solve_x_kernel(from_left, from_right, rest, *refs):
    parts, (out, natural, sems) = refs[:-3], refs[-3:]
    left, right = line_ends("gx", parts, True)
    writes = []
    for tile in range(out.shape[1] // LANES):
        span = tile_span(tile)
        for k in range(STEPS):
            here = at(tile, k)
            natural[spread_rows(tile, k), :] = (
                from_left[here, :] * left[:, span] + from_right[here, :] * right[:, span] + rest[here, :]
            )
        writes.append(tile_write(natural, out, tile, sems))
        writes[-1].start()
    for write in writes:
        write.wait()


def solve_y_kernel(inv_ref, r_ref, t_ref, w_ref, s_ref, *refs, scale):
    parts, (out, natural, sems, turned) = refs[:-4], refs[-4:]
    tiles = out.shape[1] // LANES
    ends = line_ends("gy", parts)
    ends = [jnp.broadcast_to(row, (tiles * SUB, LANES)) for row in ends]
    left, right = segment_ends(*ends, w_ref, s_ref, log2(tiles * SUB))

    def store(k, speed):
        for tile in range(tiles):
            turned[spread_rows(tile, k), :] = speed[tile * SUB : (tile + 1) * SUB, :]

    march_values(left, right, t_ref, s_ref, inv_ref, scale, r_ref, store)
    writes = []
    for tile in range(tiles):
        block = turned[tile_span(tile), :].T
        for k in range(STEPS):
            natural[spread_rows(tile, k), :] = block[k * SUB : (k + 1) * SUB, :]
        writes.append(tile_write(natural, out, tile, sems))
        writes[-1].start()
    for write in writes:
        write.wait()


def solve(kernel, name, pieces, parts, block, extra=()):
    return pl.pallas_call(
        kernel,
        out_shape=shape(*block),
        in_specs=[VMEM] * (len(pieces) + len(parts)),
        out_specs=ANY,
        scratch_shapes=write_scratch(block[1]) + list(extra),
        compiler_params=PARAMS,
        cost_estimate=pl.CostEstimate(flops=1_000_000, bytes_accessed=4_000_000, transcendentals=0),
        name=name,
    )(*pieces, *parts)


def hand_on(value, axis):
    count = lax.axis_size(axis)
    far = [i + 2 if i % 2 == 0 else i - 2 for i in range(count)]
    return lax.ppermute(value, axis, [(i, t if 0 <= t < count else i ^ 1) for i, t in enumerate(far)])


def shift_pair(value, axis):
    count = lax.axis_size(axis)
    other = [((i - 1) ^ 1) + 1 for i in range(count)]
    return lax.ppermute(value, axis, [(i, o if 0 <= o < count else i) for i, o in enumerate(other)])


def cross(value, axis, mask):
    return lax.ppermute(value, axis, [(i, i ^ mask) for i in range(lax.axis_size(axis))])


def crossed(value, axis, stage, half):
    pairs = []
    for i in range(lax.axis_size(axis)):
        upper = (i >> (stage + 1)) & 1
        pairs.append((i, i ^ ((2 if upper == half else 3) << stage)))
    return lax.ppermute(value, axis, pairs)


def parts_of_line(axis, mine, relay, beside=(), tall=None):
    parts = []
    last = log2(lax.axis_size(axis)) - 2
    for stage in range(last):
        theirs = cross(mine, axis, 1 << stage)
        parts += [mine, theirs]
        mine = merge_call(axis, stage, mine, theirs, beside)
    if relay:
        first = cross(mine, axis, 1 << last)
        second = cross(mine if tall is None else tall, axis, 2 << last)
        both = cross(second[:, 0 : mine.shape[1]], axis, 1 << last)
    else:
        first = cross(mine, axis, 1 << last)
        second, both = (crossed(mine, axis, last, n) for n in (1, 0))
    return parts + [mine, first, second, both]


def on_device(h, p, q, b, m):
    block = h.shape
    rows, cols = block
    inv_cx = 3.0 / (rows * lax.axis_size("gx") / 4.0) ** 2
    inv_cy = 3.0 / (cols * lax.axis_size("gy") / 4.0) ** 2
    slabs_x = pack_x(h, p, q, b, m)
    near_x = cross(slabs_x, "gx", 1)
    near_y, far_y = pack_y(h, p, q, b, m, after=slabs_x)
    near_y, far_y = cross(near_y, "gy", 1), shift_pair(far_y, "gy")
    hx, hy, ix, iy, tx, wx, ty, wy, coef_x, coef_y, left_x, right_x = prepare_depth(h, inv_cx, inv_cy)
    far_x = hand_on(second_of(near_x, coef_x, near_y), "gx")
    px, py, qx, qy, bx, by, mx, my = prepare_rest(p, q, b, m)
    depth_inner, push_inner, across_inner = fluxes_x_inner(hx, px, qx, bx, mx)
    mass_y, shear_y, normal_y = fluxes_y(near_y, far_y, hy, py, qy, by, my)
    depth_outer, across_outer, rx, sx, end_x = fluxes_x(
        near_x, far_x, hx, px, qx, bx, mx, ix, shear_y, push_inner, tx, wx, coef_x, inv_cx=inv_cx
    )
    depth, ry, sy, end_y, tall_y = join_y(
        depth_inner, across_inner, depth_outer, across_outer, mass_y, mx, normal_y, iy, my, ty, wy, coef_y, inv_cy=inv_cy
    )
    new_depth = write_depth(depth, block)
    parts_y = parts_of_line("gy", end_y, True, tall=tall_y if lax.axis_size("gy") == 4 else None)
    parts_x = parts_of_line("gx", end_x, False, parts_y[1:2])
    turned = [pltpu.VMEM((cols, LANES), F32)]
    solve_y_scaled = functools.partial(solve_y_kernel, scale=inv_cy)
    vy = solve(solve_y_scaled, "solve_y", (iy, ry, ty, wy, sy), parts_y, block, turned)
    own_x = rest_x(ix, rx, tx, wx, sx, scale=inv_cx)
    vx = solve(solve_x_kernel, "solve_x", (left_x, right_x, own_x), parts_x, block)
    return new_depth, vx, vy


def solution(mesh):
    spec = P("gx", "gy")
    return jax.shard_map(
        on_device,
        mesh=mesh,
        in_specs=(spec,) * 5,
        out_specs=(spec,) * 3,
        check_vma=False,
    )
```

```python
import functools

import jax
import jax.numpy as jnp
from jax import lax
from jax.experimental import pallas as pl
from jax.experimental.pallas import tpu as pltpu
from jax.sharding import PartitionSpec as P

gravity = 9.81
ratio = 0.05
LANES = 128
SUB = 8
STEPS = LANES // SUB
F32 = jnp.float32
VMEM = pl.BlockSpec(memory_space=pltpu.VMEM)
HBM = pl.BlockSpec(memory_space=pltpu.HBM)
ANY = pl.BlockSpec(memory_space=pl.ANY)
PARAMS = pltpu.CompilerParams(vmem_limit_bytes=16 * 1024 * 1024)


def lane_index(shape):
    return lax.broadcasted_iota(jnp.int32, shape, len(shape) - 1)


def row_index(shape):
    return lax.broadcasted_iota(jnp.int32, shape, len(shape) - 2)


def at(tile, step):
    first = tile * LANES + step * SUB
    return slice(first, first + SUB)


def tile_span(tile):
    return slice(tile * LANES, (tile + 1) * LANES)


def spread_rows(tile, step):
    return pl.ds(tile * LANES + step, SUB, stride=STEPS)


def shape(*dims):
    return jax.ShapeDtypeStruct(dims, F32)


def pack_x_kernel(h, p, q, b, m, slabs, top, bottom, itop, ibottom, sems):
    rows = h.shape[0]
    copies = []
    for f, src in enumerate((h, p, q, b, m)):
        for side, (target, whole, row) in enumerate(((top, itop, 0), (bottom, ibottom, rows - SUB))):
            copy = pltpu.make_async_copy(
                src.at[pl.ds(row, SUB), :], target.at[f] if f < 4 else whole, sems.at[2 * f + side]
            )
            copy.start()
            copies.append(copy)
    for copy in copies:
        copy.wait()
    first = jnp.concatenate(
        [top[0, 0:2, :], top[1, 0:2, :], top[2, 0:2, :], top[3, 0:1, :], itop[0:1, :].astype(F32)]
    )
    last = jnp.concatenate(
        [
            bottom[0, SUB - 2 : SUB, :],
            bottom[1, SUB - 2 : SUB, :],
            bottom[2, SUB - 2 : SUB, :],
            bottom[3, SUB - 1 : SUB, :],
            ibottom[SUB - 1 : SUB, :].astype(F32),
        ]
    )
    even = lax.axis_index("gx") % 2 == 0
    slabs[0] = jnp.where(even, last, first)
    slabs[1] = jnp.where(even, first, last)


def pack_x(*fields):
    cols = fields[0].shape[1]
    return pl.pallas_call(
        pack_x_kernel,
        out_shape=shape(2, SUB, cols),
        in_specs=[HBM] * 5,
        out_specs=VMEM,
        scratch_shapes=[
            pltpu.VMEM((4, SUB, cols), F32),
            pltpu.VMEM((4, SUB, cols), F32),
            pltpu.VMEM((SUB, cols), jnp.int32),
            pltpu.VMEM((SUB, cols), jnp.int32),
            pltpu.SemaphoreType.DMA((10,)),
        ],
        compiler_params=PARAMS,
        name="pack_x",
    )(*[pltpu.with_memory_space_constraint(v, pltpu.HBM) for v in fields])


def pack_y_kernel(h, p, q, b, m, _, near, far, natural):
    rows, cols = h.shape
    lane = lane_index((rows, LANES))
    out = None
    for f, src in enumerate((h, p, q, b, m)):
        both = jnp.where(lane < LANES // 2, src[:, 0:LANES], src[:, cols - LANES : cols]).astype(F32)
        moved = pltpu.roll(both, 4 * f + 2, 1)
        out = moved if out is None else jnp.where(lane >= 4 * f, moved, out)
    natural[...] = out
    turned = jnp.concatenate([natural[spread_rows(0, k), :] for k in range(STEPS)]).T
    last = jnp.concatenate([turned[0:2], turned[4:6], turned[8:10], turned[13:14], turned[17:18]])
    first = jnp.concatenate([turned[2:4], turned[6:8], turned[10:12], turned[14:15], turned[18:19]])
    even = lax.axis_index("gy") % 2 == 0
    for slab, value in ((near, jnp.where(even, last, first)), (far, jnp.where(even, first, last))):
        slab[...] = jnp.zeros_like(slab)
        slab[0:SUB, :] = value


def pack_y(*fields, after):
    rows = fields[0].shape[0]
    return pl.pallas_call(
        pack_y_kernel,
        out_shape=(shape(1 * SUB, rows), shape(4 * SUB, rows)),
        in_specs=[VMEM] * 6,
        out_specs=(VMEM, VMEM),
        scratch_shapes=[pltpu.VMEM((rows, LANES), F32)],
        compiler_params=PARAMS,
        cost_estimate=pl.CostEstimate(flops=500_000, bytes_accessed=1_000_000, transcendentals=0),
        name="pack_y",
    )(*fields, after)


def tie_kernel(both, *refs):
    refs[-1][...] = both[1]


def second_of(both, *after):
    return pl.pallas_call(
        tie_kernel,
        out_shape=shape(*both.shape[1:]),
        in_specs=[VMEM] * (1 + len(after)),
        out_specs=VMEM,
        compiler_params=PARAMS,
        name="second_of",
    )(both, *after)


def merge_coefficients(one, two):
    t1, gl1, gr1 = one
    t2, gl2, gr2 = two
    shunt = gr1 + gl2
    inverse = 1.0 / (t1 + t2 + shunt)
    w1, w2 = t1 * inverse, t2 * inverse
    return (w1 * t2, gl1 + w1 * shunt, gr2 + w2 * shunt), (w1, w2, inverse)


def merge_sources(one, two, weights):
    w1, w2, inverse = weights
    source = one[1] - two[0]
    return (one[0] - w1 * source, two[1] + w2 * source), source * inverse


def merge(one, two):
    coefficients, weights = merge_coefficients(one[:3], two[:3])
    sources, middle = merge_sources(one[3:], two[3:], weights)
    return coefficients + sources, weights[:2] + (middle,)


def log2(count):
    return (count - 1).bit_length()


def full(ref, step):
    return jnp.concatenate([ref[at(tile, step), :] for tile in range(ref.shape[0] // LANES)])


def march_depth(inv_ref, scale, out_t, out_w, levels):
    count = inv_ref.shape[0] // STEPS
    zero = jnp.zeros((count, LANES), F32)
    alpha, gamma, beta, delta = zero, zero, zero, zero
    for k in range(STEPS):
        inverse = full(inv_ref, k)
        d = scale * (inverse * inverse)
        alpha = alpha + gamma
        gamma = gamma + d * (1.0 + alpha)
        beta = beta + delta
        delta = delta + d * ((k + 1.0) + beta)
    t = 1.0 / (STEPS + beta)
    out_t[0] = t
    out_t[1] = t * alpha
    out_t[2] = 1.0 + delta
    coefficients = (t, t * alpha, t * delta)
    for level in range(levels):
        after = tuple(pltpu.roll(v, count - (1 << level), 0) for v in coefficients)
        coefficients, weights = merge_coefficients(coefficients, after)
        for j, v in enumerate(weights):
            out_w[3 * level + j] = v
    return coefficients


def lay_out(src, xs, ys, natural, turned):
    for tile in range(xs.shape[0] // LANES):
        natural[tile_span(tile), :] = src[:, tile_span(tile)].astype(F32)
        for k in range(STEPS):
            xs[at(tile, k), :] = natural[spread_rows(tile, k), :]
        turned[tile_span(tile), :] = xs[tile_span(tile), :].T
        for k in range(STEPS):
            ys[at(tile, k), :] = turned[spread_rows(tile, k), :]


def prepare_depth_kernel(
    h, hx, hy, ix, iy, tx, wx, ty, wy, endx, endy, from_left, from_right, natural, turned, *, inv_cx, inv_cy
):
    tiles = hx.shape[0] // LANES
    lay_out(h, hx, hy, natural, turned)
    ix[...] = 1.0 / hx[...]
    iy[...] = 1.0 / hy[...]
    ends_x = march_depth(ix, inv_cx, tx, wx, log2(SUB))
    ends_y = march_depth(iy, inv_cy, ty, wy, log2(SUB * tiles))
    for i in range(3):
        for tile in range(tiles):
            first = (i * tiles + tile) * LANES
            endx[0:1, first : first + LANES] = ends_x[i][tile * SUB : tile * SUB + 1, :]
        endy[0:1, i * LANES : (i + 1) * LANES] = ends_y[i][0:1, :]
    one = jnp.ones((tiles * SUB, LANES), F32)
    zero = jnp.zeros_like(one)
    for out, left, right in ((from_left, one, zero), (from_right, zero, one)):

        def store(k, speed):
            for tile in range(tiles):
                out[at(tile, k), :] = speed[tile * SUB : (tile + 1) * SUB, :]

        left, right = segment_ends(left, right, wx, None, log2(SUB))
        march_values(left, right, tx, None, ix, inv_cx, None, store)


def prepare_depth(h, inv_cx, inv_cy):
    stack = (h.shape[1], LANES)
    count = stack[0] // STEPS
    shapes = [shape(*stack)] * 4 + [
        shape(3, count, LANES),
        shape(3 * log2(SUB), count, LANES),
        shape(3, count, LANES),
        shape(3 * log2(count), count, LANES),
        shape(1, 3 * stack[0]),
        shape(1, 3 * LANES),
        shape(*stack),
        shape(*stack),
    ]
    return pl.pallas_call(
        functools.partial(prepare_depth_kernel, inv_cx=inv_cx, inv_cy=inv_cy),
        out_shape=tuple(shapes),
        in_specs=[VMEM],
        out_specs=(VMEM,) * len(shapes),
        scratch_shapes=[pltpu.VMEM(stack, F32)] * 2,
        compiler_params=PARAMS,
        cost_estimate=pl.CostEstimate(flops=2_000_000, bytes_accessed=4_000_000, transcendentals=0),
        name="prepare_depth",
    )(h)


def prepare_rest_kernel(*refs):
    fields, outs, natural, turned = refs[:4], refs[4:12], refs[12], refs[13]
    for f, src in enumerate(fields):
        lay_out(src, outs[2 * f], outs[2 * f + 1], natural.at[f % 2], turned.at[f % 2])


def prepare_rest(*fields):
    stack = (fields[0].shape[1], LANES)
    return pl.pallas_call(
        prepare_rest_kernel,
        out_shape=(shape(*stack),) * 8,
        in_specs=[VMEM] * 4,
        out_specs=(VMEM,) * 8,
        scratch_shapes=[pltpu.VMEM((2, *stack), F32)] * 2,
        compiler_params=PARAMS,
        cost_estimate=pl.CostEstimate(flops=2_000_000, bytes_accessed=6_000_000, transcendentals=0),
        name="prepare_rest",
    )(*fields)


def low_high(axis, near, far):
    index, count = lax.axis_index(axis), lax.axis_size(axis)
    even = index % 2 == 0
    low = jnp.where(index > 0, jnp.where(even, far, near), 0.0)
    high = jnp.where(index < count - 1, jnp.where(even, near, far), 0.0)
    return low, high


def half_slope(a, c):
    return 0.5 * (jnp.maximum(jnp.minimum(a, c), 0.0) + jnp.minimum(jnp.maximum(a, c), 0.0))


def face_flux(left, right, opened):
    is_open = opened > 0.5
    hl = jnp.where(is_open, left[0], 1.0)
    hr = jnp.where(is_open, right[0], 1.0)
    joint = 1.0 / (hl * hr)
    ul = left[1] * (hr * joint)
    ur = right[1] * (hl * joint)
    gl = gravity * hl
    gr = gravity * hr
    fastest = jnp.maximum(jnp.abs(ul) + gl * lax.rsqrt(gl), jnp.abs(ur) + gr * lax.rsqrt(gr))
    scale = (0.5 * ratio) * opened
    mass = (left[1] + right[1]) - fastest * (right[0] - left[0])
    push = 0.5 * (gl * hl + gr * hr) + left[1] * ul + right[1] * ur - fastest * (right[1] - left[1])
    shear = left[2] * ul + right[2] * ur - fastest * (right[2] - left[2])
    return scale * mass, scale * push, scale * shear


def extended(ref, tile, lows, highs):
    sub = row_index((SUB, LANES))
    out = {}
    for n, row in enumerate(lows, 1):
        value = ref[at(tile, STEPS - n), :]
        out[-n] = jnp.where(sub == 0, row, pltpu.roll(value, 1, 0))
    for n, row in enumerate(highs):
        value = ref[at(tile, n), :]
        out[STEPS + n] = jnp.where(sub == SUB - 1, row, pltpu.roll(value, SUB - 1, 0))
    return lambda k: out[k] if k in out else ref[at(tile, k), :]


def tile_fluxes(fields, bed, wet, store, start=0, stop=STEPS, low_face=None, high_face=None):
    def states(k):
        both = []
        for w in fields:
            here = w(k)
            both.append((here, half_slope(here - w(k - 1), w(k + 1) - here)))
        return [w + s for w, s in both], [w - s for w, s in both]

    left, before, first = None, None, None
    for k in range(start - 1, stop):
        if k == start - 1 and low_face is not None:
            face = low_face
        elif k == stop - 1 and high_face is not None:
            face = high_face
        else:
            if left is None:
                left, _ = states(k)
            left_next, right = states(k + 1)
            face = face_flux(left, right, wet(k) * wet(k + 1))
            left = left_next
        if k >= start:
            store(k, [a - c for a, c in zip(face, before)], bed(k + 1) - bed(k - 1))
        first = face if first is None else first
        before = face
    return first, before


def march_source(inv_ref, scale, r_ref, t_ref, w_ref, s_ref, levels):
    count = inv_ref.shape[0] // STEPS
    c = jnp.zeros((count, LANES), F32)
    e = c
    for k in range(STEPS):
        inverse = full(inv_ref, k)
        c = c + e
        e = e + (scale * (inverse * inverse) * c - full(r_ref, k))
    sl = t_ref[0] * c
    s_ref[0] = sl
    sources = (sl, t_ref[2] * sl - e)
    for level in range(levels):
        after = tuple(pltpu.roll(v, count - (1 << level), 0) for v in sources)
        sources, middle = merge_sources(sources, after, tuple(w_ref[3 * level + j] for j in range(3)))
        s_ref[1 + level] = middle
    return sources


def flux_y_kernel(near, far, hy, py, qy, by, my, mass, shear, normal, across, along):
    tiles = hy.shape[0] // LANES
    low, high = low_high("gy", near[0:SUB, :], far[0:SUB, :])
    for tile in range(tiles):

        def extend(ref, row, layers):
            lows, highs = [], []
            for n in range(layers):
                last = at(tile - 1, STEPS - 1 - n).stop - 1
                first = at(tile + 1, n).start
                lows.append(low[row + layers - 1 - n : row + layers - n, :] if tile == 0 else ref[last : last + 1, :])
                highs.append(high[row + n : row + n + 1, :] if tile == tiles - 1 else ref[first : first + 1, :])
            return extended(ref, tile, lows, highs)

        def store(k, difference, bed):
            here, natural = at(tile, k), spread_rows(tile, k)
            across[natural, :] = difference[0]
            along[natural, :] = difference[2]
            pull = (0.5 * ratio * gravity) * hy[here, :]
            normal[here, :] = qy[here, :] - difference[1] - pull * bed

        tile_fluxes([extend(hy, 0, 2), extend(qy, 4, 2), extend(py, 2, 2)], extend(by, 6, 1), extend(my, 7, 1), store)
        span = tile_span(tile)
        mass[span, :] = across[span, :].T
        shear[span, :] = along[span, :].T


def fluxes_y(*arrays):
    stack = arrays[2].shape
    return pl.pallas_call(
        flux_y_kernel,
        out_shape=(shape(*stack),) * 3,
        in_specs=[VMEM] * len(arrays),
        out_specs=(VMEM,) * 3,
        scratch_shapes=[pltpu.VMEM(stack, F32)] * 2,
        compiler_params=PARAMS,
        cost_estimate=pl.CostEstimate(flops=4_000_000, bytes_accessed=4_000_000, transcendentals=0),
        name="fluxes_y",
    )(*arrays)


INNER = (2, STEPS - 2)
TALL = 16


def x_store(hx, px, mx, depth, push, across):
    def of_tile(tile):
        def store(k, difference, bed):
            here = at(tile, k)
            h = hx[here, :]
            depth[here, :] = h - mx[here, :] * difference[0]
            push[here, :] = px[here, :] - difference[1] - (0.5 * ratio * gravity) * h * bed
            across[here, :] = difference[2]

        return store

    return of_tile


def flux_x_inner_kernel(hx, px, qx, bx, mx, depth, push, across, faces):
    store = x_store(hx, px, mx, depth, push, across)
    for tile in range(hx.shape[0] // LANES):
        fields = [extended(v, tile, (), ()) for v in (hx, px, qx, bx, mx)]
        ends = tile_fluxes(fields[:3], fields[3], fields[4], store(tile), *INNER)
        for n, v in enumerate(ends[0] + ends[1]):
            faces[n, tile * SUB : (tile + 1) * SUB, :] = v
        for k in (*range(INNER[0]), *range(INNER[1], STEPS)):
            for ref in (depth, push, across):
                ref[at(tile, k), :] = jnp.zeros((SUB, LANES), F32)


def fluxes_x_inner(*arrays):
    stack = arrays[0].shape
    return pl.pallas_call(
        flux_x_inner_kernel,
        out_shape=(shape(*stack),) * 3 + (shape(6, stack[0] // STEPS, LANES),),
        in_specs=[VMEM] * len(arrays),
        out_specs=(VMEM,) * 4,
        compiler_params=PARAMS,
        cost_estimate=pl.CostEstimate(flops=4_000_000, bytes_accessed=4_000_000, transcendentals=0),
        name="fluxes_x_inner",
    )(*arrays)


def flux_x_kernel(
    near, far, hx, px, qx, bx, mx, ix, shear_y, push_in, faces, tx, wx, coef,
    depth, across, rx, sx, ends,
    push,
    *, inv_cx,
):
    tiles = hx.shape[0] // LANES
    low, high = low_high("gx", near[0], far[...])
    store = x_store(hx, px, mx, depth, push, across)
    for tile in range(tiles):
        span = tile_span(tile)

        def extend(ref, row, layers):
            lows = [low[row + layers - 1 - n : row + layers - n, span] for n in range(layers)]
            highs = [high[row + n : row + n + 1, span] for n in range(layers)]
            return extended(ref, tile, lows, highs)

        fields, bed, wet = [extend(hx, 0, 2), extend(px, 2, 2), extend(qx, 4, 2)], extend(bx, 6, 1), extend(mx, 7, 1)
        known = [faces[n, tile * SUB : (tile + 1) * SUB, :] for n in range(6)]
        tile_fluxes(fields, bed, wet, store(tile), 0, INNER[0], high_face=known[:3])
        tile_fluxes(fields, bed, wet, store(tile), INNER[1], STEPS, low_face=known[3:])
        for k in range(STEPS):
            here = at(tile, k)
            inverse = ix[here, :]
            total = (push_in if INNER[0] <= k < INNER[1] else push)[here, :] - shear_y[here, :]
            rx[here, :] = (inv_cx * (inverse * inverse)) * mx[here, :] * total
    sources = march_source(ix, inv_cx, rx, tx, wx, sx, log2(SUB))
    count = tiles * LANES
    ends[0:1, 0 : 3 * count] = coef[...]
    for i in range(2):
        for tile in range(tiles):
            first = (3 + i) * count + tile * LANES
            ends[0:1, first : first + LANES] = sources[i][tile * SUB : tile * SUB + 1, :]


def fluxes_x(*arrays, inv_cx):
    stack = arrays[2].shape
    count = stack[0] // STEPS
    shapes = (
        shape(*stack),
        shape(*stack),
        shape(*stack),
        shape(1 + log2(SUB), count, LANES),
        shape(1, 5 * stack[0]),
    )
    return pl.pallas_call(
        functools.partial(flux_x_kernel, inv_cx=inv_cx),
        out_shape=shapes,
        in_specs=[VMEM] * len(arrays),
        out_specs=(VMEM,) * len(shapes),
        scratch_shapes=[pltpu.VMEM(stack, F32)],
        compiler_params=PARAMS,
        name="fluxes_x",
    )(*arrays)


def join_y_kernel(
    depth_inner, across_inner, depth_outer, across_outer, mass_y, mx, normal_y, iy, my, ty, wy, coef,
    depth, ry, sy, ends, tall,
    across, turned,
    *, inv_cy,
):
    tiles = mx.shape[0] // LANES
    for tile in range(tiles):
        span = tile_span(tile)
        for k in range(STEPS):
            here = at(tile, k)
            inner = INNER[0] <= k < INNER[1]
            across[here, :] = (across_inner if inner else across_outer)[here, :]
            depth[here, :] = (depth_inner if inner else depth_outer)[here, :] - mx[here, :] * mass_y[here, :]
        turned[span, :] = across[span, :].T
        for k in range(STEPS):
            here = at(tile, k)
            inverse = iy[here, :]
            total = normal_y[here, :] - turned[spread_rows(tile, k), :]
            ry[here, :] = (inv_cy * (inverse * inverse)) * my[here, :] * total
    sources = march_source(iy, inv_cy, ry, ty, wy, sy, log2(SUB * tiles))
    ends[0:1, 0 : 3 * LANES] = coef[...]
    for i in range(2):
        ends[0:1, (3 + i) * LANES : (4 + i) * LANES] = sources[i][0:1, :]
    tall[...] = jnp.zeros_like(tall)
    tall[0:1, 0 : 5 * LANES] = ends[...]


def join_y(*arrays, inv_cy):
    stack = arrays[0].shape
    count = stack[0] // STEPS
    shapes = (
        shape(*stack),
        shape(*stack),
        shape(1 + log2(count), count, LANES),
        shape(1, 5 * LANES),
        shape(1, TALL * LANES),
    )
    return pl.pallas_call(
        functools.partial(join_y_kernel, inv_cy=inv_cy),
        out_shape=shapes,
        in_specs=[VMEM] * len(arrays),
        out_specs=(VMEM,) * len(shapes),
        scratch_shapes=[pltpu.VMEM(stack, F32)] * 2,
        compiler_params=PARAMS,
        cost_estimate=pl.CostEstimate(flops=2_000_000, bytes_accessed=2_000_000, transcendentals=0),
        name="join_y",
    )(*arrays)


PARTS = 2


def tile_writes(tiled, whole, tile, sems):
    rows = whole.shape[0]
    part = rows // PARTS
    copies = []
    for n in range(PARTS):
        copy = pltpu.make_async_copy(
            tiled.at[pl.ds(tile * rows + n * part, part), :],
            whole.at[pl.ds(n * part, part), pl.ds(tile * LANES, LANES)],
            sems.at[tile, n],
        )
        copy.start()
        copies.append(copy)
    return copies


def write_scratch(cols):
    return [pltpu.VMEM((cols, LANES), F32), pltpu.SemaphoreType.DMA((cols // LANES, PARTS))]


def depth_kernel(depth, out, natural, sems):
    writes = []
    for tile in range(depth.shape[0] // LANES):
        for k in range(STEPS):
            natural[spread_rows(tile, k), :] = depth[at(tile, k), :]
        writes += tile_writes(natural, out, tile, sems)
    for write in writes:
        write.wait()


def write_depth(depth, block):
    return pl.pallas_call(
        depth_kernel,
        out_shape=shape(*block),
        in_specs=[VMEM],
        out_specs=ANY,
        scratch_shapes=write_scratch(block[1]),
        compiler_params=PARAMS,
        cost_estimate=pl.CostEstimate(flops=100_000, bytes_accessed=2_000_000, transcendentals=0),
        name="write_depth",
    )(depth)


def rows_of(ref, count):
    return tuple(ref[0:1, i * count : (i + 1) * count] for i in range(5))


def ordered(axis, stage, mine, theirs):
    is_low = (lax.axis_index(axis) >> stage) % 2 == 0
    one = tuple(jnp.where(is_low, a, b) for a, b in zip(mine, theirs))
    two = tuple(jnp.where(is_low, b, a) for a, b in zip(mine, theirs))
    return is_low, merge(one, two)


def merge_kernel(mine, theirs, *refs, axis, stage):
    out = refs[-1]
    count = mine.shape[1] // 5
    _, (merged, _) = ordered(axis, stage, rows_of(mine, count), rows_of(theirs, count))
    for i, v in enumerate(merged):
        out[0:1, i * v.shape[1] : (i + 1) * v.shape[1]] = v


def merge_call(axis, stage, mine, theirs, beside):
    return pl.pallas_call(
        functools.partial(merge_kernel, axis=axis, stage=stage),
        out_shape=shape(*mine.shape),
        in_specs=[VMEM] * (2 + len(beside)),
        out_specs=VMEM,
        compiler_params=PARAMS,
        name="merge",
    )(mine, theirs, *beside)


def line_ends(axis, refs, is_crossed=False):
    steps = []
    parts = [rows_of(ref, refs[0].shape[1] // 5) for ref in refs]
    stage = 0
    while len(parts) > 4:
        is_low, (_, weights) = ordered(axis, stage, *parts[:2])
        steps.append((is_low, weights))
        parts = parts[2:]
        stage += 1
    if is_crossed:
        lower = (lax.axis_index(axis) >> (stage + 1)) % 2 == 0
        both = list(zip(*parts[2:]))
        parts[2] = tuple(jnp.where(lower, a, b) for a, b in both)
        parts[3] = tuple(jnp.where(lower, b, a) for a, b in both)
    is_low, (own, weights) = ordered(axis, stage, *parts[:2])
    steps.append((is_low, weights))
    _, (other, _) = ordered(axis, stage, *parts[2:])
    is_low, (whole, weights) = ordered(axis, stage + 1, own, other)
    steps.append((is_low, weights))
    t, _, gr, _, sr = whole
    left = jnp.zeros_like(t)
    right = sr / (t + gr + 1.0)
    for is_low, (w1, w2, source) in reversed(steps):
        middle = w1 * left + w2 * right + source
        left = jnp.where(is_low, left, middle)
        right = jnp.where(is_low, middle, right)
    return left, right


def segment_ends(left, right, w_ref, s_ref, levels):
    index = row_index(left.shape)
    for level in reversed(range(levels)):
        stride = 1 << level
        middle = w_ref[3 * level] * left + w_ref[3 * level + 1] * right
        if s_ref is not None:
            middle = middle + s_ref[1 + level]
        upper = (index >> level) % 2 == 1
        left, right = (
            jnp.where(upper, pltpu.roll(middle, stride, 0), left),
            jnp.where(upper, pltpu.roll(right, stride, 0), middle),
        )
    return left, right


def march_values(left, right, t_ref, s_ref, inv_ref, scale, r_ref, store):
    value = left
    change = t_ref[0] * (right - left) - t_ref[1] * left
    if s_ref is not None:
        change = change - s_ref[0]
    for k in range(STEPS):
        inverse = full(inv_ref, k)
        value = value + change
        push = scale * (inverse * inverse) * value
        change = change + (push if r_ref is None else push - full(r_ref, k))
        store(k, value * inverse)


def rest_x_kernel(inv_ref, r_ref, t_ref, w_ref, s_ref, out, *, scale):
    tiles = out.shape[0] // LANES
    zero = jnp.zeros((tiles * SUB, LANES), F32)

    def store(k, speed):
        for tile in range(tiles):
            out[at(tile, k), :] = speed[tile * SUB : (tile + 1) * SUB, :]

    left, right = segment_ends(zero, zero, w_ref, s_ref, log2(SUB))
    march_values(left, right, t_ref, s_ref, inv_ref, scale, r_ref, store)


def rest_x(*pieces, scale):
    return pl.pallas_call(
        functools.partial(rest_x_kernel, scale=scale),
        out_shape=shape(*pieces[0].shape),
        in_specs=[VMEM] * len(pieces),
        out_specs=VMEM,
        compiler_params=PARAMS,
        cost_estimate=pl.CostEstimate(flops=1_000_000, bytes_accessed=2_000_000, transcendentals=0),
        name="rest_x",
    )(*pieces)


def solve_x_kernel(from_left, from_right, rest, *refs):
    parts, (out, natural, sems) = refs[:-3], refs[-3:]
    left, right = line_ends("gx", parts, True)
    writes = []
    for tile in range(out.shape[1] // LANES):
        span = tile_span(tile)
        for k in range(STEPS):
            here = at(tile, k)
            natural[spread_rows(tile, k), :] = (
                from_left[here, :] * left[:, span] + from_right[here, :] * right[:, span] + rest[here, :]
            )
        writes += tile_writes(natural, out, tile, sems)
    for write in writes:
        write.wait()


def solve_y_kernel(inv_ref, r_ref, t_ref, w_ref, s_ref, *refs, scale):
    parts, (out, natural, sems, turned) = refs[:-4], refs[-4:]
    tiles = out.shape[1] // LANES
    ends = line_ends("gy", parts)
    ends = [jnp.broadcast_to(row, (tiles * SUB, LANES)) for row in ends]
    left, right = segment_ends(*ends, w_ref, s_ref, log2(tiles * SUB))

    def store(k, speed):
        for tile in range(tiles):
            turned[spread_rows(tile, k), :] = speed[tile * SUB : (tile + 1) * SUB, :]

    march_values(left, right, t_ref, s_ref, inv_ref, scale, r_ref, store)
    writes = []
    for tile in range(tiles):
        block = turned[tile_span(tile), :].T
        for k in range(STEPS):
            natural[spread_rows(tile, k), :] = block[k * SUB : (k + 1) * SUB, :]
        writes += tile_writes(natural, out, tile, sems)
    for write in writes:
        write.wait()


def solve(kernel, name, pieces, parts, block, extra=()):
    return pl.pallas_call(
        kernel,
        out_shape=shape(*block),
        in_specs=[VMEM] * (len(pieces) + len(parts)),
        out_specs=ANY,
        scratch_shapes=write_scratch(block[1]) + list(extra),
        compiler_params=PARAMS,
        cost_estimate=pl.CostEstimate(flops=1_000_000, bytes_accessed=4_000_000, transcendentals=0),
        name=name,
    )(*pieces, *parts)


def hand_on(value, axis):
    count = lax.axis_size(axis)
    far = [i + 2 if i % 2 == 0 else i - 2 for i in range(count)]
    return lax.ppermute(value, axis, [(i, t if 0 <= t < count else i ^ 1) for i, t in enumerate(far)])


def shift_pair(value, axis):
    count = lax.axis_size(axis)
    other = [((i - 1) ^ 1) + 1 for i in range(count)]
    return lax.ppermute(value, axis, [(i, o if 0 <= o < count else i) for i, o in enumerate(other)])


def cross(value, axis, mask):
    return lax.ppermute(value, axis, [(i, i ^ mask) for i in range(lax.axis_size(axis))])


def crossed(value, axis, stage, half):
    pairs = []
    for i in range(lax.axis_size(axis)):
        upper = (i >> (stage + 1)) & 1
        pairs.append((i, i ^ ((2 if upper == half else 3) << stage)))
    return lax.ppermute(value, axis, pairs)


def parts_of_line(axis, mine, relay, beside=(), tall=None):
    parts = []
    last = log2(lax.axis_size(axis)) - 2
    for stage in range(last):
        theirs = cross(mine, axis, 1 << stage)
        parts += [mine, theirs]
        mine = merge_call(axis, stage, mine, theirs, beside)
    if relay:
        first = cross(mine, axis, 1 << last)
        second = cross(mine if tall is None else tall, axis, 2 << last)
        both = cross(second[:, 0 : mine.shape[1]], axis, 1 << last)
    else:
        first = cross(mine, axis, 1 << last)
        second, both = (crossed(mine, axis, last, n) for n in (1, 0))
    return parts + [mine, first, second, both]


def on_device(h, p, q, b, m):
    block = h.shape
    rows, cols = block
    inv_cx = 3.0 / (rows * lax.axis_size("gx") / 4.0) ** 2
    inv_cy = 3.0 / (cols * lax.axis_size("gy") / 4.0) ** 2
    slabs_x = pack_x(h, p, q, b, m)
    near_x = cross(slabs_x, "gx", 1)
    near_y, far_y = pack_y(h, p, q, b, m, after=slabs_x)
    near_y, far_y = cross(near_y, "gy", 1), shift_pair(far_y, "gy")
    hx, hy, ix, iy, tx, wx, ty, wy, coef_x, coef_y, left_x, right_x = prepare_depth(h, inv_cx, inv_cy)
    far_x = hand_on(second_of(near_x, coef_x, near_y), "gx")
    px, py, qx, qy, bx, by, mx, my = prepare_rest(p, q, b, m)
    depth_inner, push_inner, across_inner, faces = fluxes_x_inner(hx, px, qx, bx, mx)
    mass_y, shear_y, normal_y = fluxes_y(near_y, far_y, hy, py, qy, by, my)
    depth_outer, across_outer, rx, sx, end_x = fluxes_x(
        near_x, far_x, hx, px, qx, bx, mx, ix, shear_y, push_inner, faces, tx, wx, coef_x, inv_cx=inv_cx
    )
    depth, ry, sy, end_y, tall_y = join_y(
        depth_inner, across_inner, depth_outer, across_outer, mass_y, mx, normal_y, iy, my, ty, wy, coef_y, inv_cy=inv_cy
    )
    new_depth = write_depth(depth, block)
    parts_y = parts_of_line("gy", end_y, True, tall=tall_y if lax.axis_size("gy") == 4 else None)
    parts_x = parts_of_line("gx", end_x, False, parts_y[1:2])
    turned = [pltpu.VMEM((cols, LANES), F32)]
    solve_y_scaled = functools.partial(solve_y_kernel, scale=inv_cy)
    vy = solve(solve_y_scaled, "solve_y", (iy, ry, ty, wy, sy), parts_y, block, turned)
    own_x = rest_x(ix, rx, tx, wx, sx, scale=inv_cx)
    vx = solve(solve_x_kernel, "solve_x", (left_x, right_x, own_x), parts_x, block)
    return new_depth, vx, vy


def solution(mesh):
    spec = P("gx", "gy")
    return jax.shard_map(
        on_device,
        mesh=mesh,
        in_specs=(spec,) * 5,
        out_specs=(spec,) * 3,
        check_vma=False,
    )
```

```python
import functools

import jax
import jax.numpy as jnp
from jax import lax
from jax.experimental import pallas as pl
from jax.experimental.pallas import tpu as pltpu
from jax.sharding import PartitionSpec as P

gravity = 9.81
ratio = 0.05
LANES = 128
SUB = 8
STEPS = LANES // SUB
F32 = jnp.float32
VMEM = pl.BlockSpec(memory_space=pltpu.VMEM)
HBM = pl.BlockSpec(memory_space=pltpu.HBM)
ANY = pl.BlockSpec(memory_space=pl.ANY)
PARAMS = pltpu.CompilerParams(vmem_limit_bytes=16 * 1024 * 1024)


def lane_index(shape):
    return lax.broadcasted_iota(jnp.int32, shape, len(shape) - 1)


def row_index(shape):
    return lax.broadcasted_iota(jnp.int32, shape, len(shape) - 2)


def at(tile, step):
    first = tile * LANES + step * SUB
    return slice(first, first + SUB)


def tile_span(tile):
    return slice(tile * LANES, (tile + 1) * LANES)


def spread_rows(tile, step):
    return pl.ds(tile * LANES + step, SUB, stride=STEPS)


def shape(*dims):
    return jax.ShapeDtypeStruct(dims, F32)


def pack_x_kernel(h, p, q, b, m, slabs, top, bottom, itop, ibottom, sems):
    rows = h.shape[0]
    copies = []
    for f, src in enumerate((h, p, q, b, m)):
        for side, (target, whole, row) in enumerate(((top, itop, 0), (bottom, ibottom, rows - SUB))):
            copy = pltpu.make_async_copy(
                src.at[pl.ds(row, SUB), :], target.at[f] if f < 4 else whole, sems.at[2 * f + side]
            )
            copy.start()
            copies.append(copy)
    for copy in copies:
        copy.wait()
    first = jnp.concatenate(
        [top[0, 0:2, :], top[1, 0:2, :], top[2, 0:2, :], top[3, 0:1, :], itop[0:1, :].astype(F32)]
    )
    last = jnp.concatenate(
        [
            bottom[0, SUB - 2 : SUB, :],
            bottom[1, SUB - 2 : SUB, :],
            bottom[2, SUB - 2 : SUB, :],
            bottom[3, SUB - 1 : SUB, :],
            ibottom[SUB - 1 : SUB, :].astype(F32),
        ]
    )
    even = lax.axis_index("gx") % 2 == 0
    slabs[0] = jnp.where(even, last, first)
    slabs[1] = jnp.where(even, first, last)


def pack_x(*fields):
    cols = fields[0].shape[1]
    return pl.pallas_call(
        pack_x_kernel,
        out_shape=shape(2, SUB, cols),
        in_specs=[HBM] * 5,
        out_specs=VMEM,
        scratch_shapes=[
            pltpu.VMEM((4, SUB, cols), F32),
            pltpu.VMEM((4, SUB, cols), F32),
            pltpu.VMEM((SUB, cols), jnp.int32),
            pltpu.VMEM((SUB, cols), jnp.int32),
            pltpu.SemaphoreType.DMA((10,)),
        ],
        compiler_params=PARAMS,
        name="pack_x",
    )(*[pltpu.with_memory_space_constraint(v, pltpu.HBM) for v in fields])


def pack_y_kernel(h, p, q, b, m, _, near, far, natural):
    rows, cols = h.shape
    lane = lane_index((rows, LANES))
    out = None
    for f, src in enumerate((h, p, q, b, m)):
        both = jnp.where(lane < LANES // 2, src[:, 0:LANES], src[:, cols - LANES : cols]).astype(F32)
        moved = pltpu.roll(both, 4 * f + 2, 1)
        out = moved if out is None else jnp.where(lane >= 4 * f, moved, out)
    natural[...] = out
    turned = jnp.concatenate([natural[spread_rows(0, k), :] for k in range(STEPS)]).T
    last = jnp.concatenate([turned[0:2], turned[4:6], turned[8:10], turned[13:14], turned[17:18]])
    first = jnp.concatenate([turned[2:4], turned[6:8], turned[10:12], turned[14:15], turned[18:19]])
    even = lax.axis_index("gy") % 2 == 0
    for slab, value in ((near, jnp.where(even, last, first)), (far, jnp.where(even, first, last))):
        slab[...] = jnp.zeros_like(slab)
        slab[0:SUB, :] = value


def pack_y(*fields, after):
    rows = fields[0].shape[0]
    return pl.pallas_call(
        pack_y_kernel,
        out_shape=(shape(1 * SUB, rows), shape(4 * SUB, rows)),
        in_specs=[VMEM] * 6,
        out_specs=(VMEM, VMEM),
        scratch_shapes=[pltpu.VMEM((rows, LANES), F32)],
        compiler_params=PARAMS,
        cost_estimate=pl.CostEstimate(flops=500_000, bytes_accessed=1_000_000, transcendentals=0),
        name="pack_y",
    )(*fields, after)


def tie_kernel(both, *refs):
    refs[-1][...] = both[1]


def second_of(both, *after):
    return pl.pallas_call(
        tie_kernel,
        out_shape=shape(*both.shape[1:]),
        in_specs=[VMEM] * (1 + len(after)),
        out_specs=VMEM,
        compiler_params=PARAMS,
        name="second_of",
    )(both, *after)


def merge_coefficients(one, two):
    t1, gl1, gr1 = one
    t2, gl2, gr2 = two
    shunt = gr1 + gl2
    inverse = 1.0 / (t1 + t2 + shunt)
    w1, w2 = t1 * inverse, t2 * inverse
    return (w1 * t2, gl1 + w1 * shunt, gr2 + w2 * shunt), (w1, w2, inverse)


def merge_sources(one, two, weights):
    w1, w2, inverse = weights
    source = one[1] - two[0]
    return (one[0] - w1 * source, two[1] + w2 * source), source * inverse


def merge(one, two):
    coefficients, weights = merge_coefficients(one[:3], two[:3])
    sources, middle = merge_sources(one[3:], two[3:], weights)
    return coefficients + sources, weights[:2] + (middle,)


def log2(count):
    return (count - 1).bit_length()


def full(ref, step):
    return jnp.concatenate([ref[at(tile, step), :] for tile in range(ref.shape[0] // LANES)])


def march_depth(inv_ref, scale, out_t, out_w, levels):
    count = inv_ref.shape[0] // STEPS
    zero = jnp.zeros((count, LANES), F32)
    alpha, gamma, beta, delta = zero, zero, zero, zero
    for k in range(STEPS):
        inverse = full(inv_ref, k)
        d = scale * (inverse * inverse)
        alpha = alpha + gamma
        gamma = gamma + d * (1.0 + alpha)
        beta = beta + delta
        delta = delta + d * ((k + 1.0) + beta)
    t = 1.0 / (STEPS + beta)
    out_t[0] = t
    out_t[1] = t * alpha
    out_t[2] = 1.0 + delta
    coefficients = (t, t * alpha, t * delta)
    for level in range(levels):
        after = tuple(pltpu.roll(v, count - (1 << level), 0) for v in coefficients)
        coefficients, weights = merge_coefficients(coefficients, after)
        for j, v in enumerate(weights):
            out_w[3 * level + j] = v
    return coefficients


def lay_out(src, xs, ys, natural, turned):
    for tile in range(xs.shape[0] // LANES):
        natural[tile_span(tile), :] = src[:, tile_span(tile)].astype(F32)
        for k in range(STEPS):
            xs[at(tile, k), :] = natural[spread_rows(tile, k), :]
        turned[tile_span(tile), :] = xs[tile_span(tile), :].T
        for k in range(STEPS):
            ys[at(tile, k), :] = turned[spread_rows(tile, k), :]


def prepare_depth_kernel(
    h, hx, hy, ix, iy, tx, wx, ty, wy, endx, endy, from_left, from_right, natural, turned, *, inv_cx, inv_cy
):
    tiles = hx.shape[0] // LANES
    lay_out(h, hx, hy, natural, turned)
    ix[...] = 1.0 / hx[...]
    iy[...] = 1.0 / hy[...]
    ends_x = march_depth(ix, inv_cx, tx, wx, log2(SUB))
    ends_y = march_depth(iy, inv_cy, ty, wy, log2(SUB * tiles))
    for i in range(3):
        for tile in range(tiles):
            first = (i * tiles + tile) * LANES
            endx[0:1, first : first + LANES] = ends_x[i][tile * SUB : tile * SUB + 1, :]
        endy[0:1, i * LANES : (i + 1) * LANES] = ends_y[i][0:1, :]
    one = jnp.ones((tiles * SUB, LANES), F32)
    zero = jnp.zeros_like(one)
    for out, left, right in ((from_left, one, zero), (from_right, zero, one)):

        def store(k, speed):
            for tile in range(tiles):
                out[at(tile, k), :] = speed[tile * SUB : (tile + 1) * SUB, :]

        left, right = segment_ends(left, right, wx, None, log2(SUB))
        march_values(left, right, tx, None, ix, inv_cx, None, store)


def prepare_depth(h, inv_cx, inv_cy):
    stack = (h.shape[1], LANES)
    count = stack[0] // STEPS
    shapes = [shape(*stack)] * 4 + [
        shape(3, count, LANES),
        shape(3 * log2(SUB), count, LANES),
        shape(3, count, LANES),
        shape(3 * log2(count), count, LANES),
        shape(1, 3 * stack[0]),
        shape(1, 3 * LANES),
        shape(*stack),
        shape(*stack),
    ]
    return pl.pallas_call(
        functools.partial(prepare_depth_kernel, inv_cx=inv_cx, inv_cy=inv_cy),
        out_shape=tuple(shapes),
        in_specs=[VMEM],
        out_specs=(VMEM,) * len(shapes),
        scratch_shapes=[pltpu.VMEM(stack, F32)] * 2,
        compiler_params=PARAMS,
        cost_estimate=pl.CostEstimate(flops=2_000_000, bytes_accessed=4_000_000, transcendentals=0),
        name="prepare_depth",
    )(h)


def prepare_rest_kernel(*refs):
    fields, outs, natural, turned = refs[:4], refs[4:12], refs[12], refs[13]
    for f, src in enumerate(fields):
        lay_out(src, outs[2 * f], outs[2 * f + 1], natural.at[f % 2], turned.at[f % 2])


def prepare_rest(*fields):
    stack = (fields[0].shape[1], LANES)
    return pl.pallas_call(
        prepare_rest_kernel,
        out_shape=(shape(*stack),) * 8,
        in_specs=[VMEM] * 4,
        out_specs=(VMEM,) * 8,
        scratch_shapes=[pltpu.VMEM((2, *stack), F32)] * 2,
        compiler_params=PARAMS,
        cost_estimate=pl.CostEstimate(flops=2_000_000, bytes_accessed=6_000_000, transcendentals=0),
        name="prepare_rest",
    )(*fields)


def low_high(axis, near, far):
    index, count = lax.axis_index(axis), lax.axis_size(axis)
    even = index % 2 == 0
    low = jnp.where(index > 0, jnp.where(even, far, near), 0.0)
    high = jnp.where(index < count - 1, jnp.where(even, near, far), 0.0)
    return low, high


def half_slope(a, c):
    return 0.5 * (jnp.maximum(jnp.minimum(a, c), 0.0) + jnp.minimum(jnp.maximum(a, c), 0.0))


def face_flux(left, right, opened):
    is_open = opened > 0.5
    hl = jnp.where(is_open, left[0], 1.0)
    hr = jnp.where(is_open, right[0], 1.0)
    joint = 1.0 / (hl * hr)
    ul = left[1] * (hr * joint)
    ur = right[1] * (hl * joint)
    gl = gravity * hl
    gr = gravity * hr
    fastest = jnp.maximum(jnp.abs(ul) + gl * lax.rsqrt(gl), jnp.abs(ur) + gr * lax.rsqrt(gr))
    scale = (0.5 * ratio) * opened
    mass = (left[1] + right[1]) - fastest * (right[0] - left[0])
    push = 0.5 * (gl * hl + gr * hr) + left[1] * ul + right[1] * ur - fastest * (right[1] - left[1])
    shear = left[2] * ul + right[2] * ur - fastest * (right[2] - left[2])
    return scale * mass, scale * push, scale * shear


def extended(ref, tile, lows, highs):
    sub = row_index((SUB, LANES))
    out = {}
    for n, row in enumerate(lows, 1):
        value = ref[at(tile, STEPS - n), :]
        out[-n] = jnp.where(sub == 0, row, pltpu.roll(value, 1, 0))
    for n, row in enumerate(highs):
        value = ref[at(tile, n), :]
        out[STEPS + n] = jnp.where(sub == SUB - 1, row, pltpu.roll(value, SUB - 1, 0))
    return lambda k: out[k] if k in out else ref[at(tile, k), :]


def tile_fluxes(fields, bed, wet, store, start=0, stop=STEPS, low_face=None, high_face=None):
    def states(k):
        both = []
        for w in fields:
            here = w(k)
            both.append((here, half_slope(here - w(k - 1), w(k + 1) - here)))
        return [w + s for w, s in both], [w - s for w, s in both]

    left, before, first = None, None, None
    for k in range(start - 1, stop):
        if k == start - 1 and low_face is not None:
            face = low_face
        elif k == stop - 1 and high_face is not None:
            face = high_face
        else:
            if left is None:
                left, _ = states(k)
            left_next, right = states(k + 1)
            face = face_flux(left, right, wet(k) * wet(k + 1))
            left = left_next
        if k >= start:
            store(k, [a - c for a, c in zip(face, before)], bed(k + 1) - bed(k - 1))
        first = face if first is None else first
        before = face
    return first, before


def march_source(inv_ref, scale, r_ref, t_ref, w_ref, s_ref, levels):
    count = inv_ref.shape[0] // STEPS
    c = jnp.zeros((count, LANES), F32)
    e = c
    for k in range(STEPS):
        inverse = full(inv_ref, k)
        c = c + e
        e = e + (scale * (inverse * inverse) * c - full(r_ref, k))
    sl = t_ref[0] * c
    s_ref[0] = sl
    sources = (sl, t_ref[2] * sl - e)
    for level in range(levels):
        after = tuple(pltpu.roll(v, count - (1 << level), 0) for v in sources)
        sources, middle = merge_sources(sources, after, tuple(w_ref[3 * level + j] for j in range(3)))
        s_ref[1 + level] = middle
    return sources


def flux_y_kernel(near, far, hy, py, qy, by, my, mass, shear, normal, across, along):
    tiles = hy.shape[0] // LANES
    low, high = low_high("gy", near[0:SUB, :], far[0:SUB, :])
    for tile in range(tiles):

        def extend(ref, row, layers):
            lows, highs = [], []
            for n in range(layers):
                last = at(tile - 1, STEPS - 1 - n).stop - 1
                first = at(tile + 1, n).start
                lows.append(low[row + layers - 1 - n : row + layers - n, :] if tile == 0 else ref[last : last + 1, :])
                highs.append(high[row + n : row + n + 1, :] if tile == tiles - 1 else ref[first : first + 1, :])
            return extended(ref, tile, lows, highs)

        def store(k, difference, bed):
            here, natural = at(tile, k), spread_rows(tile, k)
            across[natural, :] = difference[0]
            along[natural, :] = difference[2]
            pull = (0.5 * ratio * gravity) * hy[here, :]
            normal[here, :] = qy[here, :] - difference[1] - pull * bed

        tile_fluxes([extend(hy, 0, 2), extend(qy, 4, 2), extend(py, 2, 2)], extend(by, 6, 1), extend(my, 7, 1), store)
        span = tile_span(tile)
        mass[span, :] = across[span, :].T
        shear[span, :] = along[span, :].T


def fluxes_y(*arrays):
    stack = arrays[2].shape
    return pl.pallas_call(
        flux_y_kernel,
        out_shape=(shape(*stack),) * 3,
        in_specs=[VMEM] * len(arrays),
        out_specs=(VMEM,) * 3,
        scratch_shapes=[pltpu.VMEM(stack, F32)] * 2,
        compiler_params=PARAMS,
        cost_estimate=pl.CostEstimate(flops=4_000_000, bytes_accessed=4_000_000, transcendentals=0),
        name="fluxes_y",
    )(*arrays)


INNER = (2, STEPS - 2)
TALL = 16


def x_store(hx, px, mx, depth, push, across):
    def of_tile(tile):
        def store(k, difference, bed):
            here = at(tile, k)
            h = hx[here, :]
            depth[here, :] = h - mx[here, :] * difference[0]
            push[here, :] = px[here, :] - difference[1] - (0.5 * ratio * gravity) * h * bed
            across[here, :] = difference[2]

        return store

    return of_tile


def flux_x_inner_kernel(hx, px, qx, bx, mx, depth, push, across, faces):
    store = x_store(hx, px, mx, depth, push, across)
    for tile in range(hx.shape[0] // LANES):
        fields = [extended(v, tile, (), ()) for v in (hx, px, qx, bx, mx)]
        ends = tile_fluxes(fields[:3], fields[3], fields[4], store(tile), *INNER)
        for n, v in enumerate(ends[0] + ends[1]):
            faces[n, tile * SUB : (tile + 1) * SUB, :] = v
        for k in (*range(INNER[0]), *range(INNER[1], STEPS)):
            for ref in (depth, push, across):
                ref[at(tile, k), :] = jnp.zeros((SUB, LANES), F32)


def fluxes_x_inner(*arrays):
    stack = arrays[0].shape
    return pl.pallas_call(
        flux_x_inner_kernel,
        out_shape=(shape(*stack),) * 3 + (shape(6, stack[0] // STEPS, LANES),),
        in_specs=[VMEM] * len(arrays),
        out_specs=(VMEM,) * 4,
        compiler_params=PARAMS,
        cost_estimate=pl.CostEstimate(flops=4_000_000, bytes_accessed=4_000_000, transcendentals=0),
        name="fluxes_x_inner",
    )(*arrays)


def flux_x_kernel(
    near, far, hx, px, qx, bx, mx, ix, shear_y, push_in, faces, tx, wx, coef,
    depth, across, rx, sx, ends,
    push,
    *, inv_cx,
):
    tiles = hx.shape[0] // LANES
    low, high = low_high("gx", near[0], far[...])
    store = x_store(hx, px, mx, depth, push, across)
    for tile in range(tiles):
        span = tile_span(tile)

        def extend(ref, row, layers):
            lows = [low[row + layers - 1 - n : row + layers - n, span] for n in range(layers)]
            highs = [high[row + n : row + n + 1, span] for n in range(layers)]
            return extended(ref, tile, lows, highs)

        fields, bed, wet = [extend(hx, 0, 2), extend(px, 2, 2), extend(qx, 4, 2)], extend(bx, 6, 1), extend(mx, 7, 1)
        known = [faces[n, tile * SUB : (tile + 1) * SUB, :] for n in range(6)]
        tile_fluxes(fields, bed, wet, store(tile), 0, INNER[0], high_face=known[:3])
        tile_fluxes(fields, bed, wet, store(tile), INNER[1], STEPS, low_face=known[3:])
        for k in range(STEPS):
            here = at(tile, k)
            inverse = ix[here, :]
            total = (push_in if INNER[0] <= k < INNER[1] else push)[here, :] - shear_y[here, :]
            rx[here, :] = (inv_cx * (inverse * inverse)) * mx[here, :] * total
    sources = march_source(ix, inv_cx, rx, tx, wx, sx, log2(SUB))
    count = tiles * LANES
    ends[0:1, 0 : 3 * count] = coef[...]
    for i in range(2):
        for tile in range(tiles):
            first = (3 + i) * count + tile * LANES
            ends[0:1, first : first + LANES] = sources[i][tile * SUB : tile * SUB + 1, :]


def fluxes_x(*arrays, inv_cx):
    stack = arrays[2].shape
    count = stack[0] // STEPS
    shapes = (
        shape(*stack),
        shape(*stack),
        shape(*stack),
        shape(1 + log2(SUB), count, LANES),
        shape(1, 5 * stack[0]),
    )
    return pl.pallas_call(
        functools.partial(flux_x_kernel, inv_cx=inv_cx),
        out_shape=shapes,
        in_specs=[VMEM] * len(arrays),
        out_specs=(VMEM,) * len(shapes),
        scratch_shapes=[pltpu.VMEM(stack, F32)],
        compiler_params=PARAMS,
        name="fluxes_x",
    )(*arrays)


def join_y_kernel(
    depth_inner, across_inner, depth_outer, across_outer, mass_y, mx, normal_y, iy, my, ty, wy, coef,
    depth, ry, sy, ends, tall,
    across, turned,
    *, inv_cy,
):
    tiles = mx.shape[0] // LANES
    for tile in range(tiles):
        span = tile_span(tile)
        for k in range(STEPS):
            here = at(tile, k)
            inner = INNER[0] <= k < INNER[1]
            across[here, :] = (across_inner if inner else across_outer)[here, :]
            depth[here, :] = (depth_inner if inner else depth_outer)[here, :] - mx[here, :] * mass_y[here, :]
        turned[span, :] = across[span, :].T
        for k in range(STEPS):
            here = at(tile, k)
            inverse = iy[here, :]
            total = normal_y[here, :] - turned[spread_rows(tile, k), :]
            ry[here, :] = (inv_cy * (inverse * inverse)) * my[here, :] * total
    sources = march_source(iy, inv_cy, ry, ty, wy, sy, log2(SUB * tiles))
    ends[0:1, 0 : 3 * LANES] = coef[...]
    for i in range(2):
        ends[0:1, (3 + i) * LANES : (4 + i) * LANES] = sources[i][0:1, :]
    tall[...] = jnp.zeros_like(tall)
    tall[0:1, 0 : 5 * LANES] = ends[...]


def join_y(*arrays, inv_cy):
    stack = arrays[0].shape
    count = stack[0] // STEPS
    shapes = (
        shape(*stack),
        shape(*stack),
        shape(1 + log2(count), count, LANES),
        shape(1, 5 * LANES),
        shape(1, TALL * LANES),
    )
    return pl.pallas_call(
        functools.partial(join_y_kernel, inv_cy=inv_cy),
        out_shape=shapes,
        in_specs=[VMEM] * len(arrays),
        out_specs=(VMEM,) * len(shapes),
        scratch_shapes=[pltpu.VMEM(stack, F32)] * 2,
        compiler_params=PARAMS,
        cost_estimate=pl.CostEstimate(flops=2_000_000, bytes_accessed=2_000_000, transcendentals=0),
        name="join_y",
    )(*arrays)


PARTS = 1


def tile_writes(tiled, whole, tile, sems):
    rows = whole.shape[0]
    part = rows // PARTS
    copies = []
    for n in range(PARTS):
        copy = pltpu.make_async_copy(
            tiled.at[pl.ds(tile * rows + n * part, part), :],
            whole.at[pl.ds(n * part, part), pl.ds(tile * LANES, LANES)],
            sems.at[tile, n],
        )
        copy.start()
        copies.append(copy)
    return copies


def write_scratch(cols):
    return [pltpu.VMEM((cols, LANES), F32), pltpu.SemaphoreType.DMA((cols // LANES, PARTS))]


def depth_kernel(depth, out, natural, sems):
    writes = []
    for tile in range(depth.shape[0] // LANES):
        for k in range(STEPS):
            natural[spread_rows(tile, k), :] = depth[at(tile, k), :]
        writes += tile_writes(natural, out, tile, sems)
    for write in writes:
        write.wait()


def write_depth(depth, block):
    return pl.pallas_call(
        depth_kernel,
        out_shape=shape(*block),
        in_specs=[VMEM],
        out_specs=ANY,
        scratch_shapes=write_scratch(block[1]),
        compiler_params=PARAMS,
        cost_estimate=pl.CostEstimate(flops=100_000, bytes_accessed=2_000_000, transcendentals=0),
        name="write_depth",
    )(depth)


def rows_of(ref, count):
    return tuple(ref[0:1, i * count : (i + 1) * count] for i in range(5))


def ordered(axis, stage, mine, theirs):
    is_low = (lax.axis_index(axis) >> stage) % 2 == 0
    one = tuple(jnp.where(is_low, a, b) for a, b in zip(mine, theirs))
    two = tuple(jnp.where(is_low, b, a) for a, b in zip(mine, theirs))
    return is_low, merge(one, two)


def merge_kernel(mine, theirs, *refs, axis, stage):
    out = refs[-1]
    count = mine.shape[1] // 5
    _, (merged, _) = ordered(axis, stage, rows_of(mine, count), rows_of(theirs, count))
    for i, v in enumerate(merged):
        out[0:1, i * v.shape[1] : (i + 1) * v.shape[1]] = v


def merge_call(axis, stage, mine, theirs, beside):
    return pl.pallas_call(
        functools.partial(merge_kernel, axis=axis, stage=stage),
        out_shape=shape(*mine.shape),
        in_specs=[VMEM] * (2 + len(beside)),
        out_specs=VMEM,
        compiler_params=PARAMS,
        name="merge",
    )(mine, theirs, *beside)


ROUTES = ((1, 3, 0, 2), (2, 1, 3, 0), (3, 0, 2, 1), (0, 2, 1, 3))


def by_distance(place, received):
    chosen = []
    for mask in (1, 2, 3):
        came = [next(n for n, route in enumerate(ROUTES) if route[at_place ^ mask] == at_place) for at_place in range(4)]
        value = received[came[0]]
        for at_place in range(1, 4):
            other = received[came[at_place]]
            value = tuple(jnp.where(place == at_place, b, a) for a, b in zip(value, other))
        chosen.append(value)
    return chosen


def line_ends(axis, refs, is_routed=False):
    steps = []
    parts = [rows_of(ref, refs[0].shape[1] // 5) for ref in refs]
    if is_routed:
        place = (lax.axis_index(axis) >> (len(parts) - 5) // 2) & 3
        parts = parts[:-4] + by_distance(place, parts[:-5:-1])
    stage = 0
    while len(parts) > 4:
        is_low, (_, weights) = ordered(axis, stage, *parts[:2])
        steps.append((is_low, weights))
        parts = parts[2:]
        stage += 1
    is_low, (own, weights) = ordered(axis, stage, *parts[:2])
    steps.append((is_low, weights))
    _, (other, _) = ordered(axis, stage, *parts[2:])
    is_low, (whole, weights) = ordered(axis, stage + 1, own, other)
    steps.append((is_low, weights))
    t, _, gr, _, sr = whole
    left = jnp.zeros_like(t)
    right = sr / (t + gr + 1.0)
    for is_low, (w1, w2, source) in reversed(steps):
        middle = w1 * left + w2 * right + source
        left = jnp.where(is_low, left, middle)
        right = jnp.where(is_low, middle, right)
    return left, right


def segment_ends(left, right, w_ref, s_ref, levels):
    index = row_index(left.shape)
    for level in reversed(range(levels)):
        stride = 1 << level
        middle = w_ref[3 * level] * left + w_ref[3 * level + 1] * right
        if s_ref is not None:
            middle = middle + s_ref[1 + level]
        upper = (index >> level) % 2 == 1
        left, right = (
            jnp.where(upper, pltpu.roll(middle, stride, 0), left),
            jnp.where(upper, pltpu.roll(right, stride, 0), middle),
        )
    return left, right


def march_values(left, right, t_ref, s_ref, inv_ref, scale, r_ref, store):
    value = left
    change = t_ref[0] * (right - left) - t_ref[1] * left
    if s_ref is not None:
        change = change - s_ref[0]
    for k in range(STEPS):
        inverse = full(inv_ref, k)
        value = value + change
        push = scale * (inverse * inverse) * value
        change = change + (push if r_ref is None else push - full(r_ref, k))
        store(k, value * inverse)


def rest_x_kernel(inv_ref, r_ref, t_ref, w_ref, s_ref, out, *, scale):
    tiles = out.shape[0] // LANES
    zero = jnp.zeros((tiles * SUB, LANES), F32)

    def store(k, speed):
        for tile in range(tiles):
            out[at(tile, k), :] = speed[tile * SUB : (tile + 1) * SUB, :]

    left, right = segment_ends(zero, zero, w_ref, s_ref, log2(SUB))
    march_values(left, right, t_ref, s_ref, inv_ref, scale, r_ref, store)


def rest_x(*pieces, scale):
    return pl.pallas_call(
        functools.partial(rest_x_kernel, scale=scale),
        out_shape=shape(*pieces[0].shape),
        in_specs=[VMEM] * len(pieces),
        out_specs=VMEM,
        compiler_params=PARAMS,
        cost_estimate=pl.CostEstimate(flops=1_000_000, bytes_accessed=2_000_000, transcendentals=0),
        name="rest_x",
    )(*pieces)


def solve_x_kernel(from_left, from_right, rest, *refs):
    parts, (out, natural, sems) = refs[:-3], refs[-3:]
    left, right = line_ends("gx", parts, True)
    writes = []
    for tile in range(out.shape[1] // LANES):
        span = tile_span(tile)
        for k in range(STEPS):
            here = at(tile, k)
            natural[spread_rows(tile, k), :] = (
                from_left[here, :] * left[:, span] + from_right[here, :] * right[:, span] + rest[here, :]
            )
        writes += tile_writes(natural, out, tile, sems)
    for write in writes:
        write.wait()


def solve_y_kernel(inv_ref, r_ref, t_ref, w_ref, s_ref, *refs, scale):
    parts, (out, natural, sems, turned) = refs[:-4], refs[-4:]
    tiles = out.shape[1] // LANES
    ends = line_ends("gy", parts)
    ends = [jnp.broadcast_to(row, (tiles * SUB, LANES)) for row in ends]
    left, right = segment_ends(*ends, w_ref, s_ref, log2(tiles * SUB))

    def store(k, speed):
        for tile in range(tiles):
            turned[spread_rows(tile, k), :] = speed[tile * SUB : (tile + 1) * SUB, :]

    march_values(left, right, t_ref, s_ref, inv_ref, scale, r_ref, store)
    writes = []
    for tile in range(tiles):
        block = turned[tile_span(tile), :].T
        for k in range(STEPS):
            natural[spread_rows(tile, k), :] = block[k * SUB : (k + 1) * SUB, :]
        writes += tile_writes(natural, out, tile, sems)
    for write in writes:
        write.wait()


def solve(kernel, name, pieces, parts, block, extra=()):
    return pl.pallas_call(
        kernel,
        out_shape=shape(*block),
        in_specs=[VMEM] * (len(pieces) + len(parts)),
        out_specs=ANY,
        scratch_shapes=write_scratch(block[1]) + list(extra),
        compiler_params=PARAMS,
        cost_estimate=pl.CostEstimate(flops=1_000_000, bytes_accessed=4_000_000, transcendentals=0),
        name=name,
    )(*pieces, *parts)


def hand_on(value, axis):
    count = lax.axis_size(axis)
    far = [i + 2 if i % 2 == 0 else i - 2 for i in range(count)]
    return lax.ppermute(value, axis, [(i, t if 0 <= t < count else i ^ 1) for i, t in enumerate(far)])


def shift_pair(value, axis):
    count = lax.axis_size(axis)
    other = [((i - 1) ^ 1) + 1 for i in range(count)]
    return lax.ppermute(value, axis, [(i, o if 0 <= o < count else i) for i, o in enumerate(other)])


def cross(value, axis, mask):
    return lax.ppermute(value, axis, [(i, i ^ mask) for i in range(lax.axis_size(axis))])


def routed(value, axis, stage, route):
    pairs = []
    for i in range(lax.axis_size(axis)):
        place = (i >> stage) & 3
        pairs.append((i, i + ((route[place] - place) << stage)))
    return lax.ppermute(value, axis, pairs)


def parts_of_line(axis, mine, relay, beside=(), tall=None):
    parts = []
    last = log2(lax.axis_size(axis)) - 2
    for stage in range(last):
        theirs = cross(mine, axis, 1 << stage)
        parts += [mine, theirs]
        mine = merge_call(axis, stage, mine, theirs, beside)
    if relay:
        first = cross(mine, axis, 1 << last)
        second = cross(mine if tall is None else tall, axis, 2 << last)
        both = cross(second[:, 0 : mine.shape[1]], axis, 1 << last)
    else:
        return parts + [mine] + [routed(mine, axis, last, route) for route in reversed(ROUTES)]
    return parts + [mine, first, second, both]


def on_device(h, p, q, b, m):
    block = h.shape
    rows, cols = block
    inv_cx = 3.0 / (rows * lax.axis_size("gx") / 4.0) ** 2
    inv_cy = 3.0 / (cols * lax.axis_size("gy") / 4.0) ** 2
    slabs_x = pack_x(h, p, q, b, m)
    near_x = cross(slabs_x, "gx", 1)
    near_y, far_y = pack_y(h, p, q, b, m, after=slabs_x)
    near_y, far_y = cross(near_y, "gy", 1), shift_pair(far_y, "gy")
    hx, hy, ix, iy, tx, wx, ty, wy, coef_x, coef_y, left_x, right_x = prepare_depth(h, inv_cx, inv_cy)
    far_x = hand_on(second_of(near_x, coef_x, near_y), "gx")
    px, py, qx, qy, bx, by, mx, my = prepare_rest(p, q, b, m)
    depth_inner, push_inner, across_inner, faces = fluxes_x_inner(hx, px, qx, bx, mx)
    mass_y, shear_y, normal_y = fluxes_y(near_y, far_y, hy, py, qy, by, my)
    depth_outer, across_outer, rx, sx, end_x = fluxes_x(
        near_x, far_x, hx, px, qx, bx, mx, ix, shear_y, push_inner, faces, tx, wx, coef_x, inv_cx=inv_cx
    )
    depth, ry, sy, end_y, tall_y = join_y(
        depth_inner, across_inner, depth_outer, across_outer, mass_y, mx, normal_y, iy, my, ty, wy, coef_y, inv_cy=inv_cy
    )
    new_depth = write_depth(depth, block)
    parts_y = parts_of_line("gy", end_y, True, tall=tall_y if lax.axis_size("gy") == 4 else None)
    parts_x = parts_of_line("gx", end_x, False, parts_y[1:2])
    turned = [pltpu.VMEM((cols, LANES), F32)]
    solve_y_scaled = functools.partial(solve_y_kernel, scale=inv_cy)
    vy = solve(solve_y_scaled, "solve_y", (iy, ry, ty, wy, sy), parts_y, block, turned)
    own_x = rest_x(ix, rx, tx, wx, sx, scale=inv_cx)
    vx = solve(solve_x_kernel, "solve_x", (left_x, right_x, own_x), parts_x, block)
    return new_depth, vx, vy


def solution(mesh):
    spec = P("gx", "gy")
    return jax.shard_map(
        on_device,
        mesh=mesh,
        in_specs=(spec,) * 5,
        out_specs=(spec,) * 3,
        check_vma=False,
    )
```

```python
import functools

import jax
import jax.numpy as jnp
from jax import lax
from jax.experimental import pallas as pl
from jax.experimental.pallas import tpu as pltpu
from jax.sharding import PartitionSpec as P

gravity = 9.81
ratio = 0.05
LANES = 128
SUB = 8
STEPS = LANES // SUB
F32 = jnp.float32
VMEM = pl.BlockSpec(memory_space=pltpu.VMEM)
HBM = pl.BlockSpec(memory_space=pltpu.HBM)
ANY = pl.BlockSpec(memory_space=pl.ANY)
PARAMS = pltpu.CompilerParams(vmem_limit_bytes=16 * 1024 * 1024)


def lane_index(shape):
    return lax.broadcasted_iota(jnp.int32, shape, len(shape) - 1)


def row_index(shape):
    return lax.broadcasted_iota(jnp.int32, shape, len(shape) - 2)


def at(tile, step):
    first = tile * LANES + step * SUB
    return slice(first, first + SUB)


def tile_span(tile):
    return slice(tile * LANES, (tile + 1) * LANES)


def spread_rows(tile, step):
    return pl.ds(tile * LANES + step, SUB, stride=STEPS)


def shape(*dims):
    return jax.ShapeDtypeStruct(dims, F32)


def pack_x_kernel(h, p, q, b, m, slabs, top, bottom, itop, ibottom, sems):
    rows = h.shape[0]
    copies = []
    for f, src in enumerate((h, p, q, b, m)):
        for side, (target, whole, row) in enumerate(((top, itop, 0), (bottom, ibottom, rows - SUB))):
            copy = pltpu.make_async_copy(
                src.at[pl.ds(row, SUB), :], target.at[f] if f < 4 else whole, sems.at[2 * f + side]
            )
            copy.start()
            copies.append(copy)
    for copy in copies:
        copy.wait()
    first = jnp.concatenate(
        [top[0, 0:2, :], top[1, 0:2, :], top[2, 0:2, :], top[3, 0:1, :], itop[0:1, :].astype(F32)]
    )
    last = jnp.concatenate(
        [
            bottom[0, SUB - 2 : SUB, :],
            bottom[1, SUB - 2 : SUB, :],
            bottom[2, SUB - 2 : SUB, :],
            bottom[3, SUB - 1 : SUB, :],
            ibottom[SUB - 1 : SUB, :].astype(F32),
        ]
    )
    even = lax.axis_index("gx") % 2 == 0
    slabs[0] = jnp.where(even, last, first)
    slabs[1] = jnp.where(even, first, last)


def pack_x(*fields):
    cols = fields[0].shape[1]
    return pl.pallas_call(
        pack_x_kernel,
        out_shape=shape(2, SUB, cols),
        in_specs=[HBM] * 5,
        out_specs=VMEM,
        scratch_shapes=[
            pltpu.VMEM((4, SUB, cols), F32),
            pltpu.VMEM((4, SUB, cols), F32),
            pltpu.VMEM((SUB, cols), jnp.int32),
            pltpu.VMEM((SUB, cols), jnp.int32),
            pltpu.SemaphoreType.DMA((10,)),
        ],
        compiler_params=PARAMS,
        name="pack_x",
    )(*[pltpu.with_memory_space_constraint(v, pltpu.HBM) for v in fields])


def pack_y_kernel(h, p, q, b, m, _, near, far, natural):
    rows, cols = h.shape
    lane = lane_index((rows, LANES))
    out = None
    for f, src in enumerate((h, p, q, b, m)):
        both = jnp.where(lane < LANES // 2, src[:, 0:LANES], src[:, cols - LANES : cols]).astype(F32)
        moved = pltpu.roll(both, 4 * f + 2, 1)
        out = moved if out is None else jnp.where(lane >= 4 * f, moved, out)
    natural[...] = out
    turned = jnp.concatenate([natural[spread_rows(0, k), :] for k in range(STEPS)]).T
    last = jnp.concatenate([turned[0:2], turned[4:6], turned[8:10], turned[13:14], turned[17:18]])
    first = jnp.concatenate([turned[2:4], turned[6:8], turned[10:12], turned[14:15], turned[18:19]])
    even = lax.axis_index("gy") % 2 == 0
    for slab, value in ((near, jnp.where(even, last, first)), (far, jnp.where(even, first, last))):
        slab[...] = jnp.zeros_like(slab)
        slab[0:SUB, :] = value


def pack_y(*fields, after):
    rows = fields[0].shape[0]
    return pl.pallas_call(
        pack_y_kernel,
        out_shape=(shape(1 * SUB, rows), shape(4 * SUB, rows)),
        in_specs=[VMEM] * 6,
        out_specs=(VMEM, VMEM),
        scratch_shapes=[pltpu.VMEM((rows, LANES), F32)],
        compiler_params=PARAMS,
        cost_estimate=pl.CostEstimate(flops=500_000, bytes_accessed=1_000_000, transcendentals=0),
        name="pack_y",
    )(*fields, after)


def tie_kernel(both, *refs):
    refs[-1][...] = both[1]


def second_of(both, *after):
    return pl.pallas_call(
        tie_kernel,
        out_shape=shape(*both.shape[1:]),
        in_specs=[VMEM] * (1 + len(after)),
        out_specs=VMEM,
        compiler_params=PARAMS,
        name="second_of",
    )(both, *after)


def merge_coefficients(one, two):
    t1, gl1, gr1 = one
    t2, gl2, gr2 = two
    shunt = gr1 + gl2
    inverse = 1.0 / (t1 + t2 + shunt)
    w1, w2 = t1 * inverse, t2 * inverse
    return (w1 * t2, gl1 + w1 * shunt, gr2 + w2 * shunt), (w1, w2, inverse)


def merge_sources(one, two, weights):
    w1, w2, inverse = weights
    source = one[1] - two[0]
    return (one[0] - w1 * source, two[1] + w2 * source), source * inverse


def merge(one, two):
    coefficients, weights = merge_coefficients(one[:3], two[:3])
    sources, middle = merge_sources(one[3:], two[3:], weights)
    return coefficients + sources, weights[:2] + (middle,)


def log2(count):
    return (count - 1).bit_length()


def full(ref, step):
    return jnp.concatenate([ref[at(tile, step), :] for tile in range(ref.shape[0] // LANES)])


def march_depth(inv_ref, scale, out_t, out_w, levels):
    count = inv_ref.shape[0] // STEPS
    zero = jnp.zeros((count, LANES), F32)
    alpha, gamma, beta, delta = zero, zero, zero, zero
    for k in range(STEPS):
        inverse = full(inv_ref, k)
        d = scale * (inverse * inverse)
        alpha = alpha + gamma
        gamma = gamma + d * (1.0 + alpha)
        beta = beta + delta
        delta = delta + d * ((k + 1.0) + beta)
    t = 1.0 / (STEPS + beta)
    out_t[0] = t
    out_t[1] = t * alpha
    out_t[2] = 1.0 + delta
    coefficients = (t, t * alpha, t * delta)
    for level in range(levels):
        after = tuple(pltpu.roll(v, count - (1 << level), 0) for v in coefficients)
        coefficients, weights = merge_coefficients(coefficients, after)
        for j, v in enumerate(weights):
            out_w[3 * level + j] = v
    return coefficients


def lay_out(src, xs, ys, natural, turned):
    for tile in range(xs.shape[0] // LANES):
        natural[tile_span(tile), :] = src[:, tile_span(tile)].astype(F32)
        for k in range(STEPS):
            xs[at(tile, k), :] = natural[spread_rows(tile, k), :]
        turned[tile_span(tile), :] = xs[tile_span(tile), :].T
        for k in range(STEPS):
            ys[at(tile, k), :] = turned[spread_rows(tile, k), :]


def prepare_depth_kernel(
    h, hx, hy, ix, iy, tx, wx, ty, wy, endx, endy, from_left, from_right, natural, turned, *, inv_cx, inv_cy
):
    tiles = hx.shape[0] // LANES
    lay_out(h, hx, hy, natural, turned)
    ix[...] = 1.0 / hx[...]
    iy[...] = 1.0 / hy[...]
    ends_x = march_depth(ix, inv_cx, tx, wx, log2(SUB))
    ends_y = march_depth(iy, inv_cy, ty, wy, log2(SUB * tiles))
    for i in range(3):
        for tile in range(tiles):
            first = (i * tiles + tile) * LANES
            endx[0:1, first : first + LANES] = ends_x[i][tile * SUB : tile * SUB + 1, :]
        endy[0:1, i * LANES : (i + 1) * LANES] = ends_y[i][0:1, :]
    one = jnp.ones((tiles * SUB, LANES), F32)
    zero = jnp.zeros_like(one)
    for out, left, right in ((from_left, one, zero), (from_right, zero, one)):

        def store(k, speed):
            for tile in range(tiles):
                out[at(tile, k), :] = speed[tile * SUB : (tile + 1) * SUB, :]

        left, right = segment_ends(left, right, wx, None, log2(SUB))
        march_values(left, right, tx, None, ix, inv_cx, None, store)


def prepare_depth(h, inv_cx, inv_cy):
    stack = (h.shape[1], LANES)
    count = stack[0] // STEPS
    shapes = [shape(*stack)] * 4 + [
        shape(3, count, LANES),
        shape(3 * log2(SUB), count, LANES),
        shape(3, count, LANES),
        shape(3 * log2(count), count, LANES),
        shape(1, 3 * stack[0]),
        shape(1, 3 * LANES),
        shape(*stack),
        shape(*stack),
    ]
    return pl.pallas_call(
        functools.partial(prepare_depth_kernel, inv_cx=inv_cx, inv_cy=inv_cy),
        out_shape=tuple(shapes),
        in_specs=[VMEM],
        out_specs=(VMEM,) * len(shapes),
        scratch_shapes=[pltpu.VMEM(stack, F32)] * 2,
        compiler_params=PARAMS,
        cost_estimate=pl.CostEstimate(flops=2_000_000, bytes_accessed=4_000_000, transcendentals=0),
        name="prepare_depth",
    )(h)


def prepare_rest_kernel(*refs):
    fields, outs, natural, turned = refs[:4], refs[4:12], refs[12], refs[13]
    for f, src in enumerate(fields):
        lay_out(src, outs[2 * f], outs[2 * f + 1], natural.at[f % 2], turned.at[f % 2])


def prepare_rest(*fields):
    stack = (fields[0].shape[1], LANES)
    return pl.pallas_call(
        prepare_rest_kernel,
        out_shape=(shape(*stack),) * 8,
        in_specs=[VMEM] * 4,
        out_specs=(VMEM,) * 8,
        scratch_shapes=[pltpu.VMEM((2, *stack), F32)] * 2,
        compiler_params=PARAMS,
        cost_estimate=pl.CostEstimate(flops=2_000_000, bytes_accessed=6_000_000, transcendentals=0),
        name="prepare_rest",
    )(*fields)


def low_high(axis, near, far):
    index, count = lax.axis_index(axis), lax.axis_size(axis)
    even = index % 2 == 0
    low = jnp.where(index > 0, jnp.where(even, far, near), 0.0)
    high = jnp.where(index < count - 1, jnp.where(even, near, far), 0.0)
    return low, high


def half_slope(a, c):
    return 0.5 * (jnp.maximum(jnp.minimum(a, c), 0.0) + jnp.minimum(jnp.maximum(a, c), 0.0))


def face_flux(left, right, opened):
    is_open = opened > 0.5
    hl = jnp.where(is_open, left[0], 1.0)
    hr = jnp.where(is_open, right[0], 1.0)
    joint = 1.0 / (hl * hr)
    ul = left[1] * (hr * joint)
    ur = right[1] * (hl * joint)
    gl = gravity * hl
    gr = gravity * hr
    fastest = jnp.maximum(jnp.abs(ul) + gl * lax.rsqrt(gl), jnp.abs(ur) + gr * lax.rsqrt(gr))
    scale = (0.5 * ratio) * opened
    mass = (left[1] + right[1]) - fastest * (right[0] - left[0])
    push = 0.5 * (gl * hl + gr * hr) + left[1] * ul + right[1] * ur - fastest * (right[1] - left[1])
    shear = left[2] * ul + right[2] * ur - fastest * (right[2] - left[2])
    return scale * mass, scale * push, scale * shear


def extended(ref, tile, lows, highs):
    sub = row_index((SUB, LANES))
    out = {}
    for n, row in enumerate(lows, 1):
        value = ref[at(tile, STEPS - n), :]
        out[-n] = jnp.where(sub == 0, row, pltpu.roll(value, 1, 0))
    for n, row in enumerate(highs):
        value = ref[at(tile, n), :]
        out[STEPS + n] = jnp.where(sub == SUB - 1, row, pltpu.roll(value, SUB - 1, 0))
    return lambda k: out[k] if k in out else ref[at(tile, k), :]


def tile_fluxes(fields, bed, wet, store, start=0, stop=STEPS, low_face=None, high_face=None):
    def states(k):
        both = []
        for w in fields:
            here = w(k)
            both.append((here, half_slope(here - w(k - 1), w(k + 1) - here)))
        return [w + s for w, s in both], [w - s for w, s in both]

    left, before, first = None, None, None
    for k in range(start - 1, stop):
        if k == start - 1 and low_face is not None:
            face = low_face
        elif k == stop - 1 and high_face is not None:
            face = high_face
        else:
            if left is None:
                left, _ = states(k)
            left_next, right = states(k + 1)
            face = face_flux(left, right, wet(k) * wet(k + 1))
            left = left_next
        if k >= start:
            store(k, [a - c for a, c in zip(face, before)], bed(k + 1) - bed(k - 1))
        first = face if first is None else first
        before = face
    return first, before


def march_source(inv_ref, scale, r_ref, t_ref, w_ref, s_ref, levels):
    count = inv_ref.shape[0] // STEPS
    c = jnp.zeros((count, LANES), F32)
    e = c
    for k in range(STEPS):
        inverse = full(inv_ref, k)
        c = c + e
        e = e + (scale * (inverse * inverse) * c - full(r_ref, k))
    sl = t_ref[0] * c
    s_ref[0] = sl
    sources = (sl, t_ref[2] * sl - e)
    for level in range(levels):
        after = tuple(pltpu.roll(v, count - (1 << level), 0) for v in sources)
        sources, middle = merge_sources(sources, after, tuple(w_ref[3 * level + j] for j in range(3)))
        s_ref[1 + level] = middle
    return sources


def flux_y_kernel(near, far, hy, py, qy, by, my, mass, shear, normal, across, along):
    tiles = hy.shape[0] // LANES
    low, high = low_high("gy", near[0:SUB, :], far[0:SUB, :])
    for tile in range(tiles):

        def extend(ref, row, layers):
            lows, highs = [], []
            for n in range(layers):
                last = at(tile - 1, STEPS - 1 - n).stop - 1
                first = at(tile + 1, n).start
                lows.append(low[row + layers - 1 - n : row + layers - n, :] if tile == 0 else ref[last : last + 1, :])
                highs.append(high[row + n : row + n + 1, :] if tile == tiles - 1 else ref[first : first + 1, :])
            return extended(ref, tile, lows, highs)

        def store(k, difference, bed):
            here, natural = at(tile, k), spread_rows(tile, k)
            across[natural, :] = difference[0]
            along[natural, :] = difference[2]
            pull = (0.5 * ratio * gravity) * hy[here, :]
            normal[here, :] = qy[here, :] - difference[1] - pull * bed

        tile_fluxes([extend(hy, 0, 2), extend(qy, 4, 2), extend(py, 2, 2)], extend(by, 6, 1), extend(my, 7, 1), store)
        span = tile_span(tile)
        mass[span, :] = across[span, :].T
        shear[span, :] = along[span, :].T


def fluxes_y(*arrays):
    stack = arrays[2].shape
    return pl.pallas_call(
        flux_y_kernel,
        out_shape=(shape(*stack),) * 3,
        in_specs=[VMEM] * len(arrays),
        out_specs=(VMEM,) * 3,
        scratch_shapes=[pltpu.VMEM(stack, F32)] * 2,
        compiler_params=PARAMS,
        cost_estimate=pl.CostEstimate(flops=4_000_000, bytes_accessed=4_000_000, transcendentals=0),
        name="fluxes_y",
    )(*arrays)


INNER = (2, STEPS - 2)
TALL = 16


def x_store(hx, px, mx, depth, push, across):
    def of_tile(tile):
        def store(k, difference, bed):
            here = at(tile, k)
            h = hx[here, :]
            depth[here, :] = h - mx[here, :] * difference[0]
            push[here, :] = px[here, :] - difference[1] - (0.5 * ratio * gravity) * h * bed
            across[here, :] = difference[2]

        return store

    return of_tile


def flux_x_inner_kernel(hx, px, qx, bx, mx, depth, push, across, faces):
    store = x_store(hx, px, mx, depth, push, across)
    for tile in range(hx.shape[0] // LANES):
        fields = [extended(v, tile, (), ()) for v in (hx, px, qx, bx, mx)]
        ends = tile_fluxes(fields[:3], fields[3], fields[4], store(tile), *INNER)
        for n, v in enumerate(ends[0] + ends[1]):
            faces[n, tile * SUB : (tile + 1) * SUB, :] = v
        for k in (*range(INNER[0]), *range(INNER[1], STEPS)):
            for ref in (depth, push, across):
                ref[at(tile, k), :] = jnp.zeros((SUB, LANES), F32)


def fluxes_x_inner(*arrays):
    stack = arrays[0].shape
    return pl.pallas_call(
        flux_x_inner_kernel,
        out_shape=(shape(*stack),) * 3 + (shape(6, stack[0] // STEPS, LANES),),
        in_specs=[VMEM] * len(arrays),
        out_specs=(VMEM,) * 4,
        compiler_params=PARAMS,
        cost_estimate=pl.CostEstimate(flops=4_000_000, bytes_accessed=4_000_000, transcendentals=0),
        name="fluxes_x_inner",
    )(*arrays)


def flux_x_kernel(
    near, far, hx, px, qx, bx, mx, ix, shear_y, push_in, faces, tx, wx, coef,
    depth, across, rx, sx, ends,
    push,
    *, inv_cx,
):
    tiles = hx.shape[0] // LANES
    low, high = low_high("gx", near[0], far[...])
    store = x_store(hx, px, mx, depth, push, across)
    for tile in range(tiles):
        span = tile_span(tile)

        def extend(ref, row, layers):
            lows = [low[row + layers - 1 - n : row + layers - n, span] for n in range(layers)]
            highs = [high[row + n : row + n + 1, span] for n in range(layers)]
            return extended(ref, tile, lows, highs)

        fields, bed, wet = [extend(hx, 0, 2), extend(px, 2, 2), extend(qx, 4, 2)], extend(bx, 6, 1), extend(mx, 7, 1)
        known = [faces[n, tile * SUB : (tile + 1) * SUB, :] for n in range(6)]
        tile_fluxes(fields, bed, wet, store(tile), 0, INNER[0], high_face=known[:3])
        tile_fluxes(fields, bed, wet, store(tile), INNER[1], STEPS, low_face=known[3:])
        for k in range(STEPS):
            here = at(tile, k)
            inverse = ix[here, :]
            total = (push_in if INNER[0] <= k < INNER[1] else push)[here, :] - shear_y[here, :]
            rx[here, :] = (inv_cx * (inverse * inverse)) * mx[here, :] * total
    sources = march_source(ix, inv_cx, rx, tx, wx, sx, log2(SUB))
    count = tiles * LANES
    ends[0:1, 0 : 3 * count] = coef[...]
    for i in range(2):
        for tile in range(tiles):
            first = (3 + i) * count + tile * LANES
            ends[0:1, first : first + LANES] = sources[i][tile * SUB : tile * SUB + 1, :]


def fluxes_x(*arrays, inv_cx):
    stack = arrays[2].shape
    count = stack[0] // STEPS
    shapes = (
        shape(*stack),
        shape(*stack),
        shape(*stack),
        shape(1 + log2(SUB), count, LANES),
        shape(1, 5 * stack[0]),
    )
    return pl.pallas_call(
        functools.partial(flux_x_kernel, inv_cx=inv_cx),
        out_shape=shapes,
        in_specs=[VMEM] * len(arrays),
        out_specs=(VMEM,) * len(shapes),
        scratch_shapes=[pltpu.VMEM(stack, F32)],
        compiler_params=PARAMS,
        name="fluxes_x",
    )(*arrays)


def join_y_kernel(
    depth_inner, across_inner, depth_outer, across_outer, mass_y, mx, normal_y, iy, my, ty, wy, coef,
    depth, ry, sy, ends, tall,
    across, turned,
    *, inv_cy,
):
    tiles = mx.shape[0] // LANES
    for tile in range(tiles):
        span = tile_span(tile)
        for k in range(STEPS):
            here = at(tile, k)
            inner = INNER[0] <= k < INNER[1]
            across[here, :] = (across_inner if inner else across_outer)[here, :]
            depth[here, :] = (depth_inner if inner else depth_outer)[here, :] - mx[here, :] * mass_y[here, :]
        turned[span, :] = across[span, :].T
        for k in range(STEPS):
            here = at(tile, k)
            inverse = iy[here, :]
            total = normal_y[here, :] - turned[spread_rows(tile, k), :]
            ry[here, :] = (inv_cy * (inverse * inverse)) * my[here, :] * total
    sources = march_source(iy, inv_cy, ry, ty, wy, sy, log2(SUB * tiles))
    ends[0:1, 0 : 3 * LANES] = coef[...]
    for i in range(2):
        ends[0:1, (3 + i) * LANES : (4 + i) * LANES] = sources[i][0:1, :]
    tall[...] = jnp.zeros_like(tall)
    tall[0:1, 0 : 5 * LANES] = ends[...]


def join_y(*arrays, inv_cy):
    stack = arrays[0].shape
    count = stack[0] // STEPS
    shapes = (
        shape(*stack),
        shape(*stack),
        shape(1 + log2(count), count, LANES),
        shape(1, 5 * LANES),
        shape(1, TALL * LANES),
    )
    return pl.pallas_call(
        functools.partial(join_y_kernel, inv_cy=inv_cy),
        out_shape=shapes,
        in_specs=[VMEM] * len(arrays),
        out_specs=(VMEM,) * len(shapes),
        scratch_shapes=[pltpu.VMEM(stack, F32)] * 2,
        compiler_params=PARAMS,
        cost_estimate=pl.CostEstimate(flops=2_000_000, bytes_accessed=2_000_000, transcendentals=0),
        name="join_y",
    )(*arrays)


PARTS = 1


def tile_writes(tiled, whole, tile, sems):
    rows = whole.shape[0]
    part = rows // PARTS
    copies = []
    for n in range(PARTS):
        copy = pltpu.make_async_copy(
            tiled.at[pl.ds(tile * rows + n * part, part), :],
            whole.at[pl.ds(n * part, part), pl.ds(tile * LANES, LANES)],
            sems.at[tile, n],
        )
        copy.start()
        copies.append(copy)
    return copies


def write_scratch(cols):
    return [pltpu.VMEM((cols, LANES), F32), pltpu.SemaphoreType.DMA((cols // LANES, PARTS))]


def depth_kernel(depth, out, natural, sems):
    writes = []
    for tile in range(depth.shape[0] // LANES):
        for k in range(STEPS):
            natural[spread_rows(tile, k), :] = depth[at(tile, k), :]
        writes += tile_writes(natural, out, tile, sems)
    for write in writes:
        write.wait()


def write_depth(depth, block):
    return pl.pallas_call(
        depth_kernel,
        out_shape=shape(*block),
        in_specs=[VMEM],
        out_specs=ANY,
        scratch_shapes=write_scratch(block[1]),
        compiler_params=PARAMS,
        cost_estimate=pl.CostEstimate(flops=100_000, bytes_accessed=2_000_000, transcendentals=0),
        name="write_depth",
    )(depth)


def rows_of(ref, count):
    return tuple(ref[0:1, i * count : (i + 1) * count] for i in range(5))


def ordered(axis, stage, mine, theirs):
    is_low = (lax.axis_index(axis) >> stage) % 2 == 0
    one = tuple(jnp.where(is_low, a, b) for a, b in zip(mine, theirs))
    two = tuple(jnp.where(is_low, b, a) for a, b in zip(mine, theirs))
    return is_low, merge(one, two)


def merge_kernel(mine, theirs, *refs, axis, stage):
    out = refs[-1]
    count = mine.shape[1] // 5
    _, (merged, _) = ordered(axis, stage, rows_of(mine, count), rows_of(theirs, count))
    for i, v in enumerate(merged):
        out[0:1, i * v.shape[1] : (i + 1) * v.shape[1]] = v


def merge_call(axis, stage, mine, theirs, beside):
    return pl.pallas_call(
        functools.partial(merge_kernel, axis=axis, stage=stage),
        out_shape=shape(*mine.shape),
        in_specs=[VMEM] * (2 + len(beside)),
        out_specs=VMEM,
        compiler_params=PARAMS,
        name="merge",
    )(mine, theirs, *beside)


def line_ends(axis, refs, is_crossed=False):
    steps = []
    parts = [rows_of(ref, refs[0].shape[1] // 5) for ref in refs]
    stage = 0
    while len(parts) > 4:
        is_low, (_, weights) = ordered(axis, stage, *parts[:2])
        steps.append((is_low, weights))
        parts = parts[2:]
        stage += 1
    if is_crossed:
        lower = (lax.axis_index(axis) >> (stage + 1)) % 2 == 0
        both = list(zip(*parts[2:]))
        parts[2] = tuple(jnp.where(lower, a, b) for a, b in both)
        parts[3] = tuple(jnp.where(lower, b, a) for a, b in both)
    is_low, (own, weights) = ordered(axis, stage, *parts[:2])
    steps.append((is_low, weights))
    _, (other, _) = ordered(axis, stage, *parts[2:])
    is_low, (whole, weights) = ordered(axis, stage + 1, own, other)
    steps.append((is_low, weights))
    t, _, gr, _, sr = whole
    left = jnp.zeros_like(t)
    right = sr / (t + gr + 1.0)
    for is_low, (w1, w2, source) in reversed(steps):
        middle = w1 * left + w2 * right + source
        left = jnp.where(is_low, left, middle)
        right = jnp.where(is_low, middle, right)
    return left, right


def segment_ends(left, right, w_ref, s_ref, levels):
    index = row_index(left.shape)
    for level in reversed(range(levels)):
        stride = 1 << level
        middle = w_ref[3 * level] * left + w_ref[3 * level + 1] * right
        if s_ref is not None:
            middle = middle + s_ref[1 + level]
        upper = (index >> level) % 2 == 1
        left, right = (
            jnp.where(upper, pltpu.roll(middle, stride, 0), left),
            jnp.where(upper, pltpu.roll(right, stride, 0), middle),
        )
    return left, right


def march_values(left, right, t_ref, s_ref, inv_ref, scale, r_ref, store):
    value = left
    change = t_ref[0] * (right - left) - t_ref[1] * left
    if s_ref is not None:
        change = change - s_ref[0]
    for k in range(STEPS):
        inverse = full(inv_ref, k)
        value = value + change
        push = scale * (inverse * inverse) * value
        change = change + (push if r_ref is None else push - full(r_ref, k))
        store(k, value * inverse)


def rest_x_kernel(inv_ref, r_ref, t_ref, w_ref, s_ref, out, *, scale):
    tiles = out.shape[0] // LANES
    zero = jnp.zeros((tiles * SUB, LANES), F32)

    def store(k, speed):
        for tile in range(tiles):
            out[at(tile, k), :] = speed[tile * SUB : (tile + 1) * SUB, :]

    left, right = segment_ends(zero, zero, w_ref, s_ref, log2(SUB))
    march_values(left, right, t_ref, s_ref, inv_ref, scale, r_ref, store)


def rest_x(*pieces, scale):
    return pl.pallas_call(
        functools.partial(rest_x_kernel, scale=scale),
        out_shape=shape(*pieces[0].shape),
        in_specs=[VMEM] * len(pieces),
        out_specs=VMEM,
        compiler_params=PARAMS,
        cost_estimate=pl.CostEstimate(flops=1_000_000, bytes_accessed=2_000_000, transcendentals=0),
        name="rest_x",
    )(*pieces)


def solve_x_kernel(from_left, from_right, rest, *refs):
    parts, (out, natural, sems) = refs[:-3], refs[-3:]
    left, right = line_ends("gx", parts, True)
    writes = []
    for tile in range(out.shape[1] // LANES):
        span = tile_span(tile)
        for k in range(STEPS):
            here = at(tile, k)
            natural[spread_rows(tile, k), :] = (
                from_left[here, :] * left[:, span] + from_right[here, :] * right[:, span] + rest[here, :]
            )
        writes += tile_writes(natural, out, tile, sems)
    for write in writes:
        write.wait()


def solve_y_kernel(inv_ref, r_ref, t_ref, w_ref, s_ref, *refs, scale):
    parts, (out, natural, sems, turned) = refs[:-4], refs[-4:]
    tiles = out.shape[1] // LANES
    ends = line_ends("gy", parts)
    ends = [jnp.broadcast_to(row, (tiles * SUB, LANES)) for row in ends]
    left, right = segment_ends(*ends, w_ref, s_ref, log2(tiles * SUB))

    def store(k, speed):
        for tile in range(tiles):
            turned[spread_rows(tile, k), :] = speed[tile * SUB : (tile + 1) * SUB, :]

    march_values(left, right, t_ref, s_ref, inv_ref, scale, r_ref, store)
    writes = []
    for tile in range(tiles):
        block = turned[tile_span(tile), :].T
        for k in range(STEPS):
            natural[spread_rows(tile, k), :] = block[k * SUB : (k + 1) * SUB, :]
        writes += tile_writes(natural, out, tile, sems)
    for write in writes:
        write.wait()


def solve(kernel, name, pieces, parts, block, extra=()):
    return pl.pallas_call(
        kernel,
        out_shape=shape(*block),
        in_specs=[VMEM] * (len(pieces) + len(parts)),
        out_specs=ANY,
        scratch_shapes=write_scratch(block[1]) + list(extra),
        compiler_params=PARAMS,
        cost_estimate=pl.CostEstimate(flops=1_000_000, bytes_accessed=4_000_000, transcendentals=0),
        name=name,
    )(*pieces, *parts)


def hand_on(value, axis):
    count = lax.axis_size(axis)
    far = [i + 2 if i % 2 == 0 else i - 2 for i in range(count)]
    return lax.ppermute(value, axis, [(i, t if 0 <= t < count else i ^ 1) for i, t in enumerate(far)])


def shift_pair(value, axis):
    count = lax.axis_size(axis)
    other = [((i - 1) ^ 1) + 1 for i in range(count)]
    return lax.ppermute(value, axis, [(i, o if 0 <= o < count else i) for i, o in enumerate(other)])


def cross(value, axis, mask):
    return lax.ppermute(value, axis, [(i, i ^ mask) for i in range(lax.axis_size(axis))])


def crossed(value, axis, stage, half):
    pairs = []
    for i in range(lax.axis_size(axis)):
        upper = (i >> (stage + 1)) & 1
        pairs.append((i, i ^ ((2 if upper == half else 3) << stage)))
    return lax.ppermute(value, axis, pairs)


def parts_of_line(axis, mine, relay, beside=(), tall=None):
    parts = []
    last = log2(lax.axis_size(axis)) - 2
    for stage in range(last):
        theirs = cross(mine, axis, 1 << stage)
        parts += [mine, theirs]
        mine = merge_call(axis, stage, mine, theirs, beside)
    if relay:
        first = cross(mine, axis, 1 << last)
        second = cross(mine if tall is None else tall, axis, 2 << last)
        both = cross(second[:, 0 : mine.shape[1]], axis, 1 << last)
    else:
        first = cross(mine, axis, 1 << last)
        second, both = (crossed(mine, axis, last, n) for n in (1, 0))
    return parts + [mine, first, second, both]


def on_device(h, p, q, b, m):
    block = h.shape
    rows, cols = block
    inv_cx = 3.0 / (rows * lax.axis_size("gx") / 4.0) ** 2
    inv_cy = 3.0 / (cols * lax.axis_size("gy") / 4.0) ** 2
    slabs_x = pack_x(h, p, q, b, m)
    near_x = cross(slabs_x, "gx", 1)
    near_y, far_y = pack_y(h, p, q, b, m, after=slabs_x)
    near_y, far_y = cross(near_y, "gy", 1), shift_pair(far_y, "gy")
    hx, hy, ix, iy, tx, wx, ty, wy, coef_x, coef_y, left_x, right_x = prepare_depth(h, inv_cx, inv_cy)
    far_x = hand_on(second_of(near_x, coef_x, near_y), "gx")
    px, py, qx, qy, bx, by, mx, my = prepare_rest(p, q, b, m)
    depth_inner, push_inner, across_inner, faces = fluxes_x_inner(hx, px, qx, bx, mx)
    mass_y, shear_y, normal_y = fluxes_y(near_y, far_y, hy, py, qy, by, my)
    depth_outer, across_outer, rx, sx, end_x = fluxes_x(
        near_x, far_x, hx, px, qx, bx, mx, ix, shear_y, push_inner, faces, tx, wx, coef_x, inv_cx=inv_cx
    )
    depth, ry, sy, end_y, tall_y = join_y(
        depth_inner, across_inner, depth_outer, across_outer, mass_y, mx, normal_y, iy, my, ty, wy, coef_y, inv_cy=inv_cy
    )
    new_depth = write_depth(depth, block)
    parts_y = parts_of_line("gy", end_y, True, tall=tall_y if lax.axis_size("gy") == 4 else None)
    parts_x = parts_of_line("gx", end_x, False, parts_y[1:2])
    turned = [pltpu.VMEM((cols, LANES), F32)]
    solve_y_scaled = functools.partial(solve_y_kernel, scale=inv_cy)
    vy = solve(solve_y_scaled, "solve_y", (iy, ry, ty, wy, sy), parts_y, block, turned)
    own_x = rest_x(ix, rx, tx, wx, sx, scale=inv_cx)
    vx = solve(solve_x_kernel, "solve_x", (left_x, right_x, own_x), parts_x, block)
    return new_depth, vx, vy


def solution(mesh):
    spec = P("gx", "gy")
    return jax.shard_map(
        on_device,
        mesh=mesh,
        in_specs=(spec,) * 5,
        out_specs=(spec,) * 3,
        check_vma=False,
    )
```

```python
import functools

import jax
import jax.numpy as jnp
from jax import lax
from jax.experimental import pallas as pl
from jax.experimental.pallas import tpu as pltpu
from jax.sharding import PartitionSpec as P

gravity = 9.81
ratio = 0.05
LANES = 128
SUB = 8
STEPS = LANES // SUB
F32 = jnp.float32
VMEM = pl.BlockSpec(memory_space=pltpu.VMEM)
HBM = pl.BlockSpec(memory_space=pltpu.HBM)
ANY = pl.BlockSpec(memory_space=pl.ANY)
PARAMS = pltpu.CompilerParams(vmem_limit_bytes=16 * 1024 * 1024)


def lane_index(shape):
    return lax.broadcasted_iota(jnp.int32, shape, len(shape) - 1)


def row_index(shape):
    return lax.broadcasted_iota(jnp.int32, shape, len(shape) - 2)


def at(tile, step):
    first = tile * LANES + step * SUB
    return slice(first, first + SUB)


def tile_span(tile):
    return slice(tile * LANES, (tile + 1) * LANES)


def spread_rows(tile, step):
    return pl.ds(tile * LANES + step, SUB, stride=STEPS)


def shape(*dims):
    return jax.ShapeDtypeStruct(dims, F32)


def pack_x_kernel(h, p, q, b, m, slabs, top, bottom, itop, ibottom, sems):
    rows = h.shape[0]
    copies = []
    for f, src in enumerate((h, p, q, b, m)):
        for side, (target, whole, row) in enumerate(((top, itop, 0), (bottom, ibottom, rows - SUB))):
            copy = pltpu.make_async_copy(
                src.at[pl.ds(row, SUB), :], target.at[f] if f < 4 else whole, sems.at[2 * f + side]
            )
            copy.start()
            copies.append(copy)
    for copy in copies:
        copy.wait()
    first = jnp.concatenate(
        [top[0, 0:2, :], top[1, 0:2, :], top[2, 0:2, :], top[3, 0:1, :], itop[0:1, :].astype(F32)]
    )
    last = jnp.concatenate(
        [
            bottom[0, SUB - 2 : SUB, :],
            bottom[1, SUB - 2 : SUB, :],
            bottom[2, SUB - 2 : SUB, :],
            bottom[3, SUB - 1 : SUB, :],
            ibottom[SUB - 1 : SUB, :].astype(F32),
        ]
    )
    even = lax.axis_index("gx") % 2 == 0
    slabs[0] = jnp.where(even, last, first)
    slabs[1] = jnp.where(even, first, last)


def pack_x(*fields):
    cols = fields[0].shape[1]
    return pl.pallas_call(
        pack_x_kernel,
        out_shape=shape(2, SUB, cols),
        in_specs=[HBM] * 5,
        out_specs=VMEM,
        scratch_shapes=[
            pltpu.VMEM((4, SUB, cols), F32),
            pltpu.VMEM((4, SUB, cols), F32),
            pltpu.VMEM((SUB, cols), jnp.int32),
            pltpu.VMEM((SUB, cols), jnp.int32),
            pltpu.SemaphoreType.DMA((10,)),
        ],
        compiler_params=PARAMS,
        name="pack_x",
    )(*[pltpu.with_memory_space_constraint(v, pltpu.HBM) for v in fields])


def pack_y_kernel(h, p, q, b, m, _, near, far, natural):
    rows, cols = h.shape
    lane = lane_index((rows, LANES))
    out = None
    for f, src in enumerate((h, p, q, b, m)):
        both = jnp.where(lane < LANES // 2, src[:, 0:LANES], src[:, cols - LANES : cols]).astype(F32)
        moved = pltpu.roll(both, 4 * f + 2, 1)
        out = moved if out is None else jnp.where(lane >= 4 * f, moved, out)
    natural[...] = out
    turned = jnp.concatenate([natural[spread_rows(0, k), :] for k in range(STEPS)]).T
    last = jnp.concatenate([turned[0:2], turned[4:6], turned[8:10], turned[13:14], turned[17:18]])
    first = jnp.concatenate([turned[2:4], turned[6:8], turned[10:12], turned[14:15], turned[18:19]])
    even = lax.axis_index("gy") % 2 == 0
    for slab, value in ((near, jnp.where(even, last, first)), (far, jnp.where(even, first, last))):
        slab[...] = jnp.zeros_like(slab)
        slab[0:SUB, :] = value


def pack_y(*fields, after):
    rows = fields[0].shape[0]
    return pl.pallas_call(
        pack_y_kernel,
        out_shape=(shape(1 * SUB, rows), shape(4 * SUB, rows)),
        in_specs=[VMEM] * 6,
        out_specs=(VMEM, VMEM),
        scratch_shapes=[pltpu.VMEM((rows, LANES), F32)],
        compiler_params=PARAMS,
        cost_estimate=pl.CostEstimate(flops=500_000, bytes_accessed=1_000_000, transcendentals=0),
        name="pack_y",
    )(*fields, after)


def tie_kernel(both, *refs):
    refs[-1][...] = both[1]


def second_of(both, *after):
    return pl.pallas_call(
        tie_kernel,
        out_shape=shape(*both.shape[1:]),
        in_specs=[VMEM] * (1 + len(after)),
        out_specs=VMEM,
        compiler_params=PARAMS,
        name="second_of",
    )(both, *after)


def merge_coefficients(one, two):
    t1, gl1, gr1 = one
    t2, gl2, gr2 = two
    shunt = gr1 + gl2
    inverse = 1.0 / (t1 + t2 + shunt)
    w1, w2 = t1 * inverse, t2 * inverse
    return (w1 * t2, gl1 + w1 * shunt, gr2 + w2 * shunt), (w1, w2, inverse)


def merge_sources(one, two, weights):
    w1, w2, inverse = weights
    source = one[1] - two[0]
    return (one[0] - w1 * source, two[1] + w2 * source), source * inverse


def merge(one, two):
    coefficients, weights = merge_coefficients(one[:3], two[:3])
    sources, middle = merge_sources(one[3:], two[3:], weights)
    return coefficients + sources, weights[:2] + (middle,)


def log2(count):
    return (count - 1).bit_length()


def full(ref, step):
    return jnp.concatenate([ref[at(tile, step), :] for tile in range(ref.shape[0] // LANES)])


def march_depth(inv_ref, scale, out_t, out_w, levels):
    count = inv_ref.shape[0] // STEPS
    zero = jnp.zeros((count, LANES), F32)
    alpha, gamma, beta, delta = zero, zero, zero, zero
    for k in range(STEPS):
        inverse = full(inv_ref, k)
        d = scale * (inverse * inverse)
        alpha = alpha + gamma
        gamma = gamma + d * (1.0 + alpha)
        beta = beta + delta
        delta = delta + d * ((k + 1.0) + beta)
    t = 1.0 / (STEPS + beta)
    out_t[0] = t
    out_t[1] = t * alpha
    out_t[2] = 1.0 + delta
    coefficients = (t, t * alpha, t * delta)
    for level in range(levels):
        after = tuple(pltpu.roll(v, count - (1 << level), 0) for v in coefficients)
        coefficients, weights = merge_coefficients(coefficients, after)
        for j, v in enumerate(weights):
            out_w[3 * level + j] = v
    return coefficients


def lay_out(src, xs, ys, natural, turned):
    for tile in range(xs.shape[0] // LANES):
        natural[tile_span(tile), :] = src[:, tile_span(tile)].astype(F32)
        for k in range(STEPS):
            xs[at(tile, k), :] = natural[spread_rows(tile, k), :]
        turned[tile_span(tile), :] = xs[tile_span(tile), :].T
        for k in range(STEPS):
            ys[at(tile, k), :] = turned[spread_rows(tile, k), :]


def prepare_depth_kernel(
    h, hx, hy, ix, iy, tx, wx, ty, wy, endx, endy, from_left, from_right, natural, turned, *, inv_cx, inv_cy
):
    tiles = hx.shape[0] // LANES
    lay_out(h, hx, hy, natural, turned)
    ix[...] = 1.0 / hx[...]
    iy[...] = 1.0 / hy[...]
    ends_x = march_depth(ix, inv_cx, tx, wx, log2(SUB))
    ends_y = march_depth(iy, inv_cy, ty, wy, log2(SUB * tiles))
    for i in range(3):
        for tile in range(tiles):
            first = (i * tiles + tile) * LANES
            endx[0:1, first : first + LANES] = ends_x[i][tile * SUB : tile * SUB + 1, :]
        endy[0:1, i * LANES : (i + 1) * LANES] = ends_y[i][0:1, :]
    one = jnp.ones((tiles * SUB, LANES), F32)
    zero = jnp.zeros_like(one)
    for out, left, right in ((from_left, one, zero), (from_right, zero, one)):

        def store(k, speed):
            for tile in range(tiles):
                out[at(tile, k), :] = speed[tile * SUB : (tile + 1) * SUB, :]

        left, right = segment_ends(left, right, wx, None, log2(SUB))
        march_values(left, right, tx, None, ix, inv_cx, None, store)


def prepare_depth(h, inv_cx, inv_cy):
    stack = (h.shape[1], LANES)
    count = stack[0] // STEPS
    shapes = [shape(*stack)] * 4 + [
        shape(3, count, LANES),
        shape(3 * log2(SUB), count, LANES),
        shape(3, count, LANES),
        shape(3 * log2(count), count, LANES),
        shape(1, 3 * stack[0]),
        shape(1, 3 * LANES),
        shape(*stack),
        shape(*stack),
    ]
    return pl.pallas_call(
        functools.partial(prepare_depth_kernel, inv_cx=inv_cx, inv_cy=inv_cy),
        out_shape=tuple(shapes),
        in_specs=[VMEM],
        out_specs=(VMEM,) * len(shapes),
        scratch_shapes=[pltpu.VMEM(stack, F32)] * 2,
        compiler_params=PARAMS,
        cost_estimate=pl.CostEstimate(flops=2_000_000, bytes_accessed=4_000_000, transcendentals=0),
        name="prepare_depth",
    )(h)


def prepare_rest_kernel(*refs):
    fields, outs, natural, turned = refs[:4], refs[4:12], refs[12], refs[13]
    for f, src in enumerate(fields):
        lay_out(src, outs[2 * f], outs[2 * f + 1], natural.at[f % 2], turned.at[f % 2])


def prepare_rest(*fields):
    stack = (fields[0].shape[1], LANES)
    return pl.pallas_call(
        prepare_rest_kernel,
        out_shape=(shape(*stack),) * 8,
        in_specs=[VMEM] * 4,
        out_specs=(VMEM,) * 8,
        scratch_shapes=[pltpu.VMEM((2, *stack), F32)] * 2,
        compiler_params=PARAMS,
        cost_estimate=pl.CostEstimate(flops=2_000_000, bytes_accessed=6_000_000, transcendentals=0),
        name="prepare_rest",
    )(*fields)


def low_high(axis, near, far):
    index, count = lax.axis_index(axis), lax.axis_size(axis)
    even = index % 2 == 0
    low = jnp.where(index > 0, jnp.where(even, far, near), 0.0)
    high = jnp.where(index < count - 1, jnp.where(even, near, far), 0.0)
    return low, high


def half_slope(a, c):
    return 0.5 * (jnp.maximum(jnp.minimum(a, c), 0.0) + jnp.minimum(jnp.maximum(a, c), 0.0))


def face_flux(left, right, opened):
    is_open = opened > 0.5
    hl = jnp.where(is_open, left[0], 1.0)
    hr = jnp.where(is_open, right[0], 1.0)
    joint = 1.0 / (hl * hr)
    ul = left[1] * (hr * joint)
    ur = right[1] * (hl * joint)
    gl = gravity * hl
    gr = gravity * hr
    fastest = jnp.maximum(jnp.abs(ul) + gl * lax.rsqrt(gl), jnp.abs(ur) + gr * lax.rsqrt(gr))
    scale = (0.5 * ratio) * opened
    mass = (left[1] + right[1]) - fastest * (right[0] - left[0])
    push = 0.5 * (gl * hl + gr * hr) + left[1] * ul + right[1] * ur - fastest * (right[1] - left[1])
    shear = left[2] * ul + right[2] * ur - fastest * (right[2] - left[2])
    return scale * mass, scale * push, scale * shear


def extended(ref, tile, lows, highs):
    sub = row_index((SUB, LANES))
    out = {}
    for n, row in enumerate(lows, 1):
        value = ref[at(tile, STEPS - n), :]
        out[-n] = jnp.where(sub == 0, row, pltpu.roll(value, 1, 0))
    for n, row in enumerate(highs):
        value = ref[at(tile, n), :]
        out[STEPS + n] = jnp.where(sub == SUB - 1, row, pltpu.roll(value, SUB - 1, 0))
    return lambda k: out[k] if k in out else ref[at(tile, k), :]


def tile_fluxes(fields, bed, wet, store, start=0, stop=STEPS, low_face=None, high_face=None):
    def states(k):
        both = []
        for w in fields:
            here = w(k)
            both.append((here, half_slope(here - w(k - 1), w(k + 1) - here)))
        return [w + s for w, s in both], [w - s for w, s in both]

    left, before, first = None, None, None
    for k in range(start - 1, stop):
        if k == start - 1 and low_face is not None:
            face = low_face
        elif k == stop - 1 and high_face is not None:
            face = high_face
        else:
            if left is None:
                left, _ = states(k)
            left_next, right = states(k + 1)
            face = face_flux(left, right, wet(k) * wet(k + 1))
            left = left_next
        if k >= start:
            store(k, [a - c for a, c in zip(face, before)], bed(k + 1) - bed(k - 1))
        first = face if first is None else first
        before = face
    return first, before


def march_source(inv_ref, scale, r_ref, t_ref, w_ref, s_ref, levels):
    count = inv_ref.shape[0] // STEPS
    c = jnp.zeros((count, LANES), F32)
    e = c
    for k in range(STEPS):
        inverse = full(inv_ref, k)
        c = c + e
        e = e + (scale * (inverse * inverse) * c - full(r_ref, k))
    sl = t_ref[0] * c
    s_ref[0] = sl
    sources = (sl, t_ref[2] * sl - e)
    for level in range(levels):
        after = tuple(pltpu.roll(v, count - (1 << level), 0) for v in sources)
        sources, middle = merge_sources(sources, after, tuple(w_ref[3 * level + j] for j in range(3)))
        s_ref[1 + level] = middle
    return sources


def flux_y_kernel(near, far, hy, py, qy, by, my, mass, shear, normal, across, along):
    tiles = hy.shape[0] // LANES
    low, high = low_high("gy", near[0:SUB, :], far[0:SUB, :])
    for tile in range(tiles):

        def extend(ref, row, layers):
            lows, highs = [], []
            for n in range(layers):
                last = at(tile - 1, STEPS - 1 - n).stop - 1
                first = at(tile + 1, n).start
                lows.append(low[row + layers - 1 - n : row + layers - n, :] if tile == 0 else ref[last : last + 1, :])
                highs.append(high[row + n : row + n + 1, :] if tile == tiles - 1 else ref[first : first + 1, :])
            return extended(ref, tile, lows, highs)

        def store(k, difference, bed):
            here, natural = at(tile, k), spread_rows(tile, k)
            across[natural, :] = difference[0]
            along[natural, :] = difference[2]
            pull = (0.5 * ratio * gravity) * hy[here, :]
            normal[here, :] = qy[here, :] - difference[1] - pull * bed

        tile_fluxes([extend(hy, 0, 2), extend(qy, 4, 2), extend(py, 2, 2)], extend(by, 6, 1), extend(my, 7, 1), store)
        span = tile_span(tile)
        mass[span, :] = across[span, :].T
        shear[span, :] = along[span, :].T


def fluxes_y(*arrays):
    stack = arrays[2].shape
    return pl.pallas_call(
        flux_y_kernel,
        out_shape=(shape(*stack),) * 3,
        in_specs=[VMEM] * len(arrays),
        out_specs=(VMEM,) * 3,
        scratch_shapes=[pltpu.VMEM(stack, F32)] * 2,
        compiler_params=PARAMS,
        cost_estimate=pl.CostEstimate(flops=4_000_000, bytes_accessed=4_000_000, transcendentals=0),
        name="fluxes_y",
    )(*arrays)


INNER = (2, STEPS - 2)
TALL = 16


def x_store(hx, px, mx, depth, push, across):
    def of_tile(tile):
        def store(k, difference, bed):
            here = at(tile, k)
            h = hx[here, :]
            depth[here, :] = h - mx[here, :] * difference[0]
            push[here, :] = px[here, :] - difference[1] - (0.5 * ratio * gravity) * h * bed
            across[here, :] = difference[2]

        return store

    return of_tile


def flux_x_inner_kernel(hx, px, qx, bx, mx, depth, push, across, faces):
    store = x_store(hx, px, mx, depth, push, across)
    for tile in range(hx.shape[0] // LANES):
        fields = [extended(v, tile, (), ()) for v in (hx, px, qx, bx, mx)]
        ends = tile_fluxes(fields[:3], fields[3], fields[4], store(tile), *INNER)
        for n, v in enumerate(ends[0] + ends[1]):
            faces[n, tile * SUB : (tile + 1) * SUB, :] = v
        for k in (*range(INNER[0]), *range(INNER[1], STEPS)):
            for ref in (depth, push, across):
                ref[at(tile, k), :] = jnp.zeros((SUB, LANES), F32)


def fluxes_x_inner(*arrays):
    stack = arrays[0].shape
    return pl.pallas_call(
        flux_x_inner_kernel,
        out_shape=(shape(*stack),) * 3 + (shape(6, stack[0] // STEPS, LANES),),
        in_specs=[VMEM] * len(arrays),
        out_specs=(VMEM,) * 4,
        compiler_params=PARAMS,
        cost_estimate=pl.CostEstimate(flops=4_000_000, bytes_accessed=4_000_000, transcendentals=0),
        name="fluxes_x_inner",
    )(*arrays)


def flux_x_kernel(
    near, far, hx, px, qx, bx, mx, ix, shear_y, push_in, faces, tx, wx, coef,
    depth, across, rx, sx, ends,
    push,
    *, inv_cx,
):
    tiles = hx.shape[0] // LANES
    low, high = low_high("gx", near[0], far[...])
    store = x_store(hx, px, mx, depth, push, across)
    for tile in range(tiles):
        span = tile_span(tile)

        def extend(ref, row, layers):
            lows = [low[row + layers - 1 - n : row + layers - n, span] for n in range(layers)]
            highs = [high[row + n : row + n + 1, span] for n in range(layers)]
            return extended(ref, tile, lows, highs)

        fields, bed, wet = [extend(hx, 0, 2), extend(px, 2, 2), extend(qx, 4, 2)], extend(bx, 6, 1), extend(mx, 7, 1)
        known = [faces[n, tile * SUB : (tile + 1) * SUB, :] for n in range(6)]
        tile_fluxes(fields, bed, wet, store(tile), 0, INNER[0], high_face=known[:3])
        tile_fluxes(fields, bed, wet, store(tile), INNER[1], STEPS, low_face=known[3:])
        for k in range(STEPS):
            here = at(tile, k)
            inverse = ix[here, :]
            total = (push_in if INNER[0] <= k < INNER[1] else push)[here, :] - shear_y[here, :]
            rx[here, :] = (inv_cx * (inverse * inverse)) * mx[here, :] * total
    sources = march_source(ix, inv_cx, rx, tx, wx, sx, log2(SUB))
    count = tiles * LANES
    ends[0:1, 0 : 3 * count] = coef[...]
    for i in range(2):
        for tile in range(tiles):
            first = (3 + i) * count + tile * LANES
            ends[0:1, first : first + LANES] = sources[i][tile * SUB : tile * SUB + 1, :]


def fluxes_x(*arrays, inv_cx):
    stack = arrays[2].shape
    count = stack[0] // STEPS
    shapes = (
        shape(*stack),
        shape(*stack),
        shape(*stack),
        shape(1 + log2(SUB), count, LANES),
        shape(1, 5 * stack[0]),
    )
    return pl.pallas_call(
        functools.partial(flux_x_kernel, inv_cx=inv_cx),
        out_shape=shapes,
        in_specs=[VMEM] * len(arrays),
        out_specs=(VMEM,) * len(shapes),
        scratch_shapes=[pltpu.VMEM(stack, F32)],
        compiler_params=PARAMS,
        name="fluxes_x",
    )(*arrays)


def join_y_kernel(
    depth_inner, across_inner, depth_outer, across_outer, mass_y, mx, normal_y, iy, my, ty, wy, coef,
    depth, ry, sy, ends, tall,
    across, turned,
    *, inv_cy,
):
    tiles = mx.shape[0] // LANES
    for tile in range(tiles):
        span = tile_span(tile)
        for k in range(STEPS):
            here = at(tile, k)
            inner = INNER[0] <= k < INNER[1]
            across[here, :] = (across_inner if inner else across_outer)[here, :]
            depth[here, :] = (depth_inner if inner else depth_outer)[here, :] - mx[here, :] * mass_y[here, :]
        turned[span, :] = across[span, :].T
        for k in range(STEPS):
            here = at(tile, k)
            inverse = iy[here, :]
            total = normal_y[here, :] - turned[spread_rows(tile, k), :]
            ry[here, :] = (inv_cy * (inverse * inverse)) * my[here, :] * total
    sources = march_source(iy, inv_cy, ry, ty, wy, sy, log2(SUB * tiles))
    ends[0:1, 0 : 3 * LANES] = coef[...]
    for i in range(2):
        ends[0:1, (3 + i) * LANES : (4 + i) * LANES] = sources[i][0:1, :]
    tall[...] = jnp.zeros_like(tall)
    tall[0:1, 0 : 5 * LANES] = ends[...]


def join_y(*arrays, inv_cy):
    stack = arrays[0].shape
    count = stack[0] // STEPS
    shapes = (
        shape(*stack),
        shape(*stack),
        shape(1 + log2(count), count, LANES),
        shape(1, 5 * LANES),
        shape(1, TALL * LANES),
    )
    return pl.pallas_call(
        functools.partial(join_y_kernel, inv_cy=inv_cy),
        out_shape=shapes,
        in_specs=[VMEM] * len(arrays),
        out_specs=(VMEM,) * len(shapes),
        scratch_shapes=[pltpu.VMEM(stack, F32)] * 2,
        compiler_params=PARAMS,
        cost_estimate=pl.CostEstimate(flops=2_000_000, bytes_accessed=2_000_000, transcendentals=0),
        name="join_y",
    )(*arrays)


PARTS = 1


def tile_writes(tiled, whole, tile, sems):
    rows = whole.shape[0]
    part = rows // PARTS
    copies = []
    for n in range(PARTS):
        copy = pltpu.make_async_copy(
            tiled.at[pl.ds(tile * rows + n * part, part), :],
            whole.at[pl.ds(n * part, part), pl.ds(tile * LANES, LANES)],
            sems.at[tile, n],
        )
        copy.start()
        copies.append(copy)
    return copies


def write_scratch(cols):
    return [pltpu.VMEM((cols, LANES), F32), pltpu.SemaphoreType.DMA((cols // LANES, PARTS))]


def depth_kernel(depth, out, natural, sems):
    writes = []
    for tile in range(depth.shape[0] // LANES):
        for k in range(STEPS):
            natural[spread_rows(tile, k), :] = depth[at(tile, k), :]
        writes += tile_writes(natural, out, tile, sems)
    for write in writes:
        write.wait()


def write_depth(depth, block):
    return pl.pallas_call(
        depth_kernel,
        out_shape=shape(*block),
        in_specs=[VMEM],
        out_specs=ANY,
        scratch_shapes=write_scratch(block[1]),
        compiler_params=PARAMS,
        cost_estimate=pl.CostEstimate(flops=100_000, bytes_accessed=2_000_000, transcendentals=0),
        name="write_depth",
    )(depth)


def rows_of(ref, count):
    return tuple(ref[0:1, i * count : (i + 1) * count] for i in range(5))


def ordered(axis, stage, mine, theirs):
    is_low = (lax.axis_index(axis) >> stage) % 2 == 0
    one = tuple(jnp.where(is_low, a, b) for a, b in zip(mine, theirs))
    two = tuple(jnp.where(is_low, b, a) for a, b in zip(mine, theirs))
    return is_low, merge(one, two)


def merge_kernel(mine, theirs, *refs, axis, stage):
    out = refs[-1]
    count = mine.shape[1] // 5
    _, (merged, _) = ordered(axis, stage, rows_of(mine, count), rows_of(theirs, count))
    for i, v in enumerate(merged):
        out[0:1, i * v.shape[1] : (i + 1) * v.shape[1]] = v


def merge_call(axis, stage, mine, theirs, beside):
    return pl.pallas_call(
        functools.partial(merge_kernel, axis=axis, stage=stage),
        out_shape=shape(*mine.shape),
        in_specs=[VMEM] * (2 + len(beside)),
        out_specs=VMEM,
        compiler_params=PARAMS,
        name="merge",
    )(mine, theirs, *beside)


def line_ends(axis, refs, is_crossed=False):
    steps = []
    parts = [rows_of(ref, refs[0].shape[1] // 5) for ref in refs]
    stage = 0
    while len(parts) > 4:
        is_low, (_, weights) = ordered(axis, stage, *parts[:2])
        steps.append((is_low, weights))
        parts = parts[2:]
        stage += 1
    if is_crossed:
        lower = (lax.axis_index(axis) >> (stage + 1)) % 2 == 0
        both = list(zip(*parts[2:]))
        parts[2] = tuple(jnp.where(lower, a, b) for a, b in both)
        parts[3] = tuple(jnp.where(lower, b, a) for a, b in both)
    is_low, (own, weights) = ordered(axis, stage, *parts[:2])
    steps.append((is_low, weights))
    _, (other, _) = ordered(axis, stage, *parts[2:])
    is_low, (whole, weights) = ordered(axis, stage + 1, own, other)
    steps.append((is_low, weights))
    t, _, gr, _, sr = whole
    left = jnp.zeros_like(t)
    right = sr / (t + gr + 1.0)
    for is_low, (w1, w2, source) in reversed(steps):
        middle = w1 * left + w2 * right + source
        left = jnp.where(is_low, left, middle)
        right = jnp.where(is_low, middle, right)
    return left, right


def segment_ends(left, right, w_ref, s_ref, levels):
    index = row_index(left.shape)
    for level in reversed(range(levels)):
        stride = 1 << level
        middle = w_ref[3 * level] * left + w_ref[3 * level + 1] * right
        if s_ref is not None:
            middle = middle + s_ref[1 + level]
        upper = (index >> level) % 2 == 1
        left, right = (
            jnp.where(upper, pltpu.roll(middle, stride, 0), left),
            jnp.where(upper, pltpu.roll(right, stride, 0), middle),
        )
    return left, right


def march_values(left, right, t_ref, s_ref, inv_ref, scale, r_ref, store):
    value = left
    change = t_ref[0] * (right - left) - t_ref[1] * left
    if s_ref is not None:
        change = change - s_ref[0]
    for k in range(STEPS):
        inverse = full(inv_ref, k)
        value = value + change
        push = scale * (inverse * inverse) * value
        change = change + (push if r_ref is None else push - full(r_ref, k))
        store(k, value * inverse)


def rest_x_kernel(inv_ref, r_ref, t_ref, w_ref, s_ref, out, *, scale):
    tiles = out.shape[0] // LANES
    zero = jnp.zeros((tiles * SUB, LANES), F32)

    def store(k, speed):
        for tile in range(tiles):
            out[at(tile, k), :] = speed[tile * SUB : (tile + 1) * SUB, :]

    left, right = segment_ends(zero, zero, w_ref, s_ref, log2(SUB))
    march_values(left, right, t_ref, s_ref, inv_ref, scale, r_ref, store)


def rest_x(*pieces, scale):
    return pl.pallas_call(
        functools.partial(rest_x_kernel, scale=scale),
        out_shape=shape(*pieces[0].shape),
        in_specs=[VMEM] * len(pieces),
        out_specs=VMEM,
        compiler_params=PARAMS,
        cost_estimate=pl.CostEstimate(flops=1_000_000, bytes_accessed=2_000_000, transcendentals=0),
        name="rest_x",
    )(*pieces)


def solve_x_kernel(from_left, from_right, rest, *refs):
    parts, (out, natural, sems) = refs[:-3], refs[-3:]
    left, right = line_ends("gx", parts, True)
    writes = []
    for tile in range(out.shape[1] // LANES):
        span = tile_span(tile)
        for k in range(STEPS):
            here = at(tile, k)
            natural[spread_rows(tile, k), :] = (
                from_left[here, :] * left[:, span] + from_right[here, :] * right[:, span] + rest[here, :]
            )
        writes += tile_writes(natural, out, tile, sems)
    for write in writes:
        write.wait()


def solve_y_kernel(inv_ref, r_ref, t_ref, w_ref, s_ref, *refs, scale):
    parts, (out, natural, sems, turned) = refs[:-4], refs[-4:]
    tiles = out.shape[1] // LANES
    ends = line_ends("gy", parts)
    ends = [jnp.broadcast_to(row, (tiles * SUB, LANES)) for row in ends]
    left, right = segment_ends(*ends, w_ref, s_ref, log2(tiles * SUB))

    def store(k, speed):
        for tile in range(tiles):
            turned[spread_rows(tile, k), :] = speed[tile * SUB : (tile + 1) * SUB, :]

    march_values(left, right, t_ref, s_ref, inv_ref, scale, r_ref, store)
    writes = []
    for tile in range(tiles):
        block = turned[tile_span(tile), :].T
        for k in range(STEPS):
            natural[spread_rows(tile, k), :] = block[k * SUB : (k + 1) * SUB, :]
        writes += tile_writes(natural, out, tile, sems)
    for write in writes:
        write.wait()


def solve(kernel, name, pieces, parts, block, extra=()):
    return pl.pallas_call(
        kernel,
        out_shape=shape(*block),
        in_specs=[VMEM] * (len(pieces) + len(parts)),
        out_specs=ANY,
        scratch_shapes=write_scratch(block[1]) + list(extra),
        compiler_params=PARAMS,
        cost_estimate=pl.CostEstimate(flops=1_000_000, bytes_accessed=4_000_000, transcendentals=0),
        name=name,
    )(*pieces, *parts)


def hand_on(value, axis):
    count = lax.axis_size(axis)
    far = [(i, i + 2 if i % 2 == 0 else i - 2) for i in range(count)]
    return lax.ppermute(value, axis, [(i, t) for i, t in far if 0 <= t < count])


def shift_pair(value, axis):
    count = lax.axis_size(axis)
    other = [((i - 1) ^ 1) + 1 for i in range(count)]
    return lax.ppermute(value, axis, [(i, o if 0 <= o < count else i) for i, o in enumerate(other)])


def cross(value, axis, mask):
    return lax.ppermute(value, axis, [(i, i ^ mask) for i in range(lax.axis_size(axis))])


def crossed(value, axis, stage, half):
    pairs = []
    for i in range(lax.axis_size(axis)):
        upper = (i >> (stage + 1)) & 1
        pairs.append((i, i ^ ((2 if upper == half else 3) << stage)))
    return lax.ppermute(value, axis, pairs)


def parts_of_line(axis, mine, relay, beside=(), tall=None):
    parts = []
    last = log2(lax.axis_size(axis)) - 2
    for stage in range(last):
        theirs = cross(mine, axis, 1 << stage)
        parts += [mine, theirs]
        mine = merge_call(axis, stage, mine, theirs, beside)
    if relay:
        first = cross(mine, axis, 1 << last)
        second = cross(mine if tall is None else tall, axis, 2 << last)
        both = cross(second[:, 0 : mine.shape[1]], axis, 1 << last)
    else:
        first = cross(mine, axis, 1 << last)
        second, both = (crossed(mine, axis, last, n) for n in (1, 0))
    return parts + [mine, first, second, both]


def on_device(h, p, q, b, m):
    block = h.shape
    rows, cols = block
    inv_cx = 3.0 / (rows * lax.axis_size("gx") / 4.0) ** 2
    inv_cy = 3.0 / (cols * lax.axis_size("gy") / 4.0) ** 2
    slabs_x = pack_x(h, p, q, b, m)
    near_x = cross(slabs_x, "gx", 1)
    near_y, far_y = pack_y(h, p, q, b, m, after=slabs_x)
    near_y, far_y = cross(near_y, "gy", 1), shift_pair(far_y, "gy")
    hx, hy, ix, iy, tx, wx, ty, wy, coef_x, coef_y, left_x, right_x = prepare_depth(h, inv_cx, inv_cy)
    far_x = hand_on(second_of(near_x, coef_x, near_y), "gx")
    px, py, qx, qy, bx, by, mx, my = prepare_rest(p, q, b, m)
    depth_inner, push_inner, across_inner, faces = fluxes_x_inner(hx, px, qx, bx, mx)
    mass_y, shear_y, normal_y = fluxes_y(near_y, far_y, hy, py, qy, by, my)
    depth_outer, across_outer, rx, sx, end_x = fluxes_x(
        near_x, far_x, hx, px, qx, bx, mx, ix, shear_y, push_inner, faces, tx, wx, coef_x, inv_cx=inv_cx
    )
    depth, ry, sy, end_y, tall_y = join_y(
        depth_inner, across_inner, depth_outer, across_outer, mass_y, mx, normal_y, iy, my, ty, wy, coef_y, inv_cy=inv_cy
    )
    new_depth = write_depth(depth, block)
    parts_y = parts_of_line("gy", end_y, True, tall=tall_y if lax.axis_size("gy") == 4 else None)
    parts_x = parts_of_line("gx", end_x, False, parts_y[1:2])
    turned = [pltpu.VMEM((cols, LANES), F32)]
    solve_y_scaled = functools.partial(solve_y_kernel, scale=inv_cy)
    vy = solve(solve_y_scaled, "solve_y", (iy, ry, ty, wy, sy), parts_y, block, turned)
    own_x = rest_x(ix, rx, tx, wx, sx, scale=inv_cx)
    vx = solve(solve_x_kernel, "solve_x", (left_x, right_x, own_x), parts_x, block)
    return new_depth, vx, vy


def solution(mesh):
    spec = P("gx", "gy")
    return jax.shard_map(
        on_device,
        mesh=mesh,
        in_specs=(spec,) * 5,
        out_specs=(spec,) * 3,
        check_vma=False,
    )
```

```python
import functools

import jax
import jax.numpy as jnp
from jax import lax
from jax.experimental import pallas as pl
from jax.experimental.pallas import tpu as pltpu
from jax.sharding import PartitionSpec as P

gravity = 9.81
ratio = 0.05
LANES = 128
SUB = 8
STEPS = LANES // SUB
F32 = jnp.float32
VMEM = pl.BlockSpec(memory_space=pltpu.VMEM)
HBM = pl.BlockSpec(memory_space=pltpu.HBM)
ANY = pl.BlockSpec(memory_space=pl.ANY)
PARAMS = pltpu.CompilerParams(vmem_limit_bytes=16 * 1024 * 1024)


def lane_index(shape):
    return lax.broadcasted_iota(jnp.int32, shape, len(shape) - 1)


def row_index(shape):
    return lax.broadcasted_iota(jnp.int32, shape, len(shape) - 2)


def at(tile, step):
    first = tile * LANES + step * SUB
    return slice(first, first + SUB)


def tile_span(tile):
    return slice(tile * LANES, (tile + 1) * LANES)


def spread_rows(tile, step):
    return pl.ds(tile * LANES + step, SUB, stride=STEPS)


def shape(*dims):
    return jax.ShapeDtypeStruct(dims, F32)


def pack_x_kernel(h, p, q, b, m, slabs, top, bottom, itop, ibottom, sems):
    rows = h.shape[0]
    copies = []
    for f, src in enumerate((h, p, q, b, m)):
        for side, (target, whole, row) in enumerate(((top, itop, 0), (bottom, ibottom, rows - SUB))):
            copy = pltpu.make_async_copy(
                src.at[pl.ds(row, SUB), :], target.at[f] if f < 4 else whole, sems.at[2 * f + side]
            )
            copy.start()
            copies.append(copy)
    for copy in copies:
        copy.wait()
    first = jnp.concatenate(
        [top[0, 0:2, :], top[1, 0:2, :], top[2, 0:2, :], top[3, 0:1, :], itop[0:1, :].astype(F32)]
    )
    last = jnp.concatenate(
        [
            bottom[0, SUB - 2 : SUB, :],
            bottom[1, SUB - 2 : SUB, :],
            bottom[2, SUB - 2 : SUB, :],
            bottom[3, SUB - 1 : SUB, :],
            ibottom[SUB - 1 : SUB, :].astype(F32),
        ]
    )
    even = lax.axis_index("gx") % 2 == 0
    slabs[0] = jnp.where(even, last, first)
    slabs[1] = jnp.where(even, first, last)


def pack_x(*fields):
    cols = fields[0].shape[1]
    return pl.pallas_call(
        pack_x_kernel,
        out_shape=shape(2, SUB, cols),
        in_specs=[HBM] * 5,
        out_specs=VMEM,
        scratch_shapes=[
            pltpu.VMEM((4, SUB, cols), F32),
            pltpu.VMEM((4, SUB, cols), F32),
            pltpu.VMEM((SUB, cols), jnp.int32),
            pltpu.VMEM((SUB, cols), jnp.int32),
            pltpu.SemaphoreType.DMA((10,)),
        ],
        compiler_params=PARAMS,
        name="pack_x",
    )(*[pltpu.with_memory_space_constraint(v, pltpu.HBM) for v in fields])


def pack_y_kernel(h, p, q, b, m, _, near, far, natural):
    rows, cols = h.shape
    lane = lane_index((rows, LANES))
    out = None
    for f, src in enumerate((h, p, q, b, m)):
        both = jnp.where(lane < LANES // 2, src[:, 0:LANES], src[:, cols - LANES : cols]).astype(F32)
        moved = pltpu.roll(both, 4 * f + 2, 1)
        out = moved if out is None else jnp.where(lane >= 4 * f, moved, out)
    natural[...] = out
    turned = jnp.concatenate([natural[spread_rows(0, k), :] for k in range(STEPS)]).T
    last = jnp.concatenate([turned[0:2], turned[4:6], turned[8:10], turned[13:14], turned[17:18]])
    first = jnp.concatenate([turned[2:4], turned[6:8], turned[10:12], turned[14:15], turned[18:19]])
    even = lax.axis_index("gy") % 2 == 0
    for slab, value in ((near, jnp.where(even, last, first)), (far, jnp.where(even, first, last))):
        slab[...] = jnp.zeros_like(slab)
        slab[0:SUB, :] = value


def pack_y(*fields, after):
    rows = fields[0].shape[0]
    return pl.pallas_call(
        pack_y_kernel,
        out_shape=(shape(1 * SUB, rows), shape(4 * SUB, rows)),
        in_specs=[VMEM] * 6,
        out_specs=(VMEM, VMEM),
        scratch_shapes=[pltpu.VMEM((rows, LANES), F32)],
        compiler_params=PARAMS,
        cost_estimate=pl.CostEstimate(flops=500_000, bytes_accessed=1_000_000, transcendentals=0),
        name="pack_y",
    )(*fields, after)


def tie_kernel(both, *refs):
    refs[-1][...] = both[1]


def second_of(both, *after):
    return pl.pallas_call(
        tie_kernel,
        out_shape=shape(*both.shape[1:]),
        in_specs=[VMEM] * (1 + len(after)),
        out_specs=VMEM,
        compiler_params=PARAMS,
        name="second_of",
    )(both, *after)


def merge_coefficients(one, two):
    t1, gl1, gr1 = one
    t2, gl2, gr2 = two
    shunt = gr1 + gl2
    inverse = 1.0 / (t1 + t2 + shunt)
    w1, w2 = t1 * inverse, t2 * inverse
    return (w1 * t2, gl1 + w1 * shunt, gr2 + w2 * shunt), (w1, w2, inverse)


def merge_sources(one, two, weights):
    w1, w2, inverse = weights
    source = one[1] - two[0]
    return (one[0] - w1 * source, two[1] + w2 * source), source * inverse


def merge(one, two):
    coefficients, weights = merge_coefficients(one[:3], two[:3])
    sources, middle = merge_sources(one[3:], two[3:], weights)
    return coefficients + sources, weights[:2] + (middle,)


def log2(count):
    return (count - 1).bit_length()


def full(ref, step):
    return jnp.concatenate([ref[at(tile, step), :] for tile in range(ref.shape[0] // LANES)])


def march_depth(inv_ref, scale, out_t, out_w, levels):
    count = inv_ref.shape[0] // STEPS
    zero = jnp.zeros((count, LANES), F32)
    alpha, gamma, beta, delta = zero, zero, zero, zero
    for k in range(STEPS):
        inverse = full(inv_ref, k)
        d = scale * (inverse * inverse)
        alpha = alpha + gamma
        gamma = gamma + d * (1.0 + alpha)
        beta = beta + delta
        delta = delta + d * ((k + 1.0) + beta)
    t = 1.0 / (STEPS + beta)
    out_t[0] = t
    out_t[1] = t * alpha
    out_t[2] = 1.0 + delta
    coefficients = (t, t * alpha, t * delta)
    for level in range(levels):
        after = tuple(pltpu.roll(v, count - (1 << level), 0) for v in coefficients)
        coefficients, weights = merge_coefficients(coefficients, after)
        for j, v in enumerate(weights):
            out_w[3 * level + j] = v
    return coefficients


def lay_out(src, xs, ys, natural, turned):
    for tile in range(xs.shape[0] // LANES):
        natural[tile_span(tile), :] = src[:, tile_span(tile)].astype(F32)
        for k in range(STEPS):
            xs[at(tile, k), :] = natural[spread_rows(tile, k), :]
        turned[tile_span(tile), :] = xs[tile_span(tile), :].T
        for k in range(STEPS):
            ys[at(tile, k), :] = turned[spread_rows(tile, k), :]


def prepare_depth_kernel(
    h, hx, hy, ix, iy, tx, wx, ty, wy, endx, endy, natural, turned, *, inv_cx, inv_cy
):
    tiles = hx.shape[0] // LANES
    lay_out(h, hx, hy, natural, turned)
    ix[...] = 1.0 / hx[...]
    iy[...] = 1.0 / hy[...]
    ends_x = march_depth(ix, inv_cx, tx, wx, log2(SUB))
    ends_y = march_depth(iy, inv_cy, ty, wy, log2(SUB * tiles))
    for i in range(3):
        for tile in range(tiles):
            first = (i * tiles + tile) * LANES
            endx[0:1, first : first + LANES] = ends_x[i][tile * SUB : tile * SUB + 1, :]
        endy[0:1, i * LANES : (i + 1) * LANES] = ends_y[i][0:1, :]


def prepare_depth(h, inv_cx, inv_cy):
    stack = (h.shape[1], LANES)
    count = stack[0] // STEPS
    shapes = [shape(*stack)] * 4 + [
        shape(3, count, LANES),
        shape(3 * log2(SUB), count, LANES),
        shape(3, count, LANES),
        shape(3 * log2(count), count, LANES),
        shape(1, 3 * stack[0]),
        shape(1, 3 * LANES),
    ]
    return pl.pallas_call(
        functools.partial(prepare_depth_kernel, inv_cx=inv_cx, inv_cy=inv_cy),
        out_shape=tuple(shapes),
        in_specs=[VMEM],
        out_specs=(VMEM,) * len(shapes),
        scratch_shapes=[pltpu.VMEM(stack, F32)] * 2,
        compiler_params=PARAMS,
        cost_estimate=pl.CostEstimate(flops=2_000_000, bytes_accessed=4_000_000, transcendentals=0),
        name="prepare_depth",
    )(h)


def prepare_rest_kernel(*refs):
    fields, outs, natural, turned = refs[:4], refs[4:12], refs[12], refs[13]
    for f, src in enumerate(fields):
        lay_out(src, outs[2 * f], outs[2 * f + 1], natural.at[f % 2], turned.at[f % 2])


def prepare_rest(*fields):
    stack = (fields[0].shape[1], LANES)
    return pl.pallas_call(
        prepare_rest_kernel,
        out_shape=(shape(*stack),) * 8,
        in_specs=[VMEM] * 4,
        out_specs=(VMEM,) * 8,
        scratch_shapes=[pltpu.VMEM((2, *stack), F32)] * 2,
        compiler_params=PARAMS,
        cost_estimate=pl.CostEstimate(flops=2_000_000, bytes_accessed=6_000_000, transcendentals=0),
        name="prepare_rest",
    )(*fields)


def low_high(axis, near, far):
    index, count = lax.axis_index(axis), lax.axis_size(axis)
    even = index % 2 == 0
    low = jnp.where(index > 0, jnp.where(even, far, near), 0.0)
    high = jnp.where(index < count - 1, jnp.where(even, near, far), 0.0)
    return low, high


def half_slope(a, c):
    return 0.5 * (jnp.maximum(jnp.minimum(a, c), 0.0) + jnp.minimum(jnp.maximum(a, c), 0.0))


def face_flux(left, right, opened):
    is_open = opened > 0.5
    hl = jnp.where(is_open, left[0], 1.0)
    hr = jnp.where(is_open, right[0], 1.0)
    joint = 1.0 / (hl * hr)
    ul = left[1] * (hr * joint)
    ur = right[1] * (hl * joint)
    gl = gravity * hl
    gr = gravity * hr
    fastest = jnp.maximum(jnp.abs(ul) + gl * lax.rsqrt(gl), jnp.abs(ur) + gr * lax.rsqrt(gr))
    scale = (0.5 * ratio) * opened
    mass = (left[1] + right[1]) - fastest * (right[0] - left[0])
    push = 0.5 * (gl * hl + gr * hr) + left[1] * ul + right[1] * ur - fastest * (right[1] - left[1])
    shear = left[2] * ul + right[2] * ur - fastest * (right[2] - left[2])
    return scale * mass, scale * push, scale * shear


def extended(ref, tile, lows, highs):
    sub = row_index((SUB, LANES))
    out = {}
    for n, row in enumerate(lows, 1):
        value = ref[at(tile, STEPS - n), :]
        out[-n] = jnp.where(sub == 0, row, pltpu.roll(value, 1, 0))
    for n, row in enumerate(highs):
        value = ref[at(tile, n), :]
        out[STEPS + n] = jnp.where(sub == SUB - 1, row, pltpu.roll(value, SUB - 1, 0))
    return lambda k: out[k] if k in out else ref[at(tile, k), :]


def tile_fluxes(fields, bed, wet, store, start=0, stop=STEPS, low_face=None, high_face=None):
    def states(k):
        both = []
        for w in fields:
            here = w(k)
            both.append((here, half_slope(here - w(k - 1), w(k + 1) - here)))
        return [w + s for w, s in both], [w - s for w, s in both]

    left, before, first = None, None, None
    for k in range(start - 1, stop):
        if k == start - 1 and low_face is not None:
            face = low_face
        elif k == stop - 1 and high_face is not None:
            face = high_face
        else:
            if left is None:
                left, _ = states(k)
            left_next, right = states(k + 1)
            face = face_flux(left, right, wet(k) * wet(k + 1))
            left = left_next
        if k >= start:
            store(k, [a - c for a, c in zip(face, before)], bed(k + 1) - bed(k - 1))
        first = face if first is None else first
        before = face
    return first, before


def march_source(inv_ref, scale, r_ref, t_ref, w_ref, s_ref, levels):
    count = inv_ref.shape[0] // STEPS
    c = jnp.zeros((count, LANES), F32)
    e = c
    for k in range(STEPS):
        inverse = full(inv_ref, k)
        c = c + e
        e = e + (scale * (inverse * inverse) * c - full(r_ref, k))
    sl = t_ref[0] * c
    s_ref[0] = sl
    sources = (sl, t_ref[2] * sl - e)
    for level in range(levels):
        after = tuple(pltpu.roll(v, count - (1 << level), 0) for v in sources)
        sources, middle = merge_sources(sources, after, tuple(w_ref[3 * level + j] for j in range(3)))
        s_ref[1 + level] = middle
    return sources


def flux_y_kernel(near, far, hy, py, qy, by, my, mass, shear, normal, across, along):
    tiles = hy.shape[0] // LANES
    low, high = low_high("gy", near[0:SUB, :], far[0:SUB, :])
    for tile in range(tiles):

        def extend(ref, row, layers):
            lows, highs = [], []
            for n in range(layers):
                last = at(tile - 1, STEPS - 1 - n).stop - 1
                first = at(tile + 1, n).start
                lows.append(low[row + layers - 1 - n : row + layers - n, :] if tile == 0 else ref[last : last + 1, :])
                highs.append(high[row + n : row + n + 1, :] if tile == tiles - 1 else ref[first : first + 1, :])
            return extended(ref, tile, lows, highs)

        def store(k, difference, bed):
            here, natural = at(tile, k), spread_rows(tile, k)
            across[natural, :] = difference[0]
            along[natural, :] = difference[2]
            pull = (0.5 * ratio * gravity) * hy[here, :]
            normal[here, :] = qy[here, :] - difference[1] - pull * bed

        tile_fluxes([extend(hy, 0, 2), extend(qy, 4, 2), extend(py, 2, 2)], extend(by, 6, 1), extend(my, 7, 1), store)
        span = tile_span(tile)
        mass[span, :] = across[span, :].T
        shear[span, :] = along[span, :].T


def fluxes_y(*arrays):
    stack = arrays[2].shape
    return pl.pallas_call(
        flux_y_kernel,
        out_shape=(shape(*stack),) * 3,
        in_specs=[VMEM] * len(arrays),
        out_specs=(VMEM,) * 3,
        scratch_shapes=[pltpu.VMEM(stack, F32)] * 2,
        compiler_params=PARAMS,
        cost_estimate=pl.CostEstimate(flops=4_000_000, bytes_accessed=4_000_000, transcendentals=0),
        name="fluxes_y",
    )(*arrays)


INNER = (2, STEPS - 2)
TALL = 16


def x_store(hx, px, mx, depth, push, across):
    def of_tile(tile):
        def store(k, difference, bed):
            here = at(tile, k)
            h = hx[here, :]
            depth[here, :] = h - mx[here, :] * difference[0]
            push[here, :] = px[here, :] - difference[1] - (0.5 * ratio * gravity) * h * bed
            across[here, :] = difference[2]

        return store

    return of_tile


def flux_x_inner_kernel(hx, px, qx, bx, mx, depth, push, across, faces):
    store = x_store(hx, px, mx, depth, push, across)
    for tile in range(hx.shape[0] // LANES):
        fields = [extended(v, tile, (), ()) for v in (hx, px, qx, bx, mx)]
        ends = tile_fluxes(fields[:3], fields[3], fields[4], store(tile), *INNER)
        for n, v in enumerate(ends[0] + ends[1]):
            faces[n, tile * SUB : (tile + 1) * SUB, :] = v
        for k in (*range(INNER[0]), *range(INNER[1], STEPS)):
            for ref in (depth, push, across):
                ref[at(tile, k), :] = jnp.zeros((SUB, LANES), F32)


def fluxes_x_inner(*arrays):
    stack = arrays[0].shape
    return pl.pallas_call(
        flux_x_inner_kernel,
        out_shape=(shape(*stack),) * 3 + (shape(6, stack[0] // STEPS, LANES),),
        in_specs=[VMEM] * len(arrays),
        out_specs=(VMEM,) * 4,
        compiler_params=PARAMS,
        cost_estimate=pl.CostEstimate(flops=4_000_000, bytes_accessed=4_000_000, transcendentals=0),
        name="fluxes_x_inner",
    )(*arrays)


def flux_x_kernel(
    near, far, hx, px, qx, bx, mx, ix, shear_y, push_in, faces, tx, wx, coef,
    depth, across, rx, sx, ends,
    push,
    *, inv_cx,
):
    tiles = hx.shape[0] // LANES
    low, high = low_high("gx", near[0], far[...])
    store = x_store(hx, px, mx, depth, push, across)
    for tile in range(tiles):
        span = tile_span(tile)

        def extend(ref, row, layers):
            lows = [low[row + layers - 1 - n : row + layers - n, span] for n in range(layers)]
            highs = [high[row + n : row + n + 1, span] for n in range(layers)]
            return extended(ref, tile, lows, highs)

        fields, bed, wet = [extend(hx, 0, 2), extend(px, 2, 2), extend(qx, 4, 2)], extend(bx, 6, 1), extend(mx, 7, 1)
        known = [faces[n, tile * SUB : (tile + 1) * SUB, :] for n in range(6)]
        tile_fluxes(fields, bed, wet, store(tile), 0, INNER[0], high_face=known[:3])
        tile_fluxes(fields, bed, wet, store(tile), INNER[1], STEPS, low_face=known[3:])
        for k in range(STEPS):
            here = at(tile, k)
            inverse = ix[here, :]
            total = (push_in if INNER[0] <= k < INNER[1] else push)[here, :] - shear_y[here, :]
            rx[here, :] = (inv_cx * (inverse * inverse)) * mx[here, :] * total
    sources = march_source(ix, inv_cx, rx, tx, wx, sx, log2(SUB))
    count = tiles * LANES
    ends[0:1, 0 : 3 * count] = coef[...]
    for i in range(2):
        for tile in range(tiles):
            first = (3 + i) * count + tile * LANES
            ends[0:1, first : first + LANES] = sources[i][tile * SUB : tile * SUB + 1, :]


def fluxes_x(*arrays, inv_cx):
    stack = arrays[2].shape
    count = stack[0] // STEPS
    shapes = (
        shape(*stack),
        shape(*stack),
        shape(*stack),
        shape(1 + log2(SUB), count, LANES),
        shape(1, 5 * stack[0]),
    )
    return pl.pallas_call(
        functools.partial(flux_x_kernel, inv_cx=inv_cx),
        out_shape=shapes,
        in_specs=[VMEM] * len(arrays),
        out_specs=(VMEM,) * len(shapes),
        scratch_shapes=[pltpu.VMEM(stack, F32)],
        compiler_params=PARAMS,
        name="fluxes_x",
    )(*arrays)


def join_y_kernel(
    depth_inner, across_inner, depth_outer, across_outer, mass_y, mx, normal_y, iy, my, ty, wy, coef,
    depth, ry, sy, ends, tall,
    across, turned,
    *, inv_cy,
):
    tiles = mx.shape[0] // LANES
    for tile in range(tiles):
        span = tile_span(tile)
        for k in range(STEPS):
            here = at(tile, k)
            inner = INNER[0] <= k < INNER[1]
            across[here, :] = (across_inner if inner else across_outer)[here, :]
            depth[here, :] = (depth_inner if inner else depth_outer)[here, :] - mx[here, :] * mass_y[here, :]
        turned[span, :] = across[span, :].T
        for k in range(STEPS):
            here = at(tile, k)
            inverse = iy[here, :]
            total = normal_y[here, :] - turned[spread_rows(tile, k), :]
            ry[here, :] = (inv_cy * (inverse * inverse)) * my[here, :] * total
    sources = march_source(iy, inv_cy, ry, ty, wy, sy, log2(SUB * tiles))
    ends[0:1, 0 : 3 * LANES] = coef[...]
    for i in range(2):
        ends[0:1, (3 + i) * LANES : (4 + i) * LANES] = sources[i][0:1, :]
    tall[...] = jnp.zeros_like(tall)
    tall[0:1, 0 : 5 * LANES] = ends[...]


def join_y(*arrays, inv_cy):
    stack = arrays[0].shape
    count = stack[0] // STEPS
    shapes = (
        shape(*stack),
        shape(*stack),
        shape(1 + log2(count), count, LANES),
        shape(1, 5 * LANES),
        shape(1, TALL * LANES),
    )
    return pl.pallas_call(
        functools.partial(join_y_kernel, inv_cy=inv_cy),
        out_shape=shapes,
        in_specs=[VMEM] * len(arrays),
        out_specs=(VMEM,) * len(shapes),
        scratch_shapes=[pltpu.VMEM(stack, F32)] * 2,
        compiler_params=PARAMS,
        cost_estimate=pl.CostEstimate(flops=2_000_000, bytes_accessed=2_000_000, transcendentals=0),
        name="join_y",
    )(*arrays)


PARTS = 1


def tile_writes(tiled, whole, tile, sems):
    rows = whole.shape[0]
    part = rows // PARTS
    copies = []
    for n in range(PARTS):
        copy = pltpu.make_async_copy(
            tiled.at[pl.ds(tile * rows + n * part, part), :],
            whole.at[pl.ds(n * part, part), pl.ds(tile * LANES, LANES)],
            sems.at[tile, n],
        )
        copy.start()
        copies.append(copy)
    return copies


def write_scratch(cols):
    return [pltpu.VMEM((cols, LANES), F32), pltpu.SemaphoreType.DMA((cols // LANES, PARTS))]


def depth_kernel(depth, out, natural, sems):
    writes = []
    for tile in range(depth.shape[0] // LANES):
        for k in range(STEPS):
            natural[spread_rows(tile, k), :] = depth[at(tile, k), :]
        writes += tile_writes(natural, out, tile, sems)
    for write in writes:
        write.wait()


def write_depth(depth, block):
    return pl.pallas_call(
        depth_kernel,
        out_shape=shape(*block),
        in_specs=[VMEM],
        out_specs=ANY,
        scratch_shapes=write_scratch(block[1]),
        compiler_params=PARAMS,
        cost_estimate=pl.CostEstimate(flops=100_000, bytes_accessed=2_000_000, transcendentals=0),
        name="write_depth",
    )(depth)


def rows_of(ref, count):
    return tuple(ref[0:1, i * count : (i + 1) * count] for i in range(5))


def ordered(axis, stage, mine, theirs):
    is_low = (lax.axis_index(axis) >> stage) % 2 == 0
    one = tuple(jnp.where(is_low, a, b) for a, b in zip(mine, theirs))
    two = tuple(jnp.where(is_low, b, a) for a, b in zip(mine, theirs))
    return is_low, merge(one, two)


def merge_kernel(mine, theirs, *refs, axis, stage):
    out = refs[-1]
    count = mine.shape[1] // 5
    _, (merged, _) = ordered(axis, stage, rows_of(mine, count), rows_of(theirs, count))
    for i, v in enumerate(merged):
        out[0:1, i * v.shape[1] : (i + 1) * v.shape[1]] = v


def merge_call(axis, stage, mine, theirs, beside):
    return pl.pallas_call(
        functools.partial(merge_kernel, axis=axis, stage=stage),
        out_shape=shape(*mine.shape),
        in_specs=[VMEM] * (2 + len(beside)),
        out_specs=VMEM,
        compiler_params=PARAMS,
        name="merge",
    )(mine, theirs, *beside)


def line_ends(axis, refs, is_crossed=False):
    steps = []
    parts = [rows_of(ref, refs[0].shape[1] // 5) for ref in refs]
    stage = 0
    while len(parts) > 4:
        is_low, (_, weights) = ordered(axis, stage, *parts[:2])
        steps.append((is_low, weights))
        parts = parts[2:]
        stage += 1
    if is_crossed:
        lower = (lax.axis_index(axis) >> (stage + 1)) % 2 == 0
        both = list(zip(*parts[2:]))
        parts[2] = tuple(jnp.where(lower, a, b) for a, b in both)
        parts[3] = tuple(jnp.where(lower, b, a) for a, b in both)
    is_low, (own, weights) = ordered(axis, stage, *parts[:2])
    steps.append((is_low, weights))
    _, (other, _) = ordered(axis, stage, *parts[2:])
    is_low, (whole, weights) = ordered(axis, stage + 1, own, other)
    steps.append((is_low, weights))
    t, _, gr, _, sr = whole
    left = jnp.zeros_like(t)
    right = sr / (t + gr + 1.0)
    for is_low, (w1, w2, source) in reversed(steps):
        middle = w1 * left + w2 * right + source
        left = jnp.where(is_low, left, middle)
        right = jnp.where(is_low, middle, right)
    return left, right


def segment_ends(left, right, w_ref, s_ref, levels):
    index = row_index(left.shape)
    for level in reversed(range(levels)):
        stride = 1 << level
        middle = w_ref[3 * level] * left + w_ref[3 * level + 1] * right
        if s_ref is not None:
            middle = middle + s_ref[1 + level]
        upper = (index >> level) % 2 == 1
        left, right = (
            jnp.where(upper, pltpu.roll(middle, stride, 0), left),
            jnp.where(upper, pltpu.roll(right, stride, 0), middle),
        )
    return left, right


def march_values(left, right, t_ref, s_ref, inv_ref, scale, r_ref, store):
    value = left
    change = t_ref[0] * (right - left) - t_ref[1] * left
    if s_ref is not None:
        change = change - s_ref[0]
    for k in range(STEPS):
        inverse = full(inv_ref, k)
        value = value + change
        push = scale * (inverse * inverse) * value
        change = change + (push if r_ref is None else push - full(r_ref, k))
        store(k, value * inverse)


def rest_x_kernel(inv_ref, r_ref, t_ref, w_ref, s_ref, from_left, from_right, rest, *, scale):
    tiles = rest.shape[0] // LANES
    zero = jnp.zeros((tiles * SUB, LANES), F32)
    one = jnp.ones_like(zero)
    for out, left, right, sources, pushes in (
        (from_left, one, zero, None, None),
        (from_right, zero, one, None, None),
        (rest, zero, zero, s_ref, r_ref),
    ):

        def store(k, speed):
            for tile in range(tiles):
                out[at(tile, k), :] = speed[tile * SUB : (tile + 1) * SUB, :]

        left, right = segment_ends(left, right, w_ref, sources, log2(SUB))
        march_values(left, right, t_ref, sources, inv_ref, scale, pushes, store)


def rest_x(*pieces, scale):
    return pl.pallas_call(
        functools.partial(rest_x_kernel, scale=scale),
        out_shape=(shape(*pieces[0].shape),) * 3,
        in_specs=[VMEM] * len(pieces),
        out_specs=(VMEM,) * 3,
        compiler_params=PARAMS,
        cost_estimate=pl.CostEstimate(flops=1_000_000, bytes_accessed=2_000_000, transcendentals=0),
        name="rest_x",
    )(*pieces)


def solve_x_kernel(from_left, from_right, rest, *refs):
    parts, (out, natural, sems) = refs[:-3], refs[-3:]
    left, right = line_ends("gx", parts, True)
    writes = []
    for tile in range(out.shape[1] // LANES):
        span = tile_span(tile)
        for k in range(STEPS):
            here = at(tile, k)
            natural[spread_rows(tile, k), :] = (
                from_left[here, :] * left[:, span] + from_right[here, :] * right[:, span] + rest[here, :]
            )
        writes += tile_writes(natural, out, tile, sems)
    for write in writes:
        write.wait()


def solve_y_kernel(inv_ref, r_ref, t_ref, w_ref, s_ref, *refs, scale):
    parts, (out, natural, sems, turned) = refs[:-4], refs[-4:]
    tiles = out.shape[1] // LANES
    ends = line_ends("gy", parts)
    ends = [jnp.broadcast_to(row, (tiles * SUB, LANES)) for row in ends]
    left, right = segment_ends(*ends, w_ref, s_ref, log2(tiles * SUB))

    def store(k, speed):
        for tile in range(tiles):
            turned[spread_rows(tile, k), :] = speed[tile * SUB : (tile + 1) * SUB, :]

    march_values(left, right, t_ref, s_ref, inv_ref, scale, r_ref, store)
    writes = []
    for tile in range(tiles):
        block = turned[tile_span(tile), :].T
        for k in range(STEPS):
            natural[spread_rows(tile, k), :] = block[k * SUB : (k + 1) * SUB, :]
        writes += tile_writes(natural, out, tile, sems)
    for write in writes:
        write.wait()


def solve(kernel, name, pieces, parts, block, extra=()):
    return pl.pallas_call(
        kernel,
        out_shape=shape(*block),
        in_specs=[VMEM] * (len(pieces) + len(parts)),
        out_specs=ANY,
        scratch_shapes=write_scratch(block[1]) + list(extra),
        compiler_params=PARAMS,
        cost_estimate=pl.CostEstimate(flops=1_000_000, bytes_accessed=4_000_000, transcendentals=0),
        name=name,
    )(*pieces, *parts)


def hand_on(value, axis):
    count = lax.axis_size(axis)
    far = [i + 2 if i % 2 == 0 else i - 2 for i in range(count)]
    return lax.ppermute(value, axis, [(i, t if 0 <= t < count else i ^ 1) for i, t in enumerate(far)])


def shift_pair(value, axis):
    count = lax.axis_size(axis)
    other = [((i - 1) ^ 1) + 1 for i in range(count)]
    return lax.ppermute(value, axis, [(i, o if 0 <= o < count else i) for i, o in enumerate(other)])


def cross(value, axis, mask):
    return lax.ppermute(value, axis, [(i, i ^ mask) for i in range(lax.axis_size(axis))])


def crossed(value, axis, stage, half):
    pairs = []
    for i in range(lax.axis_size(axis)):
        upper = (i >> (stage + 1)) & 1
        pairs.append((i, i ^ ((2 if upper == half else 3) << stage)))
    return lax.ppermute(value, axis, pairs)


def parts_of_line(axis, mine, relay, beside=(), tall=None):
    parts = []
    last = log2(lax.axis_size(axis)) - 2
    for stage in range(last):
        theirs = cross(mine, axis, 1 << stage)
        parts += [mine, theirs]
        mine = merge_call(axis, stage, mine, theirs, beside)
    if relay:
        first = cross(mine, axis, 1 << last)
        second = cross(mine if tall is None else tall, axis, 2 << last)
        both = cross(second[:, 0 : mine.shape[1]], axis, 1 << last)
    else:
        first = cross(mine, axis, 1 << last)
        second, both = (crossed(mine, axis, last, n) for n in (1, 0))
    return parts + [mine, first, second, both]


def on_device(h, p, q, b, m):
    block = h.shape
    rows, cols = block
    inv_cx = 3.0 / (rows * lax.axis_size("gx") / 4.0) ** 2
    inv_cy = 3.0 / (cols * lax.axis_size("gy") / 4.0) ** 2
    slabs_x = pack_x(h, p, q, b, m)
    near_x = cross(slabs_x, "gx", 1)
    near_y, far_y = pack_y(h, p, q, b, m, after=slabs_x)
    near_y, far_y = cross(near_y, "gy", 1), shift_pair(far_y, "gy")
    hx, hy, ix, iy, tx, wx, ty, wy, coef_x, coef_y = prepare_depth(h, inv_cx, inv_cy)
    far_x = hand_on(second_of(near_x, coef_x, near_y), "gx")
    px, py, qx, qy, bx, by, mx, my = prepare_rest(p, q, b, m)
    depth_inner, push_inner, across_inner, faces = fluxes_x_inner(hx, px, qx, bx, mx)
    mass_y, shear_y, normal_y = fluxes_y(near_y, far_y, hy, py, qy, by, my)
    depth_outer, across_outer, rx, sx, end_x = fluxes_x(
        near_x, far_x, hx, px, qx, bx, mx, ix, shear_y, push_inner, faces, tx, wx, coef_x, inv_cx=inv_cx
    )
    depth, ry, sy, end_y, tall_y = join_y(
        depth_inner, across_inner, depth_outer, across_outer, mass_y, mx, normal_y, iy, my, ty, wy, coef_y, inv_cy=inv_cy
    )
    new_depth = write_depth(depth, block)
    parts_y = parts_of_line("gy", end_y, True, tall=tall_y if lax.axis_size("gy") == 4 else None)
    parts_x = parts_of_line("gx", end_x, False, parts_y[1:2])
    turned = [pltpu.VMEM((cols, LANES), F32)]
    solve_y_scaled = functools.partial(solve_y_kernel, scale=inv_cy)
    vy = solve(solve_y_scaled, "solve_y", (iy, ry, ty, wy, sy), parts_y, block, turned)
    map_x = rest_x(ix, rx, tx, wx, sx, scale=inv_cx)
    vx = solve(solve_x_kernel, "solve_x", map_x, parts_x, block)
    return new_depth, vx, vy


def solution(mesh):
    spec = P("gx", "gy")
    return jax.shard_map(
        on_device,
        mesh=mesh,
        in_specs=(spec,) * 5,
        out_specs=(spec,) * 3,
        check_vma=False,
    )
```
